32 devices in a mesh: head: 4 (over z), seg: 8 (over y, x, core).
Axes of the slice: x: 2, y: 2, z: 4, core: 2. Of those that a mesh axis runs over, the one named last changes fastest.
Arguments:
- queries: bfloat16 [8, 256, 8192], P('seg', None, 'head'), may hold values from -6 to 6
- key_rows: bfloat16 [8, 256, 8192], P('seg', None, 'head'), may hold values from -6 to 6
- values: bfloat16 [8, 256, 8192], P('seg', None, 'head'), may hold values from -36 to 36
- cotangent: bfloat16 [8, 256, 8192], P('seg', None, 'head'), may hold values from -8 to 8
- out_gain: float32 [8192], P('head'), may hold values from 0.1 to 1.9
- parent: int32 [8], replicated, may hold values from -1 to 7, as said below
- seg_len: int32 [8], P('seg'), may hold values from 64 to 256, as said below
Outputs:
- attended: bfloat16 [8, 256, 8192], P('seg', None, 'head')
- query_grad: bfloat16 [8, 256, 8192], P('seg', None, 'head')
- key_grad: bfloat16 [8, 256, 8192], P('seg', None, 'head')
- value_grad: bfloat16 [8, 256, 8192], P('seg', None, 'head')
The draws below stay inside these ranges and needn't reach their ends.
Inputs may be any that keep to these rules, and one draw needn't show every extreme that they name: Three levels: a parent is a root or the child of a root; no segment is its own ancestor. `seg_len`: at most 256 live tokens a segment; some segment is full in every draw.
All inputs are finite; a program needn't handle non-finite values.
Results may differ from the reference program's by a relative error of at most 0.013.
Values may be sent and summed in bfloat16 or wider, within the bound.
No kernel may reach another device: no remote copies, remote signals or barrier semaphores. Data moves between devices by JAX's collectives and lax.ppermute only.
A program may use at most 64 MiB of HBM per device.

```python
import math
import jax
import jax.numpy as jnp
from jax import lax

HEADS = 64
HD = 128
SEGLEN = 256
SEGS = 8


EPSILON = 1e-06


def feature_rows(subkey):
    full_shape = (SEGS, SEGLEN, HEADS * HD)
    drawn = jnp.clip(jax.random.normal(subkey, full_shape, jnp.float32), -6.0, 6.0)
    return drawn.astype(jnp.bfloat16)


def draw_queries(key, part):
    return feature_rows(jax.random.fold_in(key, 101))


def draw_key_rows(key, part):
    return feature_rows(jax.random.fold_in(key, 102))


def draw_values(key, part):
    base_key, head_key, token_key = jax.random.split(jax.random.fold_in(key, 103), 3)
    full_shape = (SEGS, SEGLEN, HEADS * HD)
    head_place = jnp.arange(HEADS, dtype=jnp.float32) / max(HEADS - 1, 1)
    baseline = jnp.clip(jax.random.normal(base_key, full_shape, jnp.float32), -6.0, 6.0)
    rising = 3.0 ** head_place
    roughness = jnp.exp(jax.random.uniform(head_key, (HEADS,), jnp.float32, 0.0, math.log(4.0)))
    head_scale = jnp.repeat(rising * roughness / 4.0, HD)
    token_scale = jnp.exp(jax.random.uniform(token_key, (SEGS, SEGLEN, 1), jnp.float32, math.log(0.2), math.log(2.0)))
    return (baseline * head_scale[None, None, :] * token_scale).astype(jnp.bfloat16)


def draw_parent(key, part):
    order_key, root_key, middle_key = jax.random.split(jax.random.fold_in(key, 105), 3)
    holder_count = SEGS
    root_count = max(1, holder_count // 8)
    middle_count = max(1, 3 * holder_count // 8)
    order = jax.random.permutation(order_key, holder_count).astype(jnp.int32)
    neighbour = ((order[0] + 1) % holder_count).astype(jnp.int32)
    ranks = jnp.arange(holder_count, dtype=jnp.int32)
    where_neighbour = jnp.sum(jnp.where(order == neighbour, ranks, 0)).astype(jnp.int32)
    displaced = order[root_count]
    order = order.at[where_neighbour].set(displaced).at[root_count].set(neighbour)
    root_pick = jax.random.randint(root_key, (holder_count,), 0, root_count).astype(jnp.int32)
    root_pick = root_pick.at[root_count].set(0)
    middle_pick = jax.random.randint(middle_key, (holder_count,), 0, middle_count).astype(jnp.int32)
    ranked = jnp.where(ranks < root_count, -1, jnp.where(ranks < root_count + middle_count, order[root_pick], order[root_count + middle_pick]))
    return jnp.zeros((holder_count,), jnp.int32).at[order].set(ranked.astype(jnp.int32))


def draw_seg_len(key, part):
    length_key, full_key = jax.random.split(jax.random.fold_in(key, 106), 2)
    lengths = jax.random.randint(length_key, (SEGS,), SEGLEN // 4, SEGLEN + 1)
    full_at = jax.random.randint(full_key, (), 0, SEGS)
    return lengths.at[full_at].set(SEGLEN).astype(jnp.int32)


def ancestor_table(parent):
    holders = jnp.arange(parent.shape[0], dtype=jnp.int32)
    matches = parent[:, None] == holders[None, :]
    grandparent = jnp.where(parent >= 0, jnp.sum(jnp.where(matches, parent[None, :], 0), axis=1), -1).astype(jnp.int32)
    return ((parent[:, None] == holders[None, :]) | (grandparent[:, None] == holders[None, :])).astype(jnp.float32)


def normed_direction(queries, key_rows, values, parent, seg_len):
    full_shape = (SEGS, SEGLEN, HEADS, HD)
    query_all = queries.reshape(full_shape).astype(jnp.float32)
    key_all = key_rows.reshape(full_shape).astype(jnp.float32)
    value_all = values.reshape(full_shape).astype(jnp.float32)
    positions = jnp.arange(SEGLEN, dtype=jnp.int32)
    live_mask = (positions[None, :] < seg_len[:, None]).astype(jnp.float32)
    ancestors = ancestor_table(parent)
    score_scale = 1.0 / math.sqrt(HD * SEGLEN)
    own_state = jnp.einsum('sthd,sthe->shde', key_all * live_mask[:, :, None, None], value_all).astype(jnp.bfloat16)
    prefix = jnp.einsum('sj,jhde->shde', ancestors, own_state.astype(jnp.float32)).astype(jnp.bfloat16)
    causal = positions[None, :] <= positions[:, None]

    def forward(operands):
        query_seg, key_seg, value_seg, prefix_seg, length, live_seg = operands
        keep = causal & (positions[None, :] < length)
        raw_scores = jnp.einsum('thd,uhd->htu', query_seg, key_seg)
        scores = jnp.where(keep[None], raw_scores, 0.0).astype(jnp.bfloat16).astype(jnp.float32)
        carried = jnp.einsum('thd,hde->the', query_seg, prefix_seg.astype(jnp.float32))
        local_part = jnp.einsum('htu,uhe->the', scores, value_seg)
        return score_scale * (carried + local_part) * live_seg[:, None, None]
    attention_out = lax.map(forward, (query_all, key_all, value_all, prefix, seg_len, live_mask))
    squares = jnp.mean(attention_out * attention_out, axis=(2, 3), keepdims=True)
    return (attention_out * lax.rsqrt(squares + EPSILON)).reshape(SEGS, SEGLEN, HEADS * HD)


def draw_cotangent(key, part):
    queries = draw_queries(key, part)
    key_rows = draw_key_rows(key, part)
    values = draw_values(key, part)
    parent = draw_parent(key, part)
    seg_len = draw_seg_len(key, part)
    direction = normed_direction(queries, key_rows, values, parent, seg_len)
    noise_key = jax.random.fold_in(key, 104)
    full_shape = (SEGS, SEGLEN, HEADS * HD)
    noise = jnp.clip(jax.random.normal(noise_key, full_shape, jnp.float32), -6.0, 6.0)
    strength = 0.75
    return jnp.clip(noise + strength * direction, -8.0, 8.0).astype(jnp.bfloat16)


def setup_inputs(seed: int = 0) -> dict:
    splits = jax.random.split(jax.random.key(seed), 8)
    return {
        "queries": draw_queries(jax.random.fold_in(splits[7], 71), 0),
        "key_rows": draw_key_rows(jax.random.fold_in(splits[7], 71), 0),
        "values": draw_values(jax.random.fold_in(splits[7], 71), 0),
        "cotangent": draw_cotangent(jax.random.fold_in(splits[7], 71), 0),
        "out_gain": jnp.clip(1.0 + 0.18 * jax.random.normal(splits[4], (HEADS * HD,), jnp.float32), 0.1, 1.9),
        "parent": draw_parent(jax.random.fold_in(splits[7], 71), 0),
        "seg_len": draw_seg_len(jax.random.fold_in(splits[7], 71), 0),
    }


EPSILON = 1e-06

def ancestry(parent):
    holders = jnp.arange(parent.shape[0], dtype=jnp.int32)
    matches = parent[:, None] == holders[None, :]
    grandparent = jnp.where(parent >= 0, lax.optimization_barrier(jnp.sum(jnp.where(matches, parent[None, :], 0), axis=1)), -1).astype(jnp.int32)
    return ((parent[:, None] == holders[None, :]) | (grandparent[:, None] == holders[None, :])).astype(jnp.float32)

def reference(queries, key_rows, values, cotangent, out_gain, parent, seg_len):
    full_shape = (SEGS, SEGLEN, HEADS, HD)
    width = HEADS * HD
    query_all = queries.reshape(full_shape).astype(jnp.float32)
    key_all = key_rows.reshape(full_shape).astype(jnp.float32)
    value_all = values.reshape(full_shape).astype(jnp.float32)
    positions = jnp.arange(SEGLEN, dtype=jnp.int32)
    live_mask = (positions[None, :] < seg_len[:, None]).astype(jnp.float32)
    ancestors = ancestry(parent)
    score_scale = 1.0 / math.sqrt(HD * SEGLEN)
    masked_keys = key_all * live_mask[:, :, None, None]
    own_state = jnp.einsum('sthd,sthe->shde', masked_keys, value_all).astype(jnp.bfloat16)
    prefix = jnp.einsum('sj,jhde->shde', ancestors, own_state.astype(jnp.float32)).astype(jnp.bfloat16)
    causal = positions[None, :] <= positions[:, None]

    def scores_of(query_seg, key_seg, length):
        keep = causal & (positions[None, :] < length)
        raw_scores = jnp.einsum('thd,uhd->htu', query_seg, key_seg)
        return (jnp.where(keep[None], raw_scores, 0.0).astype(jnp.bfloat16), keep)

    def forward(operands):
        query_seg, key_seg, value_seg, prefix_seg, length, live_seg = operands
        scores, keep = scores_of(query_seg, key_seg, length)
        carried = jnp.einsum('thd,hde->the', query_seg, prefix_seg.astype(jnp.float32))
        local_part = jnp.einsum('htu,uhe->the', scores.astype(jnp.float32), value_seg)
        return score_scale * (carried + local_part) * live_seg[:, None, None]
    attention_out = lax.map(forward, (query_all, key_all, value_all, prefix, seg_len, live_mask))
    gain = out_gain.reshape(HEADS, HD)
    squares = lax.optimization_barrier(jnp.sum(attention_out * attention_out, axis=(2, 3)))
    inverse_rms = lax.rsqrt(squares / width + EPSILON)[:, :, None, None]
    attended = (attention_out * inverse_rms * gain).astype(jnp.bfloat16).reshape(SEGS, SEGLEN, width)
    gain_grad = cotangent.reshape(full_shape).astype(jnp.float32) * gain
    inner = lax.optimization_barrier(jnp.sum(attention_out * gain_grad, axis=(2, 3)))[:, :, None, None]
    grad_out = (live_mask[:, :, None, None] * (inverse_rms * gain_grad - attention_out * inverse_rms ** 3 * inner / width)).astype(jnp.bfloat16)
    state_grad = (score_scale * jnp.einsum('sthd,sthe->shde', query_all, grad_out.astype(jnp.float32))).astype(jnp.bfloat16)
    below = jnp.einsum('js,jhde->shde', ancestors, state_grad.astype(jnp.float32)).astype(jnp.bfloat16)

    def backward(operands):
        query_seg, key_seg, value_seg, grad_seg, prefix_seg, below_seg, length, live_seg = operands
        scores, keep = scores_of(query_seg, key_seg, length)
        grad_float = grad_seg.astype(jnp.float32)
        grad_scores = jnp.where(keep[None], jnp.einsum('the,uhe->htu', grad_float, value_seg), 0.0).astype(jnp.bfloat16).astype(jnp.float32)
        prefix_float = prefix_seg.astype(jnp.float32)
        below_float = below_seg.astype(jnp.float32)
        live_col = live_seg[:, None, None]
        query_part = score_scale * (jnp.einsum('the,hde->thd', grad_float, prefix_float) + jnp.einsum('htu,uhd->thd', grad_scores, key_seg))
        key_part = score_scale * jnp.einsum('htu,thd->uhd', grad_scores, query_seg) + live_col * jnp.einsum('uhe,hde->uhd', value_seg, below_float)
        value_part = score_scale * jnp.einsum('htu,the->uhe', scores.astype(jnp.float32), grad_float) + live_col * jnp.einsum('uhd,hde->uhe', key_seg, below_float)
        return (query_part.astype(jnp.bfloat16), key_part.astype(jnp.bfloat16), value_part.astype(jnp.bfloat16))
    query_grad, key_grad, value_grad = lax.map(backward, (query_all, key_all, value_all, grad_out, prefix, below, seg_len, live_mask))
    flat_shape = (SEGS, SEGLEN, width)
    return (attended, query_grad.reshape(flat_shape), key_grad.reshape(flat_shape), value_grad.reshape(flat_shape))
```

```python
import functools
import math

import jax
import jax.numpy as jnp
from jax import lax
from jax.experimental import pallas as pl
from jax.experimental.pallas import tpu as pltpu
from jax.sharding import PartitionSpec as P

HEADS = 64
HD = 128
EPSILON = 1e-06
F32 = jnp.float32
BF16 = jnp.bfloat16
VMEM_LIMIT = 24 * 1024 * 1024

VMEM = pl.BlockSpec(memory_space=pltpu.VMEM)
SMEM = pl.BlockSpec(memory_space=pltpu.SMEM)


def dot(a, b, contract):
    return lax.dot_general(a, b, (contract, ((), ())), preferred_element_type=F32)


def nn(a, b):
    return dot(a, b, ((1,), (0,)))


def nt(a, b):
    return dot(a, b, ((1,), (1,)))


def tn(a, b):
    return dot(a, b, ((0,), (0,)))


def head_cols(head):
    return slice(head * HD, (head + 1) * HD)


def split_rows(full, outs, me):
    parts = len(outs)
    rows = full.shape[0] // parts
    for step, out in enumerate(outs):
        place = lax.rem(me + step, parts)
        out[...] = full[pl.ds(pl.multiple_of(place * rows, rows), rows), :]


def join_rows(received, full, me):
    parts = len(received)
    rows = full.shape[0] // parts
    for step, block in enumerate(received):
        place = lax.rem(me + parts - step, parts)
        full[pl.ds(pl.multiple_of(place * rows, rows), rows), :] = block[...]


def state_kernel(heads, seg_len, keys, values, *rest):
    outs, full = rest[:-1], rest[-1]
    rows = keys.shape[0]
    live = lax.broadcasted_iota(jnp.int32, (rows, HD), 0) < seg_len[0]
    for head in range(heads):
        cols = head_cols(head)
        masked = jnp.where(live, keys[:, cols], jnp.zeros((), BF16))
        full[head * HD : (head + 1) * HD, :] = tn(masked, values[:, cols]).astype(BF16)
    split_rows(full, outs, lax.axis_index("seg"))


def mix_kernel(parts, upward, parent, *refs):
    blocks, outs = refs[:parts], refs[parts:]
    me = lax.axis_index("seg")

    def is_ancestor(child, other):
        first = parent[child]
        second = jnp.where(first >= 0, parent[jnp.maximum(first, 0)], -1)
        return jnp.logical_or(other == first, other == second)

    loaded = [block[...].astype(F32) for block in blocks]
    for out_step, out in enumerate(outs):
        target = lax.rem(me + out_step, parts)
        total = jnp.zeros(out.shape, F32)
        for in_step in range(parts):
            source = lax.rem(me + parts - in_step, parts)
            if upward:
                used = is_ancestor(target, source)
            else:
                used = is_ancestor(source, target)
            total = total + jnp.where(used, 1.0, 0.0) * loaded[in_step]
        out[...] = total.astype(BF16)


def keep_mask(rows, length):
    token = lax.broadcasted_iota(jnp.int32, (rows, rows), 0)
    other = lax.broadcasted_iota(jnp.int32, (rows, rows), 1)
    return (other <= token) & (other < length)


def local_kernel(heads, seg_len, queries, keys, values, local):
    rows = keys.shape[0]
    keep = keep_mask(rows, seg_len[0])
    for head in range(heads):
        cols = head_cols(head)
        scores = jnp.where(keep, nt(queries[:, cols], keys[:, cols]), 0.0).astype(BF16)
        local[:, cols] = nn(scores, values[:, cols])


def token_rows(total):
    return jnp.sum(jnp.transpose(total), axis=0, keepdims=True)


def token_columns(row):
    return jnp.transpose(jnp.broadcast_to(row, (HD, row.shape[1])))


def carry_kernel(heads, parts, scale, seg_len, queries, local, cotangent, gain, *rest):
    received, (attention, sums, prefix) = rest[:parts], rest[parts:]
    join_rows(received, prefix, lax.axis_index("seg"))
    rows = queries.shape[0]
    live = lax.broadcasted_iota(jnp.int32, (rows, HD), 0) < seg_len[0]
    factor = jnp.where(live, scale, 0.0)
    squares = jnp.zeros((rows, HD), F32)
    products = jnp.zeros((rows, HD), F32)
    for head in range(heads):
        cols = head_cols(head)
        carried = nn(queries[:, cols], prefix[head * HD : (head + 1) * HD, :])
        out = factor * (carried + local[:, cols])
        attention[:, cols] = out
        squares += out * out
        products += out * (cotangent[:, cols].astype(F32) * gain[:, cols])
    sums[0:1, :] = token_rows(squares)
    sums[1:2, :] = token_rows(products)


def grad_kernel(heads, parts, groups, scale, seg_len, queries, attention, cotangent, gain, *rest):
    all_sums, rest = rest[:groups], rest[groups:]
    attended, grad_out = rest[:2]
    outs, full = rest[2:-1], rest[-1]
    rows = queries.shape[0]
    width = HEADS * HD
    total = all_sums[0][...]
    for other in all_sums[1:]:
        total = total + other[...]
    inverse = lax.rsqrt(total[0:1, :] / width + EPSILON)
    live = lax.broadcasted_iota(jnp.int32, (1, rows), 1) < seg_len[0]
    live_inverse = jnp.where(live, inverse, 0.0)
    shrink = live_inverse * inverse * (inverse * total[1:2, :]) / width
    inverse = token_columns(inverse)
    live_inverse = token_columns(live_inverse)
    shrink = token_columns(shrink)
    for head in range(heads):
        cols = head_cols(head)
        out = attention[:, cols]
        head_gain = gain[:, cols]
        attended[:, cols] = (out * inverse * head_gain).astype(BF16)
        gain_grad = cotangent[:, cols].astype(F32) * head_gain
        grad = (live_inverse * gain_grad - out * shrink).astype(BF16)
        grad_out[:, cols] = grad
        full[head * HD : (head + 1) * HD, :] = (scale * tn(queries[:, cols], grad)).astype(BF16)
    split_rows(full, outs, lax.axis_index("seg"))


def back_kernel(heads, parts, scale, seg_len, queries, keys, values, grad_out, *rest):
    received, (query_grad, key_part, value_part, prefix) = rest[:parts], rest[parts:]
    join_rows(received, prefix, lax.axis_index("seg"))
    rows = queries.shape[0]
    length = seg_len[0]
    keep = keep_mask(rows, length)
    other = lax.broadcasted_iota(jnp.int32, (rows, rows), 0)
    token = lax.broadcasted_iota(jnp.int32, (rows, rows), 1)
    keep_turned = (other <= token) & (other < length)
    for head in range(heads):
        cols = head_cols(head)
        query, key, value, grad = queries[:, cols], keys[:, cols], values[:, cols], grad_out[:, cols]
        grad_scores = jnp.where(keep, nt(grad, value), 0.0).astype(BF16)
        carried = nt(grad, prefix[head * HD : (head + 1) * HD, :])
        query_grad[:, cols] = (scale * (carried + nn(grad_scores, key))).astype(BF16)
        turned = jnp.where(keep_turned, nt(value, grad), 0.0).astype(BF16)
        key_part[:, cols] = scale * nn(turned, query)
        turned = jnp.where(keep_turned, nt(key, query), 0.0).astype(BF16)
        value_part[:, cols] = scale * nn(turned, grad)


def final_kernel(heads, parts, seg_len, keys, values, key_part, value_part, *rest):
    received, (key_grad, value_grad, below) = rest[:parts], rest[parts:]
    join_rows(received, below, lax.axis_index("seg"))
    rows = keys.shape[0]
    live = lax.broadcasted_iota(jnp.int32, (rows, HD), 0) < seg_len[0]
    live = jnp.where(live, 1.0, 0.0)
    for head in range(heads):
        cols = head_cols(head)
        state = below[head * HD : (head + 1) * HD, :]
        key_grad[:, cols] = (key_part[:, cols] + live * nt(values[:, cols], state)).astype(BF16)
        value_grad[:, cols] = (value_part[:, cols] + live * nn(keys[:, cols], state)).astype(BF16)


def call(kernel, out_shape, operands, scalars, scratch=(), flops=0):
    moved = sum(math.prod(x.shape) * x.dtype.itemsize for x in operands)
    moved += sum(math.prod(x.shape) * x.dtype.itemsize for x in out_shape)
    return pl.pallas_call(
        kernel,
        out_shape=out_shape,
        in_specs=[SMEM] * scalars + [VMEM] * (len(operands) - scalars),
        out_specs=[VMEM] * len(out_shape),
        scratch_shapes=list(scratch),
        compiler_params=pltpu.CompilerParams(vmem_limit_bytes=VMEM_LIMIT),
        cost_estimate=pl.CostEstimate(flops=flops, bytes_accessed=moved, transcendentals=0),
    )(*operands)


def send_around(blocks, axis):
    size = len(blocks)
    received = [blocks[0]]
    for step in range(1, size):
        pairs = [(j, (j + step) % size) for j in range(size)]
        received.append(lax.ppermute(blocks[step], axis, pairs))
    return received


def per_device(segs, groups, queries, key_rows, values, cotangent, out_gain, parent, seg_len):
    rows, features = queries.shape[1:]
    heads = features // HD
    scale = 1.0 / math.sqrt(HD * rows)
    query, key, value, cot = queries[0], key_rows[0], values[0], cotangent[0]
    gain = out_gain[None]
    shape = jax.ShapeDtypeStruct
    part_shapes = [shape((features // segs, HD), BF16)] * segs
    state_scratch = pltpu.VMEM((features, HD), BF16)
    unit = 2 * heads * rows * HD

    own = call(
        functools.partial(state_kernel, heads),
        part_shapes, (seg_len, key, value), 1, [state_scratch], unit * HD,
    )
    mixed = call(
        functools.partial(mix_kernel, segs, True), part_shapes, (parent, *send_around(own, "seg")), 1
    )
    (local,) = call(
        functools.partial(local_kernel, heads),
        [shape((rows, features), F32)], (seg_len, query, key, value), 1, (), unit * rows * 2,
    )
    prefix = send_around(mixed, "seg")
    attention, sums = call(
        functools.partial(carry_kernel, heads, segs, scale),
        [shape((rows, features), F32), shape((2, rows), F32)],
        (seg_len, query, local, cot, gain, *prefix), 1, [state_scratch], unit * HD,
    )
    all_sums = send_around([sums] * groups, "head")
    attended, grad_out, *state_grad = call(
        functools.partial(grad_kernel, heads, segs, groups, scale),
        [shape((rows, features), BF16)] * 2 + part_shapes,
        (seg_len, query, attention, cot, gain, *all_sums), 1, [state_scratch], unit * HD,
    )
    mixed = call(
        functools.partial(mix_kernel, segs, False), part_shapes, (parent, *send_around(state_grad, "seg")), 1
    )
    query_grad, key_part, value_part = call(
        functools.partial(back_kernel, heads, segs, scale),
        [shape((rows, features), BF16)] + [shape((rows, features), F32)] * 2,
        (seg_len, query, key, value, grad_out, *prefix), 1, [state_scratch], unit * (6 * rows + HD),
    )
    below = send_around(mixed, "seg")
    key_grad, value_grad = call(
        functools.partial(final_kernel, heads, segs),
        [shape((rows, features), BF16)] * 2,
        (seg_len, key, value, key_part, value_part, *below), 1, [state_scratch], 2 * unit * HD,
    )
    return attended[None], query_grad[None], key_grad[None], value_grad[None]


def solution(mesh):
    split = P("seg", None, "head")
    return jax.shard_map(
        functools.partial(per_device, mesh.shape["seg"], mesh.shape["head"]),
        mesh=mesh,
        in_specs=(split, split, split, split, P("head"), P(), P("seg")),
        out_specs=(split, split, split, split),
        check_vma=False,
    )
```

```python
import functools
import math

import jax
import jax.numpy as jnp
from jax import lax
from jax.experimental import pallas as pl
from jax.experimental.pallas import tpu as pltpu
from jax.sharding import PartitionSpec as P

HEADS = 64
HD = 128
EPSILON = 1e-06
F32 = jnp.float32
BF16 = jnp.bfloat16
VMEM_LIMIT = 24 * 1024 * 1024

VMEM = pl.BlockSpec(memory_space=pltpu.VMEM)
SMEM = pl.BlockSpec(memory_space=pltpu.SMEM)


def dot(a, b, contract):
    return lax.dot_general(a, b, (contract, ((), ())), preferred_element_type=F32)


def nn(a, b):
    return dot(a, b, ((1,), (0,)))


def nt(a, b):
    return dot(a, b, ((1,), (1,)))


def tn(a, b):
    return dot(a, b, ((0,), (0,)))


def head_cols(head):
    return slice(head * HD, (head + 1) * HD)


def state_kernel(heads, seg_len, keys, values, full):
    rows = keys.shape[0]
    live = lax.broadcasted_iota(jnp.int32, (rows, HD), 0) < seg_len[0]
    for head in range(heads):
        cols = head_cols(head)
        masked = jnp.where(live, keys[:, cols], jnp.zeros((), BF16))
        full[head * HD : (head + 1) * HD, :] = tn(masked, values[:, cols]).astype(BF16)


def mix_kernel(parts, upward, parent, blocks, outs):
    def is_ancestor(child, other):
        first = parent[child]
        second = jnp.where(first >= 0, parent[jnp.maximum(first, 0)], -1)
        return jnp.logical_or(other == first, other == second)

    rows = blocks.shape[0] // parts
    loaded = [blocks[j * rows : (j + 1) * rows, :].astype(F32) for j in range(parts)]
    for target in range(parts):
        total = jnp.zeros((rows, HD), F32)
        for source in range(parts):
            used = is_ancestor(target, source) if upward else is_ancestor(source, target)
            total = total + jnp.where(used, 1.0, 0.0) * loaded[source]
        outs[target * rows : (target + 1) * rows, :] = total.astype(BF16)


def keep_mask(rows, length):
    token = lax.broadcasted_iota(jnp.int32, (rows, rows), 0)
    other = lax.broadcasted_iota(jnp.int32, (rows, rows), 1)
    return (other <= token) & (other < length)


def local_kernel(heads, seg_len, queries, keys, values, local):
    rows = keys.shape[0]
    keep = keep_mask(rows, seg_len[0])
    for head in range(heads):
        cols = head_cols(head)
        scores = jnp.where(keep, nt(queries[:, cols], keys[:, cols]), 0.0).astype(BF16)
        local[:, cols] = nn(scores, values[:, cols])


def token_rows(total):
    return jnp.sum(jnp.transpose(total), axis=0, keepdims=True)


def token_columns(row):
    return jnp.transpose(jnp.broadcast_to(row, (HD, row.shape[1])))


def carry_kernel(heads, scale, seg_len, queries, local, cotangent, gain, prefix, attention, sums):
    rows = queries.shape[0]
    live = lax.broadcasted_iota(jnp.int32, (rows, HD), 0) < seg_len[0]
    factor = jnp.where(live, scale, 0.0)
    squares = jnp.zeros((rows, HD), F32)
    products = jnp.zeros((rows, HD), F32)
    for head in range(heads):
        cols = head_cols(head)
        carried = nn(queries[:, cols], prefix[head * HD : (head + 1) * HD, :])
        out = factor * (carried + local[:, cols])
        attention[:, cols] = out
        squares += out * out
        products += out * (cotangent[:, cols].astype(F32) * gain[:, cols])
    sums[0:1, :] = token_rows(squares)
    sums[1:2, :] = token_rows(products)


def grad_kernel(
    heads, scale, seg_len, queries, attention, cotangent, gain, all_sums, attended, grad_out, full
):
    rows = queries.shape[0]
    width = HEADS * HD
    total = all_sums[0]
    for other in range(1, all_sums.shape[0]):
        total = total + all_sums[other]
    inverse = lax.rsqrt(total[0:1, :] / width + EPSILON)
    live = lax.broadcasted_iota(jnp.int32, (1, rows), 1) < seg_len[0]
    live_inverse = jnp.where(live, inverse, 0.0)
    shrink = live_inverse * inverse * (inverse * total[1:2, :]) / width
    inverse = token_columns(inverse)
    live_inverse = token_columns(live_inverse)
    shrink = token_columns(shrink)
    for head in range(heads):
        cols = head_cols(head)
        out = attention[:, cols]
        head_gain = gain[:, cols]
        attended[:, cols] = (out * inverse * head_gain).astype(BF16)
        gain_grad = cotangent[:, cols].astype(F32) * head_gain
        grad = (live_inverse * gain_grad - out * shrink).astype(BF16)
        grad_out[:, cols] = grad
        full[head * HD : (head + 1) * HD, :] = (scale * tn(queries[:, cols], grad)).astype(BF16)


def back_kernel(
    heads, scale, seg_len, queries, keys, values, grad_out, prefix, query_grad, key_part, value_part
):
    rows = queries.shape[0]
    length = seg_len[0]
    keep = keep_mask(rows, length)
    other = lax.broadcasted_iota(jnp.int32, (rows, rows), 0)
    token = lax.broadcasted_iota(jnp.int32, (rows, rows), 1)
    keep_turned = (other <= token) & (other < length)
    for head in range(heads):
        cols = head_cols(head)
        query, key, value, grad = queries[:, cols], keys[:, cols], values[:, cols], grad_out[:, cols]
        grad_scores = jnp.where(keep, nt(grad, value), 0.0).astype(BF16)
        carried = nt(grad, prefix[head * HD : (head + 1) * HD, :])
        query_grad[:, cols] = (scale * (carried + nn(grad_scores, key))).astype(BF16)
        turned = jnp.where(keep_turned, nt(value, grad), 0.0).astype(BF16)
        key_part[:, cols] = scale * nn(turned, query)
        turned = jnp.where(keep_turned, nt(key, query), 0.0).astype(BF16)
        value_part[:, cols] = scale * nn(turned, grad)


def final_kernel(heads, seg_len, keys, values, key_part, value_part, below, key_grad, value_grad):
    rows = keys.shape[0]
    live = lax.broadcasted_iota(jnp.int32, (rows, HD), 0) < seg_len[0]
    live = jnp.where(live, 1.0, 0.0)
    for head in range(heads):
        cols = head_cols(head)
        state = below[head * HD : (head + 1) * HD, :]
        key_grad[:, cols] = (key_part[:, cols] + live * nt(values[:, cols], state)).astype(BF16)
        value_grad[:, cols] = (value_part[:, cols] + live * nn(keys[:, cols], state)).astype(BF16)


def call(kernel, out_shape, operands, scalars, scratch=(), flops=0):
    moved = sum(math.prod(x.shape) * x.dtype.itemsize for x in operands)
    moved += sum(math.prod(x.shape) * x.dtype.itemsize for x in out_shape)
    return pl.pallas_call(
        kernel,
        out_shape=out_shape,
        in_specs=[SMEM] * scalars + [VMEM] * (len(operands) - scalars),
        out_specs=[VMEM] * len(out_shape),
        scratch_shapes=list(scratch),
        compiler_params=pltpu.CompilerParams(vmem_limit_bytes=VMEM_LIMIT),
        cost_estimate=pl.CostEstimate(flops=flops, bytes_accessed=moved, transcendentals=0),
    )(*operands)


def exchange(rows, axis):
    return lax.all_to_all(rows, axis, split_axis=0, concat_axis=0, tiled=True)


def per_device(segs, groups, queries, key_rows, values, cotangent, out_gain, parent, seg_len):
    rows, features = queries.shape[1:]
    heads = features // HD
    scale = 1.0 / math.sqrt(HD * rows)
    query, key, value, cot = queries[0], key_rows[0], values[0], cotangent[0]
    gain = out_gain[None]
    shape = jax.ShapeDtypeStruct
    state = shape((features, HD), BF16)
    narrow = shape((rows, features), BF16)
    wide = shape((rows, features), F32)
    unit = 2 * heads * rows * HD

    (own,) = call(
        functools.partial(state_kernel, heads), [state], (seg_len, key, value), 1, (), unit * HD
    )
    (mixed,) = call(
        functools.partial(mix_kernel, segs, True), [state], (parent, exchange(own, "seg")), 1
    )
    (local,) = call(
        functools.partial(local_kernel, heads),
        [wide], (seg_len, query, key, value), 1, (), unit * rows * 2,
    )
    prefix = exchange(mixed, "seg")
    attention, sums = call(
        functools.partial(carry_kernel, heads, scale),
        [wide, shape((2, rows), F32)],
        (seg_len, query, local, cot, gain, prefix), 1, (), unit * HD,
    )
    all_sums = exchange(jnp.broadcast_to(sums[None], (groups, 2, rows)), "head")
    attended, grad_out, state_grad = call(
        functools.partial(grad_kernel, heads, scale),
        [narrow, narrow, state],
        (seg_len, query, attention, cot, gain, all_sums), 1, (), unit * HD,
    )
    (mixed,) = call(
        functools.partial(mix_kernel, segs, False), [state], (parent, exchange(state_grad, "seg")), 1
    )
    query_grad, key_part, value_part = call(
        functools.partial(back_kernel, heads, scale),
        [narrow, wide, wide],
        (seg_len, query, key, value, grad_out, prefix), 1, (), unit * (6 * rows + HD),
    )
    below = exchange(mixed, "seg")
    key_grad, value_grad = call(
        functools.partial(final_kernel, heads),
        [narrow, narrow],
        (seg_len, key, value, key_part, value_part, below), 1, (), 2 * unit * HD,
    )
    return attended[None], query_grad[None], key_grad[None], value_grad[None]


def solution(mesh):
    split = P("seg", None, "head")
    return jax.shard_map(
        functools.partial(per_device, mesh.shape["seg"], mesh.shape["head"]),
        mesh=mesh,
        in_specs=(split, split, split, split, P("head"), P(), P("seg")),
        out_specs=(split, split, split, split),
        check_vma=False,
    )
```

```python
import functools
import math

import jax
import jax.numpy as jnp
from jax import lax
from jax.experimental import pallas as pl
from jax.experimental.pallas import tpu as pltpu
from jax.sharding import PartitionSpec as P

HEADS = 64
HD = 128
EPSILON = 1e-06
F32 = jnp.float32
BF16 = jnp.bfloat16
VMEM_LIMIT = 24 * 1024 * 1024

VMEM = pl.BlockSpec(memory_space=pltpu.VMEM)
SMEM = pl.BlockSpec(memory_space=pltpu.SMEM)
HBM = pl.BlockSpec(memory_space=pltpu.HBM)


def dot(a, b, contract):
    return lax.dot_general(a, b, (contract, ((), ())), preferred_element_type=F32)


def nn(a, b):
    return dot(a, b, ((1,), (0,)))


def nt(a, b):
    return dot(a, b, ((1,), (1,)))


def tn(a, b):
    return dot(a, b, ((0,), (0,)))


def head_cols(head):
    return slice(head * HD, (head + 1) * HD)


def target_of(place, step, size):
    if size & (size - 1) == 0:
        return place ^ step
    return (place + step) % size


def source_of(place, step, size):
    if size & (size - 1) == 0:
        return place ^ step
    return (place + size - step) % size


def my_chip(pair):
    me = lax.axis_index("seg")
    return lax.div(me, pair), lax.rem(me, pair)


def split_rows(full, outs, chip):
    chips = len(outs)
    rows = full.shape[0] // chips
    for step, out in enumerate(outs):
        place = target_of(chip, step, chips)
        out[...] = full[pl.ds(pl.multiple_of(place * rows, rows), rows), :]


def join_rows(received, full, chip):
    chips = len(received)
    rows = full.shape[0] // chips
    for step, block in enumerate(received):
        place = source_of(chip, step, chips)
        full[pl.ds(pl.multiple_of(place * rows, rows), rows), :] = block[...]


def state_kernel(heads, pair, seg_len, keys_hbm, values_hbm, keys, values, *rest):
    outs, full, sems = rest[:-2], rest[-2], rest[-1]
    rows, features = keys.shape
    group = 2 * HD if heads % 2 == 0 else HD
    steps = features // group
    copies = []
    for step in range(steps):
        cols = slice(step * group, (step + 1) * group)
        pieces = ((keys_hbm, keys), (values_hbm, values))
        copies.append(
            [
                pltpu.make_async_copy(src.at[:, cols], dst.at[:, cols], sems.at[j, step])
                for j, (src, dst) in enumerate(pieces)
            ]
        )
    for step in copies:
        for copy in step:
            copy.start()
    live = lax.broadcasted_iota(jnp.int32, (rows, HD), 0) < seg_len[0]
    for step in range(steps):
        for copy in copies[step]:
            copy.wait()
        for head in range(step * group // HD, (step + 1) * group // HD):
            cols = head_cols(head)
            masked = jnp.where(live, keys[:, cols], jnp.zeros((), BF16))
            full[head * HD : (head + 1) * HD, :] = tn(masked, values[:, cols]).astype(BF16)
    split_rows(full, outs, my_chip(pair)[0])


def mix_kernel(chips, pair, upward, parent, *refs):
    blocks, outs, total = refs[: chips * pair], refs[chips * pair : -1], refs[-1]
    chip, core = my_chip(pair)

    def is_ancestor(child, other):
        first = parent[child]
        second = jnp.where(first >= 0, parent[jnp.maximum(first, 0)], -1)
        return jnp.logical_or(other == first, other == second)

    for out_step, out in enumerate(outs):
        target = target_of(chip, out_step, chips) * pair + core
        total[...] = jnp.zeros_like(total)
        for flip in range(pair):
            for in_step in range(chips):
                source = source_of(chip, in_step, chips) * pair + (core ^ flip)
                block = blocks[flip * chips + in_step]
                used = is_ancestor(target, source) if upward else is_ancestor(source, target)

                @pl.when(used)
                def _():
                    total[...] += block[...].astype(F32)

        out[...] = total[...].astype(BF16)


def keep_mask(rows, length):
    token = lax.broadcasted_iota(jnp.int32, (rows, rows), 0)
    other = lax.broadcasted_iota(jnp.int32, (rows, rows), 1)
    return (other <= token) & (other < length)


def local_kernel(heads, seg_len, queries, keys, values, local):
    rows = keys.shape[0]
    keep = keep_mask(rows, seg_len[0])
    for head in range(heads):
        cols = head_cols(head)
        scores = jnp.where(keep, nt(queries[:, cols], keys[:, cols]), 0.0).astype(BF16)
        local[:, cols] = nn(scores, values[:, cols])


def token_rows(total):
    return jnp.sum(jnp.transpose(total), axis=0, keepdims=True)


def token_columns(row):
    return jnp.transpose(jnp.broadcast_to(row, (HD, row.shape[1])))


def carry_kernel(heads, chips, pair, scale, seg_len, queries, local, cotangent, gain, *rest):
    received, (attention, sums, prefix) = rest[:chips], rest[chips:]
    join_rows(received, prefix, my_chip(pair)[0])
    rows = queries.shape[0]
    live = lax.broadcasted_iota(jnp.int32, (rows, HD), 0) < seg_len[0]
    factor = jnp.where(live, scale, 0.0)
    squares = jnp.zeros((rows, HD), F32)
    products = jnp.zeros((rows, HD), F32)
    for head in range(heads):
        cols = head_cols(head)
        carried = nn(queries[:, cols], prefix[head * HD : (head + 1) * HD, :])
        out = factor * (carried + local[:, cols])
        attention[:, cols] = out
        squares += out * out
        products += out * (cotangent[:, cols].astype(F32) * gain[:, cols])
    sums[0:1, :] = token_rows(squares)
    sums[1:2, :] = token_rows(products)


def grad_kernel(heads, groups, pair, scale, seg_len, queries, attention, cotangent, gain, *rest):
    all_sums, (grad_out, inverse_rms), outs, full = (
        rest[:groups], rest[groups : groups + 2], rest[groups + 2 : -1], rest[-1]
    )
    rows = queries.shape[0]
    width = HEADS * HD
    total = all_sums[0][...]
    for other in all_sums[1:]:
        total = total + other[...]
    inverse = lax.rsqrt(total[0:1, :] / width + EPSILON)
    inverse_rms[...] = inverse
    live = lax.broadcasted_iota(jnp.int32, (1, rows), 1) < seg_len[0]
    live_inverse = jnp.where(live, inverse, 0.0)
    shrink = live_inverse * inverse * (inverse * total[1:2, :]) / width
    live_inverse = token_columns(live_inverse)
    shrink = token_columns(shrink)
    for head in range(heads):
        cols = head_cols(head)
        gain_grad = cotangent[:, cols].astype(F32) * gain[:, cols]
        grad = (live_inverse * gain_grad - attention[:, cols] * shrink).astype(BF16)
        grad_out[:, cols] = grad
        full[head * HD : (head + 1) * HD, :] = (scale * tn(queries[:, cols], grad)).astype(BF16)
    split_rows(full, outs, my_chip(pair)[0])


def query_kernel(
    heads, chips, pair, scale, seg_len, keys, values, grad_out, attention, inverse_rms, gain, *rest
):
    received, (attended, query_grad, prefix) = rest[:chips], rest[chips:]
    join_rows(received, prefix, my_chip(pair)[0])
    keep = keep_mask(keys.shape[0], seg_len[0])
    inverse = token_columns(inverse_rms[...])
    for head in range(heads):
        cols = head_cols(head)
        grad = grad_out[:, cols]
        grad_scores = jnp.where(keep, nt(grad, values[:, cols]), 0.0).astype(BF16)
        carried = nt(grad, prefix[head * HD : (head + 1) * HD, :])
        query_grad[:, cols] = (scale * (carried + nn(grad_scores, keys[:, cols]))).astype(BF16)
        attended[:, cols] = (attention[:, cols] * inverse * gain[:, cols]).astype(BF16)


def back_kernel(heads, scale, seg_len, queries, keys, values, grad_out, key_part, value_part):
    rows = queries.shape[0]
    other = lax.broadcasted_iota(jnp.int32, (rows, rows), 0)
    token = lax.broadcasted_iota(jnp.int32, (rows, rows), 1)
    keep = (other <= token) & (other < seg_len[0])
    for head in range(heads):
        cols = head_cols(head)
        query, grad = queries[:, cols], grad_out[:, cols]
        turned = jnp.where(keep, nt(values[:, cols], grad), 0.0).astype(BF16)
        key_part[:, cols] = scale * nn(turned, query)
        turned = jnp.where(keep, nt(keys[:, cols], query), 0.0).astype(BF16)
        value_part[:, cols] = scale * nn(turned, grad)


def final_kernel(heads, chips, pair, seg_len, keys, values, key_part, value_part, *rest):
    received, (key_grad, value_grad, below) = rest[:chips], rest[chips:]
    join_rows(received, below, my_chip(pair)[0])
    rows = keys.shape[0]
    live = lax.broadcasted_iota(jnp.int32, (rows, HD), 0) < seg_len[0]
    live = jnp.where(live, 1.0, 0.0)
    for head in range(heads):
        cols = head_cols(head)
        state = below[head * HD : (head + 1) * HD, :]
        key_grad[:, cols] = (key_part[:, cols] + live * nt(values[:, cols], state)).astype(BF16)
        value_grad[:, cols] = (value_part[:, cols] + live * nn(keys[:, cols], state)).astype(BF16)


def call(kernel, out_shape, operands, scalars, scratch=(), flops=0, stream=0):
    moved = sum(math.prod(x.shape) * x.dtype.itemsize for x in operands)
    moved += sum(math.prod(x.shape) * x.dtype.itemsize for x in out_shape)
    return pl.pallas_call(
        kernel,
        out_shape=out_shape,
        in_specs=[SMEM] * scalars + [HBM] * stream + [VMEM] * (len(operands) - scalars - stream),
        out_specs=[VMEM] * len(out_shape),
        scratch_shapes=list(scratch),
        compiler_params=pltpu.CompilerParams(vmem_limit_bytes=VMEM_LIMIT),
        cost_estimate=pl.CostEstimate(flops=flops, bytes_accessed=moved, transcendentals=0),
    )(*operands)


def chip_sends(blocks, pair):
    chips = len(blocks)
    received = [blocks[0]]
    for step in range(1, chips):
        moves = [
            (c * pair + k, target_of(c, step, chips) * pair + k) for c in range(chips) for k in range(pair)
        ]
        received.append(lax.ppermute(blocks[step], "seg", moves))
    return received


def core_swap(blocks, pair):
    if pair == 1:
        return []
    moves = [(j, j ^ 1) for j in range(len(blocks) * pair)]
    return [lax.ppermute(block, "seg", moves) for block in blocks]


def group_sends(sums, groups):
    received = [sums]
    for step in range(1, groups):
        moves = [(j, target_of(j, step, groups)) for j in range(groups)]
        received.append(lax.ppermute(sums, "head", moves))
    return received


def per_device(segs, groups, queries, key_rows, values, cotangent, out_gain, parent, seg_len):
    rows, features = queries.shape[1:]
    heads = features // HD
    pair = 2 if segs % 2 == 0 else 1
    chips = segs // pair
    scale = 1.0 / math.sqrt(HD * rows)
    query, cot = queries[0], cotangent[0]
    gain = out_gain[None]
    shape = jax.ShapeDtypeStruct
    narrow = shape((rows, features), BF16)
    wide = shape((rows, features), F32)
    part_shapes = [shape((features // chips, HD), BF16)] * chips
    state_scratch = pltpu.VMEM((features, HD), BF16)
    mix_scratch = pltpu.VMEM((features // chips, HD), F32)
    unit = 2 * heads * rows * HD

    def exchange(parts, upward):
        arrived = chip_sends(parts, pair)
        arrived = arrived + core_swap(arrived, pair)
        mixed = call(
            functools.partial(mix_kernel, chips, pair, upward),
            part_shapes, (parent, *arrived), 1, [mix_scratch],
        )
        return chip_sends(mixed, pair)

    key, value, *own = call(
        functools.partial(state_kernel, heads, pair),
        [narrow, narrow] + part_shapes, (seg_len, key_rows[0], values[0]), 1,
        [state_scratch, pltpu.SemaphoreType.DMA((2, heads))], unit * HD, 2,
    )
    prefix = exchange(own, True)
    (local,) = call(
        functools.partial(local_kernel, heads),
        [wide], (seg_len, query, key, value), 1, (), unit * rows * 2,
    )
    attention, sums = call(
        functools.partial(carry_kernel, heads, chips, pair, scale),
        [wide, shape((2, rows), F32)],
        (seg_len, query, local, cot, gain, *prefix), 1, [state_scratch], unit * HD,
    )
    grad_out, inverse_rms, *state_grad = call(
        functools.partial(grad_kernel, heads, groups, pair, scale),
        [narrow, shape((1, rows), F32)] + part_shapes,
        (seg_len, query, attention, cot, gain, *group_sends(sums, groups)), 1, [state_scratch], unit * HD,
    )
    below = exchange(state_grad, False)
    attended, query_grad = call(
        functools.partial(query_kernel, heads, chips, pair, scale),
        [narrow, narrow],
        (seg_len, key, value, grad_out, attention, inverse_rms, gain, *prefix), 1,
        [state_scratch], unit * (2 * rows + HD),
    )
    key_part, value_part = call(
        functools.partial(back_kernel, heads, scale),
        [wide, wide], (seg_len, query, key, value, grad_out), 1, (), unit * 4 * rows,
    )
    key_grad, value_grad = call(
        functools.partial(final_kernel, heads, chips, pair),
        [narrow, narrow],
        (seg_len, key, value, key_part, value_part, *below), 1, [state_scratch], 2 * unit * HD,
    )
    return attended[None], query_grad[None], key_grad[None], value_grad[None]


def solution(mesh):
    split = P("seg", None, "head")
    return jax.shard_map(
        functools.partial(per_device, mesh.shape["seg"], mesh.shape["head"]),
        mesh=mesh,
        in_specs=(split, split, split, split, P("head"), P(), P("seg")),
        out_specs=(split, split, split, split),
        check_vma=False,
    )
```

```python
import functools
import math

import jax
import jax.numpy as jnp
from jax import lax
from jax.experimental import pallas as pl
from jax.experimental.pallas import tpu as pltpu
from jax.sharding import PartitionSpec as P

HEADS = 64
HD = 128
EPSILON = 1e-06
F32 = jnp.float32
BF16 = jnp.bfloat16
VMEM_LIMIT = 24 * 1024 * 1024

VMEM = pl.BlockSpec(memory_space=pltpu.VMEM)
SMEM = pl.BlockSpec(memory_space=pltpu.SMEM)
HBM = pl.BlockSpec(memory_space=pltpu.HBM)


def dot(a, b, contract):
    return lax.dot_general(a, b, (contract, ((), ())), preferred_element_type=F32)


def nn(a, b):
    return dot(a, b, ((1,), (0,)))


def nt(a, b):
    return dot(a, b, ((1,), (1,)))


def tn(a, b):
    return dot(a, b, ((0,), (0,)))


def head_cols(head):
    return slice(head * HD, (head + 1) * HD)


def target_of(place, step, size):
    if size & (size - 1) == 0:
        return place ^ step
    return (place + step) % size


def source_of(place, step, size):
    if size & (size - 1) == 0:
        return place ^ step
    return (place + size - step) % size


def grid_of(segs):
    pair = 2 if segs % 2 == 0 else 1
    chips = segs // pair
    columns = next(c for c in range(1, chips + 1) if chips % c == 0 and c * c >= chips)
    return chips // columns, columns, pair


def member(grid, row, column, core):
    return (row * grid[1] + column) * grid[2] + core


def place_of(grid, device):
    chip = device // grid[2]
    return chip // grid[1], chip % grid[1], device % grid[2]


def along(grid, place, step, gather, ahead):
    row, column, core = place
    shift = target_of if ahead else source_of
    by_row = (core == 0) if gather else (core != 0)
    valid_column = step < grid[1]
    valid_row = step < grid[0]
    if isinstance(core, int):
        if by_row:
            return row, shift(column, step, grid[1]), valid_column
        return shift(row, step, grid[0]), column, valid_row
    moved_column = shift(column, min(step, grid[1] - 1), grid[1])
    moved_row = shift(row, min(step, grid[0] - 1), grid[0])
    return (
        jnp.where(by_row, row, moved_row),
        jnp.where(by_row, moved_column, column),
        jnp.where(by_row, valid_column, valid_row),
    )


def my_place(grid):
    me = lax.axis_index("seg")
    chip = lax.div(me, grid[2])
    return lax.div(chip, grid[1]), lax.rem(chip, grid[1]), lax.rem(me, grid[2])


def row_halves(full, core, pair):
    half = full.shape[0] // pair
    return [full.at[pl.ds(pl.multiple_of((core ^ j) * half, half), half), :] for j in range(pair)]


def join_halves(parts, full, core, pair):
    for half, terms in zip(row_halves(full, core, pair), parts):
        total = terms[0][...].astype(F32)
        for term in terms[1:]:
            total += term[...].astype(F32)
        half[...] = total.astype(BF16)


def state_kernel(heads, grid, seg_len, keys_hbm, values_hbm, keys, values, *rest):
    outs, full, sems = rest[:-2], rest[-2], rest[-1]
    rows, features = keys.shape
    group = 2 * HD if heads % 2 == 0 else HD
    steps = features // group
    copies = []
    for step in range(steps):
        cols = slice(step * group, (step + 1) * group)
        pieces = ((keys_hbm, keys), (values_hbm, values))
        copies.append(
            [
                pltpu.make_async_copy(src.at[:, cols], dst.at[:, cols], sems.at[j, step])
                for j, (src, dst) in enumerate(pieces)
            ]
        )
    for step in copies:
        for copy in step:
            copy.start()
    live = lax.broadcasted_iota(jnp.int32, (rows, HD), 0) < seg_len[0]
    for step in range(steps):
        for copy in copies[step]:
            copy.wait()
        for head in range(step * group // HD, (step + 1) * group // HD):
            cols = head_cols(head)
            masked = jnp.where(live, keys[:, cols], jnp.zeros((), BF16))
            full[head * HD : (head + 1) * HD, :] = tn(masked, values[:, cols]).astype(BF16)
    for half, out in zip(row_halves(full, my_place(grid)[2], grid[2]), outs):
        out[...] = half[...]


def mix_kernel(grid, upward, sources, parent, *refs):
    blocks, outs = refs[:sources], refs[-line_length(grid) * grid[2] :]
    place = my_place(grid)
    pair = grid[2]

    def is_ancestor(child, other):
        first = parent[child]
        second = jnp.where(first >= 0, parent[jnp.maximum(first, 0)], -1)
        return jnp.logical_or(other == first, other == second)

    weights = []
    for out_step in range(len(outs)):
        row, column, _ = along(grid, place, out_step // pair, False, True)
        target = member(grid, row, column, place[2] ^ (out_step % pair))
        for in_step in range(sources):
            row, column, valid = along(grid, place, in_step // pair, True, False)
            source = member(grid, row, column, place[2] ^ (in_step % pair))
            used = is_ancestor(target, source) if upward else is_ancestor(source, target)
            weights.append(jnp.where(jnp.logical_and(used, valid), 1.0, 0.0))
    rows = blocks[0].shape[0]
    chunk = min(rows, 64)
    for start in range(0, rows, chunk):
        part = slice(start, start + chunk)
        loaded = [block[part, :].astype(F32) for block in blocks]
        for out_step, out in enumerate(outs):
            total = weights[out_step * sources] * loaded[0]
            for in_step in range(1, sources):
                total += weights[out_step * sources + in_step] * loaded[in_step]
            out[part, :] = total.astype(BF16)


def line_length(grid):
    return max(grid[0], grid[1])


def keep_mask(rows, length):
    token = lax.broadcasted_iota(jnp.int32, (rows, rows), 0)
    other = lax.broadcasted_iota(jnp.int32, (rows, rows), 1)
    return (other <= token) & (other < length)


def local_kernel(heads, seg_len, queries, keys, values, local):
    rows = keys.shape[0]
    keep = keep_mask(rows, seg_len[0])
    for head in range(heads):
        cols = head_cols(head)
        scores = jnp.where(keep, nt(queries[:, cols], keys[:, cols]), 0.0).astype(BF16)
        local[:, cols] = nn(scores, values[:, cols])


def token_rows(total):
    return jnp.sum(jnp.transpose(total), axis=0, keepdims=True)


def token_columns(row):
    return jnp.transpose(jnp.broadcast_to(row, (HD, row.shape[1])))


def carry_kernel(heads, grid, counts, scale, seg_len, queries, local, cotangent, gain, *rest):
    received, (attention, sums, prefix) = rest[: sum(counts)], rest[sum(counts) :]
    join_halves(by_half(received, counts), prefix, my_place(grid)[2], grid[2])
    rows = queries.shape[0]
    live = lax.broadcasted_iota(jnp.int32, (rows, HD), 0) < seg_len[0]
    factor = jnp.where(live, scale, 0.0)
    squares = jnp.zeros((rows, HD), F32)
    products = jnp.zeros((rows, HD), F32)
    for head in range(heads):
        cols = head_cols(head)
        carried = nn(queries[:, cols], prefix[head * HD : (head + 1) * HD, :])
        out = factor * (carried + local[:, cols])
        attention[:, cols] = out
        squares += out * out
        products += out * (cotangent[:, cols].astype(F32) * gain[:, cols])
    sums[0:1, :] = token_rows(squares)
    sums[1:2, :] = token_rows(products)


def grad_kernel(heads, groups, grid, scale, seg_len, queries, attention, cotangent, gain, *rest):
    all_sums, (grad_out, inverse_rms), outs, full = (
        rest[:groups], rest[groups : groups + 2], rest[groups + 2 : -1], rest[-1]
    )
    rows = queries.shape[0]
    width = HEADS * HD
    total = all_sums[0][...]
    for other in all_sums[1:]:
        total = total + other[...]
    inverse = lax.rsqrt(total[0:1, :] / width + EPSILON)
    inverse_rms[...] = inverse
    live = lax.broadcasted_iota(jnp.int32, (1, rows), 1) < seg_len[0]
    live_inverse = jnp.where(live, inverse, 0.0)
    shrink = live_inverse * inverse * (inverse * total[1:2, :]) / width
    live_inverse = token_columns(live_inverse)
    shrink = token_columns(shrink)
    for head in range(heads):
        cols = head_cols(head)
        gain_grad = cotangent[:, cols].astype(F32) * gain[:, cols]
        grad = (live_inverse * gain_grad - attention[:, cols] * shrink).astype(BF16)
        grad_out[:, cols] = grad
        full[head * HD : (head + 1) * HD, :] = (scale * tn(queries[:, cols], grad)).astype(BF16)
    for half, out in zip(row_halves(full, my_place(grid)[2], grid[2]), outs):
        out[...] = half[...]


def query_kernel(
    heads, scale, seg_len, keys, values, grad_out, attention, inverse_rms, gain, prefix, attended, query_grad
):
    keep = keep_mask(keys.shape[0], seg_len[0])
    inverse = token_columns(inverse_rms[...])
    for head in range(heads):
        cols = head_cols(head)
        grad = grad_out[:, cols]
        grad_scores = jnp.where(keep, nt(grad, values[:, cols]), 0.0).astype(BF16)
        carried = nt(grad, prefix[head * HD : (head + 1) * HD, :])
        query_grad[:, cols] = (scale * (carried + nn(grad_scores, keys[:, cols]))).astype(BF16)
        attended[:, cols] = (attention[:, cols] * inverse * gain[:, cols]).astype(BF16)


def back_kernel(heads, scale, seg_len, queries, keys, values, grad_out, key_part, value_part):
    rows = queries.shape[0]
    other = lax.broadcasted_iota(jnp.int32, (rows, rows), 0)
    token = lax.broadcasted_iota(jnp.int32, (rows, rows), 1)
    keep = (other <= token) & (other < seg_len[0])
    for head in range(heads):
        cols = head_cols(head)
        query, grad = queries[:, cols], grad_out[:, cols]
        turned = jnp.where(keep, nt(values[:, cols], grad), 0.0).astype(BF16)
        key_part[:, cols] = scale * nn(turned, query)
        turned = jnp.where(keep, nt(keys[:, cols], query), 0.0).astype(BF16)
        value_part[:, cols] = scale * nn(turned, grad)


def final_kernel(heads, grid, counts, seg_len, keys, values, key_part, value_part, *rest):
    received, (key_hbm, value_hbm, key_grad, value_grad, below, sems) = rest[: sum(counts)], rest[sum(counts) :]
    join_halves(by_half(received, counts), below, my_place(grid)[2], grid[2])
    rows = keys.shape[0]
    live = lax.broadcasted_iota(jnp.int32, (rows, HD), 0) < seg_len[0]
    live = jnp.where(live, 1.0, 0.0)
    group = 2 if heads % 2 == 0 else 1
    copies = []
    for head in range(heads):
        cols = head_cols(head)
        state = below[head * HD : (head + 1) * HD, :]
        key_grad[:, cols] = (key_part[:, cols] + live * nt(values[:, cols], state)).astype(BF16)
        value_grad[:, cols] = (value_part[:, cols] + live * nn(keys[:, cols], state)).astype(BF16)
        if (head + 1) % group == 0:
            done = slice((head + 1 - group) * HD, (head + 1) * HD)
            for j, (src, dst) in enumerate(((key_grad, key_hbm), (value_grad, value_hbm))):
                copy = pltpu.make_async_copy(src.at[:, done], dst.at[:, done], sems.at[j, head // group])
                copy.start()
                copies.append(copy)
    for copy in copies:
        copy.wait()


def call(kernel, out_shape, operands, scalars, scratch=(), flops=0, stream=0, after=(), out_specs=None):
    moved = sum(math.prod(x.shape) * x.dtype.itemsize for x in operands)
    moved += sum(math.prod(x.shape) * x.dtype.itemsize for x in out_shape)
    in_vmem = len(operands) - scalars - stream
    specs = [SMEM] * scalars + [HBM] * stream + [VMEM] * in_vmem
    return pl.pallas_call(
        kernel,
        out_shape=out_shape,
        in_specs=specs + [HBM] * len(after),
        out_specs=out_specs or [VMEM] * len(out_shape),
        scratch_shapes=list(scratch),
        compiler_params=pltpu.CompilerParams(vmem_limit_bytes=VMEM_LIMIT),
        cost_estimate=pl.CostEstimate(flops=flops, bytes_accessed=moved, transcendentals=0),
    )(*operands, *after)


def line_send(block, grid, step, flip, gather):
    moves = []
    for device in range(grid[0] * grid[1] * grid[2]):
        place = place_of(grid, device)
        if gather and flip:
            row, column, valid = along(grid, (place[0], place[1], place[2] ^ 1), step, True, True)
        else:
            row, column, valid = along(grid, place, step, gather, True)
        if valid:
            moves.append((device, member(grid, row, column, place[2] ^ flip)))
    return lax.ppermute(block, "seg", moves)


def gather_line(halves, grid):
    arrived = []
    for step in range(line_length(grid)):
        for flip in range(grid[2]):
            if step == 0 and flip == 0:
                arrived.append(halves[0])
            else:
                arrived.append(line_send(halves[flip], grid, step, flip, True))
    return arrived


def scatter_line(sums, grid):
    pair = grid[2]
    parts = [[] for _ in range(pair)]
    for step in range(line_length(grid)):
        for flip in range(pair):
            block = sums[step * pair + flip]
            if step == 0 and flip == 0:
                parts[0].append(block)
            else:
                parts[flip].append(line_send(block, grid, step, flip, False))
    return parts


def by_half(refs, counts):
    parts, at = [], 0
    for count in counts:
        parts.append(refs[at : at + count])
        at += count
    return parts


def group_sends(sums, groups):
    received = [sums]
    for step in range(1, groups):
        moves = [(j, target_of(j, step, groups)) for j in range(groups)]
        received.append(lax.ppermute(sums, "head", moves))
    return received


def per_device(segs, groups, queries, key_rows, values, cotangent, out_gain, parent, seg_len):
    rows, features = queries.shape[1:]
    heads = features // HD
    grid = grid_of(segs)
    scale = 1.0 / math.sqrt(HD * rows)
    query, cot = queries[0], cotangent[0]
    gain = out_gain[None]
    shape = jax.ShapeDtypeStruct
    narrow = shape((rows, features), BF16)
    wide = shape((rows, features), F32)
    state = shape((features, HD), BF16)
    half = shape((features // grid[2], HD), BF16)
    state_scratch = pltpu.VMEM(state.shape, BF16)
    narrow_scratch = pltpu.VMEM(narrow.shape, BF16)
    sems = pltpu.SemaphoreType.DMA((2, heads))
    members = line_length(grid) * grid[2]
    counts = [line_length(grid)] * grid[2]
    unit = 2 * heads * rows * HD

    def mix(halves, upward, after=()):
        arrived = gather_line(halves, grid)
        return call(
            functools.partial(mix_kernel, grid, upward, members),
            [half] * members, (parent, *arrived), 1, after=after,
        )

    def sums_of(parts):
        return [block for part in parts for block in part]

    key_hbm = pltpu.with_memory_space_constraint(key_rows[0], pltpu.HBM)
    value_hbm = pltpu.with_memory_space_constraint(values[0], pltpu.HBM)
    key, value, *own = call(
        functools.partial(state_kernel, heads, grid),
        [narrow, narrow] + [half] * grid[2], (seg_len, key_hbm, value_hbm), 1,
        [state_scratch, sems], unit * HD, 2,
    )
    mixed = mix(own, True)
    (local,) = call(
        functools.partial(local_kernel, heads),
        [wide], (seg_len, query, key, value), 1, (), unit * rows * 2,
    )
    attention, sums, prefix = call(
        functools.partial(carry_kernel, heads, grid, counts, scale),
        [wide, shape((2, rows), F32), state],
        (seg_len, query, local, cot, gain, *sums_of(scatter_line(mixed, grid))), 1, (), unit * HD,
    )
    grad_out, inverse_rms, *state_grad = call(
        functools.partial(grad_kernel, heads, groups, grid, scale),
        [narrow, shape((1, rows), F32)] + [half] * grid[2],
        (seg_len, query, attention, cot, gain, *group_sends(sums, groups)), 1, [state_scratch], unit * HD,
    )
    attended, query_grad = call(
        functools.partial(query_kernel, heads, scale),
        [narrow, narrow],
        (seg_len, key, value, grad_out, attention, inverse_rms, gain, prefix), 1, (),
        unit * (2 * rows + HD),
    )
    mixed = mix(state_grad, False, (pltpu.with_memory_space_constraint(attended, pltpu.HBM),))
    key_part, value_part = call(
        functools.partial(back_kernel, heads, scale),
        [wide, wide], (seg_len, query, key, value, grad_out), 1, (), unit * 4 * rows,
    )
    key_grad, value_grad = call(
        functools.partial(final_kernel, heads, grid, counts),
        [narrow, narrow],
        (seg_len, key, value, key_part, value_part, *sums_of(scatter_line(mixed, grid))), 1,
        [narrow_scratch, narrow_scratch, state_scratch, sems], 2 * unit * HD, out_specs=[HBM, HBM],
    )
    return attended[None], query_grad[None], key_grad[None], value_grad[None]


def solution(mesh):
    split = P("seg", None, "head")
    return jax.shard_map(
        functools.partial(per_device, mesh.shape["seg"], mesh.shape["head"]),
        mesh=mesh,
        in_specs=(split, split, split, split, P("head"), P(), P("seg")),
        out_specs=(split, split, split, split),
        check_vma=False,
    )
```

```python
import functools
import math

import jax
import jax.numpy as jnp
from jax import lax
from jax.experimental import pallas as pl
from jax.experimental.pallas import tpu as pltpu
from jax.sharding import PartitionSpec as P

HEADS = 64
HD = 128
EPSILON = 1e-06
F32 = jnp.float32
BF16 = jnp.bfloat16
VMEM_LIMIT = 24 * 1024 * 1024
PIECES = 2

VMEM = pl.BlockSpec(memory_space=pltpu.VMEM)
SMEM = pl.BlockSpec(memory_space=pltpu.SMEM)
HBM = pl.BlockSpec(memory_space=pltpu.HBM)
ANY = pl.BlockSpec(memory_space=pl.ANY)


def dot(a, b, contract):
    return lax.dot_general(a, b, (contract, ((), ())), preferred_element_type=F32)


def nn(a, b):
    return dot(a, b, ((1,), (0,)))


def nt(a, b):
    return dot(a, b, ((1,), (1,)))


def tn(a, b):
    return dot(a, b, ((0,), (0,)))


def head_cols(head):
    return slice(head * HD, (head + 1) * HD)


def target_of(place, step, size):
    if size & (size - 1) == 0:
        return place ^ step
    return (place + step) % size


def source_of(place, step, size):
    if size & (size - 1) == 0:
        return place ^ step
    return (place + size - step) % size


def grid_of(segs):
    pair = 2 if segs % 2 == 0 else 1
    chips = segs // pair
    columns = next(c for c in range(1, chips + 1) if chips % c == 0 and c * c >= chips)
    return chips // columns, columns, pair


def member(grid, row, column, core):
    return (row * grid[1] + column) * grid[2] + core


def place_of(grid, device):
    chip = device // grid[2]
    return chip // grid[1], chip % grid[1], device % grid[2]


def along(grid, place, step, gather, ahead):
    row, column, core = place
    shift = target_of if ahead else source_of
    by_row = (core == 0) if gather else (core != 0)
    valid_column = step < grid[1]
    valid_row = step < grid[0]
    if isinstance(core, int):
        if by_row:
            return row, shift(column, step, grid[1]), valid_column
        return shift(row, step, grid[0]), column, valid_row
    moved_column = shift(column, min(step, grid[1] - 1), grid[1])
    moved_row = shift(row, min(step, grid[0] - 1), grid[0])
    return (
        jnp.where(by_row, row, moved_row),
        jnp.where(by_row, moved_column, column),
        jnp.where(by_row, valid_column, valid_row),
    )


def my_place(grid):
    me = lax.axis_index("seg")
    chip = lax.div(me, grid[2])
    return lax.div(chip, grid[1]), lax.rem(chip, grid[1]), lax.rem(me, grid[2])


def row_halves(full, core, pair):
    half = full.shape[0] // pair
    return [full.at[pl.ds(pl.multiple_of((core ^ j) * half, half), half), :] for j in range(pair)]


def join_halves(parts, full, core, pair):
    for half, terms in zip(row_halves(full, core, pair), parts):
        total = terms[0][...].astype(F32)
        for term in terms[1:]:
            total += term[...].astype(F32)
        half[...] = total.astype(BF16)


def line_length(grid):
    return max(grid[0], grid[1])


def write_weights(grid, parent, up, down):
    place = my_place(grid)
    pair = grid[2]
    count = line_length(grid) * pair

    def is_ancestor(child, other):
        first = parent[0, child]
        second = jnp.where(first >= 0, parent[0, jnp.maximum(first, 0)], -1)
        return jnp.logical_or(other == first, other == second)

    for out_step in range(count):
        row, column, _ = along(grid, place, out_step // pair, False, True)
        target = member(grid, row, column, place[2] ^ (out_step % pair))
        for in_step in range(count):
            row, column, valid = along(grid, place, in_step // pair, True, False)
            source = member(grid, row, column, place[2] ^ (in_step % pair))
            at = out_step * count + in_step
            for rows, used in ((up, is_ancestor(target, source)), (down, is_ancestor(source, target))):
                weight = jnp.where(jnp.logical_and(used, valid), 1.0, 0.0)
                rows[at : at + 1, :] = jnp.full((1, HD), weight, F32)


def state_kernel(piece, grid, *rest):
    pair = grid[2]
    first, last = piece == 0, piece == PIECES - 1
    keys_hbm, values_hbm, seg_len = rest[:3]
    parent_hbm, rest = (rest[3], rest[4:]) if last else (None, rest[3:])
    (keys, values), halves, rest = rest[:2], rest[2 : 2 + pair], rest[2 + pair :]
    outs, (full, sems, parent, parent_sem) = rest[:-4], rest[-4:]
    rows, width = keys.shape
    chunk = rows // 4 if rows % 64 == 0 else rows
    cols = slice(piece * width, (piece + 1) * width)
    copies = []
    for step in range(rows // chunk):
        part = slice(step * chunk, (step + 1) * chunk)
        for j, (src, dst) in enumerate(((keys_hbm, keys), (values_hbm, values))):
            copies.append(pltpu.make_async_copy(src.at[part, cols], dst.at[part, :], sems.at[j, step]))
    for copy in copies:
        copy.start()
    if first:
        outs[0][...] = jnp.full(outs[0].shape, seg_len[0], jnp.int32)
    if last:
        copy = pltpu.make_async_copy(parent_hbm, parent, parent_sem)
        copy.start()
        copy.wait()
        write_weights(grid, parent, *outs[-2:])
    live = lax.broadcasted_iota(jnp.int32, (rows, HD), 0) < seg_len[0]
    for copy in copies:
        copy.wait()
    for head in range(width // HD):
        cols = head_cols(head)
        masked = jnp.where(live, keys[:, cols], jnp.zeros((), BF16))
        full[head * HD : (head + 1) * HD, :] = tn(masked, values[:, cols]).astype(BF16)
    for half, out in zip(row_halves(full, my_place(grid)[2], pair), halves):
        out[...] = half[...]


def mix_kernel(sources, weights, *refs):
    blocks, outs = refs[:sources], refs[-sources:]
    rows = blocks[0].shape[0]
    chunk = min(rows, 64)
    for start in range(0, rows, chunk):
        part = slice(start, start + chunk)
        loaded = [block[part, :].astype(F32) for block in blocks]
        for out_step, out in enumerate(outs):
            at = out_step * sources
            total = weights[at : at + 1, :] * loaded[0]
            for in_step in range(1, sources):
                total += weights[at + in_step : at + in_step + 1, :] * loaded[in_step]
            out[part, :] = total.astype(BF16)


def live_rows(length, rows):
    return lax.broadcasted_iota(jnp.int32, (rows, HD), 0) < length[:, :HD]


def keep_mask(length, turned):
    rows = length.shape[1]
    first = lax.broadcasted_iota(jnp.int32, (rows, rows), 0)
    second = lax.broadcasted_iota(jnp.int32, (rows, rows), 1)
    if turned:
        return (first <= second) & (first < length[...])
    return (second <= first) & (second < length[...])


def split_refs(refs, *counts):
    parts, at = [], 0
    for count in counts:
        parts.append(refs[at : at + count])
        at += count
    return parts


def head_of(pieces, head):
    per_piece = pieces[0].shape[1] // HD
    return pieces[head // per_piece], head_cols(head % per_piece)


def local_kernel(heads, length, queries_hbm, *rest):
    keys, values, rest = rest[:PIECES], rest[PIECES : 2 * PIECES], rest[2 * PIECES :]
    queries, local, turned, sems = rest[-4:]
    rows = length.shape[1]
    group = 4 if heads % 4 == 0 else 1
    copies = []
    for at in range(0, heads, group):
        cols = slice(at * HD, (at + group) * HD)
        copies.append(pltpu.make_async_copy(queries_hbm.at[:, cols], queries.at[:, cols], sems.at[at // group]))
    for copy in copies:
        copy.start()
    keep = keep_mask(length, False)
    keep_turned = keep_mask(length, True)
    for head in range(heads):
        if head % group == 0:
            copies[head // group].wait()
        cols = head_cols(head)
        key_piece, at = head_of(keys, head)
        key = key_piece[:, at]
        value_piece, _ = head_of(values, head)
        query = queries[:, cols]
        scores = jnp.where(keep, nt(query, key), 0.0).astype(BF16)
        local[:, cols] = nn(scores, value_piece[:, at])
        turned[head] = jnp.where(keep_turned, nt(key, query), 0.0).astype(BF16)


def token_rows(total):
    return jnp.sum(jnp.transpose(total), axis=0, keepdims=True)


def token_columns(row):
    return jnp.transpose(jnp.broadcast_to(row, (HD, row.shape[1])))


def carry_kernel(piece, grid, counts, scale, length, queries, local, cotangent, gain, *rest):
    received, rest = rest[: sum(counts)], rest[sum(counts) :]
    before, (attention, sums, prefix) = rest[:-3], rest[-3:]
    join_halves(split_refs(received, *counts), prefix, my_place(grid)[2], grid[2])
    rows, width = attention.shape
    factor = jnp.where(live_rows(length, rows), scale, 0.0)
    squares = jnp.zeros((rows, HD), F32)
    products = jnp.zeros((rows, HD), F32)
    for head in range(width // HD):
        cols = head_cols(head)
        whole = head_cols(piece * width // HD + head)
        carried = nn(queries[:, whole], prefix[head * HD : (head + 1) * HD, :])
        out = factor * (carried + local[:, whole])
        attention[:, cols] = out
        squares += out * out
        products += out * (cotangent[:, whole].astype(F32) * gain[:, whole])
    both = jnp.concatenate([token_rows(squares), token_rows(products)], axis=0)
    for other in before:
        both += other[...]
    sums[...] = both


def grad_kernel(piece, groups, grid, scale, length, queries, attention, cotangent, gain, *rest):
    all_sums, rest = rest[:groups], rest[groups:]
    (grad_out, inverse_rms), halves, full = rest[:2], rest[2:-1], rest[-1]
    rows, width = attention.shape
    features = HEADS * HD
    total = all_sums[0][...]
    for other in all_sums[1:]:
        total = total + other[...]
    inverse = lax.rsqrt(total[0:1, :] / features + EPSILON)
    inverse_rms[...] = inverse
    live = lax.broadcasted_iota(jnp.int32, (1, rows), 1) < length[...]
    live_inverse = jnp.where(live, inverse, 0.0)
    shrink = live_inverse * inverse * (inverse * total[1:2, :]) / features
    live_inverse = token_columns(live_inverse)
    shrink = token_columns(shrink)
    for head in range(width // HD):
        cols = head_cols(head)
        whole = head_cols(piece * width // HD + head)
        gain_grad = cotangent[:, whole].astype(F32) * gain[:, whole]
        grad = (live_inverse * gain_grad - attention[:, cols] * shrink).astype(BF16)
        grad_out[:, cols] = grad
        full[head * HD : (head + 1) * HD, :] = (scale * tn(queries[:, whole], grad)).astype(BF16)
    for half, out in zip(row_halves(full, my_place(grid)[2], grid[2]), halves):
        out[...] = half[...]


def query_kernel(heads, scale, length, inverse_rms, gain, *rest):
    keys, values, grads, attention, prefix, rest = split_refs(rest, *[PIECES] * 5, len(rest) - 5 * PIECES)
    attended_hbm, query_hbm, token, attended, query_grad, sems = rest[-6:]
    token[...] = jnp.zeros_like(token)
    keep = keep_mask(length, False)
    inverse = token_columns(inverse_rms[...])
    group = 4 if heads % 4 == 0 else 1
    copies = []
    for head in range(heads):
        cols = head_cols(head)
        key_piece, at = head_of(keys, head)
        value_piece, _ = head_of(values, head)
        grad_piece, _ = head_of(grads, head)
        out_piece, _ = head_of(attention, head)
        prefix_piece, state = prefix[head // (heads // PIECES)], head % (heads // PIECES)
        grad = grad_piece[:, at]
        grad_scores = jnp.where(keep, nt(grad, value_piece[:, at]), 0.0).astype(BF16)
        carried = nt(grad, prefix_piece[state * HD : (state + 1) * HD, :])
        query_grad[:, cols] = (scale * (carried + nn(grad_scores, key_piece[:, at]))).astype(BF16)
        attended[:, cols] = (out_piece[:, at] * inverse * gain[:, cols]).astype(BF16)
        if (head + 1) % group == 0:
            done = slice((head + 1 - group) * HD, (head + 1) * HD)
            for j, (src, dst) in enumerate(((attended, attended_hbm), (query_grad, query_hbm))):
                copy = pltpu.make_async_copy(src.at[:, done], dst.at[:, done], sems.at[j, head // group])
                copy.start()
                copies.append(copy)
    for copy in copies:
        copy.wait()


def back_kernel(heads, scale, length, queries, turned, *rest):
    values, grads, rest = split_refs(rest, PIECES, PIECES, len(rest) - 2 * PIECES)
    key_part, value_part = rest[-2:]
    keep = keep_mask(length, True)
    for head in range(heads):
        cols = head_cols(head)
        value_piece, at = head_of(values, head)
        grad_piece, _ = head_of(grads, head)
        grad = grad_piece[:, at]
        grad_scores = jnp.where(keep, nt(value_piece[:, at], grad), 0.0).astype(BF16)
        key_part[:, cols] = scale * nn(grad_scores, queries[:, cols])
        value_part[:, cols] = scale * nn(turned[head], grad)


def final_kernel(piece, grid, counts, length, keys, values, key_part, value_part, *rest):
    received, rest = rest[: sum(counts)], rest[sum(counts) :]
    key_hbm, value_hbm, key_grad, value_grad, below, sems = rest[-6:]
    join_halves(split_refs(received, *counts), below, my_place(grid)[2], grid[2])
    rows, width = keys.shape
    live = jnp.where(live_rows(length, rows), 1.0, 0.0)
    heads = width // HD
    group = 2 if heads % 2 == 0 else 1
    copies = []
    for head in range(heads):
        cols = head_cols(head)
        whole = head_cols(piece * heads + head)
        state = below[head * HD : (head + 1) * HD, :]
        key_grad[:, cols] = (key_part[:, whole] + live * nt(values[:, cols], state)).astype(BF16)
        value_grad[:, cols] = (value_part[:, whole] + live * nn(keys[:, cols], state)).astype(BF16)
        if (head + 1) % group == 0:
            done = slice((head + 1 - group) * HD, (head + 1) * HD)
            there = slice(piece * width + done.start, piece * width + done.stop)
            for j, (src, dst) in enumerate(((key_grad, key_hbm), (value_grad, value_hbm))):
                copy = pltpu.make_async_copy(src.at[:, done], dst.at[:, there], sems.at[j, head // group])
                copy.start()
                copies.append(copy)
    for copy in copies:
        copy.wait()


def in_hbm(x):
    return pltpu.with_memory_space_constraint(x, pltpu.HBM)


def call(kernel, out_shape, operands, scratch=(), flops=0, stream=(), scalars=(), after=(), out_specs=None, aliases=None):
    moved = sum(math.prod(x.shape) * x.dtype.itemsize for x in operands)
    moved += sum(math.prod(x.shape) * x.dtype.itemsize for x in out_shape)
    specs = [SMEM if j in scalars else HBM if j in stream else VMEM for j in range(len(operands))]
    operands = [in_hbm(x) if j in stream else x for j, x in enumerate(operands)]
    return pl.pallas_call(
        kernel,
        out_shape=out_shape,
        in_specs=specs + [ANY] * len(after),
        out_specs=out_specs or [VMEM] * len(out_shape),
        scratch_shapes=list(scratch),
        input_output_aliases=aliases or {},
        compiler_params=pltpu.CompilerParams(vmem_limit_bytes=VMEM_LIMIT),
        cost_estimate=pl.CostEstimate(flops=flops, bytes_accessed=moved, transcendentals=0),
    )(*operands, *after)


def line_send(block, grid, step, flip, gather):
    moves = []
    for device in range(grid[0] * grid[1] * grid[2]):
        place = place_of(grid, device)
        if gather and flip:
            row, column, valid = along(grid, (place[0], place[1], place[2] ^ 1), step, True, True)
        else:
            row, column, valid = along(grid, place, step, gather, True)
        if valid:
            moves.append((device, member(grid, row, column, place[2] ^ flip)))
    return lax.ppermute(block, "seg", moves)


def gather_line(halves, grid):
    arrived = []
    for step in range(line_length(grid)):
        for flip in range(grid[2]):
            if step == 0 and flip == 0:
                arrived.append(halves[0])
            else:
                arrived.append(line_send(halves[flip], grid, step, flip, True))
    return arrived


def scatter_line(sums, grid):
    pair = grid[2]
    parts = [[] for _ in range(pair)]
    for step in range(line_length(grid)):
        for flip in range(pair):
            block = sums[step * pair + flip]
            if step == 0 and flip == 0:
                parts[0].append(block)
            else:
                parts[flip].append(line_send(block, grid, step, flip, False))
    return parts


def token_sums(sums, groups):
    if groups & (groups - 1):
        moves = [[(j, (j + step) % groups) for j in range(groups)] for step in range(1, groups)]
        return [sums] + [lax.ppermute(sums, "head", pairs) for pairs in moves]
    parts = [sums]
    step = 1
    while step < groups:
        sums = parts[0] if len(parts) == 1 else parts[0] + parts[1]
        parts = [sums, lax.ppermute(sums, "head", [(j, j ^ step) for j in range(groups)])]
        step *= 2
    return parts


def per_device(segs, groups, queries, key_rows, values, cotangent, out_gain, parent, seg_len):
    rows, features = queries.shape[1:]
    heads = features // HD
    grid = grid_of(segs)
    pair = grid[2]
    scale = 1.0 / math.sqrt(HD * rows)
    cot = cotangent[0]
    gain = out_gain[None]
    shape = jax.ShapeDtypeStruct
    width = features // PIECES
    narrow = shape((rows, features), BF16)
    wide = shape((rows, features), F32)
    narrow_piece = shape((rows, width), BF16)
    wide_piece = shape((rows, width), F32)
    state = shape((width, HD), BF16)
    half = shape((width // pair, HD), BF16)
    row = shape((1, rows), F32)
    members = line_length(grid) * pair
    weight_rows = shape((members * members, HD), F32)
    state_scratch = pltpu.VMEM(state.shape, BF16)
    sems = pltpu.SemaphoreType.DMA((2, heads))
    counts = [line_length(grid)] * pair
    unit = 2 * heads * rows * HD
    every = range(PIECES)

    def mix(arrived, weights, after=()):
        return call(functools.partial(mix_kernel, members), [half] * members, (weights, *arrived), after=after)

    def flat(parts):
        return [block for part in parts for block in part]

    keys, vals, own = [], [], []
    for piece in every:
        extra = [shape((1, rows), jnp.int32)] if piece == 0 else []
        extra += [weight_rows] * 2 if piece == PIECES - 1 else []
        key, value, *rest = call(
            functools.partial(state_kernel, piece, grid),
            [narrow_piece] * 2 + [half] * pair + extra,
            (key_rows[0], values[0], seg_len) + ((parent[None],) if piece == PIECES - 1 else ()),
            [state_scratch, sems, pltpu.SMEM((1, segs), jnp.int32), pltpu.SemaphoreType.DMA(())],
            unit * HD // PIECES, (0, 1, 3), (2,),
        )
        keys.append(key)
        vals.append(value)
        own.append(rest[:pair])
        if piece == 0:
            length = rest[pair]
    up, down = rest[-2:]
    mixed = [mix(gather_line(own[piece], grid), up) for piece in every]
    query, local, turned = call(
        functools.partial(local_kernel, heads),
        [narrow, wide, shape((heads, rows, rows), BF16)],
        (length, queries[0], *keys, *vals), [pltpu.SemaphoreType.DMA((heads,))], unit * rows * 3, (1,), after=(mixed[0][0],),
    )
    attention, prefix, sums = [], [], []
    for piece in every:
        out, total, joined = call(
            functools.partial(carry_kernel, piece, grid, counts, scale),
            [wide_piece, shape((2, rows), F32), state],
            (length, query, local, cot, gain, *flat(scatter_line(mixed[piece], grid)), *sums),
            (), unit * HD // PIECES,
        )
        attention.append(out)
        prefix.append(joined)
        sums = [total]
    sums = token_sums(sums[0], groups)
    grads, state_grad = [], []
    for piece in every:
        grad_out, inverse_rms, *halves = call(
            functools.partial(grad_kernel, piece, len(sums), grid, scale),
            [narrow_piece, row] + [half] * pair,
            (length, query, attention[piece], cot, gain, *sums), [state_scratch], unit * HD // PIECES,
        )
        grads.append(grad_out)
        state_grad.append(halves)
    mixed = []
    for piece in every:
        mixed.append(mix(gather_line(state_grad[piece], grid), down, () if piece == 0 else (token,)))
        if piece == 0:
            attended, query_grad, token = call(
                functools.partial(query_kernel, heads, scale),
                [narrow, narrow, shape((8, HD), F32)],
                (length, inverse_rms, gain, *keys, *vals, *grads, *attention, *prefix),
                [pltpu.VMEM(narrow.shape, BF16)] * 2 + [sems], unit * (2 * rows + HD),
                after=(mixed[0][0],), out_specs=[HBM, HBM, VMEM],
            )
    key_part, value_part = call(
        functools.partial(back_kernel, heads, scale),
        [wide, wide], (length, query, turned, *vals, *grads), (), unit * 3 * rows, after=(mixed[-1][0],),
    )
    results = []
    for piece in every:
        below = flat(scatter_line(mixed[piece], grid))
        operands = (length, keys[piece], vals[piece], key_part, value_part, *below, *results)
        first = len(operands) - len(results)
        results = call(
            functools.partial(final_kernel, piece, grid, counts),
            [narrow, narrow], operands,
            [pltpu.VMEM(narrow_piece.shape, BF16)] * 2 + [state_scratch, sems], 2 * unit * HD // PIECES,
            range(first, len(operands)), out_specs=[HBM, HBM],
            aliases={first + j: j for j in range(len(results))},
        )
    key_grad, value_grad = results
    return attended[None], query_grad[None], key_grad[None], value_grad[None]


def solution(mesh):
    split = P("seg", None, "head")
    return jax.shard_map(
        functools.partial(per_device, mesh.shape["seg"], mesh.shape["head"]),
        mesh=mesh,
        in_specs=(split, split, split, split, P("head"), P(), P("seg")),
        out_specs=(split, split, split, split),
        check_vma=False,
    )
```

```python
import functools
import math

import jax
import jax.numpy as jnp
from jax import lax
from jax.experimental import pallas as pl
from jax.experimental.pallas import tpu as pltpu
from jax.sharding import PartitionSpec as P

HEADS = 64
HD = 128
EPSILON = 1e-06
F32 = jnp.float32
BF16 = jnp.bfloat16
VMEM_LIMIT = 24 * 1024 * 1024
FORWARD_PIECES = 2
BACKWARD_PIECES = 1

VMEM = pl.BlockSpec(memory_space=pltpu.VMEM)
SMEM = pl.BlockSpec(memory_space=pltpu.SMEM)
HBM = pl.BlockSpec(memory_space=pltpu.HBM)
ANY = pl.BlockSpec(memory_space=pl.ANY)


def dot(a, b, contract):
    return lax.dot_general(a, b, (contract, ((), ())), preferred_element_type=F32)


def nn(a, b):
    return dot(a, b, ((1,), (0,)))


def nt(a, b):
    return dot(a, b, ((1,), (1,)))


def tn(a, b):
    return dot(a, b, ((0,), (0,)))


def head_cols(head):
    return slice(head * HD, (head + 1) * HD)


def target_of(place, step, size):
    if size & (size - 1) == 0:
        return place ^ step
    return (place + step) % size


def source_of(place, step, size):
    if size & (size - 1) == 0:
        return place ^ step
    return (place + size - step) % size


def grid_of(segs):
    pair = 2 if segs % 2 == 0 else 1
    chips = segs // pair
    columns = next(c for c in range(1, chips + 1) if chips % c == 0 and c * c >= chips)
    return chips // columns, columns, pair


def member(grid, row, column, core):
    return (row * grid[1] + column) * grid[2] + core


def place_of(grid, device):
    chip = device // grid[2]
    return chip // grid[1], chip % grid[1], device % grid[2]


def along(grid, place, step, gather, ahead):
    row, column, core = place
    shift = target_of if ahead else source_of
    by_row = (core == 0) if gather else (core != 0)
    valid_column = step < grid[1]
    valid_row = step < grid[0]
    if isinstance(core, int):
        if by_row:
            return row, shift(column, step, grid[1]), valid_column
        return shift(row, step, grid[0]), column, valid_row
    moved_column = shift(column, min(step, grid[1] - 1), grid[1])
    moved_row = shift(row, min(step, grid[0] - 1), grid[0])
    return (
        jnp.where(by_row, row, moved_row),
        jnp.where(by_row, moved_column, column),
        jnp.where(by_row, valid_column, valid_row),
    )


def my_place(grid):
    me = lax.axis_index("seg")
    chip = lax.div(me, grid[2])
    return lax.div(chip, grid[1]), lax.rem(chip, grid[1]), lax.rem(me, grid[2])


def row_halves(full, core, pair):
    half = full.shape[0] // pair
    return [full.at[pl.ds(pl.multiple_of((core ^ j) * half, half), half), :] for j in range(pair)]


def join_halves(parts, full, core, pair):
    for half, terms in zip(row_halves(full, core, pair), parts):
        total = terms[0][...].astype(F32)
        for term in terms[1:]:
            total += term[...].astype(F32)
        half[...] = total.astype(BF16)


def line_length(grid):
    return max(grid[0], grid[1])


def write_weights(grid, parent, up, down):
    place = my_place(grid)
    pair = grid[2]
    count = line_length(grid) * pair

    def is_ancestor(child, other):
        first = parent[0, child]
        second = jnp.where(first >= 0, parent[0, jnp.maximum(first, 0)], -1)
        return jnp.logical_or(other == first, other == second)

    for out_step in range(count):
        row, column, _ = along(grid, place, out_step // pair, False, True)
        target = member(grid, row, column, place[2] ^ (out_step % pair))
        for in_step in range(count):
            row, column, valid = along(grid, place, in_step // pair, True, False)
            source = member(grid, row, column, place[2] ^ (in_step % pair))
            at = out_step * count + in_step
            for rows, used in ((up, is_ancestor(target, source)), (down, is_ancestor(source, target))):
                weight = jnp.where(jnp.logical_and(used, valid), 1.0, 0.0)
                rows[at : at + 1, :] = jnp.full((1, HD), weight, F32)


def write_halves(full, outs, core, pair):
    rows = full.shape[0] * pair // len(outs)
    for piece in range(len(outs) // pair):
        halves = row_halves(full.at[pl.ds(piece * rows, rows), :], core, pair)
        for half, out in zip(halves, outs[piece * pair : (piece + 1) * pair]):
            out[...] = half[...]


def state_kernel(grid, seg_len, keys_hbm, values_hbm, parent_hbm, keys, values, length, up, down, *rest):
    outs, (full, sems, parent, parent_sem) = rest[:-4], rest[-4:]
    rows, width = keys.shape
    chunk = rows // 4 if rows % 64 == 0 else rows
    copies = []
    for step in range(rows // chunk):
        part = slice(step * chunk, (step + 1) * chunk)
        for j, (src, dst) in enumerate(((keys_hbm, keys), (values_hbm, values))):
            copies.append(pltpu.make_async_copy(src.at[part, :], dst.at[part, :], sems.at[j, step]))
    few = pltpu.make_async_copy(parent_hbm, parent, parent_sem)
    few.start()
    for copy in copies:
        copy.start()
    length[...] = jnp.full(length.shape, seg_len[0], jnp.int32)
    few.wait()
    write_weights(grid, parent, up, down)
    live = lax.broadcasted_iota(jnp.int32, (rows, HD), 0) < seg_len[0]
    for copy in copies:
        copy.wait()
    for head in range(width // HD):
        cols = head_cols(head)
        masked = jnp.where(live, keys[:, cols], jnp.zeros((), BF16))
        full[head * HD : (head + 1) * HD, :] = tn(masked, values[:, cols]).astype(BF16)
    write_halves(full, outs, my_place(grid)[2], grid[2])


def mix_kernel(sources, weights, *refs):
    blocks, outs = refs[:sources], refs[-sources:]
    rows = blocks[0].shape[0]
    chunk = min(rows, 64)
    for start in range(0, rows, chunk):
        part = slice(start, start + chunk)
        loaded = [block[part, :].astype(F32) for block in blocks]
        for out_step, out in enumerate(outs):
            at = out_step * sources
            total = weights[at : at + 1, :] * loaded[0]
            for in_step in range(1, sources):
                total += weights[at + in_step : at + in_step + 1, :] * loaded[in_step]
            out[part, :] = total.astype(BF16)


def live_rows(length, rows):
    return lax.broadcasted_iota(jnp.int32, (rows, HD), 0) < length[:, :HD]


def keep_mask(length, turned):
    rows = length.shape[1]
    first = lax.broadcasted_iota(jnp.int32, (rows, rows), 0)
    second = lax.broadcasted_iota(jnp.int32, (rows, rows), 1)
    if turned:
        return (first <= second) & (first < length[...])
    return (second <= first) & (second < length[...])


def split_refs(refs, *counts):
    parts, at = [], 0
    for count in counts:
        parts.append(refs[at : at + count])
        at += count
    return parts


def head_of(pieces, head):
    per_piece = pieces[0].shape[1] // HD
    return pieces[head // per_piece], head_cols(head % per_piece)


def local_kernel(heads, length, queries_hbm, keys, values, *rest):
    queries, local, sems = rest[-3:]
    group = 4 if heads % 4 == 0 else 1
    copies = []
    for at in range(0, heads, group):
        cols = slice(at * HD, (at + group) * HD)
        copies.append(pltpu.make_async_copy(queries_hbm.at[:, cols], queries.at[:, cols], sems.at[at // group]))
    for copy in copies:
        copy.start()
    keep = keep_mask(length, False)
    for head in range(heads):
        if head % group == 0:
            copies[head // group].wait()
        cols = head_cols(head)
        scores = jnp.where(keep, nt(queries[:, cols], keys[:, cols]), 0.0).astype(BF16)
        local[:, cols] = nn(scores, values[:, cols])


def token_rows(total):
    return jnp.sum(jnp.transpose(total), axis=0, keepdims=True)


def token_columns(row):
    return jnp.transpose(jnp.broadcast_to(row, (HD, row.shape[1])))


def carry_kernel(piece, grid, counts, scale, length, queries, local, cotangent, gain, *rest):
    received, rest = rest[: sum(counts)], rest[sum(counts) :]
    before, (attention, sums, prefix) = rest[:-3], rest[-3:]
    join_halves(split_refs(received, *counts), prefix, my_place(grid)[2], grid[2])
    rows, width = attention.shape
    factor = jnp.where(live_rows(length, rows), scale, 0.0)
    squares = jnp.zeros((rows, HD), F32)
    products = jnp.zeros((rows, HD), F32)
    for head in range(width // HD):
        cols = head_cols(head)
        whole = head_cols(piece * width // HD + head)
        carried = nn(queries[:, whole], prefix[head * HD : (head + 1) * HD, :])
        out = factor * (carried + local[:, whole])
        attention[:, cols] = out
        squares += out * out
        products += out * (cotangent[:, whole].astype(F32) * gain[:, whole])
    both = jnp.concatenate([token_rows(squares), token_rows(products)], axis=0)
    for other in before:
        both += other[...]
    sums[...] = both


def grad_kernel(piece, groups, grid, scale, length, queries, cotangent, gain, *rest):
    all_sums, attention, rest = split_refs(rest, groups, FORWARD_PIECES, len(rest) - groups - FORWARD_PIECES)
    (grad_out, inverse_rms), halves, full = rest[:2], rest[2:-1], rest[-1]
    rows, width = grad_out.shape
    features = HEADS * HD
    total = all_sums[0][...]
    for other in all_sums[1:]:
        total = total + other[...]
    inverse = lax.rsqrt(total[0:1, :] / features + EPSILON)
    inverse_rms[...] = inverse
    live = lax.broadcasted_iota(jnp.int32, (1, rows), 1) < length[...]
    live_inverse = jnp.where(live, inverse, 0.0)
    shrink = live_inverse * inverse * (inverse * total[1:2, :]) / features
    live_inverse = token_columns(live_inverse)
    shrink = token_columns(shrink)
    for head in range(width // HD):
        cols = head_cols(head)
        place = piece * width // HD + head
        whole = head_cols(place)
        out_piece, at = head_of(attention, place)
        gain_grad = cotangent[:, whole].astype(F32) * gain[:, whole]
        grad = (live_inverse * gain_grad - out_piece[:, at] * shrink).astype(BF16)
        grad_out[:, cols] = grad
        full[head * HD : (head + 1) * HD, :] = (scale * tn(queries[:, whole], grad)).astype(BF16)
    write_halves(full, halves, my_place(grid)[2], grid[2])


def query_kernel(heads, scale, length, inverse_rms, gain, keys, values, *rest):
    sizes = (BACKWARD_PIECES, FORWARD_PIECES, FORWARD_PIECES)
    grads, attention, prefix, rest = split_refs(rest, *sizes, len(rest) - sum(sizes))
    attended_hbm, query_hbm, token, attended, query_grad, sems = rest[-6:]
    token[...] = jnp.zeros_like(token)
    keep = keep_mask(length, False)
    inverse = token_columns(inverse_rms[...])
    group = 8 if heads % 8 == 0 else 1
    copies = []
    for head in range(heads):
        cols = head_cols(head)
        grad_piece, at = head_of(grads, head)
        grad = grad_piece[:, at]
        out_piece, at = head_of(attention, head)
        per_piece = heads // FORWARD_PIECES
        prefix_piece, state = prefix[head // per_piece], head % per_piece
        grad_scores = jnp.where(keep, nt(grad, values[:, cols]), 0.0).astype(BF16)
        carried = nt(grad, prefix_piece[state * HD : (state + 1) * HD, :])
        query_grad[:, cols] = (scale * (carried + nn(grad_scores, keys[:, cols]))).astype(BF16)
        attended[:, cols] = (out_piece[:, at] * inverse * gain[:, cols]).astype(BF16)
        if (head + 1) % group == 0:
            done = slice((head + 1 - group) * HD, (head + 1) * HD)
            for j, (src, dst) in enumerate(((attended, attended_hbm), (query_grad, query_hbm))):
                copy = pltpu.make_async_copy(src.at[:, done], dst.at[:, done], sems.at[j, head // group])
                copy.start()
                copies.append(copy)
    for copy in copies:
        copy.wait()


def back_kernel(heads, scale, length, queries, keys, values, *rest):
    grads, (key_part, value_part) = rest[:BACKWARD_PIECES], rest[-2:]
    keep = keep_mask(length, True)
    for head in range(heads):
        cols = head_cols(head)
        grad_piece, at = head_of(grads, head)
        query, grad = queries[:, cols], grad_piece[:, at]
        turned = jnp.where(keep, nt(values[:, cols], grad), 0.0).astype(BF16)
        key_part[:, cols] = scale * nn(turned, query)
        turned = jnp.where(keep, nt(keys[:, cols], query), 0.0).astype(BF16)
        value_part[:, cols] = scale * nn(turned, grad)


def final_kernel(piece, grid, counts, length, keys, values, key_part, value_part, *rest):
    received, rest = rest[: sum(counts)], rest[sum(counts) :]
    key_hbm, value_hbm, key_grad, value_grad, below, sems = rest[-6:]
    join_halves(split_refs(received, *counts), below, my_place(grid)[2], grid[2])
    rows, width = key_grad.shape
    live = jnp.where(live_rows(length, rows), 1.0, 0.0)
    heads = width // HD
    group = 2 if heads % 2 == 0 else 1
    copies = []
    for head in range(heads):
        cols = head_cols(head)
        whole = head_cols(piece * heads + head)
        state = below[head * HD : (head + 1) * HD, :]
        key_grad[:, cols] = (key_part[:, whole] + live * nt(values[:, whole], state)).astype(BF16)
        value_grad[:, cols] = (value_part[:, whole] + live * nn(keys[:, whole], state)).astype(BF16)
        if (head + 1) % group == 0:
            done = slice((head + 1 - group) * HD, (head + 1) * HD)
            there = slice(piece * width + done.start, piece * width + done.stop)
            for j, (src, dst) in enumerate(((key_grad, key_hbm), (value_grad, value_hbm))):
                copy = pltpu.make_async_copy(src.at[:, done], dst.at[:, there], sems.at[j, head // group])
                copy.start()
                copies.append(copy)
    for copy in copies:
        copy.wait()


def in_hbm(x):
    return pltpu.with_memory_space_constraint(x, pltpu.HBM)


def call(kernel, out_shape, operands, scratch=(), flops=0, stream=(), scalars=(), after=(), out_specs=None, aliases=None):
    moved = sum(math.prod(x.shape) * x.dtype.itemsize for x in operands)
    moved += sum(math.prod(x.shape) * x.dtype.itemsize for x in out_shape)
    specs = [SMEM if j in scalars else HBM if j in stream else VMEM for j in range(len(operands))]
    operands = [in_hbm(x) if j in stream else x for j, x in enumerate(operands)]
    return pl.pallas_call(
        kernel,
        out_shape=out_shape,
        in_specs=specs + [ANY] * len(after),
        out_specs=out_specs or [VMEM] * len(out_shape),
        scratch_shapes=list(scratch),
        input_output_aliases=aliases or {},
        compiler_params=pltpu.CompilerParams(vmem_limit_bytes=VMEM_LIMIT),
        cost_estimate=pl.CostEstimate(flops=flops, bytes_accessed=moved, transcendentals=0),
    )(*operands, *after)


def line_send(block, grid, step, flip, gather):
    moves = []
    for device in range(grid[0] * grid[1] * grid[2]):
        place = place_of(grid, device)
        if gather and flip:
            row, column, valid = along(grid, (place[0], place[1], place[2] ^ 1), step, True, True)
        else:
            row, column, valid = along(grid, place, step, gather, True)
        if valid:
            moves.append((device, member(grid, row, column, place[2] ^ flip)))
    return lax.ppermute(block, "seg", moves)


def gather_line(halves, grid):
    arrived = []
    for step in range(line_length(grid)):
        for flip in range(grid[2]):
            if step == 0 and flip == 0:
                arrived.append(halves[0])
            else:
                arrived.append(line_send(halves[flip], grid, step, flip, True))
    return arrived


def scatter_line(sums, grid):
    pair = grid[2]
    parts = [[] for _ in range(pair)]
    for step in range(line_length(grid)):
        for flip in range(pair):
            block = sums[step * pair + flip]
            if step == 0 and flip == 0:
                parts[0].append(block)
            else:
                parts[flip].append(line_send(block, grid, step, flip, False))
    return parts


def token_sums(sums, groups):
    parts = [sums]
    for step in range(1, groups):
        moves = [(j, target_of(j, step, groups)) for j in range(groups)]
        parts.append(lax.ppermute(sums, "head", moves))
    return parts


def per_device(segs, groups, queries, key_rows, values, cotangent, out_gain, parent, seg_len):
    rows, features = queries.shape[1:]
    heads = features // HD
    grid = grid_of(segs)
    pair = grid[2]
    scale = 1.0 / math.sqrt(HD * rows)
    cot = cotangent[0]
    gain = out_gain[None]
    shape = jax.ShapeDtypeStruct
    narrow = shape((rows, features), BF16)
    wide = shape((rows, features), F32)
    row = shape((1, rows), F32)
    members = line_length(grid) * pair
    weight_rows = shape((members * members, HD), F32)
    sems = pltpu.SemaphoreType.DMA((2, heads))
    counts = [line_length(grid)] * pair
    unit = 2 * heads * rows * HD

    def halves(pieces):
        return [shape((features // (pair * pieces), HD), BF16)] * pair

    def mix(arrived, weights, after=()):
        like = [shape(arrived[0].shape, BF16)] * members
        return call(functools.partial(mix_kernel, members), like, (weights, *arrived), after=after)

    def flat(parts):
        return [block for part in parts for block in part]

    key, value, length, up, down, *own = call(
        functools.partial(state_kernel, grid),
        [narrow, narrow, shape((1, rows), jnp.int32), weight_rows, weight_rows] + halves(FORWARD_PIECES) * FORWARD_PIECES,
        (seg_len, key_rows[0], values[0], parent[None]),
        [pltpu.VMEM((features, HD), BF16), sems, pltpu.SMEM((1, segs), jnp.int32), pltpu.SemaphoreType.DMA(())],
        unit * HD, (1, 2, 3), (0,),
    )
    mixed = [mix(gather_line(part, grid), up) for part in split_refs(own, *[pair] * FORWARD_PIECES)]
    query, local = call(
        functools.partial(local_kernel, heads),
        [narrow, wide],
        (length, queries[0], key, value), [pltpu.SemaphoreType.DMA((heads,))], unit * rows * 2, (1,),
        after=(mixed[0][0],),
    )
    attention, prefix, sums = [], [], []
    width = features // FORWARD_PIECES
    for piece in range(FORWARD_PIECES):
        out, total, joined = call(
            functools.partial(carry_kernel, piece, grid, counts, scale),
            [shape((rows, width), F32), shape((2, rows), F32), shape((width, HD), BF16)],
            (length, query, local, cot, gain, *flat(scatter_line(mixed[piece], grid)), *sums),
            (), unit * HD // FORWARD_PIECES,
        )
        attention.append(out)
        prefix.append(joined)
        sums = [total]
    sums = token_sums(sums[0], groups)
    grads, state_grad = [], []
    width = features // BACKWARD_PIECES
    for piece in range(BACKWARD_PIECES):
        grad_out, inverse_rms, *parts = call(
            functools.partial(grad_kernel, piece, len(sums), grid, scale),
            [shape((rows, width), BF16), row] + halves(BACKWARD_PIECES),
            (length, query, cot, gain, *sums, *attention), [pltpu.VMEM((width, HD), BF16)],
            unit * HD // BACKWARD_PIECES,
        )
        grads.append(grad_out)
        state_grad.append(parts)
    attended, query_grad, token = call(
        functools.partial(query_kernel, heads, scale),
        [narrow, narrow, shape((8, HD), F32)],
        (length, inverse_rms, gain, key, value, *grads, *attention, *prefix),
        [pltpu.VMEM(narrow.shape, BF16)] * 2 + [sems], unit * (2 * rows + HD),
        out_specs=[HBM, HBM, VMEM],
    )
    mixed = []
    for part in state_grad:
        mixed.append(mix(gather_line(part, grid), down, (token,) if len(mixed) == BACKWARD_PIECES - 1 else ()))
    key_part, value_part = call(
        functools.partial(back_kernel, heads, scale),
        [wide, wide], (length, query, key, value, *grads), (), unit * 4 * rows, after=(mixed[-1][0],),
    )
    results = []
    for piece in range(BACKWARD_PIECES):
        below = flat(scatter_line(mixed[piece], grid))
        operands = (length, key, value, key_part, value_part, *below, *results)
        first = len(operands) - len(results)
        results = call(
            functools.partial(final_kernel, piece, grid, counts),
            [narrow, narrow], operands,
            [pltpu.VMEM((rows, width), BF16)] * 2 + [pltpu.VMEM((width, HD), BF16), sems],
            2 * unit * HD // BACKWARD_PIECES,
            range(first, len(operands)), out_specs=[HBM, HBM],
            aliases={first + j: j for j in range(len(results))},
        )
    key_grad, value_grad = results
    return attended[None], query_grad[None], key_grad[None], value_grad[None]


def solution(mesh):
    split = P("seg", None, "head")
    return jax.shard_map(
        functools.partial(per_device, mesh.shape["seg"], mesh.shape["head"]),
        mesh=mesh,
        in_specs=(split, split, split, split, P("head"), P(), P("seg")),
        out_specs=(split, split, split, split),
        check_vma=False,
    )
```

```python
import functools
import math

import jax
import jax.numpy as jnp
from jax import lax
from jax.experimental import pallas as pl
from jax.experimental.pallas import tpu as pltpu
from jax.sharding import PartitionSpec as P

HEADS = 64
HD = 128
EPSILON = 1e-06
F32 = jnp.float32
BF16 = jnp.bfloat16
VMEM_LIMIT = 24 * 1024 * 1024
FORWARD_PIECES = 2
BACKWARD_PIECES = 1
RETURN_PIECES = 2

VMEM = pl.BlockSpec(memory_space=pltpu.VMEM)
SMEM = pl.BlockSpec(memory_space=pltpu.SMEM)
HBM = pl.BlockSpec(memory_space=pltpu.HBM)
ANY = pl.BlockSpec(memory_space=pl.ANY)


def dot(a, b, contract):
    return lax.dot_general(a, b, (contract, ((), ())), preferred_element_type=F32)


def nn(a, b):
    return dot(a, b, ((1,), (0,)))


def nt(a, b):
    return dot(a, b, ((1,), (1,)))


def tn(a, b):
    return dot(a, b, ((0,), (0,)))


def head_cols(head):
    return slice(head * HD, (head + 1) * HD)


def target_of(place, step, size):
    if size & (size - 1) == 0:
        return place ^ step
    return (place + step) % size


def source_of(place, step, size):
    if size & (size - 1) == 0:
        return place ^ step
    return (place + size - step) % size


def grid_of(segs):
    pair = 2 if segs % 2 == 0 else 1
    chips = segs // pair
    columns = next(c for c in range(1, chips + 1) if chips % c == 0 and c * c >= chips)
    return chips // columns, columns, pair


def member(grid, row, column, core):
    return (row * grid[1] + column) * grid[2] + core


def place_of(grid, device):
    chip = device // grid[2]
    return chip // grid[1], chip % grid[1], device % grid[2]


def along(grid, place, step, gather, ahead):
    row, column, core = place
    shift = target_of if ahead else source_of
    by_row = (core == 0) if gather else (core != 0)
    valid_column = step < grid[1]
    valid_row = step < grid[0]
    if isinstance(core, int):
        if by_row:
            return row, shift(column, step, grid[1]), valid_column
        return shift(row, step, grid[0]), column, valid_row
    moved_column = shift(column, min(step, grid[1] - 1), grid[1])
    moved_row = shift(row, min(step, grid[0] - 1), grid[0])
    return (
        jnp.where(by_row, row, moved_row),
        jnp.where(by_row, moved_column, column),
        jnp.where(by_row, valid_column, valid_row),
    )


def my_place(grid):
    me = lax.axis_index("seg")
    chip = lax.div(me, grid[2])
    return lax.div(chip, grid[1]), lax.rem(chip, grid[1]), lax.rem(me, grid[2])


def row_halves(full, core, pair):
    half = full.shape[0] // pair
    return [full.at[pl.ds(pl.multiple_of((core ^ j) * half, half), half), :] for j in range(pair)]


def join_halves(parts, full, core, pair):
    for half, terms in zip(row_halves(full, core, pair), parts):
        total = terms[0][...].astype(F32)
        for term in terms[1:]:
            total += term[...].astype(F32)
        half[...] = total.astype(BF16)


def line_length(grid):
    return max(grid[0], grid[1])


def write_weights(grid, parent, up, down):
    place = my_place(grid)
    pair = grid[2]
    count = line_length(grid) * pair

    def is_ancestor(child, other):
        first = parent[0, child]
        second = jnp.where(first >= 0, parent[0, jnp.maximum(first, 0)], -1)
        return jnp.logical_or(other == first, other == second)

    for out_step in range(count):
        row, column, _ = along(grid, place, out_step // pair, False, True)
        target = member(grid, row, column, place[2] ^ (out_step % pair))
        for in_step in range(count):
            row, column, valid = along(grid, place, in_step // pair, True, False)
            source = member(grid, row, column, place[2] ^ (in_step % pair))
            at = out_step * count + in_step
            for rows, used in ((up, is_ancestor(target, source)), (down, is_ancestor(source, target))):
                weight = jnp.where(jnp.logical_and(used, valid), 1.0, 0.0)
                rows[at : at + 1, :] = jnp.full((1, HD), weight, F32)


def write_halves(full, outs, core, pair):
    rows = full.shape[0] * pair // len(outs)
    for piece in range(len(outs) // pair):
        halves = row_halves(full.at[pl.ds(piece * rows, rows), :], core, pair)
        for half, out in zip(halves, outs[piece * pair : (piece + 1) * pair]):
            out[...] = half[...]


def state_kernel(grid, seg_len, keys_hbm, values_hbm, parent_hbm, keys, values, length, up, down, *rest):
    outs, (full, sems, parent, parent_sem) = rest[:-4], rest[-4:]
    rows, width = keys.shape
    chunk = rows // 4 if rows % 64 == 0 else rows
    copies = []
    for step in range(rows // chunk):
        part = slice(step * chunk, (step + 1) * chunk)
        for j, (src, dst) in enumerate(((keys_hbm, keys), (values_hbm, values))):
            copies.append(pltpu.make_async_copy(src.at[part, :], dst.at[part, :], sems.at[j, step]))
    few = pltpu.make_async_copy(parent_hbm, parent, parent_sem)
    few.start()
    for copy in copies:
        copy.start()
    length[...] = jnp.full(length.shape, seg_len[0], jnp.int32)
    few.wait()
    write_weights(grid, parent, up, down)
    live = lax.broadcasted_iota(jnp.int32, (rows, HD), 0) < seg_len[0]
    for copy in copies:
        copy.wait()
    for head in range(width // HD):
        cols = head_cols(head)
        masked = jnp.where(live, keys[:, cols], jnp.zeros((), BF16))
        full[head * HD : (head + 1) * HD, :] = tn(masked, values[:, cols]).astype(BF16)
    write_halves(full, outs, my_place(grid)[2], grid[2])


def mix_kernel(sources, first, weights, *refs):
    blocks, outs = refs[:sources], refs[-sources:]
    rows = outs[0].shape[0]
    chunk = min(rows, 64)
    for start in range(0, rows, chunk):
        part = slice(start, start + chunk)
        loaded = [block[first + start : first + start + chunk, :].astype(F32) for block in blocks]
        for out_step, out in enumerate(outs):
            at = out_step * sources
            total = weights[at : at + 1, :] * loaded[0]
            for in_step in range(1, sources):
                total += weights[at + in_step : at + in_step + 1, :] * loaded[in_step]
            out[part, :] = total.astype(BF16)


def live_rows(length, rows):
    return lax.broadcasted_iota(jnp.int32, (rows, HD), 0) < length[:, :HD]


def keep_mask(length, turned):
    rows = length.shape[1]
    first = lax.broadcasted_iota(jnp.int32, (rows, rows), 0)
    second = lax.broadcasted_iota(jnp.int32, (rows, rows), 1)
    if turned:
        return (first <= second) & (first < length[...])
    return (second <= first) & (second < length[...])


def split_refs(refs, *counts):
    parts, at = [], 0
    for count in counts:
        parts.append(refs[at : at + count])
        at += count
    return parts


def head_of(pieces, head):
    per_piece = pieces[0].shape[1] // HD
    return pieces[head // per_piece], head_cols(head % per_piece)


def fetch_kernel(source, _, out, sems):
    rows = out.shape[0]
    chunk = rows // 4 if rows % 64 == 0 else rows
    copies = []
    for step in range(rows // chunk):
        part = pl.ds(step * chunk, chunk)
        copies.append(pltpu.make_async_copy(source.at[part, :], out.at[part, :], sems.at[step]))
    for copy in copies:
        copy.start()
    for copy in copies:
        copy.wait()


def local_kernel(heads, length, queries, keys, values, *rest):
    local = rest[-1]
    keep = keep_mask(length, False)
    for head in range(heads):
        cols = head_cols(head)
        scores = jnp.where(keep, nt(queries[:, cols], keys[:, cols]), 0.0).astype(BF16)
        local[:, cols] = nn(scores, values[:, cols])


def token_rows(total):
    return jnp.sum(jnp.transpose(total), axis=0, keepdims=True)


def token_columns(row):
    return jnp.transpose(jnp.broadcast_to(row, (HD, row.shape[1])))


def carry_kernel(piece, grid, counts, scale, length, queries, local, cotangent, gain, *rest):
    received, rest = rest[: sum(counts)], rest[sum(counts) :]
    before, (attention, sums, prefix) = rest[:-3], rest[-3:]
    join_halves(split_refs(received, *counts), prefix, my_place(grid)[2], grid[2])
    rows, width = attention.shape
    factor = jnp.where(live_rows(length, rows), scale, 0.0)
    squares = jnp.zeros((rows, HD), F32)
    products = jnp.zeros((rows, HD), F32)
    for head in range(width // HD):
        cols = head_cols(head)
        whole = head_cols(piece * width // HD + head)
        carried = nn(queries[:, whole], prefix[head * HD : (head + 1) * HD, :])
        out = factor * (carried + local[:, whole])
        attention[:, cols] = out
        squares += out * out
        products += out * (cotangent[:, whole].astype(F32) * gain[:, whole])
    both = jnp.concatenate([token_rows(squares), token_rows(products)], axis=0)
    for other in before:
        both += other[...]
    sums[...] = both


def grad_kernel(piece, groups, grid, scale, length, queries, cotangent, gain, *rest):
    all_sums, attention, rest = split_refs(rest, groups, FORWARD_PIECES, len(rest) - groups - FORWARD_PIECES)
    (grad_out, inverse_rms), halves, full = rest[:2], rest[2:-1], rest[-1]
    rows, width = grad_out.shape
    features = HEADS * HD
    total = all_sums[0][...]
    for other in all_sums[1:]:
        total = total + other[...]
    inverse = lax.rsqrt(total[0:1, :] / features + EPSILON)
    inverse_rms[...] = inverse
    live = lax.broadcasted_iota(jnp.int32, (1, rows), 1) < length[...]
    live_inverse = jnp.where(live, inverse, 0.0)
    shrink = live_inverse * inverse * (inverse * total[1:2, :]) / features
    live_inverse = token_columns(live_inverse)
    shrink = token_columns(shrink)
    for head in range(width // HD):
        cols = head_cols(head)
        place = piece * width // HD + head
        whole = head_cols(place)
        out_piece, at = head_of(attention, place)
        gain_grad = cotangent[:, whole].astype(F32) * gain[:, whole]
        grad = (live_inverse * gain_grad - out_piece[:, at] * shrink).astype(BF16)
        grad_out[:, cols] = grad
        full[head * HD : (head + 1) * HD, :] = (scale * tn(queries[:, whole], grad)).astype(BF16)
    write_halves(full, halves, my_place(grid)[2], grid[2])


def query_kernel(heads, scale, length, inverse_rms, gain, keys, values, *rest):
    sizes = (BACKWARD_PIECES, FORWARD_PIECES, FORWARD_PIECES)
    grads, attention, prefix, rest = split_refs(rest, *sizes, len(rest) - sum(sizes))
    attended_hbm, query_hbm, token, attended, query_grad, sems = rest[-6:]
    token[...] = jnp.zeros_like(token)
    keep = keep_mask(length, False)
    inverse = token_columns(inverse_rms[...])
    group = 8 if heads % 8 == 0 else 1
    copies = []
    for head in range(heads):
        cols = head_cols(head)
        grad_piece, at = head_of(grads, head)
        grad = grad_piece[:, at]
        out_piece, at = head_of(attention, head)
        per_piece = heads // FORWARD_PIECES
        prefix_piece, state = prefix[head // per_piece], head % per_piece
        grad_scores = jnp.where(keep, nt(grad, values[:, cols]), 0.0).astype(BF16)
        carried = nt(grad, prefix_piece[state * HD : (state + 1) * HD, :])
        query_grad[:, cols] = (scale * (carried + nn(grad_scores, keys[:, cols]))).astype(BF16)
        attended[:, cols] = (out_piece[:, at] * inverse * gain[:, cols]).astype(BF16)
        if (head + 1) % group == 0:
            done = slice((head + 1 - group) * HD, (head + 1) * HD)
            for j, (src, dst) in enumerate(((attended, attended_hbm), (query_grad, query_hbm))):
                copy = pltpu.make_async_copy(src.at[:, done], dst.at[:, done], sems.at[j, head // group])
                copy.start()
                copies.append(copy)
    for copy in copies:
        copy.wait()


def back_kernel(heads, scale, length, queries, keys, values, *rest):
    grads, (key_part, value_part) = rest[:BACKWARD_PIECES], rest[-2:]
    keep = keep_mask(length, True)
    for head in range(heads):
        cols = head_cols(head)
        grad_piece, at = head_of(grads, head)
        query, grad = queries[:, cols], grad_piece[:, at]
        turned = jnp.where(keep, nt(values[:, cols], grad), 0.0).astype(BF16)
        key_part[:, cols] = scale * nn(turned, query)
        turned = jnp.where(keep, nt(keys[:, cols], query), 0.0).astype(BF16)
        value_part[:, cols] = scale * nn(turned, grad)


def final_kernel(piece, grid, counts, length, keys, values, key_part, value_part, *rest):
    received, rest = rest[: sum(counts)], rest[sum(counts) :]
    key_hbm, value_hbm, key_grad, value_grad, below, sems = rest[-6:]
    pair = grid[2]
    join_halves(split_refs(received, *counts), below, my_place(grid)[2], pair)
    rows, width = key_grad.shape
    live = jnp.where(live_rows(length, rows), 1.0, 0.0)
    per_half = width // HD // pair
    group = 2 if per_half % 2 == 0 else 1
    copies = []
    for head in range(width // HD):
        half, within = head // per_half, head % per_half
        cols = head_cols(head)
        place = half * (keys.shape[1] // HD // pair) + piece * per_half + within
        whole = head_cols(place)
        state = below[head * HD : (head + 1) * HD, :]
        key_grad[:, cols] = (key_part[:, whole] + live * nt(values[:, whole], state)).astype(BF16)
        value_grad[:, cols] = (value_part[:, whole] + live * nn(keys[:, whole], state)).astype(BF16)
        if (head + 1) % group == 0:
            done = slice((head + 1 - group) * HD, (head + 1) * HD)
            there = slice((place + 1 - group) * HD, (place + 1) * HD)
            for j, (src, dst) in enumerate(((key_grad, key_hbm), (value_grad, value_hbm))):
                copy = pltpu.make_async_copy(src.at[:, done], dst.at[:, there], sems.at[j, head // group])
                copy.start()
                copies.append(copy)
    for copy in copies:
        copy.wait()


def in_hbm(x):
    return pltpu.with_memory_space_constraint(x, pltpu.HBM)


def call(kernel, out_shape, operands, scratch=(), flops=0, stream=(), scalars=(), after=(), out_specs=None, aliases=None):
    moved = sum(math.prod(x.shape) * x.dtype.itemsize for x in operands)
    moved += sum(math.prod(x.shape) * x.dtype.itemsize for x in out_shape)
    specs = [SMEM if j in scalars else HBM if j in stream else VMEM for j in range(len(operands))]
    operands = [in_hbm(x) if j in stream else x for j, x in enumerate(operands)]
    return pl.pallas_call(
        kernel,
        out_shape=out_shape,
        in_specs=specs + [ANY] * len(after),
        out_specs=out_specs or [VMEM] * len(out_shape),
        scratch_shapes=list(scratch),
        input_output_aliases=aliases or {},
        compiler_params=pltpu.CompilerParams(vmem_limit_bytes=VMEM_LIMIT),
        cost_estimate=pl.CostEstimate(flops=flops, bytes_accessed=moved, transcendentals=0),
    )(*operands, *after)


def line_send(block, grid, step, flip, gather):
    moves = []
    for device in range(grid[0] * grid[1] * grid[2]):
        place = place_of(grid, device)
        if gather and flip:
            row, column, valid = along(grid, (place[0], place[1], place[2] ^ 1), step, True, True)
        else:
            row, column, valid = along(grid, place, step, gather, True)
        if valid:
            moves.append((device, member(grid, row, column, place[2] ^ flip)))
    return lax.ppermute(block, "seg", moves)


def gather_line(halves, grid):
    arrived = []
    for step in range(line_length(grid)):
        for flip in range(grid[2]):
            if step == 0 and flip == 0:
                arrived.append(halves[0])
            else:
                arrived.append(line_send(halves[flip], grid, step, flip, True))
    return arrived


def scatter_line(sums, grid):
    pair = grid[2]
    parts = [[] for _ in range(pair)]
    for step in range(line_length(grid)):
        for flip in range(pair):
            block = sums[step * pair + flip]
            if step == 0 and flip == 0:
                parts[0].append(block)
            else:
                parts[flip].append(line_send(block, grid, step, flip, False))
    return parts


def token_sums(sums, groups):
    parts = [sums]
    for step in [j for j in range(1, groups) if j != 2] + [2] * (groups > 2):
        moves = [(j, target_of(j, step, groups)) for j in range(groups)]
        parts.append(lax.ppermute(sums, "head", moves))
    return parts


def per_device(segs, groups, queries, key_rows, values, cotangent, out_gain, parent, seg_len):
    rows, features = queries.shape[1:]
    heads = features // HD
    grid = grid_of(segs)
    pair = grid[2]
    scale = 1.0 / math.sqrt(HD * rows)
    cot = cotangent[0]
    gain = out_gain[None]
    shape = jax.ShapeDtypeStruct
    narrow = shape((rows, features), BF16)
    wide = shape((rows, features), F32)
    row = shape((1, rows), F32)
    members = line_length(grid) * pair
    weight_rows = shape((members * members, HD), F32)
    sems = pltpu.SemaphoreType.DMA((2, heads))
    counts = [line_length(grid)] * pair
    unit = 2 * heads * rows * HD

    def halves(pieces):
        return [shape((features // (pair * pieces), HD), BF16)] * pair

    def mix(arrived, weights, piece, pieces, after=()):
        tall = arrived[0].shape[0] // pieces
        like = [shape((tall, HD), BF16)] * members
        return call(functools.partial(mix_kernel, members, piece * tall), like, (weights, *arrived), after=after)

    def flat(parts):
        return [block for part in parts for block in part]

    key, value, length, up, down, *own = call(
        functools.partial(state_kernel, grid),
        [narrow, narrow, shape((1, rows), jnp.int32), weight_rows, weight_rows] + halves(FORWARD_PIECES) * FORWARD_PIECES,
        (seg_len, key_rows[0], values[0], parent[None]),
        [pltpu.VMEM((features, HD), BF16), sems, pltpu.SMEM((1, segs), jnp.int32), pltpu.SemaphoreType.DMA(())],
        unit * HD, (1, 2, 3), (0,),
    )
    (query,) = call(fetch_kernel, [narrow], (queries[0],), [pltpu.SemaphoreType.DMA((4,))], 0, (0,), after=(own[0],))
    mixed = []
    for part in split_refs(own, *[pair] * FORWARD_PIECES):
        mixed.append(mix(gather_line(part, grid), up, 0, 1, () if mixed else (query,)))
    (local,) = call(
        functools.partial(local_kernel, heads),
        [wide], (length, query, key, value), (), unit * rows * 2, after=(mixed[0][0],),
    )
    attention, prefix, sums = [], [], []
    width = features // FORWARD_PIECES
    for piece in range(FORWARD_PIECES):
        out, total, joined = call(
            functools.partial(carry_kernel, piece, grid, counts, scale),
            [shape((rows, width), F32), shape((2, rows), F32), shape((width, HD), BF16)],
            (length, query, local, cot, gain, *flat(scatter_line(mixed[piece], grid)), *sums),
            (), unit * HD // FORWARD_PIECES,
        )
        attention.append(out)
        prefix.append(joined)
        sums = [total]
    sums = token_sums(sums[0], groups)
    grads, state_grad = [], []
    width = features // BACKWARD_PIECES
    for piece in range(BACKWARD_PIECES):
        grad_out, inverse_rms, *parts = call(
            functools.partial(grad_kernel, piece, len(sums), grid, scale),
            [shape((rows, width), BF16), row] + halves(BACKWARD_PIECES),
            (length, query, cot, gain, *sums, *attention), [pltpu.VMEM((width, HD), BF16)],
            unit * HD // BACKWARD_PIECES,
        )
        grads.append(grad_out)
        state_grad.append(parts)
    attended, query_grad, token = call(
        functools.partial(query_kernel, heads, scale),
        [narrow, narrow, shape((8, HD), F32)],
        (length, inverse_rms, gain, key, value, *grads, *attention, *prefix),
        [pltpu.VMEM(narrow.shape, BF16)] * 2 + [sems], unit * (2 * rows + HD),
        out_specs=[HBM, HBM, VMEM],
    )
    (part,) = state_grad
    arrived = gather_line(part, grid)
    mixed = []
    for piece in range(RETURN_PIECES):
        mixed.append(mix(arrived, down, piece, RETURN_PIECES, (token, *mixed[-1][:1]) if mixed else (token,)))
    key_part, value_part = call(
        functools.partial(back_kernel, heads, scale),
        [wide, wide], (length, query, key, value, *grads), (), unit * 4 * rows, after=(mixed[-1][0],),
    )
    results = []
    width = features // RETURN_PIECES
    for piece in range(RETURN_PIECES):
        below = flat(scatter_line(mixed[piece], grid))
        operands = (length, key, value, key_part, value_part, *below, *results)
        first = len(operands) - len(results)
        results = call(
            functools.partial(final_kernel, piece, grid, counts),
            [narrow, narrow], operands,
            [pltpu.VMEM((rows, width), BF16)] * 2 + [pltpu.VMEM((width, HD), BF16), sems],
            2 * unit * HD // RETURN_PIECES,
            range(first, len(operands)), out_specs=[HBM, HBM],
            aliases={first + j: j for j in range(len(results))},
        )
    key_grad, value_grad = results
    return attended[None], query_grad[None], key_grad[None], value_grad[None]


def solution(mesh):
    split = P("seg", None, "head")
    return jax.shard_map(
        functools.partial(per_device, mesh.shape["seg"], mesh.shape["head"]),
        mesh=mesh,
        in_specs=(split, split, split, split, P("head"), P(), P("seg")),
        out_specs=(split, split, split, split),
        check_vma=False,
    )
```

```python
import functools
import math

import jax
import jax.numpy as jnp
from jax import lax
from jax.experimental import pallas as pl
from jax.experimental.pallas import tpu as pltpu
from jax.sharding import PartitionSpec as P

HEADS = 64
HD = 128
EPSILON = 1e-06
F32 = jnp.float32
BF16 = jnp.bfloat16
VMEM_LIMIT = 24 * 1024 * 1024
FORWARD_PIECES = 2
BACKWARD_PIECES = 1
RETURN_PIECES = 2

VMEM = pl.BlockSpec(memory_space=pltpu.VMEM)
SMEM = pl.BlockSpec(memory_space=pltpu.SMEM)
HBM = pl.BlockSpec(memory_space=pltpu.HBM)
ANY = pl.BlockSpec(memory_space=pl.ANY)


def dot(a, b, contract):
    return lax.dot_general(a, b, (contract, ((), ())), preferred_element_type=F32)


def nn(a, b):
    return dot(a, b, ((1,), (0,)))


def nt(a, b):
    return dot(a, b, ((1,), (1,)))


def tn(a, b):
    return dot(a, b, ((0,), (0,)))


def head_cols(head):
    return slice(head * HD, (head + 1) * HD)


def target_of(place, step, size):
    if size & (size - 1) == 0:
        return place ^ step
    return (place + step) % size


def source_of(place, step, size):
    if size & (size - 1) == 0:
        return place ^ step
    return (place + size - step) % size


def grid_of(segs):
    pair = 2 if segs % 2 == 0 else 1
    chips = segs // pair
    columns = next(c for c in range(1, chips + 1) if chips % c == 0 and c * c >= chips)
    return chips // columns, columns, pair


def member(grid, row, column, core):
    return (row * grid[1] + column) * grid[2] + core


def place_of(grid, device):
    chip = device // grid[2]
    return chip // grid[1], chip % grid[1], device % grid[2]


def along(grid, place, step, gather, ahead):
    row, column, core = place
    shift = target_of if ahead else source_of
    by_row = (core == 0) if gather else (core != 0)
    valid_column = step < grid[1]
    valid_row = step < grid[0]
    if isinstance(core, int):
        if by_row:
            return row, shift(column, step, grid[1]), valid_column
        return shift(row, step, grid[0]), column, valid_row
    moved_column = shift(column, min(step, grid[1] - 1), grid[1])
    moved_row = shift(row, min(step, grid[0] - 1), grid[0])
    return (
        jnp.where(by_row, row, moved_row),
        jnp.where(by_row, moved_column, column),
        jnp.where(by_row, valid_column, valid_row),
    )


def my_place(grid):
    me = lax.axis_index("seg")
    chip = lax.div(me, grid[2])
    return lax.div(chip, grid[1]), lax.rem(chip, grid[1]), lax.rem(me, grid[2])


def row_halves(full, core, pair):
    half = full.shape[0] // pair
    return [full.at[pl.ds(pl.multiple_of((core ^ j) * half, half), half), :] for j in range(pair)]


def join_halves(parts, full, core, pair):
    for half, terms in zip(row_halves(full, core, pair), parts):
        total = terms[0][...].astype(F32)
        for term in terms[1:]:
            total += term[...].astype(F32)
        half[...] = total.astype(BF16)


def line_length(grid):
    return max(grid[0], grid[1])


def write_weights(grid, parent, up, down):
    place = my_place(grid)
    pair = grid[2]
    count = line_length(grid) * pair

    def is_ancestor(child, other):
        first = parent[0, child]
        second = jnp.where(first >= 0, parent[0, jnp.maximum(first, 0)], -1)
        return jnp.logical_or(other == first, other == second)

    for out_step in range(count):
        row, column, _ = along(grid, place, out_step // pair, False, True)
        target = member(grid, row, column, place[2] ^ (out_step % pair))
        for in_step in range(count):
            row, column, valid = along(grid, place, in_step // pair, True, False)
            source = member(grid, row, column, place[2] ^ (in_step % pair))
            at = out_step * count + in_step
            for rows, used in ((up, is_ancestor(target, source)), (down, is_ancestor(source, target))):
                weight = jnp.where(jnp.logical_and(used, valid), 1.0, 0.0)
                rows[at : at + 1, :] = jnp.full((1, HD), weight, F32)


def write_halves(full, outs, core, pair):
    rows = full.shape[0] * pair // len(outs)
    for piece in range(len(outs) // pair):
        halves = row_halves(full.at[pl.ds(piece * rows, rows), :], core, pair)
        for half, out in zip(halves, outs[piece * pair : (piece + 1) * pair]):
            out[...] = half[...]


def state_kernel(grid, seg_len, keys_hbm, values_hbm, parent_hbm, keys, values, length, up, down, *rest):
    outs, (full, sems, parent, parent_sem) = rest[:-4], rest[-4:]
    rows, width = keys.shape
    chunk = rows // 4 if rows % 64 == 0 else rows
    steps = rows // chunk
    spans = 2 if width % (2 * HD) == 0 else 1
    copies = []
    for span in range(spans):
        cols = slice(span * width // spans, (span + 1) * width // spans)
        for step in range(steps):
            part = slice(step * chunk, (step + 1) * chunk)
            for j, (src, dst) in enumerate(((keys_hbm, keys), (values_hbm, values))):
                copies.append(pltpu.make_async_copy(src.at[part, cols], dst.at[part, cols], sems.at[j, span * steps + step]))
    few = pltpu.make_async_copy(parent_hbm, parent, parent_sem)
    few.start()
    for copy in copies:
        copy.start()
    length[...] = jnp.full(length.shape, seg_len[0], jnp.int32)
    few.wait()
    write_weights(grid, parent, up, down)
    live = lax.broadcasted_iota(jnp.int32, (rows, HD), 0) < seg_len[0]
    for head in range(width // HD):
        if head % (width // HD // spans) == 0:
            span = head // (width // HD // spans)
            for copy in copies[span * 2 * steps : (span + 1) * 2 * steps]:
                copy.wait()
        cols = head_cols(head)
        masked = jnp.where(live, keys[:, cols], jnp.zeros((), BF16))
        full[head * HD : (head + 1) * HD, :] = tn(masked, values[:, cols]).astype(BF16)
    write_halves(full, outs, my_place(grid)[2], grid[2])


def mix_kernel(sources, pair, first, weights, *refs):
    blocks, outs = refs[:sources], refs[-sources:]
    blocks = blocks[:1] + blocks[sources - pair + 1 :] + blocks[1 : sources - pair + 1]
    rows = outs[0].shape[0]
    chunk = min(rows, 64)
    for start in range(0, rows, chunk):
        part = slice(start, start + chunk)
        loaded = [block[first + start : first + start + chunk, :].astype(F32) for block in blocks]
        for out_step, out in enumerate(outs):
            at = out_step * sources
            total = weights[at : at + 1, :] * loaded[0]
            for in_step in range(1, sources):
                total += weights[at + in_step : at + in_step + 1, :] * loaded[in_step]
            out[part, :] = total.astype(BF16)


def live_rows(length, rows):
    return lax.broadcasted_iota(jnp.int32, (rows, HD), 0) < length[:, :HD]


def keep_mask(length, turned):
    rows = length.shape[1]
    first = lax.broadcasted_iota(jnp.int32, (rows, rows), 0)
    second = lax.broadcasted_iota(jnp.int32, (rows, rows), 1)
    if turned:
        return (first <= second) & (first < length[...])
    return (second <= first) & (second < length[...])


def split_refs(refs, *counts):
    parts, at = [], 0
    for count in counts:
        parts.append(refs[at : at + count])
        at += count
    return parts


def head_of(pieces, head):
    per_piece = pieces[0].shape[1] // HD
    return pieces[head // per_piece], head_cols(head % per_piece)


def fetch_kernel(source, _, out, sems):
    copies = row_copies(source, out, sems)
    for copy in copies:
        copy.start()
    for copy in copies:
        copy.wait()


def local_kernel(heads, length, queries, keys, values, *rest):
    local = rest[-1]
    keep = keep_mask(length, False)
    for head in range(heads):
        cols = head_cols(head)
        scores = jnp.where(keep, nt(queries[:, cols], keys[:, cols]), 0.0).astype(BF16)
        local[:, cols] = nn(scores, values[:, cols])


def token_rows(total):
    return jnp.sum(jnp.transpose(total), axis=0, keepdims=True)


def token_columns(row):
    return jnp.transpose(jnp.broadcast_to(row, (HD, row.shape[1])))


def carry_kernel(piece, grid, counts, scale, length, queries, local, cotangent, gain, *rest):
    received, rest = rest[: sum(counts)], rest[sum(counts) :]
    before, (attention, sums, prefix) = rest[:-3], rest[-3:]
    join_halves(split_refs(received, *counts), prefix, my_place(grid)[2], grid[2])
    rows, width = attention.shape
    factor = jnp.where(live_rows(length, rows), scale, 0.0)
    squares = jnp.zeros((rows, HD), F32)
    products = jnp.zeros((rows, HD), F32)
    for head in range(width // HD):
        cols = head_cols(head)
        whole = head_cols(piece * width // HD + head)
        carried = nn(queries[:, whole], prefix[head * HD : (head + 1) * HD, :])
        out = factor * (carried + local[:, whole])
        attention[:, cols] = out
        squares += out * out
        products += out * (cotangent[:, whole].astype(F32) * gain[:, whole])
    both = jnp.concatenate([token_rows(squares), token_rows(products)], axis=0)
    for other in before:
        both += other[...]
    sums[...] = both


def grad_kernel(piece, groups, grid, scale, length, queries, cotangent, gain, *rest):
    all_sums, attention, rest = split_refs(rest, groups, FORWARD_PIECES, len(rest) - groups - FORWARD_PIECES)
    (grad_out, inverse_rms), halves, full = rest[:2], rest[2:-1], rest[-1]
    rows, width = grad_out.shape
    features = HEADS * HD
    total = all_sums[0][...]
    for other in all_sums[1:]:
        total = total + other[...]
    inverse = lax.rsqrt(total[0:1, :] / features + EPSILON)
    inverse_rms[...] = inverse
    live = lax.broadcasted_iota(jnp.int32, (1, rows), 1) < length[...]
    live_inverse = jnp.where(live, inverse, 0.0)
    shrink = live_inverse * inverse * (inverse * total[1:2, :]) / features
    live_inverse = token_columns(live_inverse)
    shrink = token_columns(shrink)
    for head in range(width // HD):
        cols = head_cols(head)
        place = piece * width // HD + head
        whole = head_cols(place)
        out_piece, at = head_of(attention, place)
        gain_grad = cotangent[:, whole].astype(F32) * gain[:, whole]
        grad = (live_inverse * gain_grad - out_piece[:, at] * shrink).astype(BF16)
        grad_out[:, cols] = grad
        full[head * HD : (head + 1) * HD, :] = (scale * tn(queries[:, whole], grad)).astype(BF16)
    write_halves(full, halves, my_place(grid)[2], grid[2])


def query_kernel(heads, scale, length, inverse_rms, gain, keys, values, *rest):
    sizes = (BACKWARD_PIECES, FORWARD_PIECES, FORWARD_PIECES)
    grads, attention, prefix, rest = split_refs(rest, *sizes, len(rest) - sum(sizes))
    attended, query_grad = rest[-2:]
    keep = keep_mask(length, False)
    inverse = token_columns(inverse_rms[...])
    for head in range(heads):
        cols = head_cols(head)
        grad_piece, at = head_of(grads, head)
        grad = grad_piece[:, at]
        out_piece, at = head_of(attention, head)
        per_piece = heads // FORWARD_PIECES
        prefix_piece, state = prefix[head // per_piece], head % per_piece
        grad_scores = jnp.where(keep, nt(grad, values[:, cols]), 0.0).astype(BF16)
        carried = nt(grad, prefix_piece[state * HD : (state + 1) * HD, :])
        query_grad[:, cols] = (scale * (carried + nn(grad_scores, keys[:, cols]))).astype(BF16)
        attended[:, cols] = (out_piece[:, at] * inverse * gain[:, cols]).astype(BF16)


def row_copies(source, target, sems):
    rows = target.shape[0]
    chunk = rows // 4 if rows % 64 == 0 else rows
    parts = [pl.ds(step * chunk, chunk) for step in range(rows // chunk)]
    return [pltpu.make_async_copy(source.at[p, :], target.at[p, :], sems.at[j]) for j, p in enumerate(parts)]


def back_kernel(heads, scale, length, queries, keys, values, attended, query_grad, *rest):
    grads, (attended_hbm, query_hbm, key_part, value_part, token, sems) = rest[:BACKWARD_PIECES], rest[-6:]
    copies = row_copies(attended, attended_hbm, sems.at[0]) + row_copies(query_grad, query_hbm, sems.at[1])
    for copy in copies:
        copy.start()
    token[...] = jnp.zeros_like(token)
    keep = keep_mask(length, True)
    for head in range(heads):
        cols = head_cols(head)
        grad_piece, at = head_of(grads, head)
        query, grad = queries[:, cols], grad_piece[:, at]
        turned = jnp.where(keep, nt(values[:, cols], grad), 0.0).astype(BF16)
        key_part[:, cols] = scale * nn(turned, query)
        turned = jnp.where(keep, nt(keys[:, cols], query), 0.0).astype(BF16)
        value_part[:, cols] = scale * nn(turned, grad)
    for copy in copies:
        copy.wait()


def final_kernel(piece, grid, counts, length, keys, values, key_part, value_part, *rest):
    received, rest = rest[: sum(counts)], rest[sum(counts) :]
    key_hbm, value_hbm, key_grad, value_grad, below, sems = rest[-6:]
    pair = grid[2]
    join_halves(split_refs(received, *counts), below, my_place(grid)[2], pair)
    rows, width = key_grad.shape
    live = jnp.where(live_rows(length, rows), 1.0, 0.0)
    per_half = width // HD // pair
    group = 2 if per_half % 2 == 0 else 1
    copies = []
    for head in range(width // HD):
        half, within = head // per_half, head % per_half
        cols = head_cols(head)
        place = half * (keys.shape[1] // HD // pair) + piece * per_half + within
        whole = head_cols(place)
        state = below[head * HD : (head + 1) * HD, :]
        key_grad[:, cols] = (key_part[:, whole] + live * nt(values[:, whole], state)).astype(BF16)
        value_grad[:, cols] = (value_part[:, whole] + live * nn(keys[:, whole], state)).astype(BF16)
        if (head + 1) % group == 0:
            done = slice((head + 1 - group) * HD, (head + 1) * HD)
            there = slice((place + 1 - group) * HD, (place + 1) * HD)
            for j, (src, dst) in enumerate(((key_grad, key_hbm), (value_grad, value_hbm))):
                copy = pltpu.make_async_copy(src.at[:, done], dst.at[:, there], sems.at[j, head // group])
                copy.start()
                copies.append(copy)
    for copy in copies:
        copy.wait()


def in_hbm(x):
    return pltpu.with_memory_space_constraint(x, pltpu.HBM)


def call(kernel, out_shape, operands, scratch=(), flops=0, stream=(), scalars=(), after=(), out_specs=None, aliases=None):
    moved = sum(math.prod(x.shape) * x.dtype.itemsize for x in operands)
    moved += sum(math.prod(x.shape) * x.dtype.itemsize for x in out_shape)
    specs = [SMEM if j in scalars else HBM if j in stream else VMEM for j in range(len(operands))]
    operands = [in_hbm(x) if j in stream else x for j, x in enumerate(operands)]
    return pl.pallas_call(
        kernel,
        out_shape=out_shape,
        in_specs=specs + [ANY] * len(after),
        out_specs=out_specs or [VMEM] * len(out_shape),
        scratch_shapes=list(scratch),
        input_output_aliases=aliases or {},
        compiler_params=pltpu.CompilerParams(vmem_limit_bytes=VMEM_LIMIT),
        cost_estimate=pl.CostEstimate(flops=flops, bytes_accessed=moved, transcendentals=0),
    )(*operands, *after)


def line_send(block, grid, step, flip, gather):
    moves = []
    for device in range(grid[0] * grid[1] * grid[2]):
        place = place_of(grid, device)
        if gather and flip:
            row, column, valid = along(grid, (place[0], place[1], place[2] ^ 1), step, True, True)
        else:
            row, column, valid = along(grid, place, step, gather, True)
        if valid:
            moves.append((device, member(grid, row, column, place[2] ^ flip)))
    return lax.ppermute(block, "seg", moves)


def gather_line(halves, grid):
    pair = grid[2]
    arrived = {0: halves[0]}
    for step in range(line_length(grid)):
        for flip in range(pair):
            if step or flip:
                arrived[step * pair + flip] = line_send(halves[flip], grid, step, flip, True)
    return [arrived[j] for j in range(len(arrived))]


def scatter_line(sums, grid):
    pair = grid[2]
    parts = [[] for _ in range(pair)]
    for step in reversed(range(line_length(grid))):
        for flip in range(pair):
            block = sums[step * pair + flip]
            parts[flip].append(line_send(block, grid, step, flip, False) if step or flip else block)
    return parts


def token_sums(sums, groups):
    parts = [sums]
    for step in [j for j in range(1, groups) if j != 2] + [2] * (groups > 2):
        moves = [(j, target_of(j, step, groups)) for j in range(groups)]
        parts.append(lax.ppermute(sums, "head", moves))
    return parts


def per_device(segs, groups, queries, key_rows, values, cotangent, out_gain, parent, seg_len):
    rows, features = queries.shape[1:]
    heads = features // HD
    grid = grid_of(segs)
    pair = grid[2]
    scale = 1.0 / math.sqrt(HD * rows)
    cot = cotangent[0]
    gain = out_gain[None]
    shape = jax.ShapeDtypeStruct
    narrow = shape((rows, features), BF16)
    wide = shape((rows, features), F32)
    row = shape((1, rows), F32)
    members = line_length(grid) * pair
    weight_rows = shape((members * members, HD), F32)
    sems = pltpu.SemaphoreType.DMA((2, heads))
    counts = [line_length(grid)] * pair
    unit = 2 * heads * rows * HD

    def halves(pieces):
        return [shape((features // (pair * pieces), HD), BF16)] * pair

    def mix(arrived, weights, piece, pieces, after=()):
        tall = arrived[0].shape[0] // pieces
        like = [shape((tall, HD), BF16)] * members
        arrived = arrived[:1] + arrived[pair:] + arrived[1:pair]
        return call(functools.partial(mix_kernel, members, pair, piece * tall), like, (weights, *arrived), after=after)

    def flat(parts):
        return [block for part in parts for block in part]

    key, value, length, up, down, *own = call(
        functools.partial(state_kernel, grid),
        [narrow, narrow, shape((1, rows), jnp.int32), weight_rows, weight_rows] + halves(FORWARD_PIECES) * FORWARD_PIECES,
        (seg_len, key_rows[0], values[0], parent[None]),
        [pltpu.VMEM((features, HD), BF16), sems, pltpu.SMEM((1, segs), jnp.int32), pltpu.SemaphoreType.DMA(())],
        unit * HD, (1, 2, 3), (0,),
    )
    (query,) = call(fetch_kernel, [narrow], (queries[0],), [pltpu.SemaphoreType.DMA((4,))], 0, (0,), after=(own[0],))
    mixed = []
    for part in split_refs(own, *[pair] * FORWARD_PIECES):
        mixed.append(mix(gather_line(part, grid), up, 0, 1, () if mixed else (query,)))
    (local,) = call(
        functools.partial(local_kernel, heads),
        [wide], (length, query, key, value), (), unit * rows * 2, after=(mixed[0][0],),
    )
    attention, prefix, sums = [], [], []
    width = features // FORWARD_PIECES
    for piece in range(FORWARD_PIECES):
        out, total, joined = call(
            functools.partial(carry_kernel, piece, grid, counts, scale),
            [shape((rows, width), F32), shape((2, rows), F32), shape((width, HD), BF16)],
            (length, query, local, cot, gain, *flat(scatter_line(mixed[piece], grid)), *sums),
            (), unit * HD // FORWARD_PIECES,
        )
        attention.append(out)
        prefix.append(joined)
        sums = [total]
    sums = token_sums(sums[0], groups)
    grads, state_grad = [], []
    width = features // BACKWARD_PIECES
    for piece in range(BACKWARD_PIECES):
        grad_out, inverse_rms, *parts = call(
            functools.partial(grad_kernel, piece, len(sums), grid, scale),
            [shape((rows, width), BF16), row] + halves(BACKWARD_PIECES),
            (length, query, cot, gain, *sums, *attention), [pltpu.VMEM((width, HD), BF16)],
            unit * HD // BACKWARD_PIECES,
        )
        grads.append(grad_out)
        state_grad.append(parts)
    attended, query_grad = call(
        functools.partial(query_kernel, heads, scale),
        [narrow, narrow],
        (length, inverse_rms, gain, key, value, *grads, *attention, *prefix),
        (), unit * (2 * rows + HD),
    )
    attended, query_grad, key_part, value_part, token = call(
        functools.partial(back_kernel, heads, scale),
        [narrow, narrow, wide, wide, shape((8, HD), F32)],
        (length, query, key, value, attended, query_grad, *grads), [pltpu.SemaphoreType.DMA((2, 4))],
        unit * 4 * rows, out_specs=[HBM, HBM, VMEM, VMEM, VMEM],
    )
    (part,) = state_grad
    arrived = gather_line(part, grid)
    mixed = []
    for piece in range(RETURN_PIECES):
        mixed.append(mix(arrived, down, piece, RETURN_PIECES, (token, *mixed[-1][:1]) if mixed else (token,)))
    results = []
    width = features // RETURN_PIECES
    for piece in range(RETURN_PIECES):
        below = flat(scatter_line(mixed[piece], grid))
        operands = (length, key, value, key_part, value_part, *below, *results)
        first = len(operands) - len(results)
        results = call(
            functools.partial(final_kernel, piece, grid, counts),
            [narrow, narrow], operands,
            [pltpu.VMEM((rows, width), BF16)] * 2 + [pltpu.VMEM((width, HD), BF16), sems],
            2 * unit * HD // RETURN_PIECES,
            range(first, len(operands)), out_specs=[HBM, HBM],
            aliases={first + j: j for j in range(len(results))},
        )
    key_grad, value_grad = results
    return attended[None], query_grad[None], key_grad[None], value_grad[None]


def solution(mesh):
    split = P("seg", None, "head")
    return jax.shard_map(
        functools.partial(per_device, mesh.shape["seg"], mesh.shape["head"]),
        mesh=mesh,
        in_specs=(split, split, split, split, P("head"), P(), P("seg")),
        out_specs=(split, split, split, split),
        check_vma=False,
    )
```

```python
import functools
import math

import jax
import jax.numpy as jnp
from jax import lax
from jax.experimental import pallas as pl
from jax.experimental.pallas import tpu as pltpu
from jax.sharding import PartitionSpec as P

HEADS = 64
HD = 128
EPSILON = 1e-06
F32 = jnp.float32
BF16 = jnp.bfloat16
VMEM_LIMIT = 24 * 1024 * 1024
FORWARD_PIECES = 2
BACKWARD_PIECES = 1
RETURN_PIECES = 2

VMEM = pl.BlockSpec(memory_space=pltpu.VMEM)
SMEM = pl.BlockSpec(memory_space=pltpu.SMEM)
HBM = pl.BlockSpec(memory_space=pltpu.HBM)
ANY = pl.BlockSpec(memory_space=pl.ANY)


def dot(a, b, contract):
    return lax.dot_general(a, b, (contract, ((), ())), preferred_element_type=F32)


def nn(a, b):
    return dot(a, b, ((1,), (0,)))


def nt(a, b):
    return dot(a, b, ((1,), (1,)))


def tn(a, b):
    return dot(a, b, ((0,), (0,)))


def head_cols(head):
    return slice(head * HD, (head + 1) * HD)


def target_of(place, step, size):
    if size & (size - 1) == 0:
        return place ^ step
    return (place + step) % size


def source_of(place, step, size):
    if size & (size - 1) == 0:
        return place ^ step
    return (place + size - step) % size


def grid_of(segs):
    pair = 2 if segs % 2 == 0 else 1
    chips = segs // pair
    columns = next(c for c in range(1, chips + 1) if chips % c == 0 and c * c >= chips)
    return chips // columns, columns, pair


def member(grid, row, column, core):
    return (row * grid[1] + column) * grid[2] + core


def place_of(grid, device):
    chip = device // grid[2]
    return chip // grid[1], chip % grid[1], device % grid[2]


def along(grid, place, step, gather, ahead):
    row, column, core = place
    shift = target_of if ahead else source_of
    by_row = (core == 0) if gather else (core != 0)
    valid_column = step < grid[1]
    valid_row = step < grid[0]
    if isinstance(core, int):
        if by_row:
            return row, shift(column, step, grid[1]), valid_column
        return shift(row, step, grid[0]), column, valid_row
    moved_column = shift(column, min(step, grid[1] - 1), grid[1])
    moved_row = shift(row, min(step, grid[0] - 1), grid[0])
    return (
        jnp.where(by_row, row, moved_row),
        jnp.where(by_row, moved_column, column),
        jnp.where(by_row, valid_column, valid_row),
    )


def my_place(grid):
    me = lax.axis_index("seg")
    chip = lax.div(me, grid[2])
    return lax.div(chip, grid[1]), lax.rem(chip, grid[1]), lax.rem(me, grid[2])


def row_halves(full, core, pair):
    half = full.shape[0] // pair
    return [full.at[pl.ds(pl.multiple_of((core ^ j) * half, half), half), :] for j in range(pair)]


def join_halves(parts, full, core, pair):
    for half, terms in zip(row_halves(full, core, pair), parts):
        total = terms[0][...].astype(F32)
        for term in terms[1:]:
            total += term[...].astype(F32)
        half[...] = total.astype(BF16)


def line_length(grid):
    return max(grid[0], grid[1])


def write_weights(grid, parent, up, down):
    place = my_place(grid)
    pair = grid[2]
    count = line_length(grid) * pair

    def is_ancestor(child, other):
        first = parent[0, child]
        second = jnp.where(first >= 0, parent[0, jnp.maximum(first, 0)], -1)
        return jnp.logical_or(other == first, other == second)

    for out_step in range(count):
        row, column, _ = along(grid, place, out_step // pair, False, True)
        target = member(grid, row, column, place[2] ^ (out_step % pair))
        for in_step in range(count):
            row, column, valid = along(grid, place, in_step // pair, True, False)
            source = member(grid, row, column, place[2] ^ (in_step % pair))
            at = out_step * count + in_step
            for rows, used in ((up, is_ancestor(target, source)), (down, is_ancestor(source, target))):
                weight = jnp.where(jnp.logical_and(used, valid), 1.0, 0.0)
                rows[at : at + 1, :] = jnp.full((1, HD), weight, F32)


def write_halves(full, outs, core, pair):
    rows = full.shape[0] * pair // len(outs)
    for piece in range(len(outs) // pair):
        halves = row_halves(full.at[pl.ds(piece * rows, rows), :], core, pair)
        for half, out in zip(halves, outs[piece * pair : (piece + 1) * pair]):
            out[...] = half[...]


def state_kernel(grid, seg_len, keys_hbm, values_hbm, parent_hbm, keys, values, length, up, down, *rest):
    outs, (full, sems, parent, parent_sem) = rest[:-4], rest[-4:]
    rows, width = keys.shape
    chunk = rows // 4 if rows % 64 == 0 else rows
    steps = rows // chunk
    spans = 2 if width % (2 * HD) == 0 else 1
    copies = []
    for span in range(spans):
        cols = slice(span * width // spans, (span + 1) * width // spans)
        for step in range(steps):
            part = slice(step * chunk, (step + 1) * chunk)
            for j, (src, dst) in enumerate(((keys_hbm, keys), (values_hbm, values))):
                copies.append(pltpu.make_async_copy(src.at[part, cols], dst.at[part, cols], sems.at[j, span * steps + step]))
    few = pltpu.make_async_copy(parent_hbm, parent, parent_sem)
    few.start()
    for copy in copies:
        copy.start()
    length[...] = jnp.full(length.shape, seg_len[0], jnp.int32)
    few.wait()
    write_weights(grid, parent, up, down)
    live = lax.broadcasted_iota(jnp.int32, (rows, HD), 0) < seg_len[0]
    for head in range(width // HD):
        if head % (width // HD // spans) == 0:
            span = head // (width // HD // spans)
            for copy in copies[span * 2 * steps : (span + 1) * 2 * steps]:
                copy.wait()
        cols = head_cols(head)
        masked = jnp.where(live, keys[:, cols], jnp.zeros((), BF16))
        full[head * HD : (head + 1) * HD, :] = tn(masked, values[:, cols]).astype(BF16)
    write_halves(full, outs, my_place(grid)[2], grid[2])


def mix_kernel(sources, first, weights, *refs):
    blocks, outs = refs[:sources], refs[-sources:]
    rows = outs[0].shape[0]
    chunk = min(rows, 64)
    for start in range(0, rows, chunk):
        part = slice(start, start + chunk)
        loaded = [block[first + start : first + start + chunk, :].astype(F32) for block in blocks]
        for out_step, out in enumerate(outs):
            at = out_step * sources
            total = weights[at : at + 1, :] * loaded[0]
            for in_step in range(1, sources):
                total += weights[at + in_step : at + in_step + 1, :] * loaded[in_step]
            out[part, :] = total.astype(BF16)


def live_rows(length, rows):
    return lax.broadcasted_iota(jnp.int32, (rows, HD), 0) < length[:, :HD]


def keep_mask(length, turned):
    rows = length.shape[1]
    first = lax.broadcasted_iota(jnp.int32, (rows, rows), 0)
    second = lax.broadcasted_iota(jnp.int32, (rows, rows), 1)
    if turned:
        return (first <= second) & (first < length[...])
    return (second <= first) & (second < length[...])


def split_refs(refs, *counts):
    parts, at = [], 0
    for count in counts:
        parts.append(refs[at : at + count])
        at += count
    return parts


def head_of(pieces, head):
    per_piece = pieces[0].shape[1] // HD
    return pieces[head // per_piece], head_cols(head % per_piece)


def fetch_kernel(source, _, out, sems):
    copies = row_copies(source, out, sems)
    for copy in copies:
        copy.start()
    for copy in copies:
        copy.wait()


def local_kernel(heads, length, queries, keys, values, *rest):
    local = rest[-1]
    keep = keep_mask(length, False)
    for head in range(heads):
        cols = head_cols(head)
        scores = jnp.where(keep, nt(queries[:, cols], keys[:, cols]), 0.0).astype(BF16)
        local[:, cols] = nn(scores, values[:, cols])


def token_rows(total):
    return jnp.sum(jnp.transpose(total), axis=0, keepdims=True)


def token_columns(row):
    return jnp.transpose(jnp.broadcast_to(row, (HD, row.shape[1])))


def carry_kernel(piece, grid, counts, scale, length, queries, local, cotangent, gain, *rest):
    received, rest = rest[: sum(counts)], rest[sum(counts) :]
    before, (attention, sums, prefix) = rest[:-3], rest[-3:]
    join_halves(split_refs(received, *counts), prefix, my_place(grid)[2], grid[2])
    rows, width = attention.shape
    factor = jnp.where(live_rows(length, rows), scale, 0.0)
    squares = jnp.zeros((rows, HD), F32)
    products = jnp.zeros((rows, HD), F32)
    for head in range(width // HD):
        cols = head_cols(head)
        whole = head_cols(piece * width // HD + head)
        carried = nn(queries[:, whole], prefix[head * HD : (head + 1) * HD, :])
        out = factor * (carried + local[:, whole])
        attention[:, cols] = out
        squares += out * out
        products += out * (cotangent[:, whole].astype(F32) * gain[:, whole])
    both = jnp.concatenate([token_rows(squares), token_rows(products)], axis=0)
    for other in before:
        both += other[...]
    sums[...] = both


def grad_kernel(piece, groups, grid, scale, length, queries, cotangent, gain, *rest):
    all_sums, attention, rest = split_refs(rest, groups, FORWARD_PIECES, len(rest) - groups - FORWARD_PIECES)
    (grad_out, inverse_rms), halves, full = rest[:2], rest[2:-1], rest[-1]
    rows, width = grad_out.shape
    features = HEADS * HD
    total = all_sums[0][...]
    for other in all_sums[1:]:
        total = total + other[...]
    inverse = lax.rsqrt(total[0:1, :] / features + EPSILON)
    inverse_rms[...] = inverse
    live = lax.broadcasted_iota(jnp.int32, (1, rows), 1) < length[...]
    live_inverse = jnp.where(live, inverse, 0.0)
    shrink = live_inverse * inverse * (inverse * total[1:2, :]) / features
    live_inverse = token_columns(live_inverse)
    shrink = token_columns(shrink)
    for head in range(width // HD):
        cols = head_cols(head)
        place = piece * width // HD + head
        whole = head_cols(place)
        out_piece, at = head_of(attention, place)
        gain_grad = cotangent[:, whole].astype(F32) * gain[:, whole]
        grad = (live_inverse * gain_grad - out_piece[:, at] * shrink).astype(BF16)
        grad_out[:, cols] = grad
        full[head * HD : (head + 1) * HD, :] = (scale * tn(queries[:, whole], grad)).astype(BF16)
    write_halves(full, halves, my_place(grid)[2], grid[2])


def row_copies(source, target, sems):
    rows = target.shape[0]
    chunk = rows // 4 if rows % 64 == 0 else rows
    parts = [pl.ds(step * chunk, chunk) for step in range(rows // chunk)]
    return [pltpu.make_async_copy(source.at[p, :], target.at[p, :], sems.at[j]) for j, p in enumerate(parts)]


def column_copies(sources, targets, first, count, sems):
    cols = slice(first * HD, (first + count) * HD)
    return [
        pltpu.make_async_copy(src.at[:, cols], dst.at[:, cols], sems.at[j])
        for j, (src, dst) in enumerate(zip(sources, targets))
    ]


def query_kernel(heads, group, scale, length, inverse_rms, gain, queries, keys, values, *rest):
    sizes = (BACKWARD_PIECES, FORWARD_PIECES, FORWARD_PIECES)
    grads, attention, prefix, rest = split_refs(rest, *sizes, len(rest) - sum(sizes))
    attended_hbm, query_hbm, attended, query_grad, key_part, token, sems = rest
    token[...] = jnp.zeros_like(token)
    keep = keep_mask(length, False)
    inverse = token_columns(inverse_rms[...])
    copies = []
    for head in range(heads):
        cols = head_cols(head)
        grad_piece, at = head_of(grads, head)
        grad = grad_piece[:, at]
        out_piece, at = head_of(attention, head)
        per_piece = heads // FORWARD_PIECES
        prefix_piece, state = prefix[head // per_piece], head % per_piece
        grad_scores = jnp.where(keep, nt(grad, values[:, cols]), 0.0).astype(BF16)
        carried = nt(grad, prefix_piece[state * HD : (state + 1) * HD, :])
        query_grad[:, cols] = (scale * (carried + nn(grad_scores, keys[:, cols]))).astype(BF16)
        key_part[:, cols] = scale * tn(grad_scores, queries[:, cols])
        attended[:, cols] = (out_piece[:, at] * inverse * gain[:, cols]).astype(BF16)
        if (head + 1) % group == 0 and head + 1 < heads:
            step = head // group
            some = column_copies(
                (attended, query_grad), (attended_hbm, query_hbm), step * group, group, sems.at[step]
            )
            for copy in some:
                copy.start()
            copies += some
    for copy in copies:
        copy.wait()


def value_kernel(heads, group, scale, length, queries, keys, attended, query_grad, *rest):
    grads, (attended_hbm, query_hbm, value_part, sems) = rest[:BACKWARD_PIECES], rest[-4:]
    copies = column_copies((attended, query_grad), (attended_hbm, query_hbm), heads - group, group, sems)
    for copy in copies:
        copy.start()
    keep = keep_mask(length, True)
    for head in range(heads):
        cols = head_cols(head)
        grad_piece, at = head_of(grads, head)
        turned = jnp.where(keep, nt(keys[:, cols], queries[:, cols]), 0.0).astype(BF16)
        value_part[:, cols] = scale * nn(turned, grad_piece[:, at])
    for copy in copies:
        copy.wait()


def final_kernel(piece, grid, counts, length, keys, values, key_part, value_part, *rest):
    received, rest = rest[: sum(counts)], rest[sum(counts) :]
    key_hbm, value_hbm, key_grad, value_grad, below, sems = rest[-6:]
    pair = grid[2]
    join_halves(split_refs(received, *counts), below, my_place(grid)[2], pair)
    rows, width = key_grad.shape
    live = jnp.where(live_rows(length, rows), 1.0, 0.0)
    per_half = width // HD // pair
    group = 2 if per_half % 2 == 0 else 1
    copies = []
    for head in range(width // HD):
        half, within = head // per_half, head % per_half
        cols = head_cols(head)
        place = half * (keys.shape[1] // HD // pair) + piece * per_half + within
        whole = head_cols(place)
        state = below[head * HD : (head + 1) * HD, :]
        key_grad[:, cols] = (key_part[:, whole] + live * nt(values[:, whole], state)).astype(BF16)
        value_grad[:, cols] = (value_part[:, whole] + live * nn(keys[:, whole], state)).astype(BF16)
        if (head + 1) % group == 0:
            done = slice((head + 1 - group) * HD, (head + 1) * HD)
            there = slice((place + 1 - group) * HD, (place + 1) * HD)
            for j, (src, dst) in enumerate(((key_grad, key_hbm), (value_grad, value_hbm))):
                copy = pltpu.make_async_copy(src.at[:, done], dst.at[:, there], sems.at[j, head // group])
                copy.start()
                copies.append(copy)
    for copy in copies:
        copy.wait()


def in_hbm(x):
    return pltpu.with_memory_space_constraint(x, pltpu.HBM)


def call(kernel, out_shape, operands, scratch=(), flops=0, stream=(), scalars=(), after=(), out_specs=None, aliases=None):
    moved = sum(math.prod(x.shape) * x.dtype.itemsize for x in operands)
    moved += sum(math.prod(x.shape) * x.dtype.itemsize for x in out_shape)
    specs = [SMEM if j in scalars else HBM if j in stream else VMEM for j in range(len(operands))]
    operands = [in_hbm(x) if j in stream else x for j, x in enumerate(operands)]
    return pl.pallas_call(
        kernel,
        out_shape=out_shape,
        in_specs=specs + [ANY] * len(after),
        out_specs=out_specs or [VMEM] * len(out_shape),
        scratch_shapes=list(scratch),
        input_output_aliases=aliases or {},
        compiler_params=pltpu.CompilerParams(vmem_limit_bytes=VMEM_LIMIT),
        cost_estimate=pl.CostEstimate(flops=flops, bytes_accessed=moved, transcendentals=0),
    )(*operands, *after)


def line_send(block, grid, step, flip, gather):
    moves = []
    for device in range(grid[0] * grid[1] * grid[2]):
        place = place_of(grid, device)
        if gather and flip:
            row, column, valid = along(grid, (place[0], place[1], place[2] ^ 1), step, True, True)
        else:
            row, column, valid = along(grid, place, step, gather, True)
        if valid:
            moves.append((device, member(grid, row, column, place[2] ^ flip)))
    return lax.ppermute(block, "seg", moves)


def gather_line(halves, grid):
    pair = grid[2]
    arrived = {0: halves[0]}
    for step in range(line_length(grid)):
        for flip in range(pair):
            if step or flip:
                arrived[step * pair + flip] = line_send(halves[flip], grid, step, flip, True)
    return [arrived[j] for j in range(len(arrived))]


def scatter_line(sums, grid):
    pair = grid[2]
    parts = [[] for _ in range(pair)]
    for step in reversed(range(line_length(grid))):
        for flip in range(pair):
            block = sums[step * pair + flip]
            parts[flip].append(line_send(block, grid, step, flip, False) if step or flip else block)
    return parts


def token_sums(sums, groups):
    parts = [sums]
    for step in [j for j in range(1, groups) if j != 2] + [2] * (groups > 2):
        moves = [(j, target_of(j, step, groups)) for j in range(groups)]
        parts.append(lax.ppermute(sums, "head", moves))
    return parts


def per_device(segs, groups, queries, key_rows, values, cotangent, out_gain, parent, seg_len):
    rows, features = queries.shape[1:]
    heads = features // HD
    grid = grid_of(segs)
    pair = grid[2]
    scale = 1.0 / math.sqrt(HD * rows)
    cot = cotangent[0]
    gain = out_gain[None]
    shape = jax.ShapeDtypeStruct
    narrow = shape((rows, features), BF16)
    wide = shape((rows, features), F32)
    row = shape((1, rows), F32)
    members = line_length(grid) * pair
    weight_rows = shape((members * members, HD), F32)
    sems = pltpu.SemaphoreType.DMA((2, heads))
    counts = [line_length(grid)] * pair
    unit = 2 * heads * rows * HD

    def halves(pieces):
        return [shape((features // (pair * pieces), HD), BF16)] * pair

    def mix(arrived, weights, piece, pieces, after=()):
        tall = arrived[0].shape[0] // pieces
        like = [shape((tall, HD), BF16)] * members
        return call(functools.partial(mix_kernel, members, piece * tall), like, (weights, *arrived), after=after)

    def flat(parts):
        return [block for part in parts for block in part]

    key, value, length, up, down, *own = call(
        functools.partial(state_kernel, grid),
        [narrow, narrow, shape((1, rows), jnp.int32), weight_rows, weight_rows] + halves(FORWARD_PIECES) * FORWARD_PIECES,
        (seg_len, key_rows[0], values[0], parent[None]),
        [pltpu.VMEM((features, HD), BF16), sems, pltpu.SMEM((1, segs), jnp.int32), pltpu.SemaphoreType.DMA(())],
        unit * HD, (1, 2, 3), (0,),
    )
    (query,) = call(fetch_kernel, [narrow], (queries[0],), [pltpu.SemaphoreType.DMA((4,))], 0, (0,), after=(own[0],))
    mixed = []
    for part in split_refs(own, *[pair] * FORWARD_PIECES):
        mixed.append(mix(gather_line(part, grid), up, 0, 1, () if mixed else (query,)))
    (local,) = call(
        functools.partial(local_kernel, heads),
        [wide], (length, query, key, value), (), unit * rows * 2, after=(mixed[0][0],),
    )
    attention, prefix, sums = [], [], []
    width = features // FORWARD_PIECES
    for piece in range(FORWARD_PIECES):
        out, total, joined = call(
            functools.partial(carry_kernel, piece, grid, counts, scale),
            [shape((rows, width), F32), shape((2, rows), F32), shape((width, HD), BF16)],
            (length, query, local, cot, gain, *flat(scatter_line(mixed[piece], grid)), *sums),
            (), unit * HD // FORWARD_PIECES,
        )
        attention.append(out)
        prefix.append(joined)
        sums = [total]
    sums = token_sums(sums[0], groups)
    grads, state_grad = [], []
    width = features // BACKWARD_PIECES
    for piece in range(BACKWARD_PIECES):
        grad_out, inverse_rms, *parts = call(
            functools.partial(grad_kernel, piece, len(sums), grid, scale),
            [shape((rows, width), BF16), row] + halves(BACKWARD_PIECES),
            (length, query, cot, gain, *sums, *attention), [pltpu.VMEM((width, HD), BF16)],
            unit * HD // BACKWARD_PIECES,
        )
        grads.append(grad_out)
        state_grad.append(parts)
    group = 4 if heads % 4 == 0 else 1
    attended, query_grad, attended_rest, query_rest, key_part, token = call(
        functools.partial(query_kernel, heads, group, scale),
        [narrow, narrow, narrow, narrow, wide, shape((8, HD), F32)],
        (length, inverse_rms, gain, query, key, value, *grads, *attention, *prefix),
        [pltpu.SemaphoreType.DMA((heads // group, 2))], unit * (3 * rows + HD),
        out_specs=[HBM, HBM] + [VMEM] * 4,
    )
    (part,) = state_grad
    arrived = gather_line(part, grid)
    mixed = []
    for piece in range(RETURN_PIECES):
        mixed.append(mix(arrived, down, piece, RETURN_PIECES, (token, *mixed[-1][:1]) if mixed else (token,)))
    operands = (length, query, key, attended_rest, query_rest, *grads, attended, query_grad)
    last = len(operands) - 2
    attended, query_grad, value_part = call(
        functools.partial(value_kernel, heads, group, scale),
        [narrow, narrow, wide], operands, [pltpu.SemaphoreType.DMA((2,))], unit * 2 * rows, (last, last + 1),
        after=(mixed[-1][0],), out_specs=[HBM, HBM, VMEM], aliases={last: 0, last + 1: 1},
    )
    results = []
    width = features // RETURN_PIECES
    for piece in range(RETURN_PIECES):
        below = flat(scatter_line(mixed[piece], grid))
        operands = (length, key, value, key_part, value_part, *below, *results)
        first = len(operands) - len(results)
        results = call(
            functools.partial(final_kernel, piece, grid, counts),
            [narrow, narrow], operands,
            [pltpu.VMEM((rows, width), BF16)] * 2 + [pltpu.VMEM((width, HD), BF16), sems],
            2 * unit * HD // RETURN_PIECES,
            range(first, len(operands)), out_specs=[HBM, HBM],
            aliases={first + j: j for j in range(len(results))},
        )
    key_grad, value_grad = results
    return attended[None], query_grad[None], key_grad[None], value_grad[None]


def solution(mesh):
    split = P("seg", None, "head")
    return jax.shard_map(
        functools.partial(per_device, mesh.shape["seg"], mesh.shape["head"]),
        mesh=mesh,
        in_specs=(split, split, split, split, P("head"), P(), P("seg")),
        out_specs=(split, split, split, split),
        check_vma=False,
    )
```

```python
import functools
import math

import jax
import jax.numpy as jnp
from jax import lax
from jax.experimental import pallas as pl
from jax.experimental.pallas import tpu as pltpu
from jax.sharding import PartitionSpec as P

HEADS = 64
HD = 128
EPSILON = 1e-06
F32 = jnp.float32
BF16 = jnp.bfloat16
VMEM_LIMIT = 24 * 1024 * 1024
FORWARD_PIECES = 2
BACKWARD_PIECES = 1
RETURN_PIECES = 2

VMEM = pl.BlockSpec(memory_space=pltpu.VMEM)
SMEM = pl.BlockSpec(memory_space=pltpu.SMEM)
HBM = pl.BlockSpec(memory_space=pltpu.HBM)
ANY = pl.BlockSpec(memory_space=pl.ANY)


def dot(a, b, contract):
    return lax.dot_general(a, b, (contract, ((), ())), preferred_element_type=F32)


def nn(a, b):
    return dot(a, b, ((1,), (0,)))


def nt(a, b):
    return dot(a, b, ((1,), (1,)))


def tn(a, b):
    return dot(a, b, ((0,), (0,)))


def head_cols(head):
    return slice(head * HD, (head + 1) * HD)


def target_of(place, step, size):
    if size & (size - 1) == 0:
        return place ^ step
    return (place + step) % size


def source_of(place, step, size):
    if size & (size - 1) == 0:
        return place ^ step
    return (place + size - step) % size


def grid_of(segs):
    pair = 2 if segs % 2 == 0 else 1
    chips = segs // pair
    columns = next(c for c in range(1, chips + 1) if chips % c == 0 and c * c >= chips)
    return chips // columns, columns, pair


def member(grid, row, column, core):
    return (row * grid[1] + column) * grid[2] + core


def place_of(grid, device):
    chip = device // grid[2]
    return chip // grid[1], chip % grid[1], device % grid[2]


def along(grid, place, step, gather, ahead):
    row, column, core = place
    shift = target_of if ahead else source_of
    by_row = (core == 0) if gather else (core != 0)
    valid_column = step < grid[1]
    valid_row = step < grid[0]
    if isinstance(core, int):
        if by_row:
            return row, shift(column, step, grid[1]), valid_column
        return shift(row, step, grid[0]), column, valid_row
    moved_column = shift(column, min(step, grid[1] - 1), grid[1])
    moved_row = shift(row, min(step, grid[0] - 1), grid[0])
    return (
        jnp.where(by_row, row, moved_row),
        jnp.where(by_row, moved_column, column),
        jnp.where(by_row, valid_column, valid_row),
    )


def my_place(grid):
    me = lax.axis_index("seg")
    chip = lax.div(me, grid[2])
    return lax.div(chip, grid[1]), lax.rem(chip, grid[1]), lax.rem(me, grid[2])


def row_halves(full, core, pair):
    half = full.shape[0] // pair
    return [full.at[pl.ds(pl.multiple_of((core ^ j) * half, half), half), :] for j in range(pair)]


def join_halves(refs, layout, full, core, pair):
    refs = iter(refs)
    for half, firsts in zip(row_halves(full, core, pair), layout):
        rows = half.shape[0]
        terms = [next(refs)[first : first + rows, :].astype(F32) for first in firsts]
        half[...] = sum(terms[1:], terms[0]).astype(BF16)


def line_length(grid):
    return max(grid[0], grid[1])


def write_weights(grid, parent, up, down):
    place = my_place(grid)
    pair = grid[2]
    count = line_length(grid) * pair

    def is_ancestor(child, other):
        first = parent[0, child]
        second = jnp.where(first >= 0, parent[0, jnp.maximum(first, 0)], -1)
        return jnp.logical_or(other == first, other == second)

    for out_step in range(count):
        row, column, _ = along(grid, place, out_step // pair, False, True)
        target = member(grid, row, column, place[2] ^ (out_step % pair))
        for in_step in range(count):
            row, column, valid = along(grid, place, in_step // pair, True, False)
            source = member(grid, row, column, place[2] ^ (in_step % pair))
            at = out_step * count + in_step
            for rows, used in ((up, is_ancestor(target, source)), (down, is_ancestor(source, target))):
                weight = jnp.where(jnp.logical_and(used, valid), 1.0, 0.0)
                rows[at : at + 1, :] = jnp.full((1, HD), weight, F32)


def write_halves(full, outs, core, pair):
    rows = full.shape[0] * pair // len(outs)
    for piece in range(len(outs) // pair):
        halves = row_halves(full.at[pl.ds(piece * rows, rows), :], core, pair)
        for half, out in zip(halves, outs[piece * pair : (piece + 1) * pair]):
            out[...] = half[...]


def state_kernel(grid, seg_len, keys_hbm, values_hbm, parent_hbm, keys, values, length, up, down, *rest):
    outs, (full, sems, parent, parent_sem) = rest[:-4], rest[-4:]
    rows, width = keys.shape
    chunk = rows // 4 if rows % 64 == 0 else rows
    steps = rows // chunk
    spans = 2 if width % (2 * HD) == 0 else 1
    copies = []
    for span in range(spans):
        cols = slice(span * width // spans, (span + 1) * width // spans)
        for step in range(steps):
            part = slice(step * chunk, (step + 1) * chunk)
            for j, (src, dst) in enumerate(((keys_hbm, keys), (values_hbm, values))):
                copies.append(pltpu.make_async_copy(src.at[part, cols], dst.at[part, cols], sems.at[j, span * steps + step]))
    few = pltpu.make_async_copy(parent_hbm, parent, parent_sem)
    few.start()
    for copy in copies:
        copy.start()
    length[...] = jnp.full(length.shape, seg_len[0], jnp.int32)
    few.wait()
    write_weights(grid, parent, up, down)
    live = lax.broadcasted_iota(jnp.int32, (rows, HD), 0) < seg_len[0]
    for head in range(width // HD):
        if head % (width // HD // spans) == 0:
            span = head // (width // HD // spans)
            for copy in copies[span * 2 * steps : (span + 1) * 2 * steps]:
                copy.wait()
        cols = head_cols(head)
        masked = jnp.where(live, keys[:, cols], jnp.zeros((), BF16))
        full[head * HD : (head + 1) * HD, :] = tn(masked, values[:, cols]).astype(BF16)
    core, pair = my_place(grid)[2], grid[2]
    parts = FORWARD_PIECES * pair
    write_halves(full, outs[:parts], core, pair)
    if pair > 1:
        tall = outs[1].shape[0]
        for piece in range(FORWARD_PIECES):
            outs[parts][piece * tall : (piece + 1) * tall, :] = outs[piece * pair + 1][...]


def mix_kernel(firsts, pair, pieces, weights, *refs):
    sources = len(firsts)
    blocks, outs = refs[:sources], refs[-pair - (sources - pair) * pieces :]
    rows = outs[0].shape[0]
    chunk = min(rows // pieces, 64)
    for start in range(0, rows, chunk):
        part = slice(start, start + chunk)
        loaded = [block[first + start : first + start + chunk, :].astype(F32) for block, first in zip(blocks, firsts)]
        for target in range(sources):
            at = target * sources
            total = weights[at : at + 1, :] * loaded[0]
            for source in range(1, sources):
                total += weights[at + source : at + source + 1, :] * loaded[source]
            if target < pair:
                outs[target][part, :] = total.astype(BF16)
            else:
                piece, inner = divmod(start, rows // pieces)
                out = outs[pair + piece * (sources - pair) + target - pair]
                out[inner : inner + chunk, :] = total.astype(BF16)


def live_rows(length, rows):
    return lax.broadcasted_iota(jnp.int32, (rows, HD), 0) < length[:, :HD]


def keep_mask(length, turned):
    rows = length.shape[1]
    first = lax.broadcasted_iota(jnp.int32, (rows, rows), 0)
    second = lax.broadcasted_iota(jnp.int32, (rows, rows), 1)
    if turned:
        return (first <= second) & (first < length[...])
    return (second <= first) & (second < length[...])


def split_refs(refs, *counts):
    parts, at = [], 0
    for count in counts:
        parts.append(refs[at : at + count])
        at += count
    return parts


def head_of(pieces, head):
    per_piece = pieces[0].shape[1] // HD
    return pieces[head // per_piece], head_cols(head % per_piece)


def fetch_kernel(source, _, out, sems):
    copies = row_copies(source, out, sems)
    for copy in copies:
        copy.start()
    for copy in copies:
        copy.wait()


def local_kernel(heads, length, queries, keys, values, *rest):
    local = rest[-1]
    keep = keep_mask(length, False)
    for head in range(heads):
        cols = head_cols(head)
        scores = jnp.where(keep, nt(queries[:, cols], keys[:, cols]), 0.0).astype(BF16)
        local[:, cols] = nn(scores, values[:, cols])


def token_rows(total):
    return jnp.sum(jnp.transpose(total), axis=0, keepdims=True)


def token_columns(row):
    return jnp.transpose(jnp.broadcast_to(row, (HD, row.shape[1])))


def carry_kernel(piece, grid, layout, scale, length, queries, local, cotangent, gain, *rest):
    count = sum(map(len, layout))
    received, rest = rest[:count], rest[count:]
    before, (attention, sums, prefix) = rest[:-3], rest[-3:]
    join_halves(received, layout, prefix, my_place(grid)[2], grid[2])
    rows, width = attention.shape
    factor = jnp.where(live_rows(length, rows), scale, 0.0)
    squares = jnp.zeros((rows, HD), F32)
    products = jnp.zeros((rows, HD), F32)
    for head in range(width // HD):
        cols = head_cols(head)
        whole = head_cols(piece * width // HD + head)
        carried = nn(queries[:, whole], prefix[head * HD : (head + 1) * HD, :])
        out = factor * (carried + local[:, whole])
        attention[:, cols] = out
        squares += out * out
        products += out * (cotangent[:, whole].astype(F32) * gain[:, whole])
    both = jnp.concatenate([token_rows(squares), token_rows(products)], axis=0)
    for other in before:
        both += other[...]
    sums[...] = both


def grad_kernel(piece, groups, grid, scale, length, queries, cotangent, gain, *rest):
    all_sums, attention, rest = split_refs(rest, groups, FORWARD_PIECES, len(rest) - groups - FORWARD_PIECES)
    (grad_out, inverse_rms), halves, full = rest[:2], rest[2:-1], rest[-1]
    rows, width = grad_out.shape
    features = HEADS * HD
    total = all_sums[0][...]
    for other in all_sums[1:]:
        total = total + other[...]
    inverse = lax.rsqrt(total[0:1, :] / features + EPSILON)
    inverse_rms[...] = inverse
    live = lax.broadcasted_iota(jnp.int32, (1, rows), 1) < length[...]
    live_inverse = jnp.where(live, inverse, 0.0)
    shrink = live_inverse * inverse * (inverse * total[1:2, :]) / features
    live_inverse = token_columns(live_inverse)
    shrink = token_columns(shrink)
    for head in range(width // HD):
        cols = head_cols(head)
        place = piece * width // HD + head
        whole = head_cols(place)
        out_piece, at = head_of(attention, place)
        gain_grad = cotangent[:, whole].astype(F32) * gain[:, whole]
        grad = (live_inverse * gain_grad - out_piece[:, at] * shrink).astype(BF16)
        grad_out[:, cols] = grad
        full[head * HD : (head + 1) * HD, :] = (scale * tn(queries[:, whole], grad)).astype(BF16)
    write_halves(full, halves, my_place(grid)[2], grid[2])


def row_copies(source, target, sems):
    rows = target.shape[0]
    chunk = rows // 4 if rows % 64 == 0 else rows
    parts = [pl.ds(step * chunk, chunk) for step in range(rows // chunk)]
    return [pltpu.make_async_copy(source.at[p, :], target.at[p, :], sems.at[j]) for j, p in enumerate(parts)]


def column_copies(sources, targets, first, count, sems):
    cols = slice(first * HD, (first + count) * HD)
    return [
        pltpu.make_async_copy(src.at[:, cols], dst.at[:, cols], sems.at[j])
        for j, (src, dst) in enumerate(zip(sources, targets))
    ]


def query_kernel(heads, group, scale, length, inverse_rms, gain, queries, keys, values, *rest):
    sizes = (BACKWARD_PIECES, FORWARD_PIECES, FORWARD_PIECES)
    grads, attention, prefix, rest = split_refs(rest, *sizes, len(rest) - sum(sizes))
    attended_hbm, query_hbm, key_part, token, attended, query_grad, sems = rest
    token[...] = jnp.zeros_like(token)
    keep = keep_mask(length, False)
    inverse = token_columns(inverse_rms[...])
    copies = []
    for head in range(heads):
        cols = head_cols(head)
        grad_piece, at = head_of(grads, head)
        grad = grad_piece[:, at]
        out_piece, at = head_of(attention, head)
        per_piece = heads // FORWARD_PIECES
        prefix_piece, state = prefix[head // per_piece], head % per_piece
        grad_scores = jnp.where(keep, nt(grad, values[:, cols]), 0.0).astype(BF16)
        carried = nt(grad, prefix_piece[state * HD : (state + 1) * HD, :])
        query_grad[:, cols] = (scale * (carried + nn(grad_scores, keys[:, cols]))).astype(BF16)
        key_part[:, cols] = scale * tn(grad_scores, queries[:, cols])
        attended[:, cols] = (out_piece[:, at] * inverse * gain[:, cols]).astype(BF16)
        if (head + 1) % group == 0:
            step = head // group
            some = column_copies(
                (attended, query_grad), (attended_hbm, query_hbm), step * group, group, sems.at[step]
            )
            for copy in some:
                copy.start()
            copies += some
    for copy in copies:
        copy.wait()


def value_kernel(heads, scale, length, queries, keys, *rest):
    grads, value_part = rest[:BACKWARD_PIECES], rest[-1]
    keep = keep_mask(length, True)
    for head in range(heads):
        cols = head_cols(head)
        grad_piece, at = head_of(grads, head)
        turned = jnp.where(keep, nt(keys[:, cols], queries[:, cols]), 0.0).astype(BF16)
        value_part[:, cols] = scale * nn(turned, grad_piece[:, at])


def final_kernel(piece, grid, layout, length, keys, values, key_part, value_part, *rest):
    received, rest = rest[: sum(map(len, layout))], rest[sum(map(len, layout)) :]
    key_hbm, value_hbm, key_grad, value_grad, below, sems = rest[-6:]
    pair = grid[2]
    join_halves(received, layout, below, my_place(grid)[2], pair)
    rows, width = key_grad.shape
    live = jnp.where(live_rows(length, rows), 1.0, 0.0)
    per_half = width // HD // pair
    group = 2 if per_half % 2 == 0 else 1
    copies = []
    for head in range(width // HD):
        half, within = head // per_half, head % per_half
        cols = head_cols(head)
        place = half * (keys.shape[1] // HD // pair) + piece * per_half + within
        whole = head_cols(place)
        state = below[head * HD : (head + 1) * HD, :]
        key_grad[:, cols] = (key_part[:, whole] + live * nt(values[:, whole], state)).astype(BF16)
        value_grad[:, cols] = (value_part[:, whole] + live * nn(keys[:, whole], state)).astype(BF16)
        if (head + 1) % group == 0:
            done = slice((head + 1 - group) * HD, (head + 1) * HD)
            there = slice((place + 1 - group) * HD, (place + 1) * HD)
            for j, (src, dst) in enumerate(((key_grad, key_hbm), (value_grad, value_hbm))):
                copy = pltpu.make_async_copy(src.at[:, done], dst.at[:, there], sems.at[j, head // group])
                copy.start()
                copies.append(copy)
    for copy in copies:
        copy.wait()


def in_hbm(x):
    return pltpu.with_memory_space_constraint(x, pltpu.HBM)


def call(kernel, out_shape, operands, scratch=(), flops=0, stream=(), scalars=(), after=(), out_specs=None, aliases=None):
    moved = sum(math.prod(x.shape) * x.dtype.itemsize for x in operands)
    moved += sum(math.prod(x.shape) * x.dtype.itemsize for x in out_shape)
    specs = [SMEM if j in scalars else HBM if j in stream else VMEM for j in range(len(operands))]
    operands = [in_hbm(x) if j in stream else x for j, x in enumerate(operands)]
    return pl.pallas_call(
        kernel,
        out_shape=out_shape,
        in_specs=specs + [ANY] * len(after),
        out_specs=out_specs or [VMEM] * len(out_shape),
        scratch_shapes=list(scratch),
        input_output_aliases=aliases or {},
        compiler_params=pltpu.CompilerParams(vmem_limit_bytes=VMEM_LIMIT),
        cost_estimate=pl.CostEstimate(flops=flops, bytes_accessed=moved, transcendentals=0),
    )(*operands, *after)


def line_send(block, grid, step, flip, gather):
    moves = []
    for device in range(grid[0] * grid[1] * grid[2]):
        place = place_of(grid, device)
        if gather and flip:
            row, column, valid = along(grid, (place[0], place[1], place[2] ^ 1), step, True, True)
        else:
            row, column, valid = along(grid, place, step, gather, True)
        if valid:
            moves.append((device, member(grid, row, column, place[2] ^ flip)))
    return lax.ppermute(block, "seg", moves)


def gather_line(pieces, whole, grid):
    pair = grid[2]
    swapped = [line_send(whole, grid, 0, flip, True) for flip in range(1, pair)]
    found = []
    for number, halves in enumerate(pieces):
        first = number * halves[0].shape[0]
        blocks = [(halves[0], 0)] + [(block, first) for block in swapped]
        for step in range(1, line_length(grid)):
            blocks += [(line_send(halves[flip], grid, step, flip, True), 0) for flip in range(pair)]
        found.append(blocks)
    return found


def scatter_line(sums, grid, pieces):
    pair = grid[2]
    others = (line_length(grid) - 1) * pair
    swapped = [line_send(sums[flip], grid, 0, flip, False) for flip in range(1, pair)]
    found = []
    for piece in range(pieces):
        first = piece * (sums[0].shape[0] // pieces)
        parts = [[] for _ in range(pair)]
        for step in range(1, line_length(grid)):
            for flip in range(pair):
                block = sums[pair + piece * others + (step - 1) * pair + flip]
                parts[flip].append((line_send(block, grid, step, flip, False), 0))
        for flip, block in enumerate([sums[0]] + swapped):
            parts[flip].append((block, first))
        found.append(parts)
    return found


def token_sums(sums, groups):
    parts = [sums]
    for step in [j for j in range(1, groups) if j != 2] + [2] * (groups > 2):
        moves = [(j, target_of(j, step, groups)) for j in range(groups)]
        parts.append(lax.ppermute(sums, "head", moves))
    return parts


def per_device(segs, groups, queries, key_rows, values, cotangent, out_gain, parent, seg_len):
    rows, features = queries.shape[1:]
    heads = features // HD
    grid = grid_of(segs)
    pair = grid[2]
    scale = 1.0 / math.sqrt(HD * rows)
    cot = cotangent[0]
    gain = out_gain[None]
    shape = jax.ShapeDtypeStruct
    narrow = shape((rows, features), BF16)
    wide = shape((rows, features), F32)
    row = shape((1, rows), F32)
    members = line_length(grid) * pair
    weight_rows = shape((members * members, HD), F32)
    sems = pltpu.SemaphoreType.DMA((2, heads))
    unit = 2 * heads * rows * HD

    def halves(pieces):
        return [shape((features // (pair * pieces), HD), BF16)] * pair

    def mix(arrived, weights, pieces, after=()):
        blocks, firsts = zip(*arrived)
        tall = blocks[0].shape[0]
        like = [shape((tall, HD), BF16)] * pair + [shape((tall // pieces, HD), BF16)] * ((members - pair) * pieces)
        return call(functools.partial(mix_kernel, firsts, pair, pieces), like, (weights, *blocks), after=after)

    def unzip(parts):
        blocks = [block for part in parts for block, _ in part]
        return blocks, [[first for _, first in part] for part in parts]

    key, value, length, up, down, *own = call(
        functools.partial(state_kernel, grid),
        [narrow, narrow, shape((1, rows), jnp.int32), weight_rows, weight_rows] + halves(FORWARD_PIECES) * FORWARD_PIECES + halves(1)[1:],
        (seg_len, key_rows[0], values[0], parent[None]),
        [pltpu.VMEM((features, HD), BF16), sems, pltpu.SMEM((1, segs), jnp.int32), pltpu.SemaphoreType.DMA(())],
        unit * HD, (1, 2, 3), (0,),
    )
    (query,) = call(fetch_kernel, [narrow], (queries[0],), [pltpu.SemaphoreType.DMA((4,))], 0, (0,), after=(own[0],))
    *parts, whole = split_refs(own, *[pair] * FORWARD_PIECES, pair - 1)
    mixed = []
    for arrived in gather_line(parts, whole[0] if whole else None, grid):
        mixed.append(mix(arrived, up, 1, () if mixed else (query,)))
    (local,) = call(
        functools.partial(local_kernel, heads),
        [wide], (length, query, key, value), (), unit * rows * 2, after=(mixed[0][0],),
    )
    attention, prefix, sums = [], [], []
    width = features // FORWARD_PIECES
    for piece in range(FORWARD_PIECES):
        blocks, layout = unzip(scatter_line(mixed[piece], grid, 1)[0])
        out, total, joined = call(
            functools.partial(carry_kernel, piece, grid, layout, scale),
            [shape((rows, width), F32), shape((2, rows), F32), shape((width, HD), BF16)],
            (length, query, local, cot, gain, *blocks, *sums),
            (), unit * HD // FORWARD_PIECES,
        )
        attention.append(out)
        prefix.append(joined)
        sums = [total]
    sums = token_sums(sums[0], groups)
    grads, state_grad = [], []
    width = features // BACKWARD_PIECES
    for piece in range(BACKWARD_PIECES):
        grad_out, inverse_rms, *parts = call(
            functools.partial(grad_kernel, piece, len(sums), grid, scale),
            [shape((rows, width), BF16), row] + halves(BACKWARD_PIECES),
            (length, query, cot, gain, *sums, *attention), [pltpu.VMEM((width, HD), BF16)],
            unit * HD // BACKWARD_PIECES,
        )
        grads.append(grad_out)
        state_grad.append(parts)
    group = 4 if heads % 4 == 0 else 1
    attended, query_grad, key_part, token = call(
        functools.partial(query_kernel, heads, group, scale),
        [narrow, narrow, wide, shape((8, HD), F32)],
        (length, inverse_rms, gain, query, key, value, *grads, *attention, *prefix),
        [pltpu.VMEM(narrow.shape, BF16)] * 2 + [pltpu.SemaphoreType.DMA((heads // group, 2))], unit * (3 * rows + HD),
        out_specs=[HBM, HBM, VMEM, VMEM],
    )
    (arrived,) = gather_line(state_grad, state_grad[0][-1], grid)
    mixed = mix(arrived, down, RETURN_PIECES, (token,))
    (value_part,) = call(
        functools.partial(value_kernel, heads, scale),
        [wide], (length, query, key, *grads), (), unit * 2 * rows, after=(mixed[0],),
    )
    returned = scatter_line(mixed, grid, RETURN_PIECES)
    results = []
    width = features // RETURN_PIECES
    for piece in range(RETURN_PIECES):
        below, layout = unzip(returned[piece])
        operands = (length, key, value, key_part, value_part, *below, *results)
        first = len(operands) - len(results)
        results = call(
            functools.partial(final_kernel, piece, grid, layout),
            [narrow, narrow], operands,
            [pltpu.VMEM((rows, width), BF16)] * 2 + [pltpu.VMEM((width, HD), BF16), sems],
            2 * unit * HD // RETURN_PIECES,
            range(first, len(operands)), out_specs=[HBM, HBM],
            aliases={first + j: j for j in range(len(results))},
        )
    key_grad, value_grad = results
    return attended[None], query_grad[None], key_grad[None], value_grad[None]


def solution(mesh):
    split = P("seg", None, "head")
    return jax.shard_map(
        functools.partial(per_device, mesh.shape["seg"], mesh.shape["head"]),
        mesh=mesh,
        in_specs=(split, split, split, split, P("head"), P(), P("seg")),
        out_specs=(split, split, split, split),
        check_vma=False,
    )
```

```python
import functools
import math

import jax
import jax.numpy as jnp
from jax import lax
from jax.experimental import pallas as pl
from jax.experimental.pallas import tpu as pltpu
from jax.sharding import PartitionSpec as P

HEADS = 64
HD = 128
EPSILON = 1e-06
F32 = jnp.float32
BF16 = jnp.bfloat16
VMEM_LIMIT = 24 * 1024 * 1024
FORWARD_PIECES = 2
BACKWARD_PIECES = 1
RETURN_PIECES = 2

VMEM = pl.BlockSpec(memory_space=pltpu.VMEM)
SMEM = pl.BlockSpec(memory_space=pltpu.SMEM)
HBM = pl.BlockSpec(memory_space=pltpu.HBM)
ANY = pl.BlockSpec(memory_space=pl.ANY)


def dot(a, b, contract):
    return lax.dot_general(a, b, (contract, ((), ())), preferred_element_type=F32)


def nn(a, b):
    return dot(a, b, ((1,), (0,)))


def nt(a, b):
    return dot(a, b, ((1,), (1,)))


def tn(a, b):
    return dot(a, b, ((0,), (0,)))


def head_cols(head):
    return slice(head * HD, (head + 1) * HD)


def target_of(place, step, size):
    if size & (size - 1) == 0:
        return place ^ step
    return (place + step) % size


def source_of(place, step, size):
    if size & (size - 1) == 0:
        return place ^ step
    return (place + size - step) % size


def grid_of(segs):
    pair = 2 if segs % 2 == 0 else 1
    chips = segs // pair
    columns = next(c for c in range(1, chips + 1) if chips % c == 0 and c * c >= chips)
    return chips // columns, columns, pair


def member(grid, row, column, core):
    return (row * grid[1] + column) * grid[2] + core


def place_of(grid, device):
    chip = device // grid[2]
    return chip // grid[1], chip % grid[1], device % grid[2]


def along(grid, place, step, gather, ahead):
    row, column, core = place
    shift = target_of if ahead else source_of
    by_row = (core == 0) if gather else (core != 0)
    valid_column = step < grid[1]
    valid_row = step < grid[0]
    if isinstance(core, int):
        if by_row:
            return row, shift(column, step, grid[1]), valid_column
        return shift(row, step, grid[0]), column, valid_row
    moved_column = shift(column, min(step, grid[1] - 1), grid[1])
    moved_row = shift(row, min(step, grid[0] - 1), grid[0])
    return (
        jnp.where(by_row, row, moved_row),
        jnp.where(by_row, moved_column, column),
        jnp.where(by_row, valid_column, valid_row),
    )


def my_place(grid):
    me = lax.axis_index("seg")
    chip = lax.div(me, grid[2])
    return lax.div(chip, grid[1]), lax.rem(chip, grid[1]), lax.rem(me, grid[2])


def row_halves(full, core, pair):
    half = full.shape[0] // pair
    return [full.at[pl.ds(pl.multiple_of((core ^ j) * half, half), half), :] for j in range(pair)]


def join_halves(parts, full, core, pair):
    for half, terms in zip(row_halves(full, core, pair), parts):
        total = terms[0][...].astype(F32)
        for term in terms[1:]:
            total += term[...].astype(F32)
        half[...] = total.astype(BF16)


def line_length(grid):
    return max(grid[0], grid[1])


def write_weights(grid, parent, up, down):
    place = my_place(grid)
    pair = grid[2]
    count = line_length(grid) * pair

    def is_ancestor(child, other):
        first = parent[0, child]
        second = jnp.where(first >= 0, parent[0, jnp.maximum(first, 0)], -1)
        return jnp.logical_or(other == first, other == second)

    for out_step in range(count):
        row, column, _ = along(grid, place, out_step // pair, False, True)
        target = member(grid, row, column, place[2] ^ (out_step % pair))
        for in_step in range(count):
            row, column, valid = along(grid, place, in_step // pair, True, False)
            source = member(grid, row, column, place[2] ^ (in_step % pair))
            at = out_step * count + in_step
            for rows, used in ((up, is_ancestor(target, source)), (down, is_ancestor(source, target))):
                weight = jnp.where(jnp.logical_and(used, valid), 1.0, 0.0)
                rows[at : at + 1, :] = jnp.full((1, HD), weight, F32)


def write_halves(full, outs, core, pair):
    rows = full.shape[0] * pair // len(outs)
    for piece in range(len(outs) // pair):
        halves = row_halves(full.at[pl.ds(piece * rows, rows), :], core, pair)
        for half, out in zip(halves, outs[piece * pair : (piece + 1) * pair]):
            out[...] = half[...]


def state_kernel(grid, seg_len, keys_hbm, values_hbm, parent_hbm, keys, values, length, up, down, *rest):
    outs, (full, sems, parent, parent_sem) = rest[:-4], rest[-4:]
    rows, width = keys.shape
    chunk = rows // 4 if rows % 64 == 0 else rows
    steps = rows // chunk
    spans = 2 if width % (2 * HD) == 0 else 1
    copies = []
    for span in range(spans):
        cols = slice(span * width // spans, (span + 1) * width // spans)
        for step in range(steps):
            part = slice(step * chunk, (step + 1) * chunk)
            for j, (src, dst) in enumerate(((keys_hbm, keys), (values_hbm, values))):
                copies.append(pltpu.make_async_copy(src.at[part, cols], dst.at[part, cols], sems.at[j, span * steps + step]))
    few = pltpu.make_async_copy(parent_hbm, parent, parent_sem)
    few.start()
    for copy in copies:
        copy.start()
    length[...] = jnp.full(length.shape, seg_len[0], jnp.int32)
    few.wait()
    write_weights(grid, parent, up, down)
    live = lax.broadcasted_iota(jnp.int32, (rows, HD), 0) < seg_len[0]
    for head in range(width // HD):
        if head % (width // HD // spans) == 0:
            span = head // (width // HD // spans)
            for copy in copies[span * 2 * steps : (span + 1) * 2 * steps]:
                copy.wait()
        cols = head_cols(head)
        masked = jnp.where(live, keys[:, cols], jnp.zeros((), BF16))
        full[head * HD : (head + 1) * HD, :] = tn(masked, values[:, cols]).astype(BF16)
    write_halves(full, outs, my_place(grid)[2], grid[2])


def mix_kernel(sources, first, weights, *refs):
    blocks, outs = refs[:sources], refs[-sources:]
    rows = outs[0].shape[0]
    chunk = min(rows, 64)
    for start in range(0, rows, chunk):
        part = slice(start, start + chunk)
        loaded = [block[first + start : first + start + chunk, :].astype(F32) for block in blocks]
        for out_step, out in enumerate(outs):
            at = out_step * sources
            total = weights[at : at + 1, :] * loaded[0]
            for in_step in range(1, sources):
                total += weights[at + in_step : at + in_step + 1, :] * loaded[in_step]
            out[part, :] = total.astype(BF16)


def live_rows(length, rows):
    return lax.broadcasted_iota(jnp.int32, (rows, HD), 0) < length[:, :HD]


def write_mask(length, keep, turned):
    rows = length.shape[1]
    first = lax.broadcasted_iota(jnp.int32, (rows, rows), 0)
    second = lax.broadcasted_iota(jnp.int32, (rows, rows), 1)
    if turned:
        used = (first <= second) & (first < length[...])
    else:
        used = (second <= first) & (second < length[...])
    keep[...] = jnp.where(used, 1.0, 0.0).astype(BF16)


def split_refs(refs, *counts):
    parts, at = [], 0
    for count in counts:
        parts.append(refs[at : at + count])
        at += count
    return parts


def head_of(pieces, head):
    per_piece = pieces[0].shape[1] // HD
    return pieces[head // per_piece], head_cols(head % per_piece)


def fetch_kernel(source, _, out, sems):
    copies = row_copies(source, out, sems)
    for copy in copies:
        copy.start()
    for copy in copies:
        copy.wait()


def local_kernel(heads, length, queries, keys, values, *rest):
    local, keep = rest[-2:]
    write_mask(length, keep, False)
    for head in range(heads):
        cols = head_cols(head)
        scores = nt(queries[:, cols], keys[:, cols]).astype(BF16) * keep[...]
        local[:, cols] = nn(scores, values[:, cols])


def token_rows(total):
    return jnp.sum(jnp.transpose(total), axis=0, keepdims=True)


def token_columns(row):
    return jnp.transpose(jnp.broadcast_to(row, (HD, row.shape[1])))


def carry_kernel(piece, grid, counts, scale, length, queries, local, cotangent, gain, *rest):
    received, rest = rest[: sum(counts)], rest[sum(counts) :]
    before, (attention, sums, prefix) = rest[:-3], rest[-3:]
    join_halves(split_refs(received, *counts), prefix, my_place(grid)[2], grid[2])
    rows, width = attention.shape
    factor = jnp.where(live_rows(length, rows), scale, 0.0)
    squares = jnp.zeros((rows, HD), F32)
    products = jnp.zeros((rows, HD), F32)
    for head in range(width // HD):
        cols = head_cols(head)
        whole = head_cols(piece * width // HD + head)
        carried = nn(queries[:, whole], prefix[head * HD : (head + 1) * HD, :])
        out = factor * (carried + local[:, whole])
        attention[:, cols] = out
        squares += out * out
        products += out * (cotangent[:, whole].astype(F32) * gain[:, whole])
    both = jnp.concatenate([token_rows(squares), token_rows(products)], axis=0)
    for other in before:
        both += other[...]
    sums[...] = both


def grad_kernel(piece, groups, grid, scale, length, queries, cotangent, gain, *rest):
    all_sums, attention, rest = split_refs(rest, groups, FORWARD_PIECES, len(rest) - groups - FORWARD_PIECES)
    (grad_out, inverse_rms), halves, full = rest[:2], rest[2:-1], rest[-1]
    rows, width = grad_out.shape
    features = HEADS * HD
    total = all_sums[0][...]
    for other in all_sums[1:]:
        total = total + other[...]
    inverse = lax.rsqrt(total[0:1, :] / features + EPSILON)
    inverse_rms[...] = inverse
    live = lax.broadcasted_iota(jnp.int32, (1, rows), 1) < length[...]
    live_inverse = jnp.where(live, inverse, 0.0)
    shrink = live_inverse * inverse * (inverse * total[1:2, :]) / features
    live_inverse = token_columns(live_inverse)
    shrink = token_columns(shrink)
    for head in range(width // HD):
        cols = head_cols(head)
        place = piece * width // HD + head
        whole = head_cols(place)
        out_piece, at = head_of(attention, place)
        gain_grad = cotangent[:, whole].astype(F32) * gain[:, whole]
        grad = (live_inverse * gain_grad - out_piece[:, at] * shrink).astype(BF16)
        grad_out[:, cols] = grad
        full[head * HD : (head + 1) * HD, :] = (scale * tn(queries[:, whole], grad)).astype(BF16)
    write_halves(full, halves, my_place(grid)[2], grid[2])


def row_copies(source, target, sems):
    rows = target.shape[0]
    chunk = rows // 4 if rows % 64 == 0 else rows
    parts = [pl.ds(step * chunk, chunk) for step in range(rows // chunk)]
    return [pltpu.make_async_copy(source.at[p, :], target.at[p, :], sems.at[j]) for j, p in enumerate(parts)]


def column_copies(sources, targets, first, count, sems):
    cols = slice(first * HD, (first + count) * HD)
    return [
        pltpu.make_async_copy(src.at[:, cols], dst.at[:, cols], sems.at[j])
        for j, (src, dst) in enumerate(zip(sources, targets))
    ]


def query_kernel(heads, group, scale, length, inverse_rms, gain, queries, keys, values, *rest):
    sizes = (BACKWARD_PIECES, FORWARD_PIECES, FORWARD_PIECES)
    grads, attention, prefix, rest = split_refs(rest, *sizes, len(rest) - sum(sizes))
    attended_hbm, query_hbm, key_part, token, attended, query_grad, keep, keep_turned, sems = rest
    token[...] = jnp.zeros_like(token)
    write_mask(length, keep, False)
    write_mask(length, keep_turned, True)
    inverse = token_columns(inverse_rms[...])
    copies = []
    for head in range(heads):
        cols = head_cols(head)
        grad_piece, at = head_of(grads, head)
        grad = grad_piece[:, at]
        out_piece, at = head_of(attention, head)
        per_piece = heads // FORWARD_PIECES
        prefix_piece, state = prefix[head // per_piece], head % per_piece
        grad_scores = nt(grad, values[:, cols]).astype(BF16) * keep[...]
        carried = nt(grad, prefix_piece[state * HD : (state + 1) * HD, :])
        query_grad[:, cols] = (scale * (carried + nn(grad_scores, keys[:, cols]))).astype(BF16)
        turned = nt(values[:, cols], grad).astype(BF16) * keep_turned[...]
        key_part[:, cols] = scale * nn(turned, queries[:, cols])
        attended[:, cols] = (out_piece[:, at] * inverse * gain[:, cols]).astype(BF16)
        if (head + 1) % group == 0:
            step = head // group
            some = column_copies(
                (attended, query_grad), (attended_hbm, query_hbm), step * group, group, sems.at[step]
            )
            for copy in some:
                copy.start()
            copies += some
    for copy in copies:
        copy.wait()


def value_kernel(heads, scale, length, queries, keys, *rest):
    grads, (value_part, keep) = rest[:BACKWARD_PIECES], rest[-2:]
    write_mask(length, keep, True)
    for head in range(heads):
        cols = head_cols(head)
        grad_piece, at = head_of(grads, head)
        turned = nt(keys[:, cols], queries[:, cols]).astype(BF16) * keep[...]
        value_part[:, cols] = scale * nn(turned, grad_piece[:, at])


def final_kernel(piece, grid, counts, length, keys, values, key_part, value_part, *rest):
    received, rest = rest[: sum(counts)], rest[sum(counts) :]
    key_hbm, value_hbm, key_grad, value_grad, below, sems = rest[-6:]
    pair = grid[2]
    join_halves(split_refs(received, *counts), below, my_place(grid)[2], pair)
    rows, width = key_grad.shape
    live = jnp.where(live_rows(length, rows), 1.0, 0.0)
    per_half = width // HD // pair
    group = 2 if per_half % 2 == 0 else 1
    copies = []
    for head in range(width // HD):
        half, within = head // per_half, head % per_half
        cols = head_cols(head)
        place = half * (keys.shape[1] // HD // pair) + piece * per_half + within
        whole = head_cols(place)
        state = below[head * HD : (head + 1) * HD, :]
        key_grad[:, cols] = (key_part[:, whole] + live * nt(values[:, whole], state)).astype(BF16)
        value_grad[:, cols] = (value_part[:, whole] + live * nn(keys[:, whole], state)).astype(BF16)
        if (head + 1) % group == 0:
            done = slice((head + 1 - group) * HD, (head + 1) * HD)
            there = slice((place + 1 - group) * HD, (place + 1) * HD)
            for j, (src, dst) in enumerate(((key_grad, key_hbm), (value_grad, value_hbm))):
                copy = pltpu.make_async_copy(src.at[:, done], dst.at[:, there], sems.at[j, head // group])
                copy.start()
                copies.append(copy)
    for copy in copies:
        copy.wait()


def in_hbm(x):
    return pltpu.with_memory_space_constraint(x, pltpu.HBM)


def call(kernel, out_shape, operands, scratch=(), flops=0, stream=(), scalars=(), after=(), out_specs=None, aliases=None):
    moved = sum(math.prod(x.shape) * x.dtype.itemsize for x in operands)
    moved += sum(math.prod(x.shape) * x.dtype.itemsize for x in out_shape)
    specs = [SMEM if j in scalars else HBM if j in stream else VMEM for j in range(len(operands))]
    operands = [in_hbm(x) if j in stream else x for j, x in enumerate(operands)]
    return pl.pallas_call(
        kernel,
        out_shape=out_shape,
        in_specs=specs + [ANY] * len(after),
        out_specs=out_specs or [VMEM] * len(out_shape),
        scratch_shapes=list(scratch),
        input_output_aliases=aliases or {},
        compiler_params=pltpu.CompilerParams(vmem_limit_bytes=VMEM_LIMIT),
        cost_estimate=pl.CostEstimate(flops=flops, bytes_accessed=moved, transcendentals=0),
    )(*operands, *after)


def line_send(block, grid, step, flip, gather):
    moves = []
    for device in range(grid[0] * grid[1] * grid[2]):
        place = place_of(grid, device)
        if gather and flip:
            row, column, valid = along(grid, (place[0], place[1], place[2] ^ 1), step, True, True)
        else:
            row, column, valid = along(grid, place, step, gather, True)
        if valid:
            moves.append((device, member(grid, row, column, place[2] ^ flip)))
    return lax.ppermute(block, "seg", moves)


def gather_line(halves, grid):
    pair = grid[2]
    arrived = {0: halves[0]}
    for step in range(line_length(grid)):
        for flip in range(pair):
            if step or flip:
                arrived[step * pair + flip] = line_send(halves[flip], grid, step, flip, True)
    return [arrived[j] for j in range(len(arrived))]


def scatter_line(sums, grid):
    pair = grid[2]
    parts = [[] for _ in range(pair)]
    for step in reversed(range(line_length(grid))):
        for flip in range(pair):
            block = sums[step * pair + flip]
            parts[flip].append(line_send(block, grid, step, flip, False) if step or flip else block)
    return parts


def token_sums(sums, groups):
    parts = [sums]
    for step in [j for j in range(1, groups) if j != 2] + [2] * (groups > 2):
        moves = [(j, target_of(j, step, groups)) for j in range(groups)]
        parts.append(lax.ppermute(sums, "head", moves))
    return parts


def per_device(segs, groups, queries, key_rows, values, cotangent, out_gain, parent, seg_len):
    rows, features = queries.shape[1:]
    heads = features // HD
    grid = grid_of(segs)
    pair = grid[2]
    scale = 1.0 / math.sqrt(HD * rows)
    cot = cotangent[0]
    gain = out_gain[None]
    shape = jax.ShapeDtypeStruct
    narrow = shape((rows, features), BF16)
    wide = shape((rows, features), F32)
    row = shape((1, rows), F32)
    members = line_length(grid) * pair
    weight_rows = shape((members * members, HD), F32)
    sems = pltpu.SemaphoreType.DMA((2, heads))
    mask = pltpu.VMEM((rows, rows), BF16)
    counts = [line_length(grid)] * pair
    unit = 2 * heads * rows * HD

    def halves(pieces):
        return [shape((features // (pair * pieces), HD), BF16)] * pair

    def mix(arrived, weights, piece, pieces, after=()):
        tall = arrived[0].shape[0] // pieces
        like = [shape((tall, HD), BF16)] * members
        return call(functools.partial(mix_kernel, members, piece * tall), like, (weights, *arrived), after=after)

    def flat(parts):
        return [block for part in parts for block in part]

    key, value, length, up, down, *own = call(
        functools.partial(state_kernel, grid),
        [narrow, narrow, shape((1, rows), jnp.int32), weight_rows, weight_rows] + halves(FORWARD_PIECES) * FORWARD_PIECES,
        (seg_len, key_rows[0], values[0], parent[None]),
        [pltpu.VMEM((features, HD), BF16), sems, pltpu.SMEM((1, segs), jnp.int32), pltpu.SemaphoreType.DMA(())],
        unit * HD, (1, 2, 3), (0,),
    )
    (query,) = call(fetch_kernel, [narrow], (queries[0],), [pltpu.SemaphoreType.DMA((4,))], 0, (0,), after=(own[0],))
    mixed = []
    for part in split_refs(own, *[pair] * FORWARD_PIECES):
        mixed.append(mix(gather_line(part, grid), up, 0, 1, () if mixed else (query,)))
    (local,) = call(
        functools.partial(local_kernel, heads),
        [wide], (length, query, key, value), [mask], unit * rows * 2, after=(mixed[0][0],),
    )
    attention, prefix, sums = [], [], []
    width = features // FORWARD_PIECES
    for piece in range(FORWARD_PIECES):
        out, total, joined = call(
            functools.partial(carry_kernel, piece, grid, counts, scale),
            [shape((rows, width), F32), shape((2, rows), F32), shape((width, HD), BF16)],
            (length, query, local, cot, gain, *flat(scatter_line(mixed[piece], grid)), *sums),
            (), unit * HD // FORWARD_PIECES,
        )
        attention.append(out)
        prefix.append(joined)
        sums = [total]
    sums = token_sums(sums[0], groups)
    grads, state_grad = [], []
    width = features // BACKWARD_PIECES
    for piece in range(BACKWARD_PIECES):
        grad_out, inverse_rms, *parts = call(
            functools.partial(grad_kernel, piece, len(sums), grid, scale),
            [shape((rows, width), BF16), row] + halves(BACKWARD_PIECES),
            (length, query, cot, gain, *sums, *attention), [pltpu.VMEM((width, HD), BF16)],
            unit * HD // BACKWARD_PIECES,
        )
        grads.append(grad_out)
        state_grad.append(parts)
    group = 4 if heads % 4 == 0 else 1
    attended, query_grad, key_part, token = call(
        functools.partial(query_kernel, heads, group, scale),
        [narrow, narrow, wide, shape((8, HD), F32)],
        (length, inverse_rms, gain, query, key, value, *grads, *attention, *prefix),
        [pltpu.VMEM(narrow.shape, BF16)] * 2 + [mask] * 2 + [pltpu.SemaphoreType.DMA((heads // group, 2))],
        unit * (4 * rows + HD), out_specs=[HBM, HBM, VMEM, VMEM],
    )
    (part,) = state_grad
    arrived = gather_line(part, grid)
    mixed = []
    for piece in range(RETURN_PIECES):
        mixed.append(mix(arrived, down, piece, RETURN_PIECES, (token, *mixed[-1][:1]) if mixed else (token,)))
    (value_part,) = call(
        functools.partial(value_kernel, heads, scale),
        [wide], (length, query, key, *grads), [mask], unit * 2 * rows, after=(mixed[-1][0],),
    )
    results = []
    width = features // RETURN_PIECES
    for piece in range(RETURN_PIECES):
        below = flat(scatter_line(mixed[piece], grid))
        operands = (length, key, value, key_part, value_part, *below, *results)
        first = len(operands) - len(results)
        results = call(
            functools.partial(final_kernel, piece, grid, counts),
            [narrow, narrow], operands,
            [pltpu.VMEM((rows, width), BF16)] * 2 + [pltpu.VMEM((width, HD), BF16), sems],
            2 * unit * HD // RETURN_PIECES,
            range(first, len(operands)), out_specs=[HBM, HBM],
            aliases={first + j: j for j in range(len(results))},
        )
    key_grad, value_grad = results
    return attended[None], query_grad[None], key_grad[None], value_grad[None]


def solution(mesh):
    split = P("seg", None, "head")
    return jax.shard_map(
        functools.partial(per_device, mesh.shape["seg"], mesh.shape["head"]),
        mesh=mesh,
        in_specs=(split, split, split, split, P("head"), P(), P("seg")),
        out_specs=(split, split, split, split),
        check_vma=False,
    )
```

```python
import functools
import math

import jax
import jax.numpy as jnp
from jax import lax
from jax.experimental import pallas as pl
from jax.experimental.pallas import tpu as pltpu
from jax.sharding import PartitionSpec as P

HEADS = 64
HD = 128
EPSILON = 1e-06
F32 = jnp.float32
BF16 = jnp.bfloat16
VMEM_LIMIT = 24 * 1024 * 1024
FORWARD_PIECES = 2
BACKWARD_PIECES = 2

VMEM = pl.BlockSpec(memory_space=pltpu.VMEM)
SMEM = pl.BlockSpec(memory_space=pltpu.SMEM)
HBM = pl.BlockSpec(memory_space=pltpu.HBM)
ANY = pl.BlockSpec(memory_space=pl.ANY)


def dot(a, b, contract):
    return lax.dot_general(a, b, (contract, ((), ())), preferred_element_type=F32)


def nn(a, b):
    return dot(a, b, ((1,), (0,)))


def nt(a, b):
    return dot(a, b, ((1,), (1,)))


def tn(a, b):
    return dot(a, b, ((0,), (0,)))


def head_cols(head):
    return slice(head * HD, (head + 1) * HD)


def target_of(place, step, size):
    if size & (size - 1) == 0:
        return place ^ step
    return (place + step) % size


def source_of(place, step, size):
    if size & (size - 1) == 0:
        return place ^ step
    return (place + size - step) % size


def grid_of(segs):
    pair = 2 if segs % 2 == 0 else 1
    chips = segs // pair
    columns = next(c for c in range(1, chips + 1) if chips % c == 0 and c * c >= chips)
    return chips // columns, columns, pair


def member(grid, row, column, core):
    return (row * grid[1] + column) * grid[2] + core


def place_of(grid, device):
    chip = device // grid[2]
    return chip // grid[1], chip % grid[1], device % grid[2]


def along(grid, place, step, gather, ahead):
    row, column, core = place
    shift = target_of if ahead else source_of
    by_row = (core == 0) if gather else (core != 0)
    valid_column = step < grid[1]
    valid_row = step < grid[0]
    if isinstance(core, int):
        if by_row:
            return row, shift(column, step, grid[1]), valid_column
        return shift(row, step, grid[0]), column, valid_row
    moved_column = shift(column, min(step, grid[1] - 1), grid[1])
    moved_row = shift(row, min(step, grid[0] - 1), grid[0])
    return (
        jnp.where(by_row, row, moved_row),
        jnp.where(by_row, moved_column, column),
        jnp.where(by_row, valid_column, valid_row),
    )


def my_place(grid):
    me = lax.axis_index("seg")
    chip = lax.div(me, grid[2])
    return lax.div(chip, grid[1]), lax.rem(chip, grid[1]), lax.rem(me, grid[2])


def row_halves(full, core, pair):
    half = full.shape[0] // pair
    return [full.at[pl.ds(pl.multiple_of((core ^ j) * half, half), half), :] for j in range(pair)]


def join_halves(parts, full, core, pair):
    for half, terms in zip(row_halves(full, core, pair), parts):
        total = terms[0][...].astype(F32)
        for term in terms[1:]:
            total += term[...].astype(F32)
        half[...] = total.astype(BF16)


def line_length(grid):
    return max(grid[0], grid[1])


def write_weights(grid, parent, up, down):
    place = my_place(grid)
    pair = grid[2]
    count = line_length(grid) * pair

    def is_ancestor(child, other):
        first = parent[0, child]
        second = jnp.where(first >= 0, parent[0, jnp.maximum(first, 0)], -1)
        return jnp.logical_or(other == first, other == second)

    for out_step in range(count):
        row, column, _ = along(grid, place, out_step // pair, False, True)
        target = member(grid, row, column, place[2] ^ (out_step % pair))
        for in_step in range(count):
            row, column, valid = along(grid, place, in_step // pair, True, False)
            source = member(grid, row, column, place[2] ^ (in_step % pair))
            at = out_step * count + in_step
            for rows, used in ((up, is_ancestor(target, source)), (down, is_ancestor(source, target))):
                weight = jnp.where(jnp.logical_and(used, valid), 1.0, 0.0)
                rows[at : at + 1, :] = jnp.full((1, HD), weight, F32)


def write_halves(full, outs, core, pair):
    rows = full.shape[0] * pair // len(outs)
    for piece in range(len(outs) // pair):
        halves = row_halves(full.at[pl.ds(piece * rows, rows), :], core, pair)
        for half, out in zip(halves, outs[piece * pair : (piece + 1) * pair]):
            out[...] = half[...]


def state_kernel(grid, seg_len, keys_hbm, values_hbm, parent_hbm, keys, values, length, up, down, *rest):
    outs, (full, sems, parent, parent_sem) = rest[:-4], rest[-4:]
    rows, width = keys.shape
    chunk = rows // 4 if rows % 64 == 0 else rows
    steps = rows // chunk
    spans = 2 if width % (2 * HD) == 0 else 1
    copies = []
    for span in range(spans):
        cols = slice(span * width // spans, (span + 1) * width // spans)
        for step in range(steps):
            part = slice(step * chunk, (step + 1) * chunk)
            for j, (src, dst) in enumerate(((keys_hbm, keys), (values_hbm, values))):
                copies.append(pltpu.make_async_copy(src.at[part, cols], dst.at[part, cols], sems.at[j, span * steps + step]))
    few = pltpu.make_async_copy(parent_hbm, parent, parent_sem)
    few.start()
    for copy in copies:
        copy.start()
    length[...] = jnp.full(length.shape, seg_len[0], jnp.int32)
    few.wait()
    write_weights(grid, parent, up, down)
    live = lax.broadcasted_iota(jnp.int32, (rows, HD), 0) < seg_len[0]
    for head in range(width // HD):
        if head % (width // HD // spans) == 0:
            span = head // (width // HD // spans)
            for copy in copies[span * 2 * steps : (span + 1) * 2 * steps]:
                copy.wait()
        cols = head_cols(head)
        masked = jnp.where(live, keys[:, cols], jnp.zeros((), BF16))
        full[head * HD : (head + 1) * HD, :] = tn(masked, values[:, cols]).astype(BF16)
    write_halves(full, outs, my_place(grid)[2], grid[2])


def mix_kernel(sources, first, weights, *refs):
    blocks, outs = refs[:sources], refs[-sources:]
    rows = outs[0].shape[0]
    chunk = min(rows, 64)
    for start in range(0, rows, chunk):
        part = slice(start, start + chunk)
        loaded = [block[first + start : first + start + chunk, :].astype(F32) for block in blocks]
        for out_step, out in enumerate(outs):
            at = out_step * sources
            total = weights[at : at + 1, :] * loaded[0]
            for in_step in range(1, sources):
                total += weights[at + in_step : at + in_step + 1, :] * loaded[in_step]
            out[part, :] = total.astype(BF16)


def live_rows(length, rows):
    return lax.broadcasted_iota(jnp.int32, (rows, HD), 0) < length[:, :HD]


def write_mask(length, keep, turned):
    rows = length.shape[1]
    first = lax.broadcasted_iota(jnp.int32, (rows, rows), 0)
    second = lax.broadcasted_iota(jnp.int32, (rows, rows), 1)
    if turned:
        used = (first <= second) & (first < length[...])
    else:
        used = (second <= first) & (second < length[...])
    keep[...] = jnp.where(used, 1.0, 0.0).astype(BF16)


def split_refs(refs, *counts):
    parts, at = [], 0
    for count in counts:
        parts.append(refs[at : at + count])
        at += count
    return parts


def head_of(pieces, head):
    per_piece = pieces[0].shape[1] // HD
    return pieces[head // per_piece], head_cols(head % per_piece)


def fetch_kernel(source, _, out, sems):
    copies = row_copies(source, out, sems)
    for copy in copies:
        copy.start()
    for copy in copies:
        copy.wait()


def local_kernel(heads, length, queries, keys, values, *rest):
    local, keep = rest[-2:]
    write_mask(length, keep, False)
    for head in range(heads):
        cols = head_cols(head)
        scores = nt(queries[:, cols], keys[:, cols]).astype(BF16) * keep[...]
        local[:, cols] = nn(scores, values[:, cols])


def token_rows(total):
    return jnp.sum(jnp.transpose(total), axis=0, keepdims=True)


def token_columns(row):
    return jnp.transpose(jnp.broadcast_to(row, (HD, row.shape[1])))


def carry_kernel(piece, grid, counts, scale, length, queries, local, cotangent, gain, *rest):
    received, rest = rest[: sum(counts)], rest[sum(counts) :]
    before, (attention, sums, prefix) = rest[:-3], rest[-3:]
    join_halves(split_refs(received, *counts), prefix, my_place(grid)[2], grid[2])
    rows, width = attention.shape
    factor = jnp.where(live_rows(length, rows), scale, 0.0)
    squares = jnp.zeros((rows, HD), F32)
    products = jnp.zeros((rows, HD), F32)
    for head in range(width // HD):
        cols = head_cols(head)
        whole = head_cols(piece * width // HD + head)
        carried = nn(queries[:, whole], prefix[head * HD : (head + 1) * HD, :])
        out = factor * (carried + local[:, whole])
        attention[:, cols] = out
        squares += out * out
        products += out * (cotangent[:, whole].astype(F32) * gain[:, whole])
    both = jnp.concatenate([token_rows(squares), token_rows(products)], axis=0)
    for other in before:
        both += other[...]
    sums[...] = both


def grad_kernel(piece, groups, grid, scale, length, queries, cotangent, gain, *rest):
    all_sums, attention, rest = split_refs(rest, groups, FORWARD_PIECES, len(rest) - groups - FORWARD_PIECES)
    grad_out, halves, full = rest[0], rest[1 : 1 + grid[2]], rest[-1]
    rows, width = grad_out.shape
    features = HEADS * HD
    total = all_sums[0][...]
    for other in all_sums[1:]:
        total = total + other[...]
    inverse = lax.rsqrt(total[0:1, :] / features + EPSILON)
    if piece == 0:
        rest[1 + grid[2]][...] = inverse
    live = lax.broadcasted_iota(jnp.int32, (1, rows), 1) < length[...]
    live_inverse = jnp.where(live, inverse, 0.0)
    shrink = live_inverse * inverse * (inverse * total[1:2, :]) / features
    live_inverse = token_columns(live_inverse)
    shrink = token_columns(shrink)
    for head in range(width // HD):
        cols = head_cols(head)
        place = piece * width // HD + head
        whole = head_cols(place)
        out_piece, at = head_of(attention, place)
        gain_grad = cotangent[:, whole].astype(F32) * gain[:, whole]
        grad = (live_inverse * gain_grad - out_piece[:, at] * shrink).astype(BF16)
        grad_out[:, cols] = grad
        full[head * HD : (head + 1) * HD, :] = (scale * tn(queries[:, whole], grad)).astype(BF16)
    write_halves(full, halves, my_place(grid)[2], grid[2])


def row_copies(source, target, sems):
    rows = target.shape[0]
    chunk = rows // 4 if rows % 64 == 0 else rows
    parts = [pl.ds(step * chunk, chunk) for step in range(rows // chunk)]
    return [pltpu.make_async_copy(source.at[p, :], target.at[p, :], sems.at[j]) for j, p in enumerate(parts)]


def query_kernel(piece, scale, length, inverse_rms, gain, queries, keys, values, grads, *rest):
    attention, prefix, rest = split_refs(rest, FORWARD_PIECES, FORWARD_PIECES, len(rest) - 2 * FORWARD_PIECES)
    attended_hbm, query_hbm, key_part, token, attended, query_grad, keep, sems = rest[-8:]
    token[...] = jnp.zeros_like(token)
    write_mask(length, keep, False)
    inverse = token_columns(inverse_rms[...])
    heads = grads.shape[1] // HD
    group = 4 if heads % 4 == 0 else 1
    copies = []
    for head in range(heads):
        cols = head_cols(head)
        place = piece * heads + head
        whole = head_cols(place)
        out_piece, at = head_of(attention, place)
        per_piece = prefix[0].shape[0] // HD
        prefix_piece, state = prefix[place // per_piece], place % per_piece
        grad = grads[:, cols]
        grad_scores = nt(grad, values[:, whole]).astype(BF16) * keep[...]
        carried = nt(grad, prefix_piece[state * HD : (state + 1) * HD, :])
        query_grad[:, cols] = (scale * (carried + nn(grad_scores, keys[:, whole]))).astype(BF16)
        key_part[:, cols] = scale * tn(grad_scores, queries[:, whole])
        attended[:, cols] = (out_piece[:, at] * inverse * gain[:, whole]).astype(BF16)
        if (head + 1) % group == 0:
            here = slice((head + 1 - group) * HD, (head + 1) * HD)
            there = slice((place + 1 - group) * HD, (place + 1) * HD)
            for j, (src, dst) in enumerate(((attended, attended_hbm), (query_grad, query_hbm))):
                copy = pltpu.make_async_copy(src.at[:, here], dst.at[:, there], sems.at[head // group, j])
                copy.start()
                copies.append(copy)
    for copy in copies:
        copy.wait()


def value_kernel(heads, scale, length, queries, keys, *rest):
    grads, (value_part, keep) = rest[:BACKWARD_PIECES], rest[-2:]
    write_mask(length, keep, True)
    for head in range(heads):
        cols = head_cols(head)
        grad_piece, at = head_of(grads, head)
        turned = nt(keys[:, cols], queries[:, cols]).astype(BF16) * keep[...]
        value_part[:, cols] = scale * nn(turned, grad_piece[:, at])


def final_kernel(grid, counts, length, keys, values, value_part, *rest):
    count = sum(counts) * BACKWARD_PIECES
    key_parts, received, rest = split_refs(rest, BACKWARD_PIECES, count, len(rest) - BACKWARD_PIECES - count)
    key_hbm, value_hbm, key_grad, value_grad, below, sems = rest[-6:]
    pair = grid[2]
    tall = below.shape[0] // BACKWARD_PIECES
    for piece, parts in enumerate(split_refs(received, *[sum(counts)] * BACKWARD_PIECES)):
        full = below.at[pl.ds(piece * tall, tall), :]
        join_halves(split_refs(parts, *counts), full, my_place(grid)[2], pair)
    rows, width = keys.shape
    live = jnp.where(live_rows(length, rows), 1.0, 0.0)
    group = 2 if width // HD % 2 == 0 else 1
    copies = []
    for head in range(width // HD):
        cols = head_cols(head)
        key_part, at = head_of(key_parts, head)
        state = below[head * HD : (head + 1) * HD, :]
        key_grad[:, cols] = (key_part[:, at] + live * nt(values[:, cols], state)).astype(BF16)
        value_grad[:, cols] = (value_part[:, cols] + live * nn(keys[:, cols], state)).astype(BF16)
        if (head + 1) % group == 0:
            done = slice((head + 1 - group) * HD, (head + 1) * HD)
            for j, (src, dst) in enumerate(((key_grad, key_hbm), (value_grad, value_hbm))):
                copy = pltpu.make_async_copy(src.at[:, done], dst.at[:, done], sems.at[j, head // group])
                copy.start()
                copies.append(copy)
    for copy in copies:
        copy.wait()


def in_hbm(x):
    return pltpu.with_memory_space_constraint(x, pltpu.HBM)


def call(kernel, out_shape, operands, scratch=(), flops=0, stream=(), scalars=(), after=(), out_specs=None, aliases=None):
    moved = sum(math.prod(x.shape) * x.dtype.itemsize for x in operands)
    moved += sum(math.prod(x.shape) * x.dtype.itemsize for x in out_shape)
    specs = [SMEM if j in scalars else HBM if j in stream else VMEM for j in range(len(operands))]
    operands = [in_hbm(x) if j in stream else x for j, x in enumerate(operands)]
    return pl.pallas_call(
        kernel,
        out_shape=out_shape,
        in_specs=specs + [ANY] * len(after),
        out_specs=out_specs or [VMEM] * len(out_shape),
        scratch_shapes=list(scratch),
        input_output_aliases=aliases or {},
        compiler_params=pltpu.CompilerParams(vmem_limit_bytes=VMEM_LIMIT),
        cost_estimate=pl.CostEstimate(flops=flops, bytes_accessed=moved, transcendentals=0),
    )(*operands, *after)


def line_send(block, grid, step, flip, gather):
    moves = []
    for device in range(grid[0] * grid[1] * grid[2]):
        place = place_of(grid, device)
        if gather and flip:
            row, column, valid = along(grid, (place[0], place[1], place[2] ^ 1), step, True, True)
        else:
            row, column, valid = along(grid, place, step, gather, True)
        if valid:
            moves.append((device, member(grid, row, column, place[2] ^ flip)))
    return lax.ppermute(block, "seg", moves)


def gather_line(halves, grid):
    pair = grid[2]
    arrived = {0: halves[0]}
    for step in range(line_length(grid)):
        for flip in range(pair):
            if step or flip:
                arrived[step * pair + flip] = line_send(halves[flip], grid, step, flip, True)
    return [arrived[j] for j in range(len(arrived))]


def scatter_line(sums, grid):
    pair = grid[2]
    parts = [[] for _ in range(pair)]
    for step in reversed(range(line_length(grid))):
        for flip in range(pair):
            block = sums[step * pair + flip]
            parts[flip].append(line_send(block, grid, step, flip, False) if step or flip else block)
    return parts


def token_sums(sums, groups):
    parts = [sums]
    for step in [j for j in range(1, groups) if j != 2] + [2] * (groups > 2):
        moves = [(j, target_of(j, step, groups)) for j in range(groups)]
        parts.append(lax.ppermute(sums, "head", moves))
    return parts


def per_device(segs, groups, queries, key_rows, values, cotangent, out_gain, parent, seg_len):
    rows, features = queries.shape[1:]
    heads = features // HD
    grid = grid_of(segs)
    pair = grid[2]
    scale = 1.0 / math.sqrt(HD * rows)
    cot = cotangent[0]
    gain = out_gain[None]
    shape = jax.ShapeDtypeStruct
    narrow = shape((rows, features), BF16)
    wide = shape((rows, features), F32)
    row = shape((1, rows), F32)
    members = line_length(grid) * pair
    weight_rows = shape((members * members, HD), F32)
    sems = pltpu.SemaphoreType.DMA((2, heads))
    mask = pltpu.VMEM((rows, rows), BF16)
    counts = [line_length(grid)] * pair
    unit = 2 * heads * rows * HD

    def halves(pieces):
        return [shape((features // (pair * pieces), HD), BF16)] * pair

    def mix(arrived, weights, piece, pieces, after=()):
        tall = arrived[0].shape[0] // pieces
        like = [shape((tall, HD), BF16)] * members
        return call(functools.partial(mix_kernel, members, piece * tall), like, (weights, *arrived), after=after)

    def flat(parts):
        return [block for part in parts for block in part]

    key, value, length, up, down, *own = call(
        functools.partial(state_kernel, grid),
        [narrow, narrow, shape((1, rows), jnp.int32), weight_rows, weight_rows] + halves(FORWARD_PIECES) * FORWARD_PIECES,
        (seg_len, key_rows[0], values[0], parent[None]),
        [pltpu.VMEM((features, HD), BF16), sems, pltpu.SMEM((1, segs), jnp.int32), pltpu.SemaphoreType.DMA(())],
        unit * HD, (1, 2, 3), (0,),
    )
    (query,) = call(fetch_kernel, [narrow], (queries[0],), [pltpu.SemaphoreType.DMA((4,))], 0, (0,), after=(own[0],))
    mixed = []
    for part in split_refs(own, *[pair] * FORWARD_PIECES):
        mixed.append(mix(gather_line(part, grid), up, 0, 1, () if mixed else (query,)))
    (local,) = call(
        functools.partial(local_kernel, heads),
        [wide], (length, query, key, value), [mask], unit * rows * 2, after=(mixed[0][0],),
    )
    attention, prefix, sums = [], [], []
    width = features // FORWARD_PIECES
    for piece in range(FORWARD_PIECES):
        out, total, joined = call(
            functools.partial(carry_kernel, piece, grid, counts, scale),
            [shape((rows, width), F32), shape((2, rows), F32), shape((width, HD), BF16)],
            (length, query, local, cot, gain, *flat(scatter_line(mixed[piece], grid)), *sums),
            (), unit * HD // FORWARD_PIECES,
        )
        attention.append(out)
        prefix.append(joined)
        sums = [total]
    sums = token_sums(sums[0], groups)
    grads, state_grad = [], []
    width = features // BACKWARD_PIECES
    for piece in range(BACKWARD_PIECES):
        grad_out, *parts = call(
            functools.partial(grad_kernel, piece, len(sums), grid, scale),
            [shape((rows, width), BF16)] + halves(BACKWARD_PIECES) + [row] * (piece == 0),
            (length, query, cot, gain, *sums, *attention), [pltpu.VMEM((width, HD), BF16)],
            unit * HD // BACKWARD_PIECES,
        )
        grads.append(grad_out)
        state_grad.append(parts[:pair])
        if piece == 0:
            inverse_rms = parts[pair]
    group = 4 if heads // BACKWARD_PIECES % 4 == 0 else 1
    narrow_piece, wide_piece = shape((rows, width), BF16), shape((rows, width), F32)
    mixed, key_parts, results = [], [], []
    for piece in range(BACKWARD_PIECES):
        operands = (length, inverse_rms, gain, query, key, value, grads[piece], *attention, *prefix, *results)
        last = len(operands) - len(results)
        *results, key_part, token = call(
            functools.partial(query_kernel, piece, scale),
            [narrow, narrow, wide_piece, shape((8, HD), F32)], operands,
            [pltpu.VMEM(narrow_piece.shape, BF16)] * 2 + [mask, pltpu.SemaphoreType.DMA((heads // group, 2))],
            unit * (3 * rows + HD) // BACKWARD_PIECES, range(last, len(operands)),
            after=tuple(sums[0] for sums in mixed), out_specs=[HBM, HBM, VMEM, VMEM],
            aliases={last + j: j for j in range(len(results))},
        )
        key_parts.append(key_part)
        if piece == 0:
            for part in state_grad:
                mixed.append(mix(gather_line(part, grid), down, 0, 1, (token,)))
    attended, query_grad = results
    (value_part,) = call(
        functools.partial(value_kernel, heads, scale),
        [wide], (length, query, key, *grads), [mask], unit * 2 * rows, after=(mixed[-1][0],),
    )
    below = [block for sums in mixed for block in flat(scatter_line(sums, grid))]
    key_grad, value_grad = call(
        functools.partial(final_kernel, grid, counts),
        [narrow, narrow], (length, key, value, value_part, *key_parts, *below),
        [pltpu.VMEM(narrow.shape, BF16)] * 2 + [pltpu.VMEM((features, HD), BF16), sems],
        2 * unit * HD, out_specs=[HBM, HBM],
    )
    return attended[None], query_grad[None], key_grad[None], value_grad[None]


def solution(mesh):
    split = P("seg", None, "head")
    return jax.shard_map(
        functools.partial(per_device, mesh.shape["seg"], mesh.shape["head"]),
        mesh=mesh,
        in_specs=(split, split, split, split, P("head"), P(), P("seg")),
        out_specs=(split, split, split, split),
        check_vma=False,
    )
```

```python
import functools
import math

import jax
import jax.numpy as jnp
from jax import lax
from jax.experimental import pallas as pl
from jax.experimental.pallas import tpu as pltpu
from jax.sharding import PartitionSpec as P

HEADS = 64
HD = 128
EPSILON = 1e-06
F32 = jnp.float32
BF16 = jnp.bfloat16
VMEM_LIMIT = 24 * 1024 * 1024
FORWARD_PIECES = 2
BACKWARD_PIECES = 2

VMEM = pl.BlockSpec(memory_space=pltpu.VMEM)
SMEM = pl.BlockSpec(memory_space=pltpu.SMEM)
HBM = pl.BlockSpec(memory_space=pltpu.HBM)
ANY = pl.BlockSpec(memory_space=pl.ANY)


def dot(a, b, contract):
    return lax.dot_general(a, b, (contract, ((), ())), preferred_element_type=F32)


def nn(a, b):
    return dot(a, b, ((1,), (0,)))


def nt(a, b):
    return dot(a, b, ((1,), (1,)))


def tn(a, b):
    return dot(a, b, ((0,), (0,)))


def head_cols(head):
    return slice(head * HD, (head + 1) * HD)


def target_of(place, step, size):
    if size & (size - 1) == 0:
        return place ^ step
    return (place + step) % size


def source_of(place, step, size):
    if size & (size - 1) == 0:
        return place ^ step
    return (place + size - step) % size


def grid_of(segs):
    pair = 2 if segs % 2 == 0 else 1
    chips = segs // pair
    columns = next(c for c in range(1, chips + 1) if chips % c == 0 and c * c >= chips)
    return chips // columns, columns, pair


def member(grid, row, column, core):
    return (row * grid[1] + column) * grid[2] + core


def place_of(grid, device):
    chip = device // grid[2]
    return chip // grid[1], chip % grid[1], device % grid[2]


def along(grid, place, step, gather, ahead):
    row, column, core = place
    shift = target_of if ahead else source_of
    by_row = (core == 0) if gather else (core != 0)
    valid_column = step < grid[1]
    valid_row = step < grid[0]
    if isinstance(core, int):
        if by_row:
            return row, shift(column, step, grid[1]), valid_column
        return shift(row, step, grid[0]), column, valid_row
    moved_column = shift(column, min(step, grid[1] - 1), grid[1])
    moved_row = shift(row, min(step, grid[0] - 1), grid[0])
    return (
        jnp.where(by_row, row, moved_row),
        jnp.where(by_row, moved_column, column),
        jnp.where(by_row, valid_column, valid_row),
    )


def my_place(grid):
    me = lax.axis_index("seg")
    chip = lax.div(me, grid[2])
    return lax.div(chip, grid[1]), lax.rem(chip, grid[1]), lax.rem(me, grid[2])


def row_halves(full, core, pair):
    half = full.shape[0] // pair
    return [full.at[pl.ds(pl.multiple_of((core ^ j) * half, half), half), :] for j in range(pair)]


def join_halves(parts, full, core, pair):
    for half, terms in zip(row_halves(full, core, pair), parts):
        total = terms[0][...].astype(F32)
        for term in terms[1:]:
            total += term[...].astype(F32)
        half[...] = total.astype(BF16)


def line_length(grid):
    return max(grid[0], grid[1])


def write_weights(grid, parent, up, down):
    place = my_place(grid)
    pair = grid[2]
    count = line_length(grid) * pair

    def is_ancestor(child, other):
        first = parent[0, child]
        second = jnp.where(first >= 0, parent[0, jnp.maximum(first, 0)], -1)
        return jnp.logical_or(other == first, other == second)

    for out_step in range(count):
        row, column, _ = along(grid, place, out_step // pair, False, True)
        target = member(grid, row, column, place[2] ^ (out_step % pair))
        for in_step in range(count):
            row, column, valid = along(grid, place, in_step // pair, True, False)
            source = member(grid, row, column, place[2] ^ (in_step % pair))
            at = out_step * count + in_step
            for rows, used in ((up, is_ancestor(target, source)), (down, is_ancestor(source, target))):
                weight = jnp.where(jnp.logical_and(used, valid), 1.0, 0.0)
                rows[at : at + 1, :] = jnp.full((1, HD), weight, F32)


def write_halves(full, outs, core, pair):
    rows = full.shape[0] * pair // len(outs)
    for piece in range(len(outs) // pair):
        halves = row_halves(full.at[pl.ds(piece * rows, rows), :], core, pair)
        for half, out in zip(halves, outs[piece * pair : (piece + 1) * pair]):
            out[...] = half[...]


def state_kernel(grid, seg_len, keys_hbm, values_hbm, parent_hbm, keys, values, length, up, down, *rest):
    outs, (full, sems, parent, parent_sem) = rest[:-4], rest[-4:]
    rows, width = keys.shape
    chunk = rows // 4 if rows % 64 == 0 else rows
    steps = rows // chunk
    spans = 2 if width % (2 * HD) == 0 else 1
    copies = []
    for span in range(spans):
        cols = slice(span * width // spans, (span + 1) * width // spans)
        for step in range(steps):
            part = slice(step * chunk, (step + 1) * chunk)
            for j, (src, dst) in enumerate(((keys_hbm, keys), (values_hbm, values))):
                copies.append(pltpu.make_async_copy(src.at[part, cols], dst.at[part, cols], sems.at[j, span * steps + step]))
    few = pltpu.make_async_copy(parent_hbm, parent, parent_sem)
    few.start()
    for copy in copies:
        copy.start()
    length[...] = jnp.full(length.shape, seg_len[0], jnp.int32)
    few.wait()
    write_weights(grid, parent, up, down)
    live = lax.broadcasted_iota(jnp.int32, (rows, HD), 0) < seg_len[0]
    for head in range(width // HD):
        if head % (width // HD // spans) == 0:
            span = head // (width // HD // spans)
            for copy in copies[span * 2 * steps : (span + 1) * 2 * steps]:
                copy.wait()
        cols = head_cols(head)
        masked = jnp.where(live, keys[:, cols], jnp.zeros((), BF16))
        full[head * HD : (head + 1) * HD, :] = tn(masked, values[:, cols]).astype(BF16)
    write_halves(full, outs, my_place(grid)[2], grid[2])


def mix_kernel(sources, first, weights, *refs):
    blocks, outs = refs[:sources], refs[-sources:]
    rows = outs[0].shape[0]
    chunk = min(rows, 64)
    for start in range(0, rows, chunk):
        part = slice(start, start + chunk)
        loaded = [block[first + start : first + start + chunk, :].astype(F32) for block in blocks]
        for out_step, out in enumerate(outs):
            at = out_step * sources
            total = weights[at : at + 1, :] * loaded[0]
            for in_step in range(1, sources):
                total += weights[at + in_step : at + in_step + 1, :] * loaded[in_step]
            out[part, :] = total.astype(BF16)


def live_rows(length, rows):
    return lax.broadcasted_iota(jnp.int32, (rows, HD), 0) < length[:, :HD]


def write_mask(length, keep, turned):
    rows = length.shape[1]
    first = lax.broadcasted_iota(jnp.int32, (rows, rows), 0)
    second = lax.broadcasted_iota(jnp.int32, (rows, rows), 1)
    if turned:
        used = (first <= second) & (first < length[...])
    else:
        used = (second <= first) & (second < length[...])
    keep[...] = jnp.where(used, 1.0, 0.0).astype(BF16)


def split_refs(refs, *counts):
    parts, at = [], 0
    for count in counts:
        parts.append(refs[at : at + count])
        at += count
    return parts


def head_of(pieces, head):
    per_piece = pieces[0].shape[1] // HD
    return pieces[head // per_piece], head_cols(head % per_piece)


def fetch_kernel(source, _, out, sems):
    copies = row_copies(source, out, sems)
    for copy in copies:
        copy.start()
    for copy in copies:
        copy.wait()


def local_kernel(heads, length, queries, keys, values, *rest):
    local, keep = rest[-2:]
    write_mask(length, keep, False)
    for head in range(heads):
        cols = head_cols(head)
        scores = nt(queries[:, cols], keys[:, cols]).astype(BF16) * keep[...]
        local[:, cols] = nn(scores, values[:, cols])


def token_rows(total):
    return jnp.sum(jnp.transpose(total), axis=0, keepdims=True)


def token_columns(row):
    return jnp.transpose(jnp.broadcast_to(row, (HD, row.shape[1])))


def carry_kernel(piece, grid, counts, scale, length, queries, local, cotangent, gain, *rest):
    received, rest = rest[: sum(counts)], rest[sum(counts) :]
    before, (attention, sums, prefix) = rest[:-3], rest[-3:]
    join_halves(split_refs(received, *counts), prefix, my_place(grid)[2], grid[2])
    rows, width = attention.shape
    factor = jnp.where(live_rows(length, rows), scale, 0.0)
    squares = jnp.zeros((rows, HD), F32)
    products = jnp.zeros((rows, HD), F32)
    for head in range(width // HD):
        cols = head_cols(head)
        whole = head_cols(piece * width // HD + head)
        carried = nn(queries[:, whole], prefix[head * HD : (head + 1) * HD, :])
        out = factor * (carried + local[:, whole])
        attention[:, cols] = out
        squares += out * out
        products += out * (cotangent[:, whole].astype(F32) * gain[:, whole])
    both = jnp.concatenate([token_rows(squares), token_rows(products)], axis=0)
    for other in before:
        both += other[...]
    sums[...] = both


def grad_kernel(piece, groups, grid, scale, length, queries, cotangent, gain, *rest):
    all_sums, attention, rest = split_refs(rest, groups, FORWARD_PIECES, len(rest) - groups - FORWARD_PIECES)
    grad_out, halves, full = rest[0], rest[1 : 1 + grid[2]], rest[-1]
    rows, width = grad_out.shape
    features = HEADS * HD
    total = all_sums[0][...]
    for other in all_sums[1:]:
        total = total + other[...]
    inverse = lax.rsqrt(total[0:1, :] / features + EPSILON)
    if piece == 0:
        rest[1 + grid[2]][...] = inverse
    live = lax.broadcasted_iota(jnp.int32, (1, rows), 1) < length[...]
    live_inverse = jnp.where(live, inverse, 0.0)
    shrink = live_inverse * inverse * (inverse * total[1:2, :]) / features
    live_inverse = token_columns(live_inverse)
    shrink = token_columns(shrink)
    for head in range(width // HD):
        cols = head_cols(head)
        place = piece * width // HD + head
        whole = head_cols(place)
        out_piece, at = head_of(attention, place)
        gain_grad = cotangent[:, whole].astype(F32) * gain[:, whole]
        grad = (live_inverse * gain_grad - out_piece[:, at] * shrink).astype(BF16)
        grad_out[:, cols] = grad
        full[head * HD : (head + 1) * HD, :] = (scale * tn(queries[:, whole], grad)).astype(BF16)
    write_halves(full, halves, my_place(grid)[2], grid[2])


def row_copies(source, target, sems):
    rows = target.shape[0]
    chunk = rows // 4 if rows % 64 == 0 else rows
    parts = [pl.ds(step * chunk, chunk) for step in range(rows // chunk)]
    return [pltpu.make_async_copy(source.at[p, :], target.at[p, :], sems.at[j]) for j, p in enumerate(parts)]


def query_kernel(piece, scale, length, inverse_rms, gain, queries, keys, values, grads, *rest):
    attention, prefix, rest = split_refs(rest, FORWARD_PIECES, FORWARD_PIECES, len(rest) - 2 * FORWARD_PIECES)
    attended_hbm, query_hbm, key_part, token, attended, query_grad, keep, sems = rest[-8:]
    token[...] = jnp.zeros_like(token)
    write_mask(length, keep, False)
    inverse = token_columns(inverse_rms[...])
    heads = grads.shape[1] // HD
    group = 4 if heads % 4 == 0 else 1
    copies = []
    for head in range(heads):
        cols = head_cols(head)
        place = piece * heads + head
        whole = head_cols(place)
        out_piece, at = head_of(attention, place)
        per_piece = prefix[0].shape[0] // HD
        prefix_piece, state = prefix[place // per_piece], place % per_piece
        grad = grads[:, cols]
        grad_scores = nt(grad, values[:, whole]).astype(BF16) * keep[...]
        carried = nt(grad, prefix_piece[state * HD : (state + 1) * HD, :])
        query_grad[:, cols] = (scale * (carried + nn(grad_scores, keys[:, whole]))).astype(BF16)
        key_part[:, cols] = scale * tn(grad_scores, queries[:, whole])
        attended[:, cols] = (out_piece[:, at] * inverse * gain[:, whole]).astype(BF16)
        if (head + 1) % group == 0:
            here = slice((head + 1 - group) * HD, (head + 1) * HD)
            there = slice((place + 1 - group) * HD, (place + 1) * HD)
            for j, (src, dst) in enumerate(((attended, attended_hbm), (query_grad, query_hbm))):
                some = row_copies(src.at[:, here], dst.at[:, there], sems.at[head // group, j])
                for copy in some:
                    copy.start()
                copies += some
    for copy in copies:
        copy.wait()


def value_kernel(heads, scale, length, queries, keys, *rest):
    grads, (value_part, keep) = rest[:BACKWARD_PIECES], rest[-2:]
    write_mask(length, keep, True)
    for head in range(heads):
        cols = head_cols(head)
        grad_piece, at = head_of(grads, head)
        turned = nt(keys[:, cols], queries[:, cols]).astype(BF16) * keep[...]
        value_part[:, cols] = scale * nn(turned, grad_piece[:, at])


def final_kernel(grid, counts, length, keys, values, value_part, *rest):
    count = sum(counts) * BACKWARD_PIECES
    key_parts, received, rest = split_refs(rest, BACKWARD_PIECES, count, len(rest) - BACKWARD_PIECES - count)
    key_hbm, value_hbm, key_grad, value_grad, below, sems = rest[-6:]
    pair = grid[2]
    tall = below.shape[0] // BACKWARD_PIECES
    for piece, parts in enumerate(split_refs(received, *[sum(counts)] * BACKWARD_PIECES)):
        full = below.at[pl.ds(piece * tall, tall), :]
        join_halves(split_refs(parts, *counts), full, my_place(grid)[2], pair)
    rows, width = keys.shape
    live = jnp.where(live_rows(length, rows), 1.0, 0.0)
    group = 2 if width // HD % 2 == 0 else 1
    copies = []
    for head in range(width // HD):
        cols = head_cols(head)
        key_part, at = head_of(key_parts, head)
        state = below[head * HD : (head + 1) * HD, :]
        key_grad[:, cols] = (key_part[:, at] + live * nt(values[:, cols], state)).astype(BF16)
        value_grad[:, cols] = (value_part[:, cols] + live * nn(keys[:, cols], state)).astype(BF16)
        if (head + 1) % group == 0:
            done = slice((head + 1 - group) * HD, (head + 1) * HD)
            for j, (src, dst) in enumerate(((key_grad, key_hbm), (value_grad, value_hbm))):
                some = row_copies(src.at[:, done], dst.at[:, done], sems.at[head // group, j])
                for copy in some:
                    copy.start()
                copies += some
    for copy in copies:
        copy.wait()


def in_hbm(x):
    return pltpu.with_memory_space_constraint(x, pltpu.HBM)


def call(kernel, out_shape, operands, scratch=(), flops=0, stream=(), scalars=(), after=(), out_specs=None, aliases=None):
    moved = sum(math.prod(x.shape) * x.dtype.itemsize for x in operands)
    moved += sum(math.prod(x.shape) * x.dtype.itemsize for x in out_shape)
    specs = [SMEM if j in scalars else HBM if j in stream else VMEM for j in range(len(operands))]
    operands = [in_hbm(x) if j in stream else x for j, x in enumerate(operands)]
    return pl.pallas_call(
        kernel,
        out_shape=out_shape,
        in_specs=specs + [ANY] * len(after),
        out_specs=out_specs or [VMEM] * len(out_shape),
        scratch_shapes=list(scratch),
        input_output_aliases=aliases or {},
        compiler_params=pltpu.CompilerParams(vmem_limit_bytes=VMEM_LIMIT),
        cost_estimate=pl.CostEstimate(flops=flops, bytes_accessed=moved, transcendentals=0),
    )(*operands, *after)


def line_send(block, grid, step, flip, gather):
    moves = []
    for device in range(grid[0] * grid[1] * grid[2]):
        place = place_of(grid, device)
        if gather and flip:
            row, column, valid = along(grid, (place[0], place[1], place[2] ^ 1), step, True, True)
        else:
            row, column, valid = along(grid, place, step, gather, True)
        if valid:
            moves.append((device, member(grid, row, column, place[2] ^ flip)))
    return lax.ppermute(block, "seg", moves)


def gather_line(halves, grid):
    pair = grid[2]
    arrived = {0: halves[0]}
    for step in range(line_length(grid)):
        for flip in range(pair):
            if step or flip:
                arrived[step * pair + flip] = line_send(halves[flip], grid, step, flip, True)
    return [arrived[j] for j in range(len(arrived))]


def scatter_line(sums, grid):
    pair = grid[2]
    parts = [[] for _ in range(pair)]
    for step in reversed(range(line_length(grid))):
        for flip in range(pair):
            block = sums[step * pair + flip]
            parts[flip].append(line_send(block, grid, step, flip, False) if step or flip else block)
    return parts


def token_sums(sums, groups):
    parts = [sums]
    for step in [j for j in range(1, groups) if j != 2] + [2] * (groups > 2):
        moves = [(j, target_of(j, step, groups)) for j in range(groups)]
        parts.append(lax.ppermute(sums, "head", moves))
    return parts


def per_device(segs, groups, queries, key_rows, values, cotangent, out_gain, parent, seg_len):
    rows, features = queries.shape[1:]
    heads = features // HD
    grid = grid_of(segs)
    pair = grid[2]
    scale = 1.0 / math.sqrt(HD * rows)
    cot = cotangent[0]
    gain = out_gain[None]
    shape = jax.ShapeDtypeStruct
    narrow = shape((rows, features), BF16)
    wide = shape((rows, features), F32)
    row = shape((1, rows), F32)
    members = line_length(grid) * pair
    weight_rows = shape((members * members, HD), F32)
    sems = pltpu.SemaphoreType.DMA((2, heads))
    mask = pltpu.VMEM((rows, rows), BF16)
    counts = [line_length(grid)] * pair
    unit = 2 * heads * rows * HD

    def halves(pieces):
        return [shape((features // (pair * pieces), HD), BF16)] * pair

    def mix(arrived, weights, piece, pieces, after=()):
        tall = arrived[0].shape[0] // pieces
        like = [shape((tall, HD), BF16)] * members
        return call(functools.partial(mix_kernel, members, piece * tall), like, (weights, *arrived), after=after)

    def flat(parts):
        return [block for part in parts for block in part]

    key, value, length, up, down, *own = call(
        functools.partial(state_kernel, grid),
        [narrow, narrow, shape((1, rows), jnp.int32), weight_rows, weight_rows] + halves(FORWARD_PIECES) * FORWARD_PIECES,
        (seg_len, key_rows[0], values[0], parent[None]),
        [pltpu.VMEM((features, HD), BF16), sems, pltpu.SMEM((1, segs), jnp.int32), pltpu.SemaphoreType.DMA(())],
        unit * HD, (1, 2, 3), (0,),
    )
    (query,) = call(fetch_kernel, [narrow], (queries[0],), [pltpu.SemaphoreType.DMA((4,))], 0, (0,), after=(own[0],))
    mixed = []
    for part in split_refs(own, *[pair] * FORWARD_PIECES):
        mixed.append(mix(gather_line(part, grid), up, 0, 1, () if mixed else (query,)))
    (local,) = call(
        functools.partial(local_kernel, heads),
        [wide], (length, query, key, value), [mask], unit * rows * 2, after=(mixed[0][0],),
    )
    attention, prefix, sums = [], [], []
    width = features // FORWARD_PIECES
    for piece in range(FORWARD_PIECES):
        out, total, joined = call(
            functools.partial(carry_kernel, piece, grid, counts, scale),
            [shape((rows, width), F32), shape((2, rows), F32), shape((width, HD), BF16)],
            (length, query, local, cot, gain, *flat(scatter_line(mixed[piece], grid)), *sums),
            (), unit * HD // FORWARD_PIECES,
        )
        attention.append(out)
        prefix.append(joined)
        sums = [total]
    sums = token_sums(sums[0], groups)
    grads, state_grad = [], []
    width = features // BACKWARD_PIECES
    for piece in range(BACKWARD_PIECES):
        grad_out, *parts = call(
            functools.partial(grad_kernel, piece, len(sums), grid, scale),
            [shape((rows, width), BF16)] + halves(BACKWARD_PIECES) + [row] * (piece == 0),
            (length, query, cot, gain, *sums, *attention), [pltpu.VMEM((width, HD), BF16)],
            unit * HD // BACKWARD_PIECES,
        )
        grads.append(grad_out)
        state_grad.append(parts[:pair])
        if piece == 0:
            inverse_rms = parts[pair]
    group = 4 if heads // BACKWARD_PIECES % 4 == 0 else 1
    narrow_piece, wide_piece = shape((rows, width), BF16), shape((rows, width), F32)
    mixed, key_parts, results = [], [], []
    for piece in range(BACKWARD_PIECES):
        operands = (length, inverse_rms, gain, query, key, value, grads[piece], *attention, *prefix, *results)
        last = len(operands) - len(results)
        *results, key_part, token = call(
            functools.partial(query_kernel, piece, scale),
            [narrow, narrow, wide_piece, shape((8, HD), F32)], operands,
            [pltpu.VMEM(narrow_piece.shape, BF16)] * 2 + [mask, pltpu.SemaphoreType.DMA((heads // group, 2, 4))],
            unit * (3 * rows + HD) // BACKWARD_PIECES, range(last, len(operands)),
            after=tuple(sums[0] for sums in mixed), out_specs=[HBM, HBM, VMEM, VMEM],
            aliases={last + j: j for j in range(len(results))},
        )
        key_parts.append(key_part)
        if piece == 0:
            for part in state_grad:
                mixed.append(mix(gather_line(part, grid), down, 0, 1, (token,)))
    attended, query_grad = results
    (value_part,) = call(
        functools.partial(value_kernel, heads, scale),
        [wide], (length, query, key, *grads), [mask], unit * 2 * rows, after=(mixed[-1][0],),
    )
    below = [block for sums in mixed for block in flat(scatter_line(sums, grid))]
    key_grad, value_grad = call(
        functools.partial(final_kernel, grid, counts),
        [narrow, narrow], (length, key, value, value_part, *key_parts, *below),
        [pltpu.VMEM(narrow.shape, BF16)] * 2 + [pltpu.VMEM((features, HD), BF16), pltpu.SemaphoreType.DMA((heads, 2, 4))],
        2 * unit * HD, out_specs=[HBM, HBM],
    )
    return attended[None], query_grad[None], key_grad[None], value_grad[None]


def solution(mesh):
    split = P("seg", None, "head")
    return jax.shard_map(
        functools.partial(per_device, mesh.shape["seg"], mesh.shape["head"]),
        mesh=mesh,
        in_specs=(split, split, split, split, P("head"), P(), P("seg")),
        out_specs=(split, split, split, split),
        check_vma=False,
    )
```

```python
import functools
import math

import jax
import jax.numpy as jnp
from jax import lax
from jax.experimental import pallas as pl
from jax.experimental.pallas import tpu as pltpu
from jax.sharding import PartitionSpec as P

HEADS = 64
HD = 128
EPSILON = 1e-06
F32 = jnp.float32
BF16 = jnp.bfloat16
VMEM_LIMIT = 24 * 1024 * 1024
FORWARD_PIECES = 2
BACKWARD_PIECES = 2

VMEM = pl.BlockSpec(memory_space=pltpu.VMEM)
SMEM = pl.BlockSpec(memory_space=pltpu.SMEM)
HBM = pl.BlockSpec(memory_space=pltpu.HBM)
ANY = pl.BlockSpec(memory_space=pl.ANY)


def dot(a, b, contract):
    return lax.dot_general(a, b, (contract, ((), ())), preferred_element_type=F32)


def nn(a, b):
    return dot(a, b, ((1,), (0,)))


def nt(a, b):
    return dot(a, b, ((1,), (1,)))


def tn(a, b):
    return dot(a, b, ((0,), (0,)))


def head_cols(head):
    return slice(head * HD, (head + 1) * HD)


def target_of(place, step, size):
    if size & (size - 1) == 0:
        return place ^ step
    return (place + step) % size


def source_of(place, step, size):
    if size & (size - 1) == 0:
        return place ^ step
    return (place + size - step) % size


def grid_of(segs):
    pair = 2 if segs % 2 == 0 else 1
    chips = segs // pair
    columns = next(c for c in range(1, chips + 1) if chips % c == 0 and c * c >= chips)
    return chips // columns, columns, pair


def member(grid, row, column, core):
    return (row * grid[1] + column) * grid[2] + core


def place_of(grid, device):
    chip = device // grid[2]
    return chip // grid[1], chip % grid[1], device % grid[2]


def along(grid, place, step, gather, ahead):
    row, column, core = place
    shift = target_of if ahead else source_of
    by_row = (core == 0) if gather else (core != 0)
    valid_column = step < grid[1]
    valid_row = step < grid[0]
    if isinstance(core, int):
        if by_row:
            return row, shift(column, step, grid[1]), valid_column
        return shift(row, step, grid[0]), column, valid_row
    moved_column = shift(column, min(step, grid[1] - 1), grid[1])
    moved_row = shift(row, min(step, grid[0] - 1), grid[0])
    return (
        jnp.where(by_row, row, moved_row),
        jnp.where(by_row, moved_column, column),
        jnp.where(by_row, valid_column, valid_row),
    )


def my_place(grid):
    me = lax.axis_index("seg")
    chip = lax.div(me, grid[2])
    return lax.div(chip, grid[1]), lax.rem(chip, grid[1]), lax.rem(me, grid[2])


def row_halves(full, core, pair):
    half = full.shape[0] // pair
    return [full.at[pl.ds(pl.multiple_of((core ^ j) * half, half), half), :] for j in range(pair)]


def join_halves(parts, full, core, pair):
    for half, terms in zip(row_halves(full, core, pair), parts):
        total = terms[0][...].astype(F32)
        for term in terms[1:]:
            total += term[...].astype(F32)
        half[...] = total.astype(BF16)


def line_length(grid):
    return max(grid[0], grid[1])


def write_weights(grid, parent, up, down):
    place = my_place(grid)
    pair = grid[2]
    count = line_length(grid) * pair

    def is_ancestor(child, other):
        first = parent[0, child]
        second = jnp.where(first >= 0, parent[0, jnp.maximum(first, 0)], -1)
        return jnp.logical_or(other == first, other == second)

    for out_step in range(count):
        row, column, _ = along(grid, place, out_step // pair, False, True)
        target = member(grid, row, column, place[2] ^ (out_step % pair))
        for in_step in range(count):
            row, column, valid = along(grid, place, in_step // pair, True, False)
            source = member(grid, row, column, place[2] ^ (in_step % pair))
            at = out_step * count + in_step
            for rows, used in ((up, is_ancestor(target, source)), (down, is_ancestor(source, target))):
                weight = jnp.where(jnp.logical_and(used, valid), 1.0, 0.0)
                rows[at : at + 1, :] = jnp.full((1, HD), weight, F32)


def write_halves(full, outs, core, pair):
    rows = full.shape[0] * pair // len(outs)
    for piece in range(len(outs) // pair):
        halves = row_halves(full.at[pl.ds(piece * rows, rows), :], core, pair)
        for half, out in zip(halves, outs[piece * pair : (piece + 1) * pair]):
            out[...] = half[...]


def state_kernel(grid, seg_len, keys_hbm, values_hbm, parent_hbm, keys, values, length, up, down, *rest):
    outs, (full, sems, parent, parent_sem) = rest[:-4], rest[-4:]
    rows, width = keys.shape
    chunk = rows // 4 if rows % 64 == 0 else rows
    steps = rows // chunk
    spans = 2 if width % (2 * HD) == 0 else 1
    copies = []
    for span in range(spans):
        cols = slice(span * width // spans, (span + 1) * width // spans)
        for step in range(steps):
            part = slice(step * chunk, (step + 1) * chunk)
            for j, (src, dst) in enumerate(((keys_hbm, keys), (values_hbm, values))):
                copies.append(pltpu.make_async_copy(src.at[part, cols], dst.at[part, cols], sems.at[j, span * steps + step]))
    few = pltpu.make_async_copy(parent_hbm, parent, parent_sem)
    few.start()
    for copy in copies:
        copy.start()
    length[...] = jnp.full(length.shape, seg_len[0], jnp.int32)
    few.wait()
    write_weights(grid, parent, up, down)
    live = lax.broadcasted_iota(jnp.int32, (rows, HD), 0) < seg_len[0]
    for head in range(width // HD):
        if head % (width // HD // spans) == 0:
            span = head // (width // HD // spans)
            for copy in copies[span * 2 * steps : (span + 1) * 2 * steps]:
                copy.wait()
        cols = head_cols(head)
        masked = jnp.where(live, keys[:, cols], jnp.zeros((), BF16))
        full[head * HD : (head + 1) * HD, :] = tn(masked, values[:, cols]).astype(BF16)
    write_halves(full, outs, my_place(grid)[2], grid[2])


def mix_kernel(sources, first, weights, *refs):
    blocks, outs = refs[:sources], refs[-sources:]
    rows = outs[0].shape[0]
    chunk = min(rows, 64)
    for start in range(0, rows, chunk):
        part = slice(start, start + chunk)
        loaded = [block[first + start : first + start + chunk, :].astype(F32) for block in blocks]
        for out_step, out in enumerate(outs):
            at = out_step * sources
            total = weights[at : at + 1, :] * loaded[0]
            for in_step in range(1, sources):
                total += weights[at + in_step : at + in_step + 1, :] * loaded[in_step]
            out[part, :] = total.astype(BF16)


def live_rows(length, rows):
    return lax.broadcasted_iota(jnp.int32, (rows, HD), 0) < length[:, :HD]


def write_mask(length, keep, turned):
    rows = length.shape[1]
    first = lax.broadcasted_iota(jnp.int32, (rows, rows), 0)
    second = lax.broadcasted_iota(jnp.int32, (rows, rows), 1)
    if turned:
        used = (first <= second) & (first < length[...])
    else:
        used = (second <= first) & (second < length[...])
    keep[...] = jnp.where(used, 1.0, 0.0).astype(BF16)


def split_refs(refs, *counts):
    parts, at = [], 0
    for count in counts:
        parts.append(refs[at : at + count])
        at += count
    return parts


def head_of(pieces, head):
    per_piece = pieces[0].shape[1] // HD
    return pieces[head // per_piece], head_cols(head % per_piece)


def fetch_kernel(source, _, out, sems):
    copies = row_copies(source, out, sems)
    for copy in copies:
        copy.start()
    for copy in copies:
        copy.wait()


def local_kernel(heads, length, queries, keys, values, *rest):
    local, keep = rest[-2:]
    write_mask(length, keep, False)
    for head in range(heads):
        cols = head_cols(head)
        scores = nt(queries[:, cols], keys[:, cols]).astype(BF16) * keep[...]
        local[:, cols] = nn(scores, values[:, cols])


def token_rows(total):
    return jnp.sum(jnp.transpose(total), axis=0, keepdims=True)


def token_columns(row):
    return jnp.transpose(jnp.broadcast_to(row, (HD, row.shape[1])))


def carry_kernel(piece, grid, counts, scale, length, queries, local, cotangent, gain, *rest):
    received, rest = rest[: sum(counts)], rest[sum(counts) :]
    before, (attention, sums, prefix) = rest[:-3], rest[-3:]
    join_halves(split_refs(received, *counts), prefix, my_place(grid)[2], grid[2])
    rows, width = attention.shape
    factor = jnp.where(live_rows(length, rows), scale, 0.0)
    squares = jnp.zeros((rows, HD), F32)
    products = jnp.zeros((rows, HD), F32)
    for head in range(width // HD):
        cols = head_cols(head)
        whole = head_cols(piece * width // HD + head)
        carried = nn(queries[:, whole], prefix[head * HD : (head + 1) * HD, :])
        out = factor * (carried + local[:, whole])
        attention[:, cols] = out
        squares += out * out
        products += out * (cotangent[:, whole].astype(F32) * gain[:, whole])
    both = jnp.concatenate([token_rows(squares), token_rows(products)], axis=0)
    for other in before:
        both += other[...]
    sums[...] = both


def grad_kernel(piece, groups, grid, scale, length, queries, cotangent, gain, *rest):
    all_sums, attention, rest = split_refs(rest, groups, FORWARD_PIECES, len(rest) - groups - FORWARD_PIECES)
    grad_out, halves, full = rest[0], rest[1 : 1 + grid[2]], rest[-1]
    rows, width = grad_out.shape
    features = HEADS * HD
    total = all_sums[0][...]
    for other in all_sums[1:]:
        total = total + other[...]
    inverse = lax.rsqrt(total[0:1, :] / features + EPSILON)
    if piece == 0:
        rest[1 + grid[2]][...] = inverse
    live = lax.broadcasted_iota(jnp.int32, (1, rows), 1) < length[...]
    live_inverse = jnp.where(live, inverse, 0.0)
    shrink = live_inverse * inverse * (inverse * total[1:2, :]) / features
    live_inverse = token_columns(live_inverse)
    shrink = token_columns(shrink)
    for head in range(width // HD):
        cols = head_cols(head)
        place = piece * width // HD + head
        whole = head_cols(place)
        out_piece, at = head_of(attention, place)
        gain_grad = cotangent[:, whole].astype(F32) * gain[:, whole]
        grad = (live_inverse * gain_grad - out_piece[:, at] * shrink).astype(BF16)
        grad_out[:, cols] = grad
        full[head * HD : (head + 1) * HD, :] = (scale * tn(queries[:, whole], grad)).astype(BF16)
    write_halves(full, halves, my_place(grid)[2], grid[2])


def row_copies(source, target, sems):
    rows = target.shape[0]
    chunk = rows // 4 if rows % 64 == 0 else rows
    parts = [pl.ds(step * chunk, chunk) for step in range(rows // chunk)]
    return [pltpu.make_async_copy(source.at[p, :], target.at[p, :], sems.at[j]) for j, p in enumerate(parts)]


def write_out(piece, sources, targets, sems):
    copies = []
    for j, (source, target) in enumerate(zip(sources, targets)):
        width = source.shape[1]
        copies += row_copies(source, target.at[:, pl.ds(piece * width, width)], sems.at[j])
    for copy in copies:
        copy.start()
    return copies


def query_kernel(piece, scale, length, inverse_rms, gain, queries, keys, values, grads, *rest):
    attention, prefix, rest = split_refs(rest, FORWARD_PIECES, FORWARD_PIECES, len(rest) - 2 * FORWARD_PIECES)
    attended, query_grad, key_part, token = rest[-8:-4] if piece else rest[-6:-2]
    keep, sems = rest[-2:]
    copies = write_out(piece - 1, rest[:2], rest[-4:-2], sems) if piece else []
    token[...] = jnp.zeros_like(token)
    write_mask(length, keep, False)
    inverse = token_columns(inverse_rms[...])
    heads = grads.shape[1] // HD
    for head in range(heads):
        cols = head_cols(head)
        place = piece * heads + head
        whole = head_cols(place)
        out_piece, at = head_of(attention, place)
        per_piece = prefix[0].shape[0] // HD
        prefix_piece, state = prefix[place // per_piece], place % per_piece
        grad = grads[:, cols]
        grad_scores = nt(grad, values[:, whole]).astype(BF16) * keep[...]
        carried = nt(grad, prefix_piece[state * HD : (state + 1) * HD, :])
        query_grad[:, cols] = (scale * (carried + nn(grad_scores, keys[:, whole]))).astype(BF16)
        key_part[:, cols] = scale * tn(grad_scores, queries[:, whole])
        attended[:, cols] = (out_piece[:, at] * inverse * gain[:, whole]).astype(BF16)
    for copy in copies:
        copy.wait()


def value_kernel(heads, scale, length, queries, keys, *rest):
    grads, rest = rest[:BACKWARD_PIECES], rest[BACKWARD_PIECES:]
    value_part, attended_hbm, query_hbm, keep, sems = rest[-5:]
    copies = write_out(BACKWARD_PIECES - 1, rest[:2], (attended_hbm, query_hbm), sems)
    write_mask(length, keep, True)
    for head in range(heads):
        cols = head_cols(head)
        grad_piece, at = head_of(grads, head)
        turned = nt(keys[:, cols], queries[:, cols]).astype(BF16) * keep[...]
        value_part[:, cols] = scale * nn(turned, grad_piece[:, at])
    for copy in copies:
        copy.wait()


def final_kernel(grid, counts, length, keys, values, value_part, *rest):
    count = sum(counts) * BACKWARD_PIECES
    key_parts, received, rest = split_refs(rest, BACKWARD_PIECES, count, len(rest) - BACKWARD_PIECES - count)
    key_hbm, value_hbm, key_grad, value_grad, below, sems = rest[-6:]
    pair = grid[2]
    tall = below.shape[0] // BACKWARD_PIECES
    for piece, parts in enumerate(split_refs(received, *[sum(counts)] * BACKWARD_PIECES)):
        full = below.at[pl.ds(piece * tall, tall), :]
        join_halves(split_refs(parts, *counts), full, my_place(grid)[2], pair)
    rows, width = keys.shape
    live = jnp.where(live_rows(length, rows), 1.0, 0.0)
    group = 2 if width // HD % 2 == 0 else 1
    copies = []
    for head in range(width // HD):
        cols = head_cols(head)
        key_part, at = head_of(key_parts, head)
        state = below[head * HD : (head + 1) * HD, :]
        key_grad[:, cols] = (key_part[:, at] + live * nt(values[:, cols], state)).astype(BF16)
        value_grad[:, cols] = (value_part[:, cols] + live * nn(keys[:, cols], state)).astype(BF16)
        if (head + 1) % group == 0:
            done = slice((head + 1 - group) * HD, (head + 1) * HD)
            for j, (src, dst) in enumerate(((key_grad, key_hbm), (value_grad, value_hbm))):
                copy = pltpu.make_async_copy(src.at[:, done], dst.at[:, done], sems.at[j, head // group])
                copy.start()
                copies.append(copy)
    for copy in copies:
        copy.wait()


def in_hbm(x):
    return pltpu.with_memory_space_constraint(x, pltpu.HBM)


def call(kernel, out_shape, operands, scratch=(), flops=0, stream=(), scalars=(), after=(), out_specs=None, aliases=None):
    moved = sum(math.prod(x.shape) * x.dtype.itemsize for x in operands)
    moved += sum(math.prod(x.shape) * x.dtype.itemsize for x in out_shape)
    specs = [SMEM if j in scalars else HBM if j in stream else VMEM for j in range(len(operands))]
    operands = [in_hbm(x) if j in stream else x for j, x in enumerate(operands)]
    return pl.pallas_call(
        kernel,
        out_shape=out_shape,
        in_specs=specs + [ANY] * len(after),
        out_specs=out_specs or [VMEM] * len(out_shape),
        scratch_shapes=list(scratch),
        input_output_aliases=aliases or {},
        compiler_params=pltpu.CompilerParams(vmem_limit_bytes=VMEM_LIMIT),
        cost_estimate=pl.CostEstimate(flops=flops, bytes_accessed=moved, transcendentals=0),
    )(*operands, *after)


def line_send(block, grid, step, flip, gather):
    moves = []
    for device in range(grid[0] * grid[1] * grid[2]):
        place = place_of(grid, device)
        if gather and flip:
            row, column, valid = along(grid, (place[0], place[1], place[2] ^ 1), step, True, True)
        else:
            row, column, valid = along(grid, place, step, gather, True)
        if valid:
            moves.append((device, member(grid, row, column, place[2] ^ flip)))
    return lax.ppermute(block, "seg", moves)


def gather_line(halves, grid):
    pair = grid[2]
    arrived = {0: halves[0]}
    for step in range(line_length(grid)):
        for flip in range(pair):
            if step or flip:
                arrived[step * pair + flip] = line_send(halves[flip], grid, step, flip, True)
    return [arrived[j] for j in range(len(arrived))]


def scatter_line(sums, grid):
    pair = grid[2]
    parts = [[] for _ in range(pair)]
    for step in reversed(range(line_length(grid))):
        for flip in range(pair):
            block = sums[step * pair + flip]
            parts[flip].append(line_send(block, grid, step, flip, False) if step or flip else block)
    return parts


def token_sums(sums, groups):
    parts = [sums]
    for step in [j for j in range(1, groups) if j != 2] + [2] * (groups > 2):
        moves = [(j, target_of(j, step, groups)) for j in range(groups)]
        parts.append(lax.ppermute(sums, "head", moves))
    return parts


def per_device(segs, groups, queries, key_rows, values, cotangent, out_gain, parent, seg_len):
    rows, features = queries.shape[1:]
    heads = features // HD
    grid = grid_of(segs)
    pair = grid[2]
    scale = 1.0 / math.sqrt(HD * rows)
    cot = cotangent[0]
    gain = out_gain[None]
    shape = jax.ShapeDtypeStruct
    narrow = shape((rows, features), BF16)
    wide = shape((rows, features), F32)
    row = shape((1, rows), F32)
    members = line_length(grid) * pair
    weight_rows = shape((members * members, HD), F32)
    sems = pltpu.SemaphoreType.DMA((2, heads))
    mask = pltpu.VMEM((rows, rows), BF16)
    counts = [line_length(grid)] * pair
    unit = 2 * heads * rows * HD

    def halves(pieces):
        return [shape((features // (pair * pieces), HD), BF16)] * pair

    def mix(arrived, weights, piece, pieces, after=()):
        tall = arrived[0].shape[0] // pieces
        like = [shape((tall, HD), BF16)] * members
        return call(functools.partial(mix_kernel, members, piece * tall), like, (weights, *arrived), after=after)

    def flat(parts):
        return [block for part in parts for block in part]

    key, value, length, up, down, *own = call(
        functools.partial(state_kernel, grid),
        [narrow, narrow, shape((1, rows), jnp.int32), weight_rows, weight_rows] + halves(FORWARD_PIECES) * FORWARD_PIECES,
        (seg_len, key_rows[0], values[0], parent[None]),
        [pltpu.VMEM((features, HD), BF16), sems, pltpu.SMEM((1, segs), jnp.int32), pltpu.SemaphoreType.DMA(())],
        unit * HD, (1, 2, 3), (0,),
    )
    (query,) = call(fetch_kernel, [narrow], (queries[0],), [pltpu.SemaphoreType.DMA((4,))], 0, (0,), after=(own[0],))
    mixed = []
    for part in split_refs(own, *[pair] * FORWARD_PIECES):
        mixed.append(mix(gather_line(part, grid), up, 0, 1, () if mixed else (query,)))
    (local,) = call(
        functools.partial(local_kernel, heads),
        [wide], (length, query, key, value), [mask], unit * rows * 2, after=(mixed[0][0],),
    )
    attention, prefix, sums = [], [], []
    width = features // FORWARD_PIECES
    for piece in range(FORWARD_PIECES):
        out, total, joined = call(
            functools.partial(carry_kernel, piece, grid, counts, scale),
            [shape((rows, width), F32), shape((2, rows), F32), shape((width, HD), BF16)],
            (length, query, local, cot, gain, *flat(scatter_line(mixed[piece], grid)), *sums),
            (), unit * HD // FORWARD_PIECES,
        )
        attention.append(out)
        prefix.append(joined)
        sums = [total]
    sums = token_sums(sums[0], groups)
    grads, state_grad = [], []
    width = features // BACKWARD_PIECES
    for piece in range(BACKWARD_PIECES):
        grad_out, *parts = call(
            functools.partial(grad_kernel, piece, len(sums), grid, scale),
            [shape((rows, width), BF16)] + halves(BACKWARD_PIECES) + [row] * (piece == 0),
            (length, query, cot, gain, *sums, *attention), [pltpu.VMEM((width, HD), BF16)],
            unit * HD // BACKWARD_PIECES,
        )
        grads.append(grad_out)
        state_grad.append(parts[:pair])
        if piece == 0:
            inverse_rms = parts[pair]
    narrow_piece, wide_piece = shape((rows, width), BF16), shape((rows, width), F32)
    copy_sems = pltpu.SemaphoreType.DMA((2, 4))
    mixed, key_parts, left, results = [], [], [], []

    def with_results(kernel, out_shape, operands, scratch, flops, after):
        operands = (*operands, *left, *results)
        last = len(operands) - len(results)
        outs = [narrow] * 2 if left else []
        return call(
            kernel, out_shape + outs, operands, [*scratch, copy_sems], flops, range(last, len(operands)), after=after,
            out_specs=[VMEM] * len(out_shape) + [HBM] * len(outs),
            aliases={last + j: len(out_shape) + j for j in range(len(results))},
        )

    for piece in range(BACKWARD_PIECES):
        *left, key_part, token, first, second = [
            *with_results(
                functools.partial(query_kernel, piece, scale),
                [narrow_piece, narrow_piece, wide_piece, shape((8, HD), F32)],
                (length, inverse_rms, gain, query, key, value, grads[piece], *attention, *prefix),
                [mask], unit * (3 * rows + HD) // BACKWARD_PIECES, tuple(sums[0] for sums in mixed),
            ),
            None,
            None,
        ][:6]
        results = [] if first is None else [first, second]
        key_parts.append(key_part)
        if piece == 0:
            for part in state_grad:
                mixed.append(mix(gather_line(part, grid), down, 0, 1, (token,)))
    value_part, attended, query_grad = with_results(
        functools.partial(value_kernel, heads, scale),
        [wide], (length, query, key, *grads), [mask], unit * 2 * rows, (mixed[-1][0],),
    )
    below = [block for sums in mixed for block in flat(scatter_line(sums, grid))]
    key_grad, value_grad = call(
        functools.partial(final_kernel, grid, counts),
        [narrow, narrow], (length, key, value, value_part, *key_parts, *below),
        [pltpu.VMEM(narrow.shape, BF16)] * 2 + [pltpu.VMEM((features, HD), BF16), sems],
        2 * unit * HD, out_specs=[HBM, HBM],
    )
    return attended[None], query_grad[None], key_grad[None], value_grad[None]


def solution(mesh):
    split = P("seg", None, "head")
    return jax.shard_map(
        functools.partial(per_device, mesh.shape["seg"], mesh.shape["head"]),
        mesh=mesh,
        in_specs=(split, split, split, split, P("head"), P(), P("seg")),
        out_specs=(split, split, split, split),
        check_vma=False,
    )
```

```python
import functools
import math

import jax
import jax.numpy as jnp
from jax import lax
from jax.experimental import pallas as pl
from jax.experimental.pallas import tpu as pltpu
from jax.sharding import PartitionSpec as P

HEADS = 64
HD = 128
EPSILON = 1e-06
F32 = jnp.float32
BF16 = jnp.bfloat16
VMEM_LIMIT = 24 * 1024 * 1024
FORWARD_PIECES = 2
BACKWARD_PIECES = 2

VMEM = pl.BlockSpec(memory_space=pltpu.VMEM)
SMEM = pl.BlockSpec(memory_space=pltpu.SMEM)
HBM = pl.BlockSpec(memory_space=pltpu.HBM)
ANY = pl.BlockSpec(memory_space=pl.ANY)


def dot(a, b, contract):
    return lax.dot_general(a, b, (contract, ((), ())), preferred_element_type=F32)


def nn(a, b):
    return dot(a, b, ((1,), (0,)))


def nt(a, b):
    return dot(a, b, ((1,), (1,)))


def tn(a, b):
    return dot(a, b, ((0,), (0,)))


def head_cols(head):
    return slice(head * HD, (head + 1) * HD)


def target_of(place, step, size):
    if size & (size - 1) == 0:
        return place ^ step
    return (place + step) % size


def source_of(place, step, size):
    if size & (size - 1) == 0:
        return place ^ step
    return (place + size - step) % size


def grid_of(segs):
    pair = 2 if segs % 2 == 0 else 1
    chips = segs // pair
    columns = next(c for c in range(1, chips + 1) if chips % c == 0 and c * c >= chips)
    return chips // columns, columns, pair


def member(grid, row, column, core):
    return (row * grid[1] + column) * grid[2] + core


def place_of(grid, device):
    chip = device // grid[2]
    return chip // grid[1], chip % grid[1], device % grid[2]


def along(grid, place, step, gather, ahead):
    row, column, core = place
    shift = target_of if ahead else source_of
    by_row = (core == 0) if gather else (core != 0)
    valid_column = step < grid[1]
    valid_row = step < grid[0]
    if isinstance(core, int):
        if by_row:
            return row, shift(column, step, grid[1]), valid_column
        return shift(row, step, grid[0]), column, valid_row
    moved_column = shift(column, min(step, grid[1] - 1), grid[1])
    moved_row = shift(row, min(step, grid[0] - 1), grid[0])
    return (
        jnp.where(by_row, row, moved_row),
        jnp.where(by_row, moved_column, column),
        jnp.where(by_row, valid_column, valid_row),
    )


def my_place(grid):
    me = lax.axis_index("seg")
    chip = lax.div(me, grid[2])
    return lax.div(chip, grid[1]), lax.rem(chip, grid[1]), lax.rem(me, grid[2])


def row_halves(full, core, pair):
    half = full.shape[0] // pair
    return [full.at[pl.ds(pl.multiple_of((core ^ j) * half, half), half), :] for j in range(pair)]


def join_halves(parts, full, core, pair):
    for half, terms in zip(row_halves(full, core, pair), parts):
        total = terms[0][...].astype(F32)
        for term in terms[1:]:
            total += term[...].astype(F32)
        half[...] = total.astype(BF16)


def line_length(grid):
    return max(grid[0], grid[1])


def write_weights(grid, parent, up, down):
    place = my_place(grid)
    pair = grid[2]
    count = line_length(grid) * pair

    def is_ancestor(child, other):
        first = parent[0, child]
        second = jnp.where(first >= 0, parent[0, jnp.maximum(first, 0)], -1)
        return jnp.logical_or(other == first, other == second)

    for out_step in range(count):
        row, column, _ = along(grid, place, out_step // pair, False, True)
        target = member(grid, row, column, place[2] ^ (out_step % pair))
        for in_step in range(count):
            row, column, valid = along(grid, place, in_step // pair, True, False)
            source = member(grid, row, column, place[2] ^ (in_step % pair))
            at = out_step * count + in_step
            for rows, used in ((up, is_ancestor(target, source)), (down, is_ancestor(source, target))):
                weight = jnp.where(jnp.logical_and(used, valid), 1.0, 0.0)
                rows[at : at + 1, :] = jnp.full((1, HD), weight, F32)


def write_halves(full, outs, core, pair):
    rows = full.shape[0] * pair // len(outs)
    for piece in range(len(outs) // pair):
        halves = row_halves(full.at[pl.ds(piece * rows, rows), :], core, pair)
        for half, out in zip(halves, outs[piece * pair : (piece + 1) * pair]):
            out[...] = half[...]


def state_kernel(grid, seg_len, keys_hbm, values_hbm, parent_hbm, keys, values, length, up, down, *rest):
    outs, (full, sems, parent, parent_sem) = rest[:-4], rest[-4:]
    rows, width = keys.shape
    chunk = rows // 4 if rows % 64 == 0 else rows
    steps = rows // chunk
    spans = 2 if width % (2 * HD) == 0 else 1
    copies = []
    for span in range(spans):
        cols = slice(span * width // spans, (span + 1) * width // spans)
        for step in range(steps):
            part = slice(step * chunk, (step + 1) * chunk)
            for j, (src, dst) in enumerate(((keys_hbm, keys), (values_hbm, values))):
                copies.append(pltpu.make_async_copy(src.at[part, cols], dst.at[part, cols], sems.at[j, span * steps + step]))
    few = pltpu.make_async_copy(parent_hbm, parent, parent_sem)
    few.start()
    for copy in copies:
        copy.start(priority=1)
    length[...] = jnp.full(length.shape, seg_len[0], jnp.int32)
    few.wait()
    write_weights(grid, parent, up, down)
    live = lax.broadcasted_iota(jnp.int32, (rows, HD), 0) < seg_len[0]
    for head in range(width // HD):
        if head % (width // HD // spans) == 0:
            span = head // (width // HD // spans)
            for copy in copies[span * 2 * steps : (span + 1) * 2 * steps]:
                copy.wait()
        cols = head_cols(head)
        masked = jnp.where(live, keys[:, cols], jnp.zeros((), BF16))
        full[head * HD : (head + 1) * HD, :] = tn(masked, values[:, cols]).astype(BF16)
    write_halves(full, outs, my_place(grid)[2], grid[2])


def mix_kernel(sources, first, weights, *refs):
    blocks, outs = refs[:sources], refs[-sources:]
    rows = outs[0].shape[0]
    chunk = min(rows, 64)
    for start in range(0, rows, chunk):
        part = slice(start, start + chunk)
        loaded = [block[first + start : first + start + chunk, :].astype(F32) for block in blocks]
        for out_step, out in enumerate(outs):
            at = out_step * sources
            total = weights[at : at + 1, :] * loaded[0]
            for in_step in range(1, sources):
                total += weights[at + in_step : at + in_step + 1, :] * loaded[in_step]
            out[part, :] = total.astype(BF16)


def live_rows(length, rows):
    return lax.broadcasted_iota(jnp.int32, (rows, HD), 0) < length[:, :HD]


def write_mask(length, keep, turned):
    rows = length.shape[1]
    first = lax.broadcasted_iota(jnp.int32, (rows, rows), 0)
    second = lax.broadcasted_iota(jnp.int32, (rows, rows), 1)
    if turned:
        used = (first <= second) & (first < length[...])
    else:
        used = (second <= first) & (second < length[...])
    keep[...] = jnp.where(used, 1.0, 0.0).astype(BF16)


def split_refs(refs, *counts):
    parts, at = [], 0
    for count in counts:
        parts.append(refs[at : at + count])
        at += count
    return parts


def head_of(pieces, head):
    per_piece = pieces[0].shape[1] // HD
    return pieces[head // per_piece], head_cols(head % per_piece)


def fetch_kernel(source, _, out, sems):
    copies = row_copies(source, out, sems)
    for copy in copies:
        copy.start(priority=1)
    for copy in copies:
        copy.wait()


def local_kernel(heads, length, queries, keys, values, *rest):
    local, keep = rest[-2:]
    write_mask(length, keep, False)
    for head in range(heads):
        cols = head_cols(head)
        scores = nt(queries[:, cols], keys[:, cols]).astype(BF16) * keep[...]
        local[:, cols] = nn(scores, values[:, cols])


def token_rows(total):
    return jnp.sum(jnp.transpose(total), axis=0, keepdims=True)


def token_columns(row):
    return jnp.transpose(jnp.broadcast_to(row, (HD, row.shape[1])))


def carry_kernel(piece, grid, counts, scale, length, queries, local, cotangent, gain, *rest):
    received, rest = rest[: sum(counts)], rest[sum(counts) :]
    before, (attention, sums, prefix) = rest[:-3], rest[-3:]
    join_halves(split_refs(received, *counts), prefix, my_place(grid)[2], grid[2])
    rows, width = attention.shape
    factor = jnp.where(live_rows(length, rows), scale, 0.0)
    squares = jnp.zeros((rows, HD), F32)
    products = jnp.zeros((rows, HD), F32)
    for head in range(width // HD):
        cols = head_cols(head)
        whole = head_cols(piece * width // HD + head)
        carried = nn(queries[:, whole], prefix[head * HD : (head + 1) * HD, :])
        out = factor * (carried + local[:, whole])
        attention[:, cols] = out
        squares += out * out
        products += out * (cotangent[:, whole].astype(F32) * gain[:, whole])
    both = jnp.concatenate([token_rows(squares), token_rows(products)], axis=0)
    for other in before:
        both += other[...]
    sums[...] = both


def grad_kernel(piece, groups, grid, scale, length, queries, cotangent, gain, *rest):
    all_sums, attention, rest = split_refs(rest, groups, FORWARD_PIECES, len(rest) - groups - FORWARD_PIECES)
    grad_out, halves, full = rest[0], rest[1 : 1 + grid[2]], rest[-1]
    rows, width = grad_out.shape
    features = HEADS * HD
    total = all_sums[0][...]
    for other in all_sums[1:]:
        total = total + other[...]
    inverse = lax.rsqrt(total[0:1, :] / features + EPSILON)
    if piece == 0:
        rest[1 + grid[2]][...] = inverse
    live = lax.broadcasted_iota(jnp.int32, (1, rows), 1) < length[...]
    live_inverse = jnp.where(live, inverse, 0.0)
    shrink = live_inverse * inverse * (inverse * total[1:2, :]) / features
    live_inverse = token_columns(live_inverse)
    shrink = token_columns(shrink)
    for head in range(width // HD):
        cols = head_cols(head)
        place = piece * width // HD + head
        whole = head_cols(place)
        out_piece, at = head_of(attention, place)
        gain_grad = cotangent[:, whole].astype(F32) * gain[:, whole]
        grad = (live_inverse * gain_grad - out_piece[:, at] * shrink).astype(BF16)
        grad_out[:, cols] = grad
        full[head * HD : (head + 1) * HD, :] = (scale * tn(queries[:, whole], grad)).astype(BF16)
    write_halves(full, halves, my_place(grid)[2], grid[2])


def row_copies(source, target, sems):
    rows = target.shape[0]
    chunk = rows // 4 if rows % 64 == 0 else rows
    parts = [pl.ds(step * chunk, chunk) for step in range(rows // chunk)]
    return [pltpu.make_async_copy(source.at[p, :], target.at[p, :], sems.at[j]) for j, p in enumerate(parts)]


def write_out(piece, sources, targets, sems):
    copies = []
    for j, (source, target) in enumerate(zip(sources, targets)):
        width = source.shape[1]
        copies += row_copies(source, target.at[:, pl.ds(piece * width, width)], sems.at[j])
    for copy in copies:
        copy.start(priority=1)
    return copies


def query_kernel(piece, scale, length, inverse_rms, gain, queries, keys, values, grads, *rest):
    attention, prefix, rest = split_refs(rest, FORWARD_PIECES, FORWARD_PIECES, len(rest) - 2 * FORWARD_PIECES)
    attended, query_grad, key_part, token = rest[-8:-4] if piece else rest[-6:-2]
    keep, sems = rest[-2:]
    copies = write_out(piece - 1, rest[:2], rest[-4:-2], sems) if piece else []
    token[...] = jnp.zeros_like(token)
    write_mask(length, keep, False)
    inverse = token_columns(inverse_rms[...])
    heads = grads.shape[1] // HD
    for head in range(heads):
        cols = head_cols(head)
        place = piece * heads + head
        whole = head_cols(place)
        out_piece, at = head_of(attention, place)
        per_piece = prefix[0].shape[0] // HD
        prefix_piece, state = prefix[place // per_piece], place % per_piece
        grad = grads[:, cols]
        grad_scores = nt(grad, values[:, whole]).astype(BF16) * keep[...]
        carried = nt(grad, prefix_piece[state * HD : (state + 1) * HD, :])
        query_grad[:, cols] = (scale * (carried + nn(grad_scores, keys[:, whole]))).astype(BF16)
        key_part[:, cols] = scale * tn(grad_scores, queries[:, whole])
        attended[:, cols] = (out_piece[:, at] * inverse * gain[:, whole]).astype(BF16)
    for copy in copies:
        copy.wait()


def value_kernel(heads, scale, length, queries, keys, *rest):
    grads, rest = rest[:BACKWARD_PIECES], rest[BACKWARD_PIECES:]
    value_part, attended_hbm, query_hbm, keep, sems = rest[-5:]
    copies = write_out(BACKWARD_PIECES - 1, rest[:2], (attended_hbm, query_hbm), sems)
    write_mask(length, keep, True)
    for head in range(heads):
        cols = head_cols(head)
        grad_piece, at = head_of(grads, head)
        turned = nt(keys[:, cols], queries[:, cols]).astype(BF16) * keep[...]
        value_part[:, cols] = scale * nn(turned, grad_piece[:, at])
    for copy in copies:
        copy.wait()


def final_kernel(grid, counts, length, keys, values, value_part, *rest):
    count = sum(counts) * BACKWARD_PIECES
    key_parts, received, rest = split_refs(rest, BACKWARD_PIECES, count, len(rest) - BACKWARD_PIECES - count)
    key_hbm, value_hbm, key_grad, value_grad, below, sems = rest[-6:]
    pair = grid[2]
    tall = below.shape[0] // BACKWARD_PIECES
    for piece, parts in enumerate(split_refs(received, *[sum(counts)] * BACKWARD_PIECES)):
        full = below.at[pl.ds(piece * tall, tall), :]
        join_halves(split_refs(parts, *counts), full, my_place(grid)[2], pair)
    rows, width = keys.shape
    live = jnp.where(live_rows(length, rows), 1.0, 0.0)
    group = 2 if width // HD % 2 == 0 else 1
    copies = []
    for head in range(width // HD):
        cols = head_cols(head)
        key_part, at = head_of(key_parts, head)
        state = below[head * HD : (head + 1) * HD, :]
        key_grad[:, cols] = (key_part[:, at] + live * nt(values[:, cols], state)).astype(BF16)
        value_grad[:, cols] = (value_part[:, cols] + live * nn(keys[:, cols], state)).astype(BF16)
        if (head + 1) % group == 0:
            done = slice((head + 1 - group) * HD, (head + 1) * HD)
            for j, (src, dst) in enumerate(((key_grad, key_hbm), (value_grad, value_hbm))):
                copy = pltpu.make_async_copy(src.at[:, done], dst.at[:, done], sems.at[j, head // group])
                copy.start(priority=1)
                copies.append(copy)
    for copy in copies:
        copy.wait()


def in_hbm(x):
    return pltpu.with_memory_space_constraint(x, pltpu.HBM)


def call(kernel, out_shape, operands, scratch=(), flops=0, stream=(), scalars=(), after=(), out_specs=None, aliases=None):
    moved = sum(math.prod(x.shape) * x.dtype.itemsize for x in operands)
    moved += sum(math.prod(x.shape) * x.dtype.itemsize for x in out_shape)
    specs = [SMEM if j in scalars else HBM if j in stream else VMEM for j in range(len(operands))]
    operands = [in_hbm(x) if j in stream else x for j, x in enumerate(operands)]
    return pl.pallas_call(
        kernel,
        out_shape=out_shape,
        in_specs=specs + [ANY] * len(after),
        out_specs=out_specs or [VMEM] * len(out_shape),
        scratch_shapes=list(scratch),
        input_output_aliases=aliases or {},
        compiler_params=pltpu.CompilerParams(vmem_limit_bytes=VMEM_LIMIT),
        cost_estimate=pl.CostEstimate(flops=flops, bytes_accessed=moved, transcendentals=0),
    )(*operands, *after)


def line_send(block, grid, step, flip, gather):
    moves = []
    for device in range(grid[0] * grid[1] * grid[2]):
        place = place_of(grid, device)
        if gather and flip:
            row, column, valid = along(grid, (place[0], place[1], place[2] ^ 1), step, True, True)
        else:
            row, column, valid = along(grid, place, step, gather, True)
        if valid:
            moves.append((device, member(grid, row, column, place[2] ^ flip)))
    return lax.ppermute(block, "seg", moves)


def gather_line(halves, grid):
    pair = grid[2]
    arrived = {0: halves[0]}
    for step in range(line_length(grid)):
        for flip in range(pair):
            if step or flip:
                arrived[step * pair + flip] = line_send(halves[flip], grid, step, flip, True)
    return [arrived[j] for j in range(len(arrived))]


def scatter_line(sums, grid):
    pair = grid[2]
    parts = [[] for _ in range(pair)]
    for step in reversed(range(line_length(grid))):
        for flip in range(pair):
            block = sums[step * pair + flip]
            parts[flip].append(line_send(block, grid, step, flip, False) if step or flip else block)
    return parts


def token_sums(sums, groups):
    parts = [sums]
    for step in [j for j in range(1, groups) if j != 2] + [2] * (groups > 2):
        moves = [(j, target_of(j, step, groups)) for j in range(groups)]
        parts.append(lax.ppermute(sums, "head", moves))
    return parts


def per_device(segs, groups, queries, key_rows, values, cotangent, out_gain, parent, seg_len):
    rows, features = queries.shape[1:]
    heads = features // HD
    grid = grid_of(segs)
    pair = grid[2]
    scale = 1.0 / math.sqrt(HD * rows)
    cot = cotangent[0]
    gain = out_gain[None]
    shape = jax.ShapeDtypeStruct
    narrow = shape((rows, features), BF16)
    wide = shape((rows, features), F32)
    row = shape((1, rows), F32)
    members = line_length(grid) * pair
    weight_rows = shape((members * members, HD), F32)
    sems = pltpu.SemaphoreType.DMA((2, heads))
    mask = pltpu.VMEM((rows, rows), BF16)
    counts = [line_length(grid)] * pair
    unit = 2 * heads * rows * HD

    def halves(pieces):
        return [shape((features // (pair * pieces), HD), BF16)] * pair

    def mix(arrived, weights, piece, pieces, after=()):
        tall = arrived[0].shape[0] // pieces
        like = [shape((tall, HD), BF16)] * members
        return call(functools.partial(mix_kernel, members, piece * tall), like, (weights, *arrived), after=after)

    def flat(parts):
        return [block for part in parts for block in part]

    key, value, length, up, down, *own = call(
        functools.partial(state_kernel, grid),
        [narrow, narrow, shape((1, rows), jnp.int32), weight_rows, weight_rows] + halves(FORWARD_PIECES) * FORWARD_PIECES,
        (seg_len, key_rows[0], values[0], parent[None]),
        [pltpu.VMEM((features, HD), BF16), sems, pltpu.SMEM((1, segs), jnp.int32), pltpu.SemaphoreType.DMA(())],
        unit * HD, (1, 2, 3), (0,),
    )
    (query,) = call(fetch_kernel, [narrow], (queries[0],), [pltpu.SemaphoreType.DMA((4,))], 0, (0,), after=(own[0],))
    mixed = []
    for part in split_refs(own, *[pair] * FORWARD_PIECES):
        mixed.append(mix(gather_line(part, grid), up, 0, 1, () if mixed else (query,)))
    (local,) = call(
        functools.partial(local_kernel, heads),
        [wide], (length, query, key, value), [mask], unit * rows * 2, after=(mixed[0][0],),
    )
    attention, prefix, sums = [], [], []
    width = features // FORWARD_PIECES
    for piece in range(FORWARD_PIECES):
        out, total, joined = call(
            functools.partial(carry_kernel, piece, grid, counts, scale),
            [shape((rows, width), F32), shape((2, rows), F32), shape((width, HD), BF16)],
            (length, query, local, cot, gain, *flat(scatter_line(mixed[piece], grid)), *sums),
            (), unit * HD // FORWARD_PIECES,
        )
        attention.append(out)
        prefix.append(joined)
        sums = [total]
    sums = token_sums(sums[0], groups)
    grads, state_grad = [], []
    width = features // BACKWARD_PIECES
    for piece in range(BACKWARD_PIECES):
        grad_out, *parts = call(
            functools.partial(grad_kernel, piece, len(sums), grid, scale),
            [shape((rows, width), BF16)] + halves(BACKWARD_PIECES) + [row] * (piece == 0),
            (length, query, cot, gain, *sums, *attention), [pltpu.VMEM((width, HD), BF16)],
            unit * HD // BACKWARD_PIECES,
        )
        grads.append(grad_out)
        state_grad.append(parts[:pair])
        if piece == 0:
            inverse_rms = parts[pair]
    narrow_piece, wide_piece = shape((rows, width), BF16), shape((rows, width), F32)
    copy_sems = pltpu.SemaphoreType.DMA((2, 4))
    mixed, key_parts, left, results = [], [], [], []

    def with_results(kernel, out_shape, operands, scratch, flops, after):
        operands = (*operands, *left, *results)
        last = len(operands) - len(results)
        outs = [narrow] * 2 if left else []
        return call(
            kernel, out_shape + outs, operands, [*scratch, copy_sems], flops, range(last, len(operands)), after=after,
            out_specs=[VMEM] * len(out_shape) + [HBM] * len(outs),
            aliases={last + j: len(out_shape) + j for j in range(len(results))},
        )

    for piece in range(BACKWARD_PIECES):
        *left, key_part, token, first, second = [
            *with_results(
                functools.partial(query_kernel, piece, scale),
                [narrow_piece, narrow_piece, wide_piece, shape((8, HD), F32)],
                (length, inverse_rms, gain, query, key, value, grads[piece], *attention, *prefix),
                [mask], unit * (3 * rows + HD) // BACKWARD_PIECES, tuple(sums[0] for sums in mixed),
            ),
            None,
            None,
        ][:6]
        results = [] if first is None else [first, second]
        key_parts.append(key_part)
        if piece == 0:
            for part in state_grad:
                mixed.append(mix(gather_line(part, grid), down, 0, 1, (token,)))
    value_part, attended, query_grad = with_results(
        functools.partial(value_kernel, heads, scale),
        [wide], (length, query, key, *grads), [mask], unit * 2 * rows, (mixed[-1][0],),
    )
    below = [block for sums in mixed for block in flat(scatter_line(sums, grid))]
    key_grad, value_grad = call(
        functools.partial(final_kernel, grid, counts),
        [narrow, narrow], (length, key, value, value_part, *key_parts, *below),
        [pltpu.VMEM(narrow.shape, BF16)] * 2 + [pltpu.VMEM((features, HD), BF16), sems],
        2 * unit * HD, out_specs=[HBM, HBM],
    )
    return attended[None], query_grad[None], key_grad[None], value_grad[None]


def solution(mesh):
    split = P("seg", None, "head")
    return jax.shard_map(
        functools.partial(per_device, mesh.shape["seg"], mesh.shape["head"]),
        mesh=mesh,
        in_specs=(split, split, split, split, P("head"), P(), P("seg")),
        out_specs=(split, split, split, split),
        check_vma=False,
    )
```

```python
import functools
import math

import jax
import jax.numpy as jnp
from jax import lax
from jax.experimental import pallas as pl
from jax.experimental.pallas import tpu as pltpu
from jax.sharding import PartitionSpec as P

HEADS = 64
HD = 128
EPSILON = 1e-06
F32 = jnp.float32
BF16 = jnp.bfloat16
VMEM_LIMIT = 24 * 1024 * 1024
FORWARD_PIECES = 2

VMEM = pl.BlockSpec(memory_space=pltpu.VMEM)
SMEM = pl.BlockSpec(memory_space=pltpu.SMEM)
HBM = pl.BlockSpec(memory_space=pltpu.HBM)
ANY = pl.BlockSpec(memory_space=pl.ANY)


def dot(a, b, contract):
    return lax.dot_general(a, b, (contract, ((), ())), preferred_element_type=F32)


def nn(a, b):
    return dot(a, b, ((1,), (0,)))


def nt(a, b):
    return dot(a, b, ((1,), (1,)))


def tn(a, b):
    return dot(a, b, ((0,), (0,)))


def head_cols(head):
    return slice(head * HD, (head + 1) * HD)


def target_of(place, step, size):
    if size & (size - 1) == 0:
        return place ^ step
    return (place + step) % size


def source_of(place, step, size):
    if size & (size - 1) == 0:
        return place ^ step
    return (place + size - step) % size


def grid_of(segs):
    pair = 2 if segs % 2 == 0 else 1
    chips = segs // pair
    columns = next(c for c in range(1, chips + 1) if chips % c == 0 and c * c >= chips)
    return chips // columns, columns, pair


def member(grid, row, column, core):
    return (row * grid[1] + column) * grid[2] + core


def place_of(grid, device):
    chip = device // grid[2]
    return chip // grid[1], chip % grid[1], device % grid[2]


def along(grid, place, step, gather, ahead):
    row, column, core = place
    shift = target_of if ahead else source_of
    by_row = (core == 0) if gather else (core != 0)
    valid_column = step < grid[1]
    valid_row = step < grid[0]
    if isinstance(core, int):
        if by_row:
            return row, shift(column, step, grid[1]), valid_column
        return shift(row, step, grid[0]), column, valid_row
    moved_column = shift(column, min(step, grid[1] - 1), grid[1])
    moved_row = shift(row, min(step, grid[0] - 1), grid[0])
    return (
        jnp.where(by_row, row, moved_row),
        jnp.where(by_row, moved_column, column),
        jnp.where(by_row, valid_column, valid_row),
    )


def my_place(grid):
    me = lax.axis_index("seg")
    chip = lax.div(me, grid[2])
    return lax.div(chip, grid[1]), lax.rem(chip, grid[1]), lax.rem(me, grid[2])


def row_halves(full, core, pair):
    half = full.shape[0] // pair
    return [full.at[pl.ds(pl.multiple_of((core ^ j) * half, half), half), :] for j in range(pair)]


def join_halves(parts, full, core, pair):
    for half, terms in zip(row_halves(full, core, pair), parts):
        total = terms[0][...].astype(F32)
        for term in terms[1:]:
            total += term[...].astype(F32)
        half[...] = total.astype(BF16)


def line_length(grid):
    return max(grid[0], grid[1])


def write_weights(grid, parent, up, down):
    place = my_place(grid)
    pair = grid[2]
    count = line_length(grid) * pair

    def is_ancestor(child, other):
        first = parent[0, child]
        second = jnp.where(first >= 0, parent[0, jnp.maximum(first, 0)], -1)
        return jnp.logical_or(other == first, other == second)

    for out_step in range(count):
        row, column, _ = along(grid, place, out_step // pair, False, True)
        target = member(grid, row, column, place[2] ^ (out_step % pair))
        for in_step in range(count):
            row, column, valid = along(grid, place, in_step // pair, True, False)
            source = member(grid, row, column, place[2] ^ (in_step % pair))
            at = out_step * count + in_step
            for rows, used in ((up, is_ancestor(target, source)), (down, is_ancestor(source, target))):
                weight = jnp.where(jnp.logical_and(used, valid), 1.0, 0.0)
                rows[at : at + 1, :] = jnp.full((1, HD), weight, F32)


def own_states(piece, grid, keys, values, live, full, outs):
    heads = full.shape[0] // HD
    for head in range(heads):
        cols = head_cols(piece * heads + head)
        masked = jnp.where(live, keys[:, cols], jnp.zeros((), BF16))
        full[head * HD : (head + 1) * HD, :] = tn(masked, values[:, cols]).astype(BF16)
    for half, out in zip(row_halves(full, my_place(grid)[2], grid[2]), outs):
        out[...] = half[...]


def state_kernel(grid, seg_len, keys_hbm, values_hbm, parent_hbm, keys, values, length, up, down, *rest):
    outs, (full, sems, parent, parent_sem) = rest[:-4], rest[-4:]
    rows, width = keys.shape
    chunk = rows // 2 if rows % 32 == 0 else rows
    steps = rows // chunk
    spans = [slice(0, full.shape[0]), slice(full.shape[0], width)][:FORWARD_PIECES]
    copies = []
    for number, cols in enumerate(spans):
        for step in range(steps):
            part = slice(step * chunk, (step + 1) * chunk)
            for j, (src, dst) in enumerate(((keys_hbm, keys), (values_hbm, values))):
                copies.append(
                    pltpu.make_async_copy(src.at[part, cols], dst.at[part, cols], sems.at[j, number * steps + step])
                )
    few = pltpu.make_async_copy(parent_hbm, parent, parent_sem)
    few.start()
    for copy in copies:
        copy.start()
    length[...] = jnp.full(length.shape, seg_len[0], jnp.int32)
    few.wait()
    write_weights(grid, parent, up, down)
    live = lax.broadcasted_iota(jnp.int32, (rows, HD), 0) < seg_len[0]
    for copy in copies[: 2 * steps]:
        copy.wait()
    own_states(0, grid, keys, values, live, full, outs)
    for copy in copies[2 * steps :]:
        copy.wait()


def next_state_kernel(piece, grid, length, keys, values, *rest):
    outs, full = rest[:-1], rest[-1]
    own_states(piece, grid, keys, values, live_rows(length, keys.shape[0]), full, outs)


def mix_kernel(sources, first, weights, *refs):
    blocks, outs = refs[:sources], refs[-sources:]
    rows = outs[0].shape[0]
    chunk = min(rows, 64)
    for start in range(0, rows, chunk):
        part = slice(start, start + chunk)
        loaded = [block[first + start : first + start + chunk, :].astype(F32) for block in blocks]
        for out_step, out in enumerate(outs):
            at = out_step * sources
            total = weights[at : at + 1, :] * loaded[0]
            for in_step in range(1, sources):
                total += weights[at + in_step : at + in_step + 1, :] * loaded[in_step]
            out[part, :] = total.astype(BF16)


def live_rows(length, rows):
    return lax.broadcasted_iota(jnp.int32, (rows, HD), 0) < length[:, :HD]


def write_mask(length, keep, turned):
    rows = length.shape[1]
    first = lax.broadcasted_iota(jnp.int32, (rows, rows), 0)
    second = lax.broadcasted_iota(jnp.int32, (rows, rows), 1)
    if turned:
        used = (first <= second) & (first < length[...])
    else:
        used = (second <= first) & (second < length[...])
    keep[...] = jnp.where(used, 1.0, 0.0).astype(BF16)


def split_refs(refs, *counts):
    parts, at = [], 0
    for count in counts:
        parts.append(refs[at : at + count])
        at += count
    return parts


def fetch_kernel(source, _, out, sems):
    copies = row_copies(source, out, sems)
    for copy in copies:
        copy.start()
    for copy in copies:
        copy.wait()


def local_kernel(heads, length, queries, keys, values, *rest):
    local, keep = rest[-2:]
    write_mask(length, keep, False)
    for head in range(heads):
        cols = head_cols(head)
        scores = nt(queries[:, cols], keys[:, cols]).astype(BF16) * keep[...]
        local[:, cols] = nn(scores, values[:, cols])


def token_rows(total):
    return jnp.sum(jnp.transpose(total), axis=0, keepdims=True)


def token_columns(row):
    return jnp.transpose(jnp.broadcast_to(row, (HD, row.shape[1])))


def carry_kernel(piece, grid, counts, scale, length, queries, local, cotangent, gain, *rest):
    received, rest = rest[: sum(counts)], rest[sum(counts) :]
    before, (attention, sums, prefix) = rest[: (piece > 0)], rest[-3:]
    join_halves(split_refs(received, *counts), prefix, my_place(grid)[2], grid[2])
    rows, width = queries.shape[0], prefix.shape[0]
    factor = jnp.where(live_rows(length, rows), scale, 0.0)
    squares = jnp.zeros((rows, HD), F32)
    products = jnp.zeros((rows, HD), F32)
    for head in range(width // HD):
        whole = head_cols(piece * width // HD + head)
        carried = nn(queries[:, whole], prefix[head * HD : (head + 1) * HD, :])
        out = factor * (carried + local[:, whole])
        attention[:, whole] = out
        squares += out * out
        products += out * (cotangent[:, whole].astype(F32) * gain[:, whole])
    both = jnp.concatenate([token_rows(squares), token_rows(products)], axis=0)
    for other in before:
        both += other[...]
    sums[...] = both


def grad_kernel(groups, grid, scale, length, queries, cotangent, gain, attention, *rest):
    all_sums, (grad_out, inverse_rms, *halves, full) = rest[:groups], rest[groups:]
    rows = queries.shape[0]
    features = HEADS * HD
    total = all_sums[0][...]
    for other in all_sums[1:]:
        total = total + other[...]
    inverse = lax.rsqrt(total[0:1, :] / features + EPSILON)
    inverse_rms[...] = inverse
    live = lax.broadcasted_iota(jnp.int32, (1, rows), 1) < length[...]
    live_inverse = jnp.where(live, inverse, 0.0)
    shrink = live_inverse * inverse * (inverse * total[1:2, :]) / features
    live_inverse = token_columns(live_inverse)
    shrink = token_columns(shrink)
    for head in range(queries.shape[1] // HD):
        cols = head_cols(head)
        gain_grad = cotangent[:, cols].astype(F32) * gain[:, cols]
        grad = (live_inverse * gain_grad - attention[:, cols] * shrink).astype(BF16)
        grad_out[:, cols] = grad
        full[head * HD : (head + 1) * HD, :] = (scale * tn(queries[:, cols], grad)).astype(BF16)
    for half, out in zip(row_halves(full, my_place(grid)[2], grid[2]), halves):
        out[...] = half[...]


def row_copies(source, target, sems):
    rows = target.shape[0]
    chunk = rows // 4 if rows % 64 == 0 else rows
    parts = [pl.ds(step * chunk, chunk) for step in range(rows // chunk)]
    return [pltpu.make_async_copy(source.at[p, :], target.at[p, :], sems.at[j]) for j, p in enumerate(parts)]


def query_kernel(heads, group, scale, length, inverse_rms, gain, queries, keys, values, grads, attention, *rest):
    prefix, rest = split_refs(rest, FORWARD_PIECES, len(rest) - FORWARD_PIECES)
    attended_hbm, query_hbm, key_part, token, attended, query_grad, keep, sems = rest
    token[...] = jnp.zeros_like(token)
    write_mask(length, keep, False)
    inverse = token_columns(inverse_rms[...])
    copies = []
    for head in range(heads):
        cols = head_cols(head)
        grad = grads[:, cols]
        per_piece = heads // FORWARD_PIECES
        prefix_piece, state = prefix[head // per_piece], head % per_piece
        grad_scores = nt(grad, values[:, cols]).astype(BF16) * keep[...]
        carried = nt(grad, prefix_piece[state * HD : (state + 1) * HD, :])
        query_grad[:, cols] = (scale * (carried + nn(grad_scores, keys[:, cols]))).astype(BF16)
        key_part[:, cols] = scale * tn(grad_scores, queries[:, cols])
        attended[:, cols] = (attention[:, cols] * inverse * gain[:, cols]).astype(BF16)
        if (head + 1) % group == 0:
            step = head // group
            done = slice(step * group * HD, (head + 1) * HD)
            for j, (src, dst) in enumerate(((attended, attended_hbm), (query_grad, query_hbm))):
                copy = pltpu.make_async_copy(src.at[:, done], dst.at[:, done], sems.at[step, j])
                copy.start()
                copies.append(copy)
    for copy in copies:
        copy.wait()


def value_kernel(heads, scale, length, queries, keys, grads, *rest):
    value_part, keep = rest[-2:]
    write_mask(length, keep, True)
    for head in range(heads):
        cols = head_cols(head)
        turned = nt(keys[:, cols], queries[:, cols]).astype(BF16) * keep[...]
        value_part[:, cols] = scale * nn(turned, grads[:, cols])


def final_kernel(begin, count, grid, counts, length, keys, values, key_part, value_part, *rest):
    received, rest = rest[: sum(counts)], rest[sum(counts) :]
    key_hbm, value_hbm, key_grad, value_grad, below, sems = rest[-6:]
    pair = grid[2]
    join_halves(split_refs(received, *counts), below, my_place(grid)[2], pair)
    rows = keys.shape[0]
    live = jnp.where(live_rows(length, rows), 1.0, 0.0)
    copies, pending = [], 0
    for head in range(pair * count):
        half, within = divmod(head, count)
        cols = head_cols(head)
        place = half * (keys.shape[1] // HD // pair) + begin + within
        whole = head_cols(place)
        state = below[head * HD : (head + 1) * HD, :]
        key_grad[:, cols] = (key_part[:, whole] + live * nt(values[:, whole], state)).astype(BF16)
        value_grad[:, cols] = (value_part[:, whole] + live * nn(keys[:, whole], state)).astype(BF16)
        pending += 1
        if pending == 2 or within == count - 1:
            done = slice((head + 1 - pending) * HD, (head + 1) * HD)
            there = slice((place + 1 - pending) * HD, (place + 1) * HD)
            pending = 0
            for j, (src, dst) in enumerate(((key_grad, key_hbm), (value_grad, value_hbm))):
                copy = pltpu.make_async_copy(src.at[:, done], dst.at[:, there], sems.at[j, head])
                copy.start()
                copies.append(copy)
    for copy in copies:
        copy.wait()


def in_hbm(x):
    return pltpu.with_memory_space_constraint(x, pltpu.HBM)


def call(kernel, out_shape, operands, scratch=(), flops=0, stream=(), scalars=(), after=(), out_specs=None, aliases=None):
    moved = sum(math.prod(x.shape) * x.dtype.itemsize for x in operands)
    moved += sum(math.prod(x.shape) * x.dtype.itemsize for x in out_shape)
    specs = [SMEM if j in scalars else HBM if j in stream else VMEM for j in range(len(operands))]
    operands = [in_hbm(x) if j in stream else x for j, x in enumerate(operands)]
    return pl.pallas_call(
        kernel,
        out_shape=out_shape,
        in_specs=specs + [ANY] * len(after),
        out_specs=out_specs or [VMEM] * len(out_shape),
        scratch_shapes=list(scratch),
        input_output_aliases=aliases or {},
        compiler_params=pltpu.CompilerParams(vmem_limit_bytes=VMEM_LIMIT),
        cost_estimate=pl.CostEstimate(flops=flops, bytes_accessed=moved, transcendentals=0),
    )(*operands, *after)


def line_send(block, grid, step, flip, gather):
    moves = []
    for device in range(grid[0] * grid[1] * grid[2]):
        place = place_of(grid, device)
        if gather and flip:
            row, column, valid = along(grid, (place[0], place[1], place[2] ^ 1), step, True, True)
        else:
            row, column, valid = along(grid, place, step, gather, True)
        if valid:
            moves.append((device, member(grid, row, column, place[2] ^ flip)))
    return lax.ppermute(block, "seg", moves)


def gather_line(halves, grid):
    pair = grid[2]
    arrived = {0: halves[0]}
    for step in range(line_length(grid)):
        for flip in range(pair):
            if step or flip:
                arrived[step * pair + flip] = line_send(halves[flip], grid, step, flip, True)
    return [arrived[j] for j in range(len(arrived))]


def scatter_line(sums, grid):
    pair = grid[2]
    parts = [[] for _ in range(pair)]
    for step in reversed(range(line_length(grid))):
        for flip in range(pair):
            block = sums[step * pair + flip]
            parts[flip].append(line_send(block, grid, step, flip, False) if step or flip else block)
    return parts


def token_sums(sums, groups):
    parts = [sums]
    for step in [j for j in range(1, groups) if j != 2] + [2] * (groups > 2):
        moves = [(j, target_of(j, step, groups)) for j in range(groups)]
        parts.append(lax.ppermute(sums, "head", moves))
    return parts


def per_device(segs, groups, queries, key_rows, values, cotangent, out_gain, parent, seg_len):
    rows, features = queries.shape[1:]
    heads = features // HD
    grid = grid_of(segs)
    pair = grid[2]
    scale = 1.0 / math.sqrt(HD * rows)
    cot = cotangent[0]
    gain = out_gain[None]
    shape = jax.ShapeDtypeStruct
    narrow = shape((rows, features), BF16)
    wide = shape((rows, features), F32)
    row = shape((1, rows), F32)
    members = line_length(grid) * pair
    weight_rows = shape((members * members, HD), F32)
    sems = pltpu.SemaphoreType.DMA((2, heads))
    mask = pltpu.VMEM((rows, rows), BF16)
    counts = [line_length(grid)] * pair
    unit = 2 * heads * rows * HD

    def halves(pieces):
        return [shape((features // (pair * pieces), HD), BF16)] * pair

    def mix(arrived, weights, first, tall, after=()):
        like = [shape((tall, HD), BF16)] * members
        return call(functools.partial(mix_kernel, members, first), like, (weights, *arrived), after=after)

    def flat(parts):
        return [block for part in parts for block in part]

    state_scratch = pltpu.VMEM((features // FORWARD_PIECES, HD), BF16)
    key, value, length, up, down, *own = call(
        functools.partial(state_kernel, grid),
        [narrow, narrow, shape((1, rows), jnp.int32), weight_rows, weight_rows] + halves(FORWARD_PIECES),
        (seg_len, key_rows[0], values[0], parent[None]),
        [state_scratch, sems, pltpu.SMEM((1, segs), jnp.int32), pltpu.SemaphoreType.DMA(())],
        unit * HD // FORWARD_PIECES, (1, 2, 3), (0,),
    )
    for piece in range(1, FORWARD_PIECES):
        own += call(
            functools.partial(next_state_kernel, piece, grid), halves(FORWARD_PIECES),
            (length, key, value), [state_scratch], unit * HD // FORWARD_PIECES,
        )
    (query,) = call(fetch_kernel, [narrow], (queries[0],), [pltpu.SemaphoreType.DMA((4,))], 0, (0,), after=(own[0],))
    mixed = []
    for part in split_refs(own, *[pair] * FORWARD_PIECES):
        mixed.append(mix(gather_line(part, grid), up, 0, part[0].shape[0], () if mixed else (query,)))
    (local,) = call(
        functools.partial(local_kernel, heads),
        [wide], (length, query, key, value), [mask], unit * rows * 2, after=(mixed[0][0],),
    )
    attention, prefix, sums = [], [], []
    width = features // FORWARD_PIECES
    for piece in range(FORWARD_PIECES):
        blocks = flat(scatter_line(mixed[piece], grid))
        operands = (length, query, local, cot, gain, *blocks, *sums, *attention)
        out, total, joined = call(
            functools.partial(carry_kernel, piece, grid, counts, scale),
            [wide, shape((2, rows), F32), shape((width, HD), BF16)], operands,
            (), unit * HD // FORWARD_PIECES, aliases={len(operands) - 1: 0} if attention else None,
        )
        attention, sums = [out], [total]
        prefix.append(joined)
    (attention,) = attention
    sums = token_sums(sums[0], groups)
    grads, inverse_rms, *state_grad = call(
        functools.partial(grad_kernel, len(sums), grid, scale),
        [narrow, row] + halves(1), (length, query, cot, gain, attention, *sums),
        [pltpu.VMEM((features, HD), BF16)], unit * HD,
    )
    group = 4 if heads % 4 == 0 else 1
    attended, query_grad, key_part, token = call(
        functools.partial(query_kernel, heads, group, scale),
        [narrow, narrow, wide, shape((8, HD), F32)],
        (length, inverse_rms, gain, query, key, value, grads, attention, *prefix),
        [pltpu.VMEM(narrow.shape, BF16)] * 2 + [mask, pltpu.SemaphoreType.DMA((heads // group, 2))],
        unit * (3 * rows + HD), out_specs=[HBM, HBM, VMEM, VMEM],
    )
    arrived = gather_line(state_grad, grid)
    half_heads = heads // pair
    last = max(half_heads * 3 // 8, min(half_heads - 1, 1))
    pieces = [(0, half_heads - last), (half_heads - last, last)] if last else [(0, half_heads)]
    mixed = []
    for begin, count in pieces:
        before = (token, *mixed[-1][:1]) if mixed else (token,)
        mixed.append(mix(arrived, down, begin * HD, count * HD, before))
    (value_part,) = call(
        functools.partial(value_kernel, heads, scale),
        [wide], (length, query, key, grads), [mask], unit * 2 * rows, after=(mixed[-1][0],),
    )
    results = []
    for (begin, count), sums in zip(pieces, mixed):
        below = flat(scatter_line(sums, grid))
        operands = (length, key, value, key_part, value_part, *below, *results)
        first = len(operands) - len(results)
        width = pair * count * HD
        results = call(
            functools.partial(final_kernel, begin, count, grid, counts),
            [narrow, narrow], operands,
            [pltpu.VMEM((rows, width), BF16)] * 2 + [pltpu.VMEM((width, HD), BF16), sems],
            2 * unit * HD * pair * count // heads,
            range(first, len(operands)), out_specs=[HBM, HBM],
            aliases={first + j: j for j in range(len(results))},
        )
    key_grad, value_grad = results
    return attended[None], query_grad[None], key_grad[None], value_grad[None]


def solution(mesh):
    split = P("seg", None, "head")
    return jax.shard_map(
        functools.partial(per_device, mesh.shape["seg"], mesh.shape["head"]),
        mesh=mesh,
        in_specs=(split, split, split, split, P("head"), P(), P("seg")),
        out_specs=(split, split, split, split),
        check_vma=False,
    )
```

```python
import functools
import math

import jax
import jax.numpy as jnp
from jax import lax
from jax.experimental import pallas as pl
from jax.experimental.pallas import tpu as pltpu
from jax.sharding import PartitionSpec as P

HEADS = 64
HD = 128
EPSILON = 1e-06
F32 = jnp.float32
BF16 = jnp.bfloat16
VMEM_LIMIT = 24 * 1024 * 1024
FORWARD_PIECES = 2

VMEM = pl.BlockSpec(memory_space=pltpu.VMEM)
SMEM = pl.BlockSpec(memory_space=pltpu.SMEM)
HBM = pl.BlockSpec(memory_space=pltpu.HBM)
ANY = pl.BlockSpec(memory_space=pl.ANY)


def dot(a, b, contract):
    return lax.dot_general(a, b, (contract, ((), ())), preferred_element_type=F32)


def nn(a, b):
    return dot(a, b, ((1,), (0,)))


def nt(a, b):
    return dot(a, b, ((1,), (1,)))


def tn(a, b):
    return dot(a, b, ((0,), (0,)))


def head_cols(head):
    return slice(head * HD, (head + 1) * HD)


def target_of(place, step, size):
    if size & (size - 1) == 0:
        return place ^ step
    return (place + step) % size


def source_of(place, step, size):
    if size & (size - 1) == 0:
        return place ^ step
    return (place + size - step) % size


def grid_of(segs):
    pair = 2 if segs % 2 == 0 else 1
    chips = segs // pair
    columns = next(c for c in range(1, chips + 1) if chips % c == 0 and c * c >= chips)
    return chips // columns, columns, pair


def member(grid, row, column, core):
    return (row * grid[1] + column) * grid[2] + core


def place_of(grid, device):
    chip = device // grid[2]
    return chip // grid[1], chip % grid[1], device % grid[2]


def along(grid, place, step, gather, ahead):
    row, column, core = place
    shift = target_of if ahead else source_of
    by_row = (core == 0) if gather else (core != 0)
    valid_column = step < grid[1]
    valid_row = step < grid[0]
    if isinstance(core, int):
        if by_row:
            return row, shift(column, step, grid[1]), valid_column
        return shift(row, step, grid[0]), column, valid_row
    moved_column = shift(column, min(step, grid[1] - 1), grid[1])
    moved_row = shift(row, min(step, grid[0] - 1), grid[0])
    return (
        jnp.where(by_row, row, moved_row),
        jnp.where(by_row, moved_column, column),
        jnp.where(by_row, valid_column, valid_row),
    )


def my_place(grid):
    me = lax.axis_index("seg")
    chip = lax.div(me, grid[2])
    return lax.div(chip, grid[1]), lax.rem(chip, grid[1]), lax.rem(me, grid[2])


def row_halves(full, core, pair):
    half = full.shape[0] // pair
    return [full.at[pl.ds(pl.multiple_of((core ^ j) * half, half), half), :] for j in range(pair)]


def join_halves(parts, full, core, pair):
    for half, terms in zip(row_halves(full, core, pair), parts):
        total = terms[0][...].astype(F32)
        for term in terms[1:]:
            total += term[...].astype(F32)
        half[...] = total.astype(BF16)


def line_length(grid):
    return max(grid[0], grid[1])


def write_weights(grid, parent, up, down):
    place = my_place(grid)
    pair = grid[2]
    count = line_length(grid) * pair

    def is_ancestor(child, other):
        first = parent[0, child]
        second = jnp.where(first >= 0, parent[0, jnp.maximum(first, 0)], -1)
        return jnp.logical_or(other == first, other == second)

    for out_step in range(count):
        row, column, _ = along(grid, place, out_step // pair, False, True)
        target = member(grid, row, column, place[2] ^ (out_step % pair))
        for in_step in range(count):
            row, column, valid = along(grid, place, in_step // pair, True, False)
            source = member(grid, row, column, place[2] ^ (in_step % pair))
            at = out_step * count + in_step
            for rows, used in ((up, is_ancestor(target, source)), (down, is_ancestor(source, target))):
                weight = jnp.where(jnp.logical_and(used, valid), 1.0, 0.0)
                rows[at : at + 1, :] = jnp.full((1, HD), weight, F32)


def own_states(piece, grid, keys, values, live, full, outs):
    heads = full.shape[0] // HD
    for head in range(heads):
        cols = head_cols(piece * heads + head)
        masked = jnp.where(live, keys[:, cols], jnp.zeros((), BF16))
        full[head * HD : (head + 1) * HD, :] = tn(masked, values[:, cols]).astype(BF16)
    for half, out in zip(row_halves(full, my_place(grid)[2], grid[2]), outs):
        out[...] = half[...]


def state_kernel(grid, seg_len, keys_hbm, values_hbm, parent_hbm, keys, values, length, up, down, *rest):
    outs, (full, sems, parent, parent_sem) = rest[:-4], rest[-4:]
    rows, width = keys.shape
    chunk = rows // 2 if rows % 32 == 0 else rows
    steps = rows // chunk
    spans = [slice(0, full.shape[0]), slice(full.shape[0], width)][:FORWARD_PIECES]
    copies = []
    for number, cols in enumerate(spans):
        for step in range(steps):
            part = slice(step * chunk, (step + 1) * chunk)
            for j, (src, dst) in enumerate(((keys_hbm, keys), (values_hbm, values))):
                copies.append(
                    pltpu.make_async_copy(src.at[part, cols], dst.at[part, cols], sems.at[j, number * steps + step])
                )
    few = pltpu.make_async_copy(parent_hbm, parent, parent_sem)
    few.start()
    for copy in copies:
        copy.start()
    length[...] = jnp.full(length.shape, seg_len[0], jnp.int32)
    few.wait()
    write_weights(grid, parent, up, down)
    live = lax.broadcasted_iota(jnp.int32, (rows, HD), 0) < seg_len[0]
    for copy in copies[: 2 * steps]:
        copy.wait()
    own_states(0, grid, keys, values, live, full, outs)
    for copy in copies[2 * steps :]:
        copy.wait()


def next_state_kernel(piece, grid, length, keys, values, *rest):
    outs, full = rest[:-1], rest[-1]
    own_states(piece, grid, keys, values, live_rows(length, keys.shape[0]), full, outs)


def mix_kernel(sources, first, weights, *refs):
    blocks, outs = refs[:sources], refs[-sources:]
    rows = outs[0].shape[0]
    chunk = min(rows, 64)
    for start in range(0, rows, chunk):
        part = slice(start, start + chunk)
        loaded = [block[first + start : first + start + chunk, :].astype(F32) for block in blocks]
        for out_step, out in enumerate(outs):
            at = out_step * sources
            total = weights[at : at + 1, :] * loaded[0]
            for in_step in range(1, sources):
                total += weights[at + in_step : at + in_step + 1, :] * loaded[in_step]
            out[part, :] = total.astype(BF16)


def live_rows(length, rows):
    return lax.broadcasted_iota(jnp.int32, (rows, HD), 0) < length[:, :HD]


def write_mask(length, keep, turned):
    rows = length.shape[1]
    first = lax.broadcasted_iota(jnp.int32, (rows, rows), 0)
    second = lax.broadcasted_iota(jnp.int32, (rows, rows), 1)
    if turned:
        used = (first <= second) & (first < length[...])
    else:
        used = (second <= first) & (second < length[...])
    keep[...] = jnp.where(used, 1.0, 0.0).astype(BF16)


def split_refs(refs, *counts):
    parts, at = [], 0
    for count in counts:
        parts.append(refs[at : at + count])
        at += count
    return parts


def fetch_kernel(source, _, out, sems):
    copies = row_copies(source, out, sems)
    for copy in copies:
        copy.start()
    for copy in copies:
        copy.wait()


def local_kernel(heads, length, queries, keys, values, *rest):
    local, keep = rest[-2:]
    write_mask(length, keep, False)
    for head in range(heads):
        cols = head_cols(head)
        scores = nt(queries[:, cols], keys[:, cols]).astype(BF16) * keep[...]
        local[:, cols] = nn(scores, values[:, cols])


def token_rows(total):
    return jnp.sum(jnp.transpose(total), axis=0, keepdims=True)


def token_columns(row):
    return jnp.transpose(jnp.broadcast_to(row, (HD, row.shape[1])))


def carry_kernel(piece, grid, counts, scale, length, queries, local, cotangent, gain, *rest):
    received, rest = rest[: sum(counts)], rest[sum(counts) :]
    before, (attention, sums, prefix) = rest[: (piece > 0)], rest[-3:]
    join_halves(split_refs(received, *counts), prefix, my_place(grid)[2], grid[2])
    rows, width = queries.shape[0], prefix.shape[0]
    factor = jnp.where(live_rows(length, rows), scale, 0.0)
    squares = jnp.zeros((rows, HD), F32)
    products = jnp.zeros((rows, HD), F32)
    for head in range(width // HD):
        whole = head_cols(piece * width // HD + head)
        carried = nn(queries[:, whole], prefix[head * HD : (head + 1) * HD, :])
        out = factor * (carried + local[:, whole])
        attention[:, whole] = out
        squares += out * out
        products += out * (cotangent[:, whole].astype(F32) * gain[:, whole])
    both = jnp.concatenate([token_rows(squares), token_rows(products)], axis=0)
    for other in before:
        both += other[...]
    sums[...] = both


def grad_kernel(groups, grid, scale, length, queries, cotangent, gain, attention, *rest):
    all_sums, (grad_out, inverse_rms, *halves) = rest[:groups], rest[groups:]
    rows = queries.shape[0]
    features = HEADS * HD
    total = all_sums[0][...]
    for other in all_sums[1:]:
        total = total + other[...]
    inverse = lax.rsqrt(total[0:1, :] / features + EPSILON)
    inverse_rms[...] = inverse
    live = lax.broadcasted_iota(jnp.int32, (1, rows), 1) < length[...]
    live_inverse = jnp.where(live, inverse, 0.0)
    shrink = live_inverse * inverse * (inverse * total[1:2, :]) / features
    live_inverse = token_columns(live_inverse)
    shrink = token_columns(shrink)
    core = my_place(grid)[2]
    for flip, half in enumerate(halves):
        height = half.shape[0]
        first = (core ^ flip) * height
        for head in range(height // HD):
            cols = pl.ds(pl.multiple_of(first + head * HD, HD), HD)
            gain_grad = cotangent[:, cols].astype(F32) * gain[:, cols]
            grad = (live_inverse * gain_grad - attention[:, cols] * shrink).astype(BF16)
            grad_out[:, cols] = grad
            half[head * HD : (head + 1) * HD, :] = (scale * tn(queries[:, cols], grad)).astype(BF16)


def row_copies(source, target, sems):
    rows = target.shape[0]
    chunk = rows // 4 if rows % 64 == 0 else rows
    parts = [pl.ds(step * chunk, chunk) for step in range(rows // chunk)]
    return [pltpu.make_async_copy(source.at[p, :], target.at[p, :], sems.at[j]) for j, p in enumerate(parts)]


def query_kernel(heads, group, scale, length, inverse_rms, gain, queries, keys, values, grads, attention, *rest):
    prefix, rest = split_refs(rest, FORWARD_PIECES, len(rest) - FORWARD_PIECES)
    attended_hbm, query_hbm, key_part, token, attended, query_grad, keep, sems = rest
    token[...] = jnp.zeros_like(token)
    write_mask(length, keep, False)
    inverse = token_columns(inverse_rms[...])
    copies = []
    for head in range(heads):
        cols = head_cols(head)
        grad = grads[:, cols]
        per_piece = heads // FORWARD_PIECES
        prefix_piece, state = prefix[head // per_piece], head % per_piece
        grad_scores = nt(grad, values[:, cols]).astype(BF16) * keep[...]
        carried = nt(grad, prefix_piece[state * HD : (state + 1) * HD, :])
        query_grad[:, cols] = (scale * (carried + nn(grad_scores, keys[:, cols]))).astype(BF16)
        key_part[:, cols] = scale * tn(grad_scores, queries[:, cols])
        attended[:, cols] = (attention[:, cols] * inverse * gain[:, cols]).astype(BF16)
        if (head + 1) % group == 0:
            step = head // group
            done = slice(step * group * HD, (head + 1) * HD)
            for j, (src, dst) in enumerate(((attended, attended_hbm), (query_grad, query_hbm))):
                copy = pltpu.make_async_copy(src.at[:, done], dst.at[:, done], sems.at[step, j])
                copy.start()
                copies.append(copy)
    for copy in copies:
        copy.wait()


def value_kernel(heads, scale, length, queries, keys, grads, *rest):
    value_part, keep = rest[-2:]
    write_mask(length, keep, True)
    for head in range(heads):
        cols = head_cols(head)
        turned = nt(keys[:, cols], queries[:, cols]).astype(BF16) * keep[...]
        value_part[:, cols] = scale * nn(turned, grads[:, cols])


def final_kernel(begin, count, grid, counts, length, keys, values, key_part, value_part, *rest):
    received, rest = rest[: sum(counts)], rest[sum(counts) :]
    key_hbm, value_hbm, key_grad, value_grad, below, sems = rest[-6:]
    pair = grid[2]
    join_halves(split_refs(received, *counts), below, my_place(grid)[2], pair)
    rows = keys.shape[0]
    live = jnp.where(live_rows(length, rows), 1.0, 0.0)
    copies, pending = [], 0
    for head in range(pair * count):
        half, within = divmod(head, count)
        cols = head_cols(head)
        place = half * (keys.shape[1] // HD // pair) + begin + within
        whole = head_cols(place)
        state = below[head * HD : (head + 1) * HD, :]
        key_grad[:, cols] = (key_part[:, whole] + live * nt(values[:, whole], state)).astype(BF16)
        value_grad[:, cols] = (value_part[:, whole] + live * nn(keys[:, whole], state)).astype(BF16)
        pending += 1
        if pending == 2 or within == count - 1:
            done = slice((head + 1 - pending) * HD, (head + 1) * HD)
            there = slice((place + 1 - pending) * HD, (place + 1) * HD)
            pending = 0
            for j, (src, dst) in enumerate(((key_grad, key_hbm), (value_grad, value_hbm))):
                copy = pltpu.make_async_copy(src.at[:, done], dst.at[:, there], sems.at[j, head])
                copy.start()
                copies.append(copy)
    for copy in copies:
        copy.wait()


def in_hbm(x):
    return pltpu.with_memory_space_constraint(x, pltpu.HBM)


def call(kernel, out_shape, operands, scratch=(), flops=0, stream=(), scalars=(), after=(), out_specs=None, aliases=None):
    moved = sum(math.prod(x.shape) * x.dtype.itemsize for x in operands)
    moved += sum(math.prod(x.shape) * x.dtype.itemsize for x in out_shape)
    specs = [SMEM if j in scalars else HBM if j in stream else VMEM for j in range(len(operands))]
    operands = [in_hbm(x) if j in stream else x for j, x in enumerate(operands)]
    return pl.pallas_call(
        kernel,
        out_shape=out_shape,
        in_specs=specs + [ANY] * len(after),
        out_specs=out_specs or [VMEM] * len(out_shape),
        scratch_shapes=list(scratch),
        input_output_aliases=aliases or {},
        compiler_params=pltpu.CompilerParams(vmem_limit_bytes=VMEM_LIMIT),
        cost_estimate=pl.CostEstimate(flops=flops, bytes_accessed=moved, transcendentals=0),
    )(*operands, *after)


def line_send(block, grid, step, flip, gather):
    moves = []
    for device in range(grid[0] * grid[1] * grid[2]):
        place = place_of(grid, device)
        if gather and flip:
            row, column, valid = along(grid, (place[0], place[1], place[2] ^ 1), step, True, True)
        else:
            row, column, valid = along(grid, place, step, gather, True)
        if valid:
            moves.append((device, member(grid, row, column, place[2] ^ flip)))
    return lax.ppermute(block, "seg", moves)


def gather_line(halves, grid):
    pair = grid[2]
    arrived = {0: halves[0]}
    for step in range(line_length(grid)):
        for flip in range(pair):
            if step or flip:
                arrived[step * pair + flip] = line_send(halves[flip], grid, step, flip, True)
    return [arrived[j] for j in range(len(arrived))]


def scatter_line(sums, grid):
    pair = grid[2]
    parts = [[] for _ in range(pair)]
    for step in reversed(range(line_length(grid))):
        for flip in range(pair):
            block = sums[step * pair + flip]
            parts[flip].append(line_send(block, grid, step, flip, False) if step or flip else block)
    return parts


def token_sums(sums, groups):
    parts = [sums]
    for step in [j for j in range(1, groups) if j != 2] + [2] * (groups > 2):
        moves = [(j, target_of(j, step, groups)) for j in range(groups)]
        parts.append(lax.ppermute(sums, "head", moves))
    return parts


def per_device(segs, groups, queries, key_rows, values, cotangent, out_gain, parent, seg_len):
    rows, features = queries.shape[1:]
    heads = features // HD
    grid = grid_of(segs)
    pair = grid[2]
    scale = 1.0 / math.sqrt(HD * rows)
    cot = cotangent[0]
    gain = out_gain[None]
    shape = jax.ShapeDtypeStruct
    narrow = shape((rows, features), BF16)
    wide = shape((rows, features), F32)
    row = shape((1, rows), F32)
    members = line_length(grid) * pair
    weight_rows = shape((members * members, HD), F32)
    sems = pltpu.SemaphoreType.DMA((2, heads))
    mask = pltpu.VMEM((rows, rows), BF16)
    counts = [line_length(grid)] * pair
    unit = 2 * heads * rows * HD

    def halves(pieces):
        return [shape((features // (pair * pieces), HD), BF16)] * pair

    def mix(arrived, weights, first, tall, after=()):
        like = [shape((tall, HD), BF16)] * members
        return call(functools.partial(mix_kernel, members, first), like, (weights, *arrived), after=after)

    def flat(parts):
        return [block for part in parts for block in part]

    state_scratch = pltpu.VMEM((features // FORWARD_PIECES, HD), BF16)
    key, value, length, up, down, *own = call(
        functools.partial(state_kernel, grid),
        [narrow, narrow, shape((1, rows), jnp.int32), weight_rows, weight_rows] + halves(FORWARD_PIECES),
        (seg_len, key_rows[0], values[0], parent[None]),
        [state_scratch, sems, pltpu.SMEM((1, segs), jnp.int32), pltpu.SemaphoreType.DMA(())],
        unit * HD // FORWARD_PIECES, (1, 2, 3), (0,),
    )
    for piece in range(1, FORWARD_PIECES):
        own += call(
            functools.partial(next_state_kernel, piece, grid), halves(FORWARD_PIECES),
            (length, key, value), [state_scratch], unit * HD // FORWARD_PIECES,
        )
    mixed = []
    for part in split_refs(own, *[pair] * FORWARD_PIECES):
        mixed.append(mix(gather_line(part, grid), up, 0, part[0].shape[0], () if len(mixed) != 1 else (query,)))
        if len(mixed) == 1:
            (query,) = call(
                fetch_kernel, [narrow], (queries[0],), [pltpu.SemaphoreType.DMA((4,))], 0, (0,), after=(mixed[0][0],)
            )
    (local,) = call(
        functools.partial(local_kernel, heads),
        [wide], (length, query, key, value), [mask], unit * rows * 2, after=(mixed[0][0],),
    )
    attention, prefix, sums = [], [], []
    width = features // FORWARD_PIECES
    for piece in range(FORWARD_PIECES):
        blocks = flat(scatter_line(mixed[piece], grid))
        operands = (length, query, local, cot, gain, *blocks, *sums, *attention)
        out, total, joined = call(
            functools.partial(carry_kernel, piece, grid, counts, scale),
            [wide, shape((2, rows), F32), shape((width, HD), BF16)], operands,
            (), unit * HD // FORWARD_PIECES, aliases={len(operands) - 1: 0} if attention else None,
        )
        attention, sums = [out], [total]
        prefix.append(joined)
    (attention,) = attention
    sums = token_sums(sums[0], groups)
    grads, inverse_rms, *state_grad = call(
        functools.partial(grad_kernel, len(sums), grid, scale),
        [narrow, row] + halves(1), (length, query, cot, gain, attention, *sums),
        (), unit * HD,
    )
    group = 4 if heads % 4 == 0 else 1
    attended, query_grad, key_part, token = call(
        functools.partial(query_kernel, heads, group, scale),
        [narrow, narrow, wide, shape((8, HD), F32)],
        (length, inverse_rms, gain, query, key, value, grads, attention, *prefix),
        [pltpu.VMEM(narrow.shape, BF16)] * 2 + [mask, pltpu.SemaphoreType.DMA((heads // group, 2))],
        unit * (3 * rows + HD), out_specs=[HBM, HBM, VMEM, VMEM],
    )
    arrived = gather_line(state_grad, grid)
    half_heads = heads // pair
    last = max(half_heads * 3 // 8, min(half_heads - 1, 1))
    pieces = [(0, half_heads - last), (half_heads - last, last)] if last else [(0, half_heads)]
    mixed = []
    for begin, count in pieces:
        before = (token, *mixed[-1][:1]) if mixed else (token,)
        mixed.append(mix(arrived, down, begin * HD, count * HD, before))
    (value_part,) = call(
        functools.partial(value_kernel, heads, scale),
        [wide], (length, query, key, grads), [mask], unit * 2 * rows, after=(mixed[-1][0],),
    )
    results = []
    for (begin, count), sums in zip(pieces, mixed):
        below = flat(scatter_line(sums, grid))
        operands = (length, key, value, key_part, value_part, *below, *results)
        first = len(operands) - len(results)
        width = pair * count * HD
        results = call(
            functools.partial(final_kernel, begin, count, grid, counts),
            [narrow, narrow], operands,
            [pltpu.VMEM((rows, width), BF16)] * 2 + [pltpu.VMEM((width, HD), BF16), sems],
            2 * unit * HD * pair * count // heads,
            range(first, len(operands)), out_specs=[HBM, HBM],
            aliases={first + j: j for j in range(len(results))},
        )
    key_grad, value_grad = results
    return attended[None], query_grad[None], key_grad[None], value_grad[None]


def solution(mesh):
    split = P("seg", None, "head")
    return jax.shard_map(
        functools.partial(per_device, mesh.shape["seg"], mesh.shape["head"]),
        mesh=mesh,
        in_specs=(split, split, split, split, P("head"), P(), P("seg")),
        out_specs=(split, split, split, split),
        check_vma=False,
    )
```

```python
import functools
import math

import jax
import jax.numpy as jnp
from jax import lax
from jax.experimental import pallas as pl
from jax.experimental.pallas import tpu as pltpu
from jax.sharding import PartitionSpec as P

HEADS = 64
HD = 128
EPSILON = 1e-06
F32 = jnp.float32
BF16 = jnp.bfloat16
VMEM_LIMIT = 24 * 1024 * 1024
FORWARD_PIECES = 2

VMEM = pl.BlockSpec(memory_space=pltpu.VMEM)
SMEM = pl.BlockSpec(memory_space=pltpu.SMEM)
HBM = pl.BlockSpec(memory_space=pltpu.HBM)
ANY = pl.BlockSpec(memory_space=pl.ANY)


def dot(a, b, contract):
    return lax.dot_general(a, b, (contract, ((), ())), preferred_element_type=F32)


def nn(a, b):
    return dot(a, b, ((1,), (0,)))


def nt(a, b):
    return dot(a, b, ((1,), (1,)))


def tn(a, b):
    return dot(a, b, ((0,), (0,)))


def head_cols(head):
    return slice(head * HD, (head + 1) * HD)


def target_of(place, step, size):
    if size & (size - 1) == 0:
        return place ^ step
    return (place + step) % size


def source_of(place, step, size):
    if size & (size - 1) == 0:
        return place ^ step
    return (place + size - step) % size


def grid_of(segs):
    pair = 2 if segs % 2 == 0 else 1
    chips = segs // pair
    columns = next(c for c in range(1, chips + 1) if chips % c == 0 and c * c >= chips)
    return chips // columns, columns, pair


def member(grid, row, column, core):
    return (row * grid[1] + column) * grid[2] + core


def place_of(grid, device):
    chip = device // grid[2]
    return chip // grid[1], chip % grid[1], device % grid[2]


def along(grid, place, step, gather, ahead):
    row, column, core = place
    shift = target_of if ahead else source_of
    by_row = (core == 0) if gather else (core != 0)
    valid_column = step < grid[1]
    valid_row = step < grid[0]
    if isinstance(core, int):
        if by_row:
            return row, shift(column, step, grid[1]), valid_column
        return shift(row, step, grid[0]), column, valid_row
    moved_column = shift(column, min(step, grid[1] - 1), grid[1])
    moved_row = shift(row, min(step, grid[0] - 1), grid[0])
    return (
        jnp.where(by_row, row, moved_row),
        jnp.where(by_row, moved_column, column),
        jnp.where(by_row, valid_column, valid_row),
    )


def my_place(grid):
    me = lax.axis_index("seg")
    chip = lax.div(me, grid[2])
    return lax.div(chip, grid[1]), lax.rem(chip, grid[1]), lax.rem(me, grid[2])


def for_each_core(grid, body):
    core = my_place(grid)[2]
    for number in range(grid[2]):
        pl.when(core == number)(functools.partial(body, number))


def arrived_state(parts, core, head, count):
    half, within = divmod(head, count)
    terms = [term[within * HD : (within + 1) * HD, :].astype(F32) for term in parts[half ^ core]]
    return sum(terms[1:], terms[0]).astype(BF16)


def line_length(grid):
    return max(grid[0], grid[1])


def write_weights(grid, parent, up, down):
    place = my_place(grid)
    pair = grid[2]
    count = line_length(grid) * pair

    def is_ancestor(child, other):
        first = parent[0, child]
        second = jnp.where(first >= 0, parent[0, jnp.maximum(first, 0)], -1)
        return jnp.logical_or(other == first, other == second)

    for out_step in range(count):
        row, column, _ = along(grid, place, out_step // pair, False, True)
        target = member(grid, row, column, place[2] ^ (out_step % pair))
        for in_step in range(count):
            row, column, valid = along(grid, place, in_step // pair, True, False)
            source = member(grid, row, column, place[2] ^ (in_step % pair))
            at = out_step * count + in_step
            for rows, used in ((up, is_ancestor(target, source)), (down, is_ancestor(source, target))):
                weight = jnp.where(jnp.logical_and(used, valid), 1.0, 0.0)
                rows[at : at + 1, :] = jnp.full((1, HD), weight, F32)


def own_states(piece, grid, keys, values, live, outs):
    def body(core):
        count = outs[0].shape[0] // HD
        for head in range(count * len(outs)):
            half, within = divmod(head, count)
            cols = head_cols(piece * count * len(outs) + head)
            masked = jnp.where(live, keys[:, cols], jnp.zeros((), BF16))
            outs[half ^ core][within * HD : (within + 1) * HD, :] = tn(masked, values[:, cols]).astype(BF16)

    for_each_core(grid, body)


def state_kernel(grid, seg_len, keys_hbm, values_hbm, parent_hbm, keys, values, length, up, down, *rest):
    outs, (sems, parent, parent_sem) = rest[:-3], rest[-3:]
    rows, width = keys.shape
    chunk = rows // 2 if rows % 32 == 0 else rows
    steps = rows // chunk
    first = width // FORWARD_PIECES
    spans = [slice(0, first), slice(first, width)][:FORWARD_PIECES]
    copies = []
    for number, cols in enumerate(spans):
        for step in range(steps):
            part = slice(step * chunk, (step + 1) * chunk)
            for j, (src, dst) in enumerate(((keys_hbm, keys), (values_hbm, values))):
                copies.append(
                    pltpu.make_async_copy(src.at[part, cols], dst.at[part, cols], sems.at[j, number * steps + step])
                )
    few = pltpu.make_async_copy(parent_hbm, parent, parent_sem)
    few.start()
    for copy in copies:
        copy.start()
    length[...] = jnp.full(length.shape, seg_len[0], jnp.int32)
    few.wait()
    write_weights(grid, parent, up, down)
    live = lax.broadcasted_iota(jnp.int32, (rows, HD), 0) < seg_len[0]
    for copy in copies[: 2 * steps]:
        copy.wait()
    own_states(0, grid, keys, values, live, outs)
    for copy in copies[2 * steps :]:
        copy.wait()


def next_state_kernel(piece, grid, length, keys, values, *outs):
    own_states(piece, grid, keys, values, live_rows(length, keys.shape[0]), outs)


def mix_kernel(sources, first, weights, *refs):
    blocks, outs = refs[:sources], refs[-sources:]
    rows = outs[0].shape[0]
    chunk = min(rows, 64)
    for start in range(0, rows, chunk):
        part = slice(start, start + chunk)
        loaded = [block[first + start : first + start + chunk, :].astype(F32) for block in blocks]
        for out_step, out in enumerate(outs):
            at = out_step * sources
            total = weights[at : at + 1, :] * loaded[0]
            for in_step in range(1, sources):
                total += weights[at + in_step : at + in_step + 1, :] * loaded[in_step]
            out[part, :] = total.astype(BF16)


def live_rows(length, rows):
    return lax.broadcasted_iota(jnp.int32, (rows, HD), 0) < length[:, :HD]


def write_mask(length, keep, turned):
    rows = length.shape[1]
    first = lax.broadcasted_iota(jnp.int32, (rows, rows), 0)
    second = lax.broadcasted_iota(jnp.int32, (rows, rows), 1)
    if turned:
        used = (first <= second) & (first < length[...])
    else:
        used = (second <= first) & (second < length[...])
    keep[...] = jnp.where(used, 1.0, 0.0).astype(BF16)


def split_refs(refs, *counts):
    parts, at = [], 0
    for count in counts:
        parts.append(refs[at : at + count])
        at += count
    return parts


def fetch_kernel(source, _, out, sems):
    copies = row_copies(source, out, sems)
    for copy in copies:
        copy.start()
    for copy in copies:
        copy.wait()


def local_kernel(heads, length, queries, keys, values, *rest):
    local, keep = rest[-2:]
    write_mask(length, keep, False)
    for head in range(heads):
        cols = head_cols(head)
        scores = nt(queries[:, cols], keys[:, cols]).astype(BF16) * keep[...]
        local[:, cols] = nn(scores, values[:, cols])


def token_rows(total):
    return jnp.sum(jnp.transpose(total), axis=0, keepdims=True)


def token_columns(row):
    return jnp.transpose(jnp.broadcast_to(row, (HD, row.shape[1])))


def carry_kernel(piece, grid, counts, scale, length, queries, local, cotangent, gain, *rest):
    received, rest = rest[: sum(counts)], rest[sum(counts) :]
    before, (attention, sums, prefix) = rest[: (piece > 0)], rest[-3:]
    parts = split_refs(received, *counts)
    rows, heads = queries.shape[0], prefix.shape[0] // HD
    factor = jnp.where(live_rows(length, rows), scale, 0.0)

    def body(core):
        squares = jnp.zeros((rows, HD), F32)
        products = jnp.zeros((rows, HD), F32)
        for head in range(heads):
            whole = head_cols(piece * heads + head)
            state = arrived_state(parts, core, head, heads // grid[2])
            prefix[head * HD : (head + 1) * HD, :] = state
            out = factor * (nn(queries[:, whole], state) + local[:, whole])
            attention[:, whole] = out
            squares += out * out
            products += out * (cotangent[:, whole].astype(F32) * gain[:, whole])
        both = jnp.concatenate([token_rows(squares), token_rows(products)], axis=0)
        for other in before:
            both += other[...]
        sums[...] = both

    for_each_core(grid, body)


def grad_kernel(groups, grid, scale, length, queries, cotangent, gain, attention, *rest):
    all_sums, (grad_out, inverse_rms, *halves) = rest[:groups], rest[groups:]
    rows = queries.shape[0]
    features = HEADS * HD
    total = all_sums[0][...]
    for other in all_sums[1:]:
        total = total + other[...]
    inverse = lax.rsqrt(total[0:1, :] / features + EPSILON)
    inverse_rms[...] = inverse
    live = lax.broadcasted_iota(jnp.int32, (1, rows), 1) < length[...]
    live_inverse = jnp.where(live, inverse, 0.0)
    shrink = live_inverse * inverse * (inverse * total[1:2, :]) / features
    live_inverse = token_columns(live_inverse)
    shrink = token_columns(shrink)

    def body(core):
        count = halves[0].shape[0] // HD
        for head in range(queries.shape[1] // HD):
            cols = head_cols(head)
            half, within = divmod(head, count)
            gain_grad = cotangent[:, cols].astype(F32) * gain[:, cols]
            grad = (live_inverse * gain_grad - attention[:, cols] * shrink).astype(BF16)
            grad_out[:, cols] = grad
            state = (scale * tn(queries[:, cols], grad)).astype(BF16)
            halves[half ^ core][within * HD : (within + 1) * HD, :] = state

    for_each_core(grid, body)


def row_copies(source, target, sems):
    rows = target.shape[0]
    chunk = rows // 4 if rows % 64 == 0 else rows
    parts = [pl.ds(step * chunk, chunk) for step in range(rows // chunk)]
    return [pltpu.make_async_copy(source.at[p, :], target.at[p, :], sems.at[j]) for j, p in enumerate(parts)]


def query_kernel(heads, group, scale, length, inverse_rms, gain, queries, keys, values, grads, attention, *rest):
    prefix, rest = split_refs(rest, FORWARD_PIECES, len(rest) - FORWARD_PIECES)
    attended_hbm, query_hbm, key_part, token, attended, query_grad, keep, sems = rest
    token[...] = jnp.zeros_like(token)
    write_mask(length, keep, False)
    inverse = token_columns(inverse_rms[...])
    copies = []
    for head in range(heads):
        cols = head_cols(head)
        grad = grads[:, cols]
        per_piece = heads // FORWARD_PIECES
        prefix_piece, state = prefix[head // per_piece], head % per_piece
        grad_scores = nt(grad, values[:, cols]).astype(BF16) * keep[...]
        carried = nt(grad, prefix_piece[state * HD : (state + 1) * HD, :])
        query_grad[:, cols] = (scale * (carried + nn(grad_scores, keys[:, cols]))).astype(BF16)
        key_part[:, cols] = scale * tn(grad_scores, queries[:, cols])
        attended[:, cols] = (attention[:, cols] * inverse * gain[:, cols]).astype(BF16)
        if (head + 1) % group == 0:
            step = head // group
            done = slice(step * group * HD, (head + 1) * HD)
            for j, (src, dst) in enumerate(((attended, attended_hbm), (query_grad, query_hbm))):
                copy = pltpu.make_async_copy(src.at[:, done], dst.at[:, done], sems.at[step, j])
                copy.start()
                copies.append(copy)
    for copy in copies:
        copy.wait()


def value_kernel(heads, scale, length, queries, keys, grads, *rest):
    value_part, keep = rest[-2:]
    write_mask(length, keep, True)
    for head in range(heads):
        cols = head_cols(head)
        turned = nt(keys[:, cols], queries[:, cols]).astype(BF16) * keep[...]
        value_part[:, cols] = scale * nn(turned, grads[:, cols])


def final_kernel(begin, count, grid, counts, length, keys, values, key_part, value_part, *rest):
    received, rest = rest[: sum(counts)], rest[sum(counts) :]
    key_hbm, value_hbm, key_grad, value_grad, sems = rest[-5:]
    parts = split_refs(received, *counts)
    pair = grid[2]
    rows = keys.shape[0]
    live = jnp.where(live_rows(length, rows), 1.0, 0.0)

    def body(core):
        copies, pending = [], 0
        for head in range(pair * count):
            half, within = divmod(head, count)
            cols = head_cols(head)
            place = half * (keys.shape[1] // HD // pair) + begin + within
            whole = head_cols(place)
            state = arrived_state(parts, core, head, count)
            key_grad[:, cols] = (key_part[:, whole] + live * nt(values[:, whole], state)).astype(BF16)
            value_grad[:, cols] = (value_part[:, whole] + live * nn(keys[:, whole], state)).astype(BF16)
            pending += 1
            if pending == 2 or within == count - 1:
                done = slice((head + 1 - pending) * HD, (head + 1) * HD)
                there = slice((place + 1 - pending) * HD, (place + 1) * HD)
                pending = 0
                for j, (src, dst) in enumerate(((key_grad, key_hbm), (value_grad, value_hbm))):
                    copy = pltpu.make_async_copy(src.at[:, done], dst.at[:, there], sems.at[j, head])
                    copy.start()
                    copies.append(copy)
        for copy in copies:
            copy.wait()

    for_each_core(grid, body)


def in_hbm(x):
    return pltpu.with_memory_space_constraint(x, pltpu.HBM)


def call(kernel, out_shape, operands, scratch=(), flops=0, stream=(), scalars=(), after=(), out_specs=None, aliases=None):
    moved = sum(math.prod(x.shape) * x.dtype.itemsize for x in operands)
    moved += sum(math.prod(x.shape) * x.dtype.itemsize for x in out_shape)
    specs = [SMEM if j in scalars else HBM if j in stream else VMEM for j in range(len(operands))]
    operands = [in_hbm(x) if j in stream else x for j, x in enumerate(operands)]
    return pl.pallas_call(
        kernel,
        out_shape=out_shape,
        in_specs=specs + [ANY] * len(after),
        out_specs=out_specs or [VMEM] * len(out_shape),
        scratch_shapes=list(scratch),
        input_output_aliases=aliases or {},
        compiler_params=pltpu.CompilerParams(vmem_limit_bytes=VMEM_LIMIT),
        cost_estimate=pl.CostEstimate(flops=flops, bytes_accessed=moved, transcendentals=0),
    )(*operands, *after)


def line_send(block, grid, step, flip, gather):
    moves = []
    for device in range(grid[0] * grid[1] * grid[2]):
        place = place_of(grid, device)
        if gather and flip:
            row, column, valid = along(grid, (place[0], place[1], place[2] ^ 1), step, True, True)
        else:
            row, column, valid = along(grid, place, step, gather, True)
        if valid:
            moves.append((device, member(grid, row, column, place[2] ^ flip)))
    return lax.ppermute(block, "seg", moves)


def gather_line(halves, grid):
    pair = grid[2]
    arrived = {0: halves[0]}
    for step in range(line_length(grid)):
        for flip in range(pair):
            if step or flip:
                arrived[step * pair + flip] = line_send(halves[flip], grid, step, flip, True)
    return [arrived[j] for j in range(len(arrived))]


def scatter_line(sums, grid):
    pair = grid[2]
    parts = [[] for _ in range(pair)]
    for step in reversed(range(line_length(grid))):
        for flip in range(pair):
            block = sums[step * pair + flip]
            parts[flip].append(line_send(block, grid, step, flip, False) if step or flip else block)
    return parts


def token_sums(sums, groups):
    parts = [sums]
    for step in [j for j in range(1, groups) if j != 2] + [2] * (groups > 2):
        moves = [(j, target_of(j, step, groups)) for j in range(groups)]
        parts.append(lax.ppermute(sums, "head", moves))
    return parts


def per_device(segs, groups, queries, key_rows, values, cotangent, out_gain, parent, seg_len):
    rows, features = queries.shape[1:]
    heads = features // HD
    grid = grid_of(segs)
    pair = grid[2]
    scale = 1.0 / math.sqrt(HD * rows)
    cot = cotangent[0]
    gain = out_gain[None]
    shape = jax.ShapeDtypeStruct
    narrow = shape((rows, features), BF16)
    wide = shape((rows, features), F32)
    row = shape((1, rows), F32)
    members = line_length(grid) * pair
    weight_rows = shape((members * members, HD), F32)
    sems = pltpu.SemaphoreType.DMA((2, heads))
    mask = pltpu.VMEM((rows, rows), BF16)
    counts = [line_length(grid)] * pair
    unit = 2 * heads * rows * HD

    def halves(pieces):
        return [shape((features // (pair * pieces), HD), BF16)] * pair

    def mix(arrived, weights, first, tall, after=()):
        like = [shape((tall, HD), BF16)] * members
        return call(functools.partial(mix_kernel, members, first), like, (weights, *arrived), after=after)

    def flat(parts):
        return [block for part in parts for block in part]

    key, value, length, up, down, *own = call(
        functools.partial(state_kernel, grid),
        [narrow, narrow, shape((1, rows), jnp.int32), weight_rows, weight_rows] + halves(FORWARD_PIECES),
        (seg_len, key_rows[0], values[0], parent[None]),
        [sems, pltpu.SMEM((1, segs), jnp.int32), pltpu.SemaphoreType.DMA(())],
        unit * HD // FORWARD_PIECES, (1, 2, 3), (0,),
    )
    for piece in range(1, FORWARD_PIECES):
        own += call(
            functools.partial(next_state_kernel, piece, grid), halves(FORWARD_PIECES),
            (length, key, value), (), unit * HD // FORWARD_PIECES,
        )
    (query,) = call(fetch_kernel, [narrow], (queries[0],), [pltpu.SemaphoreType.DMA((4,))], 0, (0,), after=(own[0],))
    mixed = []
    for part in split_refs(own, *[pair] * FORWARD_PIECES):
        mixed.append(mix(gather_line(part, grid), up, 0, part[0].shape[0], () if mixed else (query,)))
    (local,) = call(
        functools.partial(local_kernel, heads),
        [wide], (length, query, key, value), [mask], unit * rows * 2, after=(mixed[0][0],),
    )
    attention, prefix, sums = [], [], []
    width = features // FORWARD_PIECES
    for piece in range(FORWARD_PIECES):
        blocks = flat(scatter_line(mixed[piece], grid))
        operands = (length, query, local, cot, gain, *blocks, *sums, *attention)
        out, total, joined = call(
            functools.partial(carry_kernel, piece, grid, counts, scale),
            [wide, shape((2, rows), F32), shape((width, HD), BF16)], operands,
            (), unit * HD // FORWARD_PIECES, aliases={len(operands) - 1: 0} if attention else None,
        )
        attention, sums = [out], [total]
        prefix.append(joined)
    (attention,) = attention
    sums = token_sums(sums[0], groups)
    grads, inverse_rms, *state_grad = call(
        functools.partial(grad_kernel, len(sums), grid, scale),
        [narrow, row] + halves(1), (length, query, cot, gain, attention, *sums),
        (), unit * HD,
    )
    group = 4 if heads % 4 == 0 else 1
    attended, query_grad, key_part, token = call(
        functools.partial(query_kernel, heads, group, scale),
        [narrow, narrow, wide, shape((8, HD), F32)],
        (length, inverse_rms, gain, query, key, value, grads, attention, *prefix),
        [pltpu.VMEM(narrow.shape, BF16)] * 2 + [mask, pltpu.SemaphoreType.DMA((heads // group, 2))],
        unit * (3 * rows + HD), out_specs=[HBM, HBM, VMEM, VMEM],
    )
    arrived = gather_line(state_grad, grid)
    half_heads = heads // pair
    last = max(half_heads * 3 // 8, min(half_heads - 1, 1))
    pieces = [(0, half_heads - last), (half_heads - last, last)] if last else [(0, half_heads)]
    mixed = []
    for begin, count in pieces:
        before = (token, *mixed[-1][:1]) if mixed else (token,)
        mixed.append(mix(arrived, down, begin * HD, count * HD, before))
    (value_part,) = call(
        functools.partial(value_kernel, heads, scale),
        [wide], (length, query, key, grads), [mask], unit * 2 * rows, after=(mixed[-1][0],),
    )
    results = []
    for (begin, count), sums in zip(pieces, mixed):
        below = flat(scatter_line(sums, grid))
        operands = (length, key, value, key_part, value_part, *below, *results)
        first = len(operands) - len(results)
        width = pair * count * HD
        results = call(
            functools.partial(final_kernel, begin, count, grid, counts),
            [narrow, narrow], operands,
            [pltpu.VMEM((rows, width), BF16)] * 2 + [sems],
            2 * unit * HD * pair * count // heads,
            range(first, len(operands)), out_specs=[HBM, HBM],
            aliases={first + j: j for j in range(len(results))},
        )
    key_grad, value_grad = results
    return attended[None], query_grad[None], key_grad[None], value_grad[None]


def solution(mesh):
    split = P("seg", None, "head")
    return jax.shard_map(
        functools.partial(per_device, mesh.shape["seg"], mesh.shape["head"]),
        mesh=mesh,
        in_specs=(split, split, split, split, P("head"), P(), P("seg")),
        out_specs=(split, split, split, split),
        check_vma=False,
    )
```

```python
import functools
import math

import jax
import jax.numpy as jnp
from jax import lax
from jax.experimental import pallas as pl
from jax.experimental.pallas import tpu as pltpu
from jax.sharding import PartitionSpec as P

HEADS = 64
HD = 128
EPSILON = 1e-06
F32 = jnp.float32
BF16 = jnp.bfloat16
VMEM_LIMIT = 24 * 1024 * 1024
FORWARD_PIECES = 2
VALUE_PIECES = 2

VMEM = pl.BlockSpec(memory_space=pltpu.VMEM)
SMEM = pl.BlockSpec(memory_space=pltpu.SMEM)
HBM = pl.BlockSpec(memory_space=pltpu.HBM)
ANY = pl.BlockSpec(memory_space=pl.ANY)


def dot(a, b, contract):
    return lax.dot_general(a, b, (contract, ((), ())), preferred_element_type=F32)


def nn(a, b):
    return dot(a, b, ((1,), (0,)))


def nt(a, b):
    return dot(a, b, ((1,), (1,)))


def tn(a, b):
    return dot(a, b, ((0,), (0,)))


def head_cols(head):
    return slice(head * HD, (head + 1) * HD)


def target_of(place, step, size):
    if size & (size - 1) == 0:
        return place ^ step
    return (place + step) % size


def source_of(place, step, size):
    if size & (size - 1) == 0:
        return place ^ step
    return (place + size - step) % size


def grid_of(segs):
    pair = 2 if segs % 2 == 0 else 1
    chips = segs // pair
    columns = next(c for c in range(1, chips + 1) if chips % c == 0 and c * c >= chips)
    return chips // columns, columns, pair


def member(grid, row, column, core):
    return (row * grid[1] + column) * grid[2] + core


def place_of(grid, device):
    chip = device // grid[2]
    return chip // grid[1], chip % grid[1], device % grid[2]


def along(grid, place, step, gather, ahead):
    row, column, core = place
    shift = target_of if ahead else source_of
    by_row = (core == 0) if gather else (core != 0)
    valid_column = step < grid[1]
    valid_row = step < grid[0]
    if isinstance(core, int):
        if by_row:
            return row, shift(column, step, grid[1]), valid_column
        return shift(row, step, grid[0]), column, valid_row
    moved_column = shift(column, min(step, grid[1] - 1), grid[1])
    moved_row = shift(row, min(step, grid[0] - 1), grid[0])
    return (
        jnp.where(by_row, row, moved_row),
        jnp.where(by_row, moved_column, column),
        jnp.where(by_row, valid_column, valid_row),
    )


def my_place(grid):
    me = lax.axis_index("seg")
    chip = lax.div(me, grid[2])
    return lax.div(chip, grid[1]), lax.rem(chip, grid[1]), lax.rem(me, grid[2])


def for_each_core(grid, body):
    core = my_place(grid)[2]
    for number in range(grid[2]):
        pl.when(core == number)(functools.partial(body, number))


def arrived_state(parts, core, head, count):
    half, within = divmod(head, count)
    terms = [term[within * HD : (within + 1) * HD, :].astype(F32) for term in parts[half ^ core]]
    return sum(terms[1:], terms[0]).astype(BF16)


def line_length(grid):
    return max(grid[0], grid[1])


def write_weights(grid, parent, up, down):
    place = my_place(grid)
    pair = grid[2]
    count = line_length(grid) * pair

    def is_ancestor(child, other):
        first = parent[0, child]
        second = jnp.where(first >= 0, parent[0, jnp.maximum(first, 0)], -1)
        return jnp.logical_or(other == first, other == second)

    for out_step in range(count):
        row, column, _ = along(grid, place, out_step // pair, False, True)
        target = member(grid, row, column, place[2] ^ (out_step % pair))
        for in_step in range(count):
            row, column, valid = along(grid, place, in_step // pair, True, False)
            source = member(grid, row, column, place[2] ^ (in_step % pair))
            at = out_step * count + in_step
            for rows, used in ((up, is_ancestor(target, source)), (down, is_ancestor(source, target))):
                weight = jnp.where(jnp.logical_and(used, valid), 1.0, 0.0)
                rows[at : at + 1, :] = jnp.full((1, HD), weight, F32)


def own_states(piece, grid, keys, values, live, outs):
    def body(core):
        count = outs[0].shape[0] // HD
        for head in range(count * len(outs)):
            half, within = divmod(head, count)
            cols = head_cols(piece * count * len(outs) + head)
            masked = jnp.where(live, keys[:, cols], jnp.zeros((), BF16))
            outs[half ^ core][within * HD : (within + 1) * HD, :] = tn(masked, values[:, cols]).astype(BF16)

    for_each_core(grid, body)


def state_kernel(grid, seg_len, keys_hbm, values_hbm, parent_hbm, keys, values, length, up, down, *rest):
    outs, (sems, parent, parent_sem) = rest[:-3], rest[-3:]
    rows, width = keys.shape
    chunk = rows // 2 if rows % 32 == 0 else rows
    steps = rows // chunk
    first = width // FORWARD_PIECES
    spans = [slice(0, first), slice(first, width)][:FORWARD_PIECES]
    copies = []
    for number, cols in enumerate(spans):
        for step in range(steps):
            part = slice(step * chunk, (step + 1) * chunk)
            for j, (src, dst) in enumerate(((keys_hbm, keys), (values_hbm, values))):
                copies.append(
                    pltpu.make_async_copy(src.at[part, cols], dst.at[part, cols], sems.at[j, number * steps + step])
                )
    few = pltpu.make_async_copy(parent_hbm, parent, parent_sem)
    few.start()
    for copy in copies:
        copy.start()
    length[...] = jnp.full(length.shape, seg_len[0], jnp.int32)
    few.wait()
    write_weights(grid, parent, up, down)
    live = lax.broadcasted_iota(jnp.int32, (rows, HD), 0) < seg_len[0]
    for copy in copies[: 2 * steps]:
        copy.wait()
    own_states(0, grid, keys, values, live, outs)
    for copy in copies[2 * steps :]:
        copy.wait()


def next_state_kernel(piece, grid, length, keys, values, *outs):
    own_states(piece, grid, keys, values, live_rows(length, keys.shape[0]), outs)


def mix_kernel(sources, first, weights, *refs):
    blocks, outs = refs[:sources], refs[-sources:]
    rows = outs[0].shape[0]
    chunk = min(rows, 64)
    for start in range(0, rows, chunk):
        part = slice(start, start + chunk)
        loaded = [block[first + start : first + start + chunk, :].astype(F32) for block in blocks]
        for out_step, out in enumerate(outs):
            at = out_step * sources
            total = weights[at : at + 1, :] * loaded[0]
            for in_step in range(1, sources):
                total += weights[at + in_step : at + in_step + 1, :] * loaded[in_step]
            out[part, :] = total.astype(BF16)


def live_rows(length, rows):
    return lax.broadcasted_iota(jnp.int32, (rows, HD), 0) < length[:, :HD]


def write_mask(length, keep, turned):
    rows = length.shape[1]
    first = lax.broadcasted_iota(jnp.int32, (rows, rows), 0)
    second = lax.broadcasted_iota(jnp.int32, (rows, rows), 1)
    if turned:
        used = (first <= second) & (first < length[...])
    else:
        used = (second <= first) & (second < length[...])
    keep[...] = jnp.where(used, 1.0, 0.0).astype(BF16)


def split_refs(refs, *counts):
    parts, at = [], 0
    for count in counts:
        parts.append(refs[at : at + count])
        at += count
    return parts


def fetch_kernel(source, _, out, sems):
    copies = row_copies(source, out, sems)
    for copy in copies:
        copy.start()
    for copy in copies:
        copy.wait()


def local_kernel(heads, length, queries, keys, values, *rest):
    local, keep = rest[-2:]
    write_mask(length, keep, False)
    for head in range(heads):
        cols = head_cols(head)
        scores = nt(queries[:, cols], keys[:, cols]).astype(BF16) * keep[...]
        local[:, cols] = nn(scores, values[:, cols])


def token_rows(total):
    return jnp.sum(jnp.transpose(total), axis=0, keepdims=True)


def token_columns(row):
    return jnp.transpose(jnp.broadcast_to(row, (HD, row.shape[1])))


def carry_kernel(piece, grid, counts, scale, length, queries, local, cotangent, gain, *rest):
    received, rest = rest[: sum(counts)], rest[sum(counts) :]
    before, (attention, sums, prefix) = rest[: (piece > 0)], rest[-3:]
    parts = split_refs(received, *counts)
    rows, heads = queries.shape[0], prefix.shape[0] // HD
    factor = jnp.where(live_rows(length, rows), scale, 0.0)

    def body(core):
        squares = jnp.zeros((rows, HD), F32)
        products = jnp.zeros((rows, HD), F32)
        for head in range(heads):
            whole = head_cols(piece * heads + head)
            state = arrived_state(parts, core, head, heads // grid[2])
            prefix[head * HD : (head + 1) * HD, :] = state
            out = factor * (nn(queries[:, whole], state) + local[:, whole])
            attention[:, whole] = out
            squares += out * out
            products += out * (cotangent[:, whole].astype(F32) * gain[:, whole])
        both = jnp.concatenate([token_rows(squares), token_rows(products)], axis=0)
        for other in before:
            both += other[...]
        sums[...] = both

    for_each_core(grid, body)


def grad_kernel(groups, grid, scale, length, queries, cotangent, gain, attention, *rest):
    all_sums, (grad_out, inverse_rms, *halves) = rest[:groups], rest[groups:]
    rows = queries.shape[0]
    features = HEADS * HD
    total = all_sums[0][...]
    for other in all_sums[1:]:
        total = total + other[...]
    inverse = lax.rsqrt(total[0:1, :] / features + EPSILON)
    inverse_rms[...] = inverse
    live = lax.broadcasted_iota(jnp.int32, (1, rows), 1) < length[...]
    live_inverse = jnp.where(live, inverse, 0.0)
    shrink = live_inverse * inverse * (inverse * total[1:2, :]) / features
    live_inverse = token_columns(live_inverse)
    shrink = token_columns(shrink)

    def body(core):
        count = halves[0].shape[0] // HD
        for head in range(queries.shape[1] // HD):
            cols = head_cols(head)
            half, within = divmod(head, count)
            gain_grad = cotangent[:, cols].astype(F32) * gain[:, cols]
            grad = (live_inverse * gain_grad - attention[:, cols] * shrink).astype(BF16)
            grad_out[:, cols] = grad
            state = (scale * tn(queries[:, cols], grad)).astype(BF16)
            halves[half ^ core][within * HD : (within + 1) * HD, :] = state

    for_each_core(grid, body)


def row_copies(source, target, sems):
    rows = target.shape[0]
    chunk = rows // 4 if rows % 64 == 0 else rows
    parts = [pl.ds(step * chunk, chunk) for step in range(rows // chunk)]
    return [pltpu.make_async_copy(source.at[p, :], target.at[p, :], sems.at[j]) for j, p in enumerate(parts)]


def query_kernel(heads, group, scale, length, inverse_rms, gain, queries, keys, values, grads, attention, block, *rest):
    prefix, rest = split_refs(rest, FORWARD_PIECES, len(rest) - FORWARD_PIECES)
    attended_hbm, query_hbm, key_part, token, attended, query_grad, keep, sems = rest
    token[...] = block[...]
    write_mask(length, keep, False)
    inverse = token_columns(inverse_rms[...])
    copies = []
    for head in range(heads):
        cols = head_cols(head)
        grad = grads[:, cols]
        per_piece = heads // FORWARD_PIECES
        prefix_piece, state = prefix[head // per_piece], head % per_piece
        grad_scores = nt(grad, values[:, cols]).astype(BF16) * keep[...]
        carried = nt(grad, prefix_piece[state * HD : (state + 1) * HD, :])
        query_grad[:, cols] = (scale * (carried + nn(grad_scores, keys[:, cols]))).astype(BF16)
        key_part[:, cols] = scale * tn(grad_scores, queries[:, cols])
        attended[:, cols] = (attention[:, cols] * inverse * gain[:, cols]).astype(BF16)
        if (head + 1) % group == 0:
            step = head // group
            done = slice(step * group * HD, (head + 1) * HD)
            for j, (src, dst) in enumerate(((attended, attended_hbm), (query_grad, query_hbm))):
                copy = pltpu.make_async_copy(src.at[:, done], dst.at[:, done], sems.at[step, j])
                copy.start()
                copies.append(copy)
    for copy in copies:
        copy.wait()


def value_kernel(first, scale, length, queries, keys, grads, *rest):
    value_part, keep = rest[-2:]
    write_mask(length, keep, True)
    for head in range(value_part.shape[1] // HD):
        whole = head_cols(first + head)
        turned = nt(keys[:, whole], queries[:, whole]).astype(BF16) * keep[...]
        value_part[:, head_cols(head)] = scale * nn(turned, grads[:, whole])


def final_kernel(begin, count, grid, counts, length, keys, values, key_part, *rest):
    value_parts, received, rest = split_refs(rest, VALUE_PIECES, sum(counts), len(rest) - VALUE_PIECES - sum(counts))
    key_hbm, value_hbm, key_grad, value_grad, sems = rest[-5:]
    parts = split_refs(received, *counts)
    pair = grid[2]
    rows = keys.shape[0]
    live = jnp.where(live_rows(length, rows), 1.0, 0.0)

    def body(core):
        copies, pending = [], 0
        for head in range(pair * count):
            half, within = divmod(head, count)
            cols = head_cols(head)
            place = half * (keys.shape[1] // HD // pair) + begin + within
            whole = head_cols(place)
            state = arrived_state(parts, core, head, count)
            key_grad[:, cols] = (key_part[:, whole] + live * nt(values[:, whole], state)).astype(BF16)
            number, inner = divmod(place, value_parts[0].shape[1] // HD)
            value_part = value_parts[number][:, head_cols(inner)]
            value_grad[:, cols] = (value_part + live * nn(keys[:, whole], state)).astype(BF16)
            pending += 1
            if pending == 2 or within == count - 1:
                done = slice((head + 1 - pending) * HD, (head + 1) * HD)
                there = slice((place + 1 - pending) * HD, (place + 1) * HD)
                pending = 0
                for j, (src, dst) in enumerate(((key_grad, key_hbm), (value_grad, value_hbm))):
                    copy = pltpu.make_async_copy(src.at[:, done], dst.at[:, there], sems.at[j, head])
                    copy.start()
                    copies.append(copy)
        for copy in copies:
            copy.wait()

    for_each_core(grid, body)


def in_hbm(x):
    return pltpu.with_memory_space_constraint(x, pltpu.HBM)


def call(kernel, out_shape, operands, scratch=(), flops=0, stream=(), scalars=(), after=(), out_specs=None, aliases=None):
    moved = sum(math.prod(x.shape) * x.dtype.itemsize for x in operands)
    moved += sum(math.prod(x.shape) * x.dtype.itemsize for x in out_shape)
    specs = [SMEM if j in scalars else HBM if j in stream else VMEM for j in range(len(operands))]
    operands = [in_hbm(x) if j in stream else x for j, x in enumerate(operands)]
    return pl.pallas_call(
        kernel,
        out_shape=out_shape,
        in_specs=specs + [ANY] * len(after),
        out_specs=out_specs or [VMEM] * len(out_shape),
        scratch_shapes=list(scratch),
        input_output_aliases=aliases or {},
        compiler_params=pltpu.CompilerParams(vmem_limit_bytes=VMEM_LIMIT),
        cost_estimate=pl.CostEstimate(flops=flops, bytes_accessed=moved, transcendentals=0),
    )(*operands, *after)


def line_send(block, grid, step, flip, gather):
    moves = []
    for device in range(grid[0] * grid[1] * grid[2]):
        place = place_of(grid, device)
        if gather and flip:
            row, column, valid = along(grid, (place[0], place[1], place[2] ^ 1), step, True, True)
        else:
            row, column, valid = along(grid, place, step, gather, True)
        if valid:
            moves.append((device, member(grid, row, column, place[2] ^ flip)))
    return lax.ppermute(block, "seg", moves)


def gather_line(halves, grid, swapped=None):
    pair = grid[2]
    arrived = {0: halves[0]}
    for step in range(line_length(grid)):
        for flip in range(pair):
            if step or flip:
                arrived[step * pair + flip] = line_send(halves[flip] if step or swapped is None else swapped, grid, step, flip, True)
    return [arrived[j] for j in range(len(arrived))]


def scatter_line(sums, grid):
    pair = grid[2]
    parts = [[] for _ in range(pair)]
    for step in reversed(range(line_length(grid))):
        for flip in range(pair):
            block = sums[step * pair + flip]
            parts[flip].append(line_send(block, grid, step, flip, False) if step or flip else block)
    return parts


def token_sums(sums, groups):
    parts = [sums]
    for step in [j for j in range(1, groups) if j != 2] + [2] * (groups > 2):
        moves = [(j, target_of(j, step, groups)) for j in range(groups)]
        parts.append(lax.ppermute(sums, "head", moves))
    return parts


def per_device(segs, groups, queries, key_rows, values, cotangent, out_gain, parent, seg_len):
    rows, features = queries.shape[1:]
    heads = features // HD
    grid = grid_of(segs)
    pair = grid[2]
    scale = 1.0 / math.sqrt(HD * rows)
    cot = cotangent[0]
    gain = out_gain[None]
    shape = jax.ShapeDtypeStruct
    narrow = shape((rows, features), BF16)
    wide = shape((rows, features), F32)
    row = shape((1, rows), F32)
    members = line_length(grid) * pair
    weight_rows = shape((members * members, HD), F32)
    sems = pltpu.SemaphoreType.DMA((2, heads))
    mask = pltpu.VMEM((rows, rows), BF16)
    counts = [line_length(grid)] * pair
    unit = 2 * heads * rows * HD

    def halves(pieces):
        return [shape((features // (pair * pieces), HD), BF16)] * pair

    def mix(arrived, weights, first, tall, after=()):
        like = [shape((tall, HD), BF16)] * members
        return call(functools.partial(mix_kernel, members, first), like, (weights, *arrived), after=after)

    def flat(parts):
        return [block for part in parts for block in part]

    key, value, length, up, down, *own = call(
        functools.partial(state_kernel, grid),
        [narrow, narrow, shape((1, rows), jnp.int32), weight_rows, weight_rows] + halves(FORWARD_PIECES),
        (seg_len, key_rows[0], values[0], parent[None]),
        [sems, pltpu.SMEM((1, segs), jnp.int32), pltpu.SemaphoreType.DMA(())],
        unit * HD // FORWARD_PIECES, (1, 2, 3), (0,),
    )
    for piece in range(1, FORWARD_PIECES):
        own += call(
            functools.partial(next_state_kernel, piece, grid), halves(FORWARD_PIECES),
            (length, key, value), (), unit * HD // FORWARD_PIECES,
        )
    (query,) = call(fetch_kernel, [narrow], (queries[0],), [pltpu.SemaphoreType.DMA((4,))], 0, (0,), after=(own[0],))
    mixed = []
    for part in split_refs(own, *[pair] * FORWARD_PIECES):
        mixed.append(mix(gather_line(part, grid), up, 0, part[0].shape[0], () if mixed else (query,)))
    (local,) = call(
        functools.partial(local_kernel, heads),
        [wide], (length, query, key, value), [mask], unit * rows * 2, after=(mixed[0][0],),
    )
    attention, prefix, sums = [], [], []
    width = features // FORWARD_PIECES
    for piece in range(FORWARD_PIECES):
        blocks = flat(scatter_line(mixed[piece], grid))
        operands = (length, query, local, cot, gain, *blocks, *sums, *attention)
        out, total, joined = call(
            functools.partial(carry_kernel, piece, grid, counts, scale),
            [wide, shape((2, rows), F32), shape((width, HD), BF16)], operands,
            (), unit * HD // FORWARD_PIECES, aliases={len(operands) - 1: 0} if attention else None,
        )
        attention, sums = [out], [total]
        prefix.append(joined)
    (attention,) = attention
    sums = token_sums(sums[0], groups)
    grads, inverse_rms, *state_grad = call(
        functools.partial(grad_kernel, len(sums), grid, scale),
        [narrow, row] + halves(1), (length, query, cot, gain, attention, *sums),
        (), unit * HD,
    )
    group = 4 if heads % 4 == 0 else 1
    attended, query_grad, key_part, token = call(
        functools.partial(query_kernel, heads, group, scale),
        [narrow, narrow, wide, shape(state_grad[-1].shape, BF16)],
        (length, inverse_rms, gain, query, key, value, grads, attention, state_grad[-1], *prefix),
        [pltpu.VMEM(narrow.shape, BF16)] * 2 + [mask, pltpu.SemaphoreType.DMA((heads // group, 2))],
        unit * (3 * rows + HD), out_specs=[HBM, HBM, VMEM, VMEM],
    )
    def value_piece(number, after):
        width = features // VALUE_PIECES
        (out,) = call(
            functools.partial(value_kernel, number * heads // VALUE_PIECES, scale),
            [shape((rows, width), F32)], (length, query, key, grads), [mask], unit * 2 * rows // VALUE_PIECES,
            after=after,
        )
        return out

    value_parts = [value_piece(0, (token,))]
    arrived = gather_line(state_grad, grid, token)
    half_heads = heads // pair
    last = max(half_heads * 3 // 8, min(half_heads - 1, 1))
    pieces = [(0, half_heads - last), (half_heads - last, last)] if last else [(0, half_heads)]
    mixed = []
    for begin, count in pieces:
        before = (value_parts[0], *mixed[-1][:1]) if mixed else (value_parts[0],)
        mixed.append(mix(arrived, down, begin * HD, count * HD, before))
    value_parts += [value_piece(number, (mixed[-1][0],)) for number in range(1, VALUE_PIECES)]
    results = []
    for (begin, count), sums in zip(pieces, mixed):
        below = flat(scatter_line(sums, grid))
        operands = (length, key, value, key_part, *value_parts, *below, *results)
        first = len(operands) - len(results)
        width = pair * count * HD
        results = call(
            functools.partial(final_kernel, begin, count, grid, counts),
            [narrow, narrow], operands,
            [pltpu.VMEM((rows, width), BF16)] * 2 + [sems],
            2 * unit * HD * pair * count // heads,
            range(first, len(operands)), out_specs=[HBM, HBM],
            aliases={first + j: j for j in range(len(results))},
        )
    key_grad, value_grad = results
    return attended[None], query_grad[None], key_grad[None], value_grad[None]


def solution(mesh):
    split = P("seg", None, "head")
    return jax.shard_map(
        functools.partial(per_device, mesh.shape["seg"], mesh.shape["head"]),
        mesh=mesh,
        in_specs=(split, split, split, split, P("head"), P(), P("seg")),
        out_specs=(split, split, split, split),
        check_vma=False,
    )
```

```python
import functools
import math

import jax
import jax.numpy as jnp
from jax import lax
from jax.experimental import pallas as pl
from jax.experimental.pallas import tpu as pltpu
from jax.sharding import PartitionSpec as P

HEADS = 64
HD = 128
EPSILON = 1e-06
F32 = jnp.float32
BF16 = jnp.bfloat16
VMEM_LIMIT = 24 * 1024 * 1024
FORWARD_PIECES = 2
VALUE_PIECES = 2

VMEM = pl.BlockSpec(memory_space=pltpu.VMEM)
SMEM = pl.BlockSpec(memory_space=pltpu.SMEM)
HBM = pl.BlockSpec(memory_space=pltpu.HBM)
ANY = pl.BlockSpec(memory_space=pl.ANY)


def dot(a, b, contract):
    return lax.dot_general(a, b, (contract, ((), ())), preferred_element_type=F32)


def nn(a, b):
    return dot(a, b, ((1,), (0,)))


def nt(a, b):
    return dot(a, b, ((1,), (1,)))


def tn(a, b):
    return dot(a, b, ((0,), (0,)))


def head_cols(head):
    return slice(head * HD, (head + 1) * HD)


def target_of(place, step, size):
    if size & (size - 1) == 0:
        return place ^ step
    return (place + step) % size


def source_of(place, step, size):
    if size & (size - 1) == 0:
        return place ^ step
    return (place + size - step) % size


def grid_of(segs):
    pair = 2 if segs % 2 == 0 else 1
    chips = segs // pair
    columns = next(c for c in range(1, chips + 1) if chips % c == 0 and c * c >= chips)
    return chips // columns, columns, pair


def member(grid, row, column, core):
    return (row * grid[1] + column) * grid[2] + core


def place_of(grid, device):
    chip = device // grid[2]
    return chip // grid[1], chip % grid[1], device % grid[2]


def along(grid, place, step, gather, ahead):
    row, column, core = place
    shift = target_of if ahead else source_of
    by_row = (core == 0) if gather else (core != 0)
    valid_column = step < grid[1]
    valid_row = step < grid[0]
    if isinstance(core, int):
        if by_row:
            return row, shift(column, step, grid[1]), valid_column
        return shift(row, step, grid[0]), column, valid_row
    moved_column = shift(column, min(step, grid[1] - 1), grid[1])
    moved_row = shift(row, min(step, grid[0] - 1), grid[0])
    return (
        jnp.where(by_row, row, moved_row),
        jnp.where(by_row, moved_column, column),
        jnp.where(by_row, valid_column, valid_row),
    )


def my_place(grid):
    me = lax.axis_index("seg")
    chip = lax.div(me, grid[2])
    return lax.div(chip, grid[1]), lax.rem(chip, grid[1]), lax.rem(me, grid[2])


def for_each_core(grid, body):
    core = my_place(grid)[2]
    for number in range(grid[2]):
        pl.when(core == number)(functools.partial(body, number))


def arrived_state(parts, core, head, count):
    half, within = divmod(head, count)
    terms = [term[within * HD : (within + 1) * HD, :].astype(F32) for term in parts[half ^ core]]
    return sum(terms[1:], terms[0]).astype(BF16)


def line_length(grid):
    return max(grid[0], grid[1])


def write_weights(grid, parent, up, down):
    place = my_place(grid)
    pair = grid[2]
    count = line_length(grid) * pair

    def is_ancestor(child, other):
        first = parent[0, child]
        second = jnp.where(first >= 0, parent[0, jnp.maximum(first, 0)], -1)
        return jnp.logical_or(other == first, other == second)

    for out_step in range(count):
        row, column, _ = along(grid, place, out_step // pair, False, True)
        target = member(grid, row, column, place[2] ^ (out_step % pair))
        for in_step in range(count):
            row, column, valid = along(grid, place, in_step // pair, True, False)
            source = member(grid, row, column, place[2] ^ (in_step % pair))
            at = out_step * count + in_step
            for rows, used in ((up, is_ancestor(target, source)), (down, is_ancestor(source, target))):
                weight = jnp.where(jnp.logical_and(used, valid), 1.0, 0.0)
                rows[at : at + 1, :] = jnp.full((1, HD), weight, F32)


def own_states(piece, grid, keys, values, live, outs):
    def body(core):
        count = outs[0].shape[0] // HD
        for head in range(count * len(outs)):
            half, within = divmod(head, count)
            cols = head_cols(piece * count * len(outs) + head)
            masked = jnp.where(live, keys[:, cols], jnp.zeros((), BF16))
            outs[half ^ core][within * HD : (within + 1) * HD, :] = tn(masked, values[:, cols]).astype(BF16)

    for_each_core(grid, body)


def state_kernel(grid, seg_len, keys_hbm, values_hbm, parent_hbm, keys, values, length, up, down, *rest):
    outs, (sems, parent, parent_sem) = rest[:-3], rest[-3:]
    rows, width = keys.shape
    chunk = rows // 2 if rows % 32 == 0 else rows
    steps = rows // chunk
    first = width // FORWARD_PIECES
    spans = [slice(0, first), slice(first, width)][:FORWARD_PIECES]
    copies = []
    for number, cols in enumerate(spans):
        for step in range(steps):
            part = slice(step * chunk, (step + 1) * chunk)
            for j, (src, dst) in enumerate(((keys_hbm, keys), (values_hbm, values))):
                copies.append(
                    pltpu.make_async_copy(src.at[part, cols], dst.at[part, cols], sems.at[j, number * steps + step])
                )
    few = pltpu.make_async_copy(parent_hbm, parent, parent_sem)
    few.start()
    for copy in copies:
        copy.start()
    length[...] = jnp.full(length.shape, seg_len[0], jnp.int32)
    few.wait()
    write_weights(grid, parent, up, down)
    live = lax.broadcasted_iota(jnp.int32, (rows, HD), 0) < seg_len[0]
    for copy in copies[: 2 * steps]:
        copy.wait()
    own_states(0, grid, keys, values, live, outs)
    for copy in copies[2 * steps :]:
        copy.wait()


def next_state_kernel(piece, grid, length, keys, values, block, *outs):
    outs, handed = outs[:-1], outs[-1]
    handed[...] = block[...]
    own_states(piece, grid, keys, values, live_rows(length, keys.shape[0]), outs)


def mix_kernel(sources, first, weights, *refs):
    blocks, outs = refs[:sources], refs[-sources:]
    rows = outs[0].shape[0]
    chunk = min(rows, 64)
    for start in range(0, rows, chunk):
        part = slice(start, start + chunk)
        loaded = [block[first + start : first + start + chunk, :].astype(F32) for block in blocks]
        for out_step, out in enumerate(outs):
            at = out_step * sources
            total = weights[at : at + 1, :] * loaded[0]
            for in_step in range(1, sources):
                total += weights[at + in_step : at + in_step + 1, :] * loaded[in_step]
            out[part, :] = total.astype(BF16)


def live_rows(length, rows):
    return lax.broadcasted_iota(jnp.int32, (rows, HD), 0) < length[:, :HD]


def write_mask(length, keep, turned):
    rows = length.shape[1]
    first = lax.broadcasted_iota(jnp.int32, (rows, rows), 0)
    second = lax.broadcasted_iota(jnp.int32, (rows, rows), 1)
    if turned:
        used = (first <= second) & (first < length[...])
    else:
        used = (second <= first) & (second < length[...])
    keep[...] = jnp.where(used, 1.0, 0.0).astype(BF16)


def split_refs(refs, *counts):
    parts, at = [], 0
    for count in counts:
        parts.append(refs[at : at + count])
        at += count
    return parts


def fetch_kernel(source, _, out, sems):
    copies = row_copies(source, out, sems)
    for copy in copies:
        copy.start()
    for copy in copies:
        copy.wait()


def local_kernel(heads, length, queries, keys, values, *rest):
    local, keep = rest[-2:]
    write_mask(length, keep, False)
    for head in range(heads):
        cols = head_cols(head)
        scores = nt(queries[:, cols], keys[:, cols]).astype(BF16) * keep[...]
        local[:, cols] = nn(scores, values[:, cols])


def token_rows(total):
    return jnp.sum(jnp.transpose(total), axis=0, keepdims=True)


def token_columns(row):
    return jnp.transpose(jnp.broadcast_to(row, (HD, row.shape[1])))


def carry_kernel(piece, grid, counts, scale, length, queries, local, cotangent, gain, *rest):
    received, rest = rest[: sum(counts)], rest[sum(counts) :]
    before, (attention, sums, prefix) = rest[: (piece > 0)], rest[-3:]
    parts = split_refs(received, *counts)
    rows, heads = queries.shape[0], prefix.shape[0] // HD
    factor = jnp.where(live_rows(length, rows), scale, 0.0)

    def body(core):
        squares = jnp.zeros((rows, HD), F32)
        products = jnp.zeros((rows, HD), F32)
        for head in range(heads):
            whole = head_cols(piece * heads + head)
            state = arrived_state(parts, core, head, heads // grid[2])
            prefix[head * HD : (head + 1) * HD, :] = state
            out = factor * (nn(queries[:, whole], state) + local[:, whole])
            attention[:, whole] = out
            squares += out * out
            products += out * (cotangent[:, whole].astype(F32) * gain[:, whole])
        both = jnp.concatenate([token_rows(squares), token_rows(products)], axis=0)
        for other in before:
            both += other[...]
        sums[...] = both

    for_each_core(grid, body)


def grad_kernel(groups, grid, scale, length, queries, cotangent, gain, attention, *rest):
    all_sums, (grad_out, inverse_rms, *halves) = rest[:groups], rest[groups:]
    rows = queries.shape[0]
    features = HEADS * HD
    total = all_sums[0][...]
    for other in all_sums[1:]:
        total = total + other[...]
    inverse = lax.rsqrt(total[0:1, :] / features + EPSILON)
    inverse_rms[...] = inverse
    live = lax.broadcasted_iota(jnp.int32, (1, rows), 1) < length[...]
    live_inverse = jnp.where(live, inverse, 0.0)
    shrink = live_inverse * inverse * (inverse * total[1:2, :]) / features
    live_inverse = token_columns(live_inverse)
    shrink = token_columns(shrink)

    def body(core):
        count = halves[0].shape[0] // HD
        for head in range(queries.shape[1] // HD):
            cols = head_cols(head)
            half, within = divmod(head, count)
            gain_grad = cotangent[:, cols].astype(F32) * gain[:, cols]
            grad = (live_inverse * gain_grad - attention[:, cols] * shrink).astype(BF16)
            grad_out[:, cols] = grad
            state = (scale * tn(queries[:, cols], grad)).astype(BF16)
            halves[half ^ core][within * HD : (within + 1) * HD, :] = state

    for_each_core(grid, body)


def row_copies(source, target, sems):
    rows = target.shape[0]
    chunk = rows // 4 if rows % 64 == 0 else rows
    parts = [pl.ds(step * chunk, chunk) for step in range(rows // chunk)]
    return [pltpu.make_async_copy(source.at[p, :], target.at[p, :], sems.at[j]) for j, p in enumerate(parts)]


def query_kernel(heads, group, scale, length, inverse_rms, gain, queries, keys, values, grads, attention, block, *rest):
    prefix, rest = split_refs(rest, FORWARD_PIECES, len(rest) - FORWARD_PIECES)
    attended_hbm, query_hbm, key_part, token, attended, query_grad, keep, sems = rest
    token[...] = block[...]
    write_mask(length, keep, False)
    inverse = token_columns(inverse_rms[...])
    copies = []
    for head in range(heads):
        cols = head_cols(head)
        grad = grads[:, cols]
        per_piece = heads // FORWARD_PIECES
        prefix_piece, state = prefix[head // per_piece], head % per_piece
        grad_scores = nt(grad, values[:, cols]).astype(BF16) * keep[...]
        carried = nt(grad, prefix_piece[state * HD : (state + 1) * HD, :])
        query_grad[:, cols] = (scale * (carried + nn(grad_scores, keys[:, cols]))).astype(BF16)
        key_part[:, cols] = scale * tn(grad_scores, queries[:, cols])
        attended[:, cols] = (attention[:, cols] * inverse * gain[:, cols]).astype(BF16)
        if (head + 1) % group == 0:
            step = head // group
            done = slice(step * group * HD, (head + 1) * HD)
            for j, (src, dst) in enumerate(((attended, attended_hbm), (query_grad, query_hbm))):
                copy = pltpu.make_async_copy(src.at[:, done], dst.at[:, done], sems.at[step, j])
                copy.start()
                copies.append(copy)
    for copy in copies:
        copy.wait()


def value_kernel(first, scale, length, queries, keys, grads, *rest):
    value_part, keep = rest[-2:]
    write_mask(length, keep, True)
    for head in range(value_part.shape[1] // HD):
        whole = head_cols(first + head)
        turned = nt(keys[:, whole], queries[:, whole]).astype(BF16) * keep[...]
        value_part[:, head_cols(head)] = scale * nn(turned, grads[:, whole])


def final_kernel(begin, count, grid, counts, length, keys, values, key_part, *rest):
    value_parts, received, rest = split_refs(rest, VALUE_PIECES, sum(counts), len(rest) - VALUE_PIECES - sum(counts))
    key_hbm, value_hbm, key_grad, value_grad, sems = rest[-5:]
    parts = split_refs(received, *counts)
    pair = grid[2]
    rows = keys.shape[0]
    live = jnp.where(live_rows(length, rows), 1.0, 0.0)

    def body(core):
        copies, pending = [], 0
        for head in range(pair * count):
            half, within = divmod(head, count)
            cols = head_cols(head)
            place = half * (keys.shape[1] // HD // pair) + begin + within
            whole = head_cols(place)
            state = arrived_state(parts, core, head, count)
            key_grad[:, cols] = (key_part[:, whole] + live * nt(values[:, whole], state)).astype(BF16)
            number, inner = divmod(place, value_parts[0].shape[1] // HD)
            value_part = value_parts[number][:, head_cols(inner)]
            value_grad[:, cols] = (value_part + live * nn(keys[:, whole], state)).astype(BF16)
            pending += 1
            if pending == 2 or within == count - 1:
                done = slice((head + 1 - pending) * HD, (head + 1) * HD)
                there = slice((place + 1 - pending) * HD, (place + 1) * HD)
                pending = 0
                for j, (src, dst) in enumerate(((key_grad, key_hbm), (value_grad, value_hbm))):
                    copy = pltpu.make_async_copy(src.at[:, done], dst.at[:, there], sems.at[j, head])
                    copy.start()
                    copies.append(copy)
        for copy in copies:
            copy.wait()

    for_each_core(grid, body)


def in_hbm(x):
    return pltpu.with_memory_space_constraint(x, pltpu.HBM)


def call(kernel, out_shape, operands, scratch=(), flops=0, stream=(), scalars=(), after=(), out_specs=None, aliases=None):
    moved = sum(math.prod(x.shape) * x.dtype.itemsize for x in operands)
    moved += sum(math.prod(x.shape) * x.dtype.itemsize for x in out_shape)
    specs = [SMEM if j in scalars else HBM if j in stream else VMEM for j in range(len(operands))]
    operands = [in_hbm(x) if j in stream else x for j, x in enumerate(operands)]
    return pl.pallas_call(
        kernel,
        out_shape=out_shape,
        in_specs=specs + [ANY] * len(after),
        out_specs=out_specs or [VMEM] * len(out_shape),
        scratch_shapes=list(scratch),
        input_output_aliases=aliases or {},
        compiler_params=pltpu.CompilerParams(vmem_limit_bytes=VMEM_LIMIT),
        cost_estimate=pl.CostEstimate(flops=flops, bytes_accessed=moved, transcendentals=0),
    )(*operands, *after)


def line_send(block, grid, step, flip, gather):
    moves = []
    for device in range(grid[0] * grid[1] * grid[2]):
        place = place_of(grid, device)
        if gather and flip:
            row, column, valid = along(grid, (place[0], place[1], place[2] ^ 1), step, True, True)
        else:
            row, column, valid = along(grid, place, step, gather, True)
        if valid:
            moves.append((device, member(grid, row, column, place[2] ^ flip)))
    return lax.ppermute(block, "seg", moves)


def gather_line(halves, grid, swapped=None):
    pair = grid[2]
    arrived = {0: halves[0]}
    for step in range(line_length(grid)):
        for flip in range(pair):
            if step or flip:
                arrived[step * pair + flip] = line_send(halves[flip] if step or swapped is None else swapped, grid, step, flip, True)
    return [arrived[j] for j in range(len(arrived))]


def scatter_line(sums, grid):
    pair = grid[2]
    parts = [[] for _ in range(pair)]
    for step in reversed(range(line_length(grid))):
        for flip in range(pair):
            block = sums[step * pair + flip]
            parts[flip].append(line_send(block, grid, step, flip, False) if step or flip else block)
    return parts


def token_sums(sums, groups):
    parts = [sums]
    for step in [j for j in range(1, groups) if j != 2] + [2] * (groups > 2):
        moves = [(j, target_of(j, step, groups)) for j in range(groups)]
        parts.append(lax.ppermute(sums, "head", moves))
    return parts


def per_device(segs, groups, queries, key_rows, values, cotangent, out_gain, parent, seg_len):
    rows, features = queries.shape[1:]
    heads = features // HD
    grid = grid_of(segs)
    pair = grid[2]
    scale = 1.0 / math.sqrt(HD * rows)
    cot = cotangent[0]
    gain = out_gain[None]
    shape = jax.ShapeDtypeStruct
    narrow = shape((rows, features), BF16)
    wide = shape((rows, features), F32)
    row = shape((1, rows), F32)
    members = line_length(grid) * pair
    weight_rows = shape((members * members, HD), F32)
    sems = pltpu.SemaphoreType.DMA((2, heads))
    mask = pltpu.VMEM((rows, rows), BF16)
    counts = [line_length(grid)] * pair
    unit = 2 * heads * rows * HD

    def halves(pieces):
        return [shape((features // (pair * pieces), HD), BF16)] * pair

    def mix(arrived, weights, first, tall, after=()):
        like = [shape((tall, HD), BF16)] * members
        return call(functools.partial(mix_kernel, members, first), like, (weights, *arrived), after=after)

    def flat(parts):
        return [block for part in parts for block in part]

    key, value, length, up, down, *own = call(
        functools.partial(state_kernel, grid),
        [narrow, narrow, shape((1, rows), jnp.int32), weight_rows, weight_rows] + halves(FORWARD_PIECES),
        (seg_len, key_rows[0], values[0], parent[None]),
        [sems, pltpu.SMEM((1, segs), jnp.int32), pltpu.SemaphoreType.DMA(())],
        unit * HD // FORWARD_PIECES, (1, 2, 3), (0,),
    )
    swapped = []
    for piece in range(1, FORWARD_PIECES):
        *states, handed = call(
            functools.partial(next_state_kernel, piece, grid), halves(FORWARD_PIECES) + halves(FORWARD_PIECES)[:1],
            (length, key, value, own[-1]), (), unit * HD // FORWARD_PIECES,
        )
        own += states
        swapped.append(handed)
    (query,) = call(fetch_kernel, [narrow], (queries[0],), [pltpu.SemaphoreType.DMA((4,))], 0, (0,), after=(own[0],))
    mixed = []
    for part in split_refs(own, *[pair] * FORWARD_PIECES):
        late = swapped[len(mixed)] if len(mixed) < len(swapped) else None
        mixed.append(mix(gather_line(part, grid, late), up, 0, part[0].shape[0], () if mixed else (query,)))
    (local,) = call(
        functools.partial(local_kernel, heads),
        [wide], (length, query, key, value), [mask], unit * rows * 2, after=(mixed[0][0],),
    )
    attention, prefix, sums = [], [], []
    width = features // FORWARD_PIECES
    for piece in range(FORWARD_PIECES):
        blocks = flat(scatter_line(mixed[piece], grid))
        operands = (length, query, local, cot, gain, *blocks, *sums, *attention)
        out, total, joined = call(
            functools.partial(carry_kernel, piece, grid, counts, scale),
            [wide, shape((2, rows), F32), shape((width, HD), BF16)], operands,
            (), unit * HD // FORWARD_PIECES, aliases={len(operands) - 1: 0} if attention else None,
        )
        attention, sums = [out], [total]
        prefix.append(joined)
    (attention,) = attention
    sums = token_sums(sums[0], groups)
    grads, inverse_rms, *state_grad = call(
        functools.partial(grad_kernel, len(sums), grid, scale),
        [narrow, row] + halves(1), (length, query, cot, gain, attention, *sums),
        (), unit * HD,
    )
    group = 4 if heads % 4 == 0 else 1
    attended, query_grad, key_part, token = call(
        functools.partial(query_kernel, heads, group, scale),
        [narrow, narrow, wide, shape(state_grad[-1].shape, BF16)],
        (length, inverse_rms, gain, query, key, value, grads, attention, state_grad[-1], *prefix),
        [pltpu.VMEM(narrow.shape, BF16)] * 2 + [mask, pltpu.SemaphoreType.DMA((heads // group, 2))],
        unit * (3 * rows + HD), out_specs=[HBM, HBM, VMEM, VMEM],
    )
    def value_piece(number, after):
        width = features // VALUE_PIECES
        (out,) = call(
            functools.partial(value_kernel, number * heads // VALUE_PIECES, scale),
            [shape((rows, width), F32)], (length, query, key, grads), [mask], unit * 2 * rows // VALUE_PIECES,
            after=after,
        )
        return out

    value_parts = [value_piece(0, (token,))]
    arrived = gather_line(state_grad, grid, token)
    half_heads = heads // pair
    last = max(half_heads * 3 // 8, min(half_heads - 1, 1))
    pieces = [(0, half_heads - last), (half_heads - last, last)] if last else [(0, half_heads)]
    mixed = []
    for begin, count in pieces:
        before = (value_parts[0], *mixed[-1][:1]) if mixed else (value_parts[0],)
        mixed.append(mix(arrived, down, begin * HD, count * HD, before))
    value_parts += [value_piece(number, (mixed[-1][0],)) for number in range(1, VALUE_PIECES)]
    results = []
    for (begin, count), sums in zip(pieces, mixed):
        below = flat(scatter_line(sums, grid))
        operands = (length, key, value, key_part, *value_parts, *below, *results)
        first = len(operands) - len(results)
        width = pair * count * HD
        results = call(
            functools.partial(final_kernel, begin, count, grid, counts),
            [narrow, narrow], operands,
            [pltpu.VMEM((rows, width), BF16)] * 2 + [sems],
            2 * unit * HD * pair * count // heads,
            range(first, len(operands)), out_specs=[HBM, HBM],
            aliases={first + j: j for j in range(len(results))},
        )
    key_grad, value_grad = results
    return attended[None], query_grad[None], key_grad[None], value_grad[None]


def solution(mesh):
    split = P("seg", None, "head")
    return jax.shard_map(
        functools.partial(per_device, mesh.shape["seg"], mesh.shape["head"]),
        mesh=mesh,
        in_specs=(split, split, split, split, P("head"), P(), P("seg")),
        out_specs=(split, split, split, split),
        check_vma=False,
    )
```
